32 devices in a mesh: gx: 8 (over z, y), gy: 4 (over x, core).
Axes of the slice: x: 2, y: 2, z: 4, core: 2. Of those that a mesh axis runs over, the one named last changes fastest.
Arguments:
- hamiltonian: float32 [8, 4, 5, 128, 128], P('gx', 'gy'), may hold values from -0.25 to 0.25
- inverse_margin: float32 [8, 4, 5, 128, 128], P('gx', 'gy'), may hold values from -0.25 to 0.25
- density: float32 [2, 8, 4, 5, 128, 128], P(None, 'gx', 'gy'), may hold values from -6 to 6
- cutoff: int32 [8, 4, 5], P('gx', 'gy'), may hold values 0 or 1
- derivative: float32 [3, 8, 4, 5, 128, 128], P(None, 'gx', 'gy'), may hold values from -0.046875 to 0.046875
- atom_of: int32 [8, 4, 128], P('gx', 'gy'), may hold values from 0 to 63, as said below
Outputs:
- new_density: float32 [2, 8, 4, 5, 128, 128], P(None, 'gx', 'gy')
- forces: float32 [8, 4, 3, 64], P('gx', 'gy')
The draws below stay inside these ranges and needn't reach their ends.
Inputs may be any that keep to these rules, and one draw needn't show every extreme that they name: `atom_of`: within each group the map never falls and each of the 64 atoms owns at least one of the 128 orbitals.
All inputs are finite; a program needn't handle non-finite values. No bound on the sum of `cutoff` on one device may be relied on, other than what follows from the above.
Results may differ from the reference program's by a relative error of at most 0.0001.
Values sent between devices are 32-bit elements; how exact they have to be, the bound alone decides.
No kernel may reach another device: no remote copies, remote signals or barrier semaphores. Data moves between devices by JAX's collectives and lax.ppermute only.
A program may use at most 64 MiB of HBM per device.

```python
import jax
import jax.numpy as jnp
from jax import lax

B = 128
ATOMS = 64
STEPS = 1
CELLS_X = 8
CELLS_Y = 4


def draw_atom_of(key, part):
    scores = jax.random.randint(key, (CELLS_X, CELLS_Y, B - 1), 0, 1048576)
    scores = scores * B + jnp.arange(B - 1, dtype=jnp.int32)
    ranks = jnp.argsort(jnp.argsort(scores, axis=-1), axis=-1)
    breaks = (ranks < ATOMS - 1).astype(jnp.int32)
    counted = jnp.cumsum(breaks, axis=-1).astype(jnp.int32)
    first = jnp.zeros((CELLS_X, CELLS_Y, 1), jnp.int32)
    return jnp.concatenate([first, counted], axis=-1)


def set_ends(array, own_key, low, high):
    shape = array.shape
    place = [jax.random.randint(jax.random.fold_in(own_key, axis), (), 0, shape[axis]) for axis in range(len(shape))]
    array = array.at[tuple(place)].set(low)
    longest = shape.index(max(shape))
    place[longest] = (place[longest] + 1) % shape[longest]
    return array.at[tuple(place)].set(high)


def block_scale(rng, dims, shards, low, largest):
    gain, own = 1.0, jax.random.fold_in(rng, 6)
    for axis_at, blocks in shards:
        draws = jnp.exp(jax.random.uniform(jax.random.fold_in(own, axis_at), (blocks,), jnp.float32, low / len(shards), largest / len(shards)))
        gain = gain * jnp.repeat(draws, dims[axis_at] // blocks).reshape([-1 if axis == axis_at else 1 for axis in range(len(dims))])
    return gain


def gaussian(stream_key, shape, scale, bound, cuts=(), kind=jnp.bfloat16):
    values = jax.random.normal(stream_key, shape, jnp.float32) * scale
    if len(cuts) > 0:
        values = block_scale(stream_key, shape, cuts, -0.22, 0.18) * values
    return jnp.clip(values, min=-bound, max=bound).astype(kind)


def setup_inputs(seed: int = 0) -> dict:
    streams_of = jax.random.split(jax.random.key(seed), 7)
    return {
        "hamiltonian": gaussian(streams_of[0], (CELLS_X, CELLS_Y, 5, B, B), (5 * B) ** -0.5, 0.25, ((0, 8), (1, 4)), jnp.float32),
        "inverse_margin": gaussian(streams_of[1], (CELLS_X, CELLS_Y, 5, B, B), (5 * B) ** -0.5, 0.25, ((0, 8), (1, 4)), jnp.float32),
        "density": gaussian(streams_of[2], (2, CELLS_X, CELLS_Y, 5, B, B), 1.0, 6.0, ((1, 8), (2, 4)), jnp.float32),
        "cutoff": set_ends((jax.random.randint(streams_of[3], (CELLS_X, CELLS_Y, 5), 0, 4) < 3).astype(jnp.int32), jax.random.fold_in(streams_of[3], 1), 0, 1),
        "derivative": gaussian(streams_of[4], (3, CELLS_X, CELLS_Y, 5, B, B), (1.0 / B), 0.046875, ((1, 8), (2, 4)), jnp.float32),
        "atom_of": draw_atom_of(jax.random.fold_in(streams_of[6], 71), 0),
    }


opposite = (0, 2, 1, 4, 3)
time_step = 0.25
highest = lax.Precision.HIGHEST


def neighbour_row(block, offset):
    if offset == 1:
        return jnp.roll(block, -1, 0)
    if offset == 2:
        return jnp.roll(block, 1, 0)
    if offset == 3:
        return jnp.roll(block, -1, 1)
    return jnp.roll(block, 1, 1)


def block_mul(left, right):
    return jnp.einsum("xyuv,xyvw->xyuw", left, right, precision=highest)


def product(left, right, keep):
    diagonal = block_mul(left[:, :, 0], right[:, :, 0])
    others = []
    for offset in range(1, 5):
        diagonal = diagonal + block_mul(left[:, :, offset], neighbour_row(right[:, :, opposite[offset]], offset))
        others.append(block_mul(left[:, :, 0], right[:, :, offset]) + block_mul(left[:, :, offset], neighbour_row(right[:, :, 0], offset)))
    return jnp.stack([diagonal] + others, axis=2) * keep[:, :, :, None, None]


def reference(hamiltonian, inverse_margin, density, cutoff, derivative, atom_of):
    keep = jnp.concatenate([jnp.ones_like(cutoff[:, :, :1]), cutoff[:, :, 1:]], axis=2).astype(jnp.float32)
    weight = keep[:, :, :, None, None]
    ham = hamiltonian * weight
    inverse = inverse_margin * weight
    real_part = density[0] * weight
    imag_part = density[1] * weight
    propagator = product(inverse, ham, keep)
    for step in range(STEPS):
        real_comm = product(propagator, real_part, keep) - product(product(real_part, ham, keep), inverse, keep)
        imag_comm = product(propagator, imag_part, keep) - product(product(imag_part, ham, keep), inverse, keep)
        real_part, imag_part = real_part + time_step * imag_comm, imag_part - time_step * real_comm
    members = (atom_of[:, :, None, :] == jnp.arange(ATOMS, dtype=jnp.int32)[None, None, :, None]).astype(jnp.float32)
    results = []
    for direction in range(3):
        weighted = real_part * (derivative[direction] * weight)
        row_part = jnp.sum(weighted, axis=(2, 4))
        column_part = jnp.sum(weighted, axis=3)
        orbital = row_part + column_part[:, :, 0]
        orbital = orbital + jnp.roll(column_part[:, :, 1], 1, 0) + jnp.roll(column_part[:, :, 2], -1, 0)
        orbital = orbital + jnp.roll(column_part[:, :, 3], 1, 1) + jnp.roll(column_part[:, :, 4], -1, 1)
        results.append(-jnp.einsum("xyaw,xyw->xya", members, orbital, precision=highest))
    forces = jnp.stack(results, axis=2)
    return jnp.stack([real_part, imag_part], 0), forces
```

```python
import functools

import jax
import jax.numpy as jnp
from jax import lax
from jax.experimental import pallas as pl
from jax.experimental.pallas import tpu as pltpu
from jax.sharding import PartitionSpec as P

B = 128
ATOMS = 64

opposite = (0, 2, 1, 4, 3)
time_step = 0.25
vmem = pl.BlockSpec(memory_space=pltpu.VMEM)
smem = pl.BlockSpec(memory_space=pltpu.SMEM)
f32 = jnp.float32
bf16 = jnp.bfloat16


def shifted(cells, offset):
    axis = "gx" if offset < 3 else "gy"
    count = lax.axis_size(axis)
    if offset in (1, 3):
        pairs = [((i + 1) % count, i) for i in range(count)]
    else:
        pairs = [(i, (i + 1) % count) for i in range(count)]
    return lax.ppermute(cells, axis, pairs)


def cols(offset, count=1):
    return slice(offset * B, (offset + count) * B)


def split(values):
    high = values.astype(bf16)
    return high, (values - high.astype(f32)).astype(bf16)


def dot(left, right):
    def one(a, b):
        return jnp.dot(a, b, preferred_element_type=f32)

    return one(left[0], right[0]) + (one(left[0], right[1]) + one(left[1], right[0]))


def part(pair, rows, columns):
    return pair[0][rows, columns], pair[1][rows, columns]


def keep_of(cutoff_ref, offset):
    return cutoff_ref[0, 0, offset].astype(f32)


def first_kernel(cutoff_ref, ham_ref, *outs):
    for offset in range(1, 5):
        back = opposite[offset]
        outs[offset - 1][0] = ham_ref[0, 0, 0]
        outs[offset - 1][1] = ham_ref[0, 0, back] * keep_of(cutoff_ref, back)


def second_kernel(cutoff_ref, ham_ref, inv_ref, rho_ref, send, left_high, left_low, ham_high, ham_low, start):
    for offset in range(5):
        here = cols(offset)
        keep = None if offset == 0 else keep_of(cutoff_ref, offset)
        blocks = (inv_ref[0, 0, offset], rho_ref[0, 0, 0, offset], rho_ref[1, 0, 0, offset])
        for place, block in enumerate(blocks):
            block = block if offset == 0 else block * keep
            if offset == 0:
                send[place] = block
            rows = slice(place * B, (place + 1) * B)
            left_high[rows, here], left_low[rows, here] = split(block)
        block = ham_ref[0, 0, offset]
        block = block if offset == 0 else block * keep
        ham_high[:, here], ham_low[:, here] = split(block)
    every = slice(0, 3 * B)
    left = (left_high, left_low)
    ham = (ham_high, ham_low)
    start[...] = dot(part(left, every, cols(0)), part(ham, slice(0, B), slice(0, 5 * B)))


def third_kernel(cutoff_ref, inv_ref, rho_ref, start, left_high, left_low, one, two, three, four, *outs):
    sends = outs[:4]
    mixed_high, mixed_low, base = outs[4:]
    for offset in range(1, 5):
        back = opposite[offset]
        keep = keep_of(cutoff_ref, back)
        sends[offset - 1][0] = inv_ref[0, 0, back] * keep
        sends[offset - 1][1] = rho_ref[0, 0, 0, back] * keep
        sends[offset - 1][2] = rho_ref[1, 0, 0, back] * keep
    left = (left_high, left_low)
    every = slice(0, 3 * B)
    diagonal = start[:, cols(0)]
    for offset, near in enumerate((one, two, three, four), 1):
        here = part(left, every, cols(offset))
        diagonal = diagonal + dot(here, split(near[1]))
        other = start[:, cols(offset)] + dot(here, split(near[0]))
        mixed_high[:, cols(offset)], mixed_low[:, cols(offset)] = split(other)
    mixed = split(diagonal)
    mixed_high[:, cols(0)], mixed_low[:, cols(0)] = mixed
    top = slice(0, B)
    whole = slice(0, 5 * B)
    prop = (mixed[0][top], mixed[1][top])
    rest = (mixed[0][B:], mixed[1][B:])
    inner = dot(rest, part(left, top, whole))
    base[0] = dot(prop, part(left, slice(B, 2 * B), whole)) - inner[:B]
    base[1] = dot(prop, part(left, slice(2 * B, 3 * B), whole)) - inner[B:]


def fourth_kernel(cutoff_ref, rho_ref, der_ref, base, mixed_high, mixed_low, one, two, three, four, new, row_part, *columns):
    mixed = (mixed_high, mixed_low)
    weighted = [jnp.zeros((B, B), f32) for _ in range(3)]
    for offset, near in enumerate((one, two, three, four), 1):
        keep = keep_of(cutoff_ref, offset)
        here = cols(offset)
        prop = part(mixed, slice(0, B), here)
        inner = dot(part(mixed, slice(B, 3 * B), here), split(near[0]))
        imag_comm = base[1, :, here] + dot(prop, split(near[2])) - inner[B:]
        real_new = rho_ref[0, 0, 0, offset] * keep + time_step * imag_comm
        new[0, offset - 1] = real_new
        for direction in range(3):
            product = real_new * der_ref[direction, 0, 0, offset]
            weighted[direction] = weighted[direction] + product
            columns[offset - 1][direction : direction + 1, :] = jnp.sum(product, axis=0, keepdims=True)
        real_comm = base[0, :, here] + dot(prop, split(near[1])) - inner[:B]
        new[1, offset - 1] = rho_ref[1, 0, 0, offset] * keep - time_step * real_comm
    for direction in range(3):
        row_part[direction] = weighted[direction]


def fifth_kernel(rho_ref, der_ref, atom_ref, base, mixed_high, mixed_low, new, row_part, one, two, three, four, c1, c2, c3, c4, out_ref, forces_ref):
    mixed = (mixed_high, mixed_low)
    real_comm = base[0, :, cols(0)]
    imag_comm = base[1, :, cols(0)]
    for offset, near in enumerate((one, two, three, four), 1):
        here = cols(offset)
        prop = part(mixed, slice(0, B), here)
        inner = dot(part(mixed, slice(B, 3 * B), here), split(near[0]))
        imag_comm = imag_comm + dot(prop, split(near[2])) - inner[B:]
        real_comm = real_comm + dot(prop, split(near[1])) - inner[:B]
    real_new = rho_ref[0, 0, 0, 0] + time_step * imag_comm
    out_ref[0, 0, 0, 0] = real_new
    out_ref[1, 0, 0, 0] = rho_ref[1, 0, 0, 0] - time_step * real_comm
    for offset in range(1, 5):
        out_ref[0, 0, 0, offset] = new[0, offset - 1]
        out_ref[1, 0, 0, offset] = new[1, offset - 1]
    parts = []
    for direction in range(3):
        product = real_new * der_ref[direction, 0, 0, 0]
        total = jnp.sum(product + (product + row_part[direction]).T, axis=0, keepdims=True)
        parts.append(total)
    orbital = jnp.concatenate(parts, axis=0) + ((c1[...] + c2[...]) + (c3[...] + c4[...]))
    members = (
        lax.broadcasted_iota(jnp.int32, (ATOMS, B), 0) == jnp.broadcast_to(atom_ref[0], (ATOMS, B))
    ).astype(f32)
    forces_ref[0, 0] = -lax.dot_general(
        orbital, members, (((1,), (1,)), ((), ())), precision=lax.Precision.HIGHEST, preferred_element_type=f32
    )


def call(kernel, shapes, in_specs, flops, bytes_accessed, *args):
    return pl.pallas_call(
        kernel,
        out_shape=shapes,
        in_specs=in_specs,
        out_specs=[vmem] * len(shapes),
        compiler_params=pltpu.CompilerParams(vmem_limit_bytes=32 * 2**20),
        cost_estimate=pl.CostEstimate(flops=flops, bytes_accessed=bytes_accessed, transcendentals=0),
    )(*args)


def local(hamiltonian, inverse_margin, density, cutoff, derivative, atom_of):
    shape = jax.ShapeDtypeStruct
    unit = B * B * 4
    product = 6 * B**3
    first = call(first_kernel, [shape((2, B, B), f32)] * 4, [smem, vmem], 0, 13 * unit, cutoff, hamiltonian)
    near_ham = [shifted(first[offset - 1], offset) for offset in range(1, 5)]
    pair = [shape((3 * B, 5 * B), bf16)] * 2 + [shape((B, 5 * B), bf16)] * 2
    send, left_high, left_low, ham_high, ham_low, start = call(
        second_kernel,
        [shape((3, B, B), f32)] + pair + [shape((3 * B, 5 * B), f32)],
        [smem, vmem, vmem, vmem],
        15 * product,
        60 * unit,
        cutoff,
        hamiltonian,
        inverse_margin,
        density,
    )
    near_zero = [shifted(send, offset) for offset in range(1, 5)]
    third = call(
        third_kernel,
        [shape((3, B, B), f32)] * 4 + [shape((3 * B, 5 * B), bf16)] * 2 + [shape((2, B, 5 * B), f32)],
        [smem] + [vmem] * 9,
        44 * product,
        100 * unit,
        cutoff,
        inverse_margin,
        density,
        start,
        left_high,
        left_low,
        *near_ham,
    )
    near_back = [shifted(third[offset - 1], offset) for offset in range(1, 5)]
    mixed_high, mixed_low, base = third[4:]
    fourth = call(
        fourth_kernel,
        [shape((2, 4, B, B), f32), shape((3, B, B), f32)] + [shape((3, B), f32)] * 4,
        [smem] + [vmem] * 9,
        16 * product,
        60 * unit,
        cutoff,
        density,
        derivative,
        base,
        mixed_high,
        mixed_low,
        *near_zero,
    )
    new, row_part = fourth[:2]
    columns = [shifted(fourth[offset + 1], opposite[offset]) for offset in range(1, 5)]
    return call(
        fifth_kernel,
        [shape(density.shape, f32), shape((1, 1, 3, ATOMS), f32)],
        [vmem] * 16,
        16 * product,
        60 * unit,
        density,
        derivative,
        atom_of,
        base,
        mixed_high,
        mixed_low,
        new,
        row_part,
        *near_back,
        *columns,
    )


def solution(mesh):
    placed = (
        P("gx", "gy", None, None, None),
        P("gx", "gy", None, None, None),
        P(None, "gx", "gy", None, None, None),
        P("gx", "gy", None),
        P(None, "gx", "gy", None, None, None),
        P("gx", "gy", None),
    )
    return jax.shard_map(
        lambda *args: tuple(local(*args)),
        mesh=mesh,
        in_specs=placed,
        out_specs=(P(None, "gx", "gy", None, None, None), P("gx", "gy", None, None)),
        check_vma=False,
    )
```

```python
import jax
import jax.numpy as jnp
from jax import lax
from jax.experimental import pallas as pl
from jax.experimental.pallas import tpu as pltpu
from jax.sharding import PartitionSpec as P

B = 128
ATOMS = 64

opposite = (0, 2, 1, 4, 3)
time_step = 0.25
vmem = pl.BlockSpec(memory_space=pltpu.VMEM)
smem = pl.BlockSpec(memory_space=pltpu.SMEM)
hbm = pl.BlockSpec(memory_space=pltpu.HBM)
f32 = jnp.float32
bf16 = jnp.bfloat16


def shifted(cells, offset):
    axis = "gx" if offset < 3 else "gy"
    count = lax.axis_size(axis)
    if offset in (1, 3):
        pairs = [((i + 1) % count, i) for i in range(count)]
    else:
        pairs = [(i, (i + 1) % count) for i in range(count)]
    return lax.ppermute(cells, axis, pairs)


def cols(offset, count=1):
    return slice(offset * B, (offset + count) * B)


def split(values):
    high = values.astype(bf16)
    return high, (values - high.astype(f32)).astype(bf16)


def dot(left, right):
    def one(a, b):
        return jnp.dot(a, b, preferred_element_type=f32)

    return one(left[0], right[0]) + (one(left[0], right[1]) + one(left[1], right[0]))


def part(pair, rows, columns):
    return pair[0][rows, columns], pair[1][rows, columns]


def keep_of(cutoff_ref, offset):
    return cutoff_ref[0, 0, offset].astype(f32)


def first_kernel(cutoff_ref, ham_ref, one, two, ham):
    ham[0] = ham_ref[0, 0, 0]
    for offset in range(1, 5):
        ham[offset] = ham_ref[0, 0, offset] * keep_of(cutoff_ref, offset)
    for offset, out in ((1, one), (2, two)):
        out[0] = ham[0]
        out[1] = ham[opposite[offset]]


def second_kernel(
    cutoff_ref, inv_ref, rho_ref, atom_ref, ham_ref, send, three, four, left_high, left_low, start, members, ham_high, ham_low
):
    for offset in range(5):
        here = cols(offset)
        blocks = (inv_ref[0, 0, offset], rho_ref[0, 0, 0, offset], rho_ref[1, 0, 0, offset])
        if offset > 0:
            blocks = [block * keep_of(cutoff_ref, offset) for block in blocks]
        for place, block in enumerate((*blocks, ham_ref[offset])):
            if offset == 0:
                if place < 3:
                    send[place] = block
                three[place] = block
                four[place] = block
            elif offset > 2:
                (four if offset == 3 else three)[4 + place] = block
            if place < 3:
                rows = slice(place * B, (place + 1) * B)
                left_high[rows, here], left_low[rows, here] = split(block)
            else:
                ham_high[:, here], ham_low[:, here] = split(block)
    left = (left_high, left_low)
    ham = (ham_high, ham_low)
    start[...] = dot(part(left, slice(0, 3 * B), cols(0)), part(ham, slice(0, B), slice(0, 5 * B)))
    atoms = jnp.broadcast_to(atom_ref[0], (ATOMS, B))
    members[...] = -(lax.broadcasted_iota(jnp.int32, (ATOMS, B), 0) == atoms).astype(f32)


def mixed_kernel(offsets, left_high, left_low, start, near_zero, near_back, mixed_high, mixed_low):
    left = (left_high, left_low)
    every = slice(0, 3 * B)
    diagonal = start[:, cols(0)]
    for offset, zero, back in zip(offsets, near_zero, near_back):
        here = part(left, every, cols(offset))
        diagonal = diagonal + dot(here, split(back))
        other = start[:, cols(offset)] + dot(here, split(zero))
        at = cols(offset - offsets[0])
        mixed_high[:, at], mixed_low[:, at] = split(other)
    return diagonal


def third_kernel(left_high, left_low, start, one, two, mixed_high, mixed_low, diagonal):
    diagonal[...] = mixed_kernel(
        (1, 2), left_high, left_low, start, (one[0], two[0]), (one[1], two[1]), mixed_high, mixed_low
    )


def fourth_kernel(
    cutoff_ref, inv_ref, rho_ref, left_high, left_low, start, diagonal, three, four, send_one, send_two, mixed_high, mixed_low, base
):
    for offset, send in ((1, send_one), (2, send_two)):
        back = opposite[offset]
        keep = keep_of(cutoff_ref, back)
        send[0] = inv_ref[0, 0, back] * keep
        send[1] = rho_ref[0, 0, 0, back] * keep
        send[2] = rho_ref[1, 0, 0, back] * keep
    left = (left_high, left_low)
    total = mixed_kernel(
        (3, 4), left_high, left_low, start, (three[3], four[3]), (three[7], four[7]), mixed_high, mixed_low
    )
    mixed = split(total - start[:, cols(0)] + diagonal[...])
    top = slice(0, B)
    whole = slice(0, 5 * B)
    prop = (mixed[0][top], mixed[1][top])
    rest = (mixed[0][B:], mixed[1][B:])
    inner = dot(rest, part(left, top, whole))
    base[0] = dot(prop, part(left, slice(B, 2 * B), whole)) - inner[:B]
    base[1] = dot(prop, part(left, slice(2 * B, 3 * B), whole)) - inner[B:]


def fifth_kernel(
    cutoff_ref, rho_ref, der_ref, base, high_x, low_x, high_y, low_y, one, two, three, four, out_hbm, row_part, *refs
):
    columns, (new, sems) = refs[:4], refs[4:]
    weighted = [jnp.zeros((B, B), f32) for _ in range(3)]
    copies = []
    for offset, near in enumerate((one, two, three, four), 1):
        keep = keep_of(cutoff_ref, offset)
        here = cols(offset)
        mixed = (high_x, low_x) if offset < 3 else (high_y, low_y)
        at = cols((offset - 1) % 2)
        prop = part(mixed, slice(0, B), at)
        inner = dot(part(mixed, slice(B, 3 * B), at), split(near[0]))
        imag_comm = base[1, :, here] + dot(prop, split(near[2])) - inner[B:]
        real_new = rho_ref[0, 0, 0, offset] * keep + time_step * imag_comm
        new[0, offset - 1] = real_new
        for direction in range(3):
            product = real_new * der_ref[direction, 0, 0, offset]
            weighted[direction] = weighted[direction] + product
            columns[offset - 1][direction : direction + 1, :] = jnp.sum(product, axis=0, keepdims=True)
        real_comm = base[0, :, here] + dot(prop, split(near[1])) - inner[:B]
        new[1, offset - 1] = rho_ref[1, 0, 0, offset] * keep - time_step * real_comm
        for place in range(2):
            copy = pltpu.make_async_copy(
                new.at[place, offset - 1], out_hbm.at[place, 0, 0, offset], sems.at[place, offset - 1]
            )
            copy.start()
            copies.append(copy)
    for direction in range(3):
        row_part[direction : direction + 1, :] = jnp.sum(weighted[direction].T, axis=0, keepdims=True)
    for copy in copies:
        copy.wait()


def sixth_kernel(
    rho_ref, der_ref, members, base, high_x, low_x, high_y, low_y, row_part, one, two, three, four, c1, c2, c3, c4, old_hbm,
    out_hbm, forces_ref, new, sems
):
    real_comm = base[0, :, cols(0)]
    imag_comm = base[1, :, cols(0)]
    for offset, near in enumerate((one, two, three, four), 1):
        mixed = (high_x, low_x) if offset < 3 else (high_y, low_y)
        at = cols((offset - 1) % 2)
        first = 0 if offset < 3 else 4
        prop = part(mixed, slice(0, B), at)
        inner = dot(part(mixed, slice(B, 3 * B), at), split(near[first]))
        imag_comm = imag_comm + dot(prop, split(near[first + 2])) - inner[B:]
        real_comm = real_comm + dot(prop, split(near[first + 1])) - inner[:B]
    real_new = rho_ref[0, 0, 0, 0] + time_step * imag_comm
    new[0] = real_new
    new[1] = rho_ref[1, 0, 0, 0] - time_step * real_comm
    copies = [pltpu.make_async_copy(new.at[place], out_hbm.at[place, 0, 0, 0], sems.at[place]) for place in range(2)]
    for copy in copies:
        copy.start()
    parts = []
    for direction in range(3):
        product = real_new * der_ref[direction, 0, 0, 0]
        parts.append(jnp.sum(product + product.T, axis=0, keepdims=True))
    orbital = jnp.concatenate(parts, axis=0) + row_part[...] + ((c1[...] + c2[...]) + (c3[...] + c4[...]))
    forces = lax.dot_general(
        orbital, members[...], (((1,), (1,)), ((), ())), precision=lax.Precision.HIGHEST, preferred_element_type=f32
    )
    for direction in range(3):
        forces_ref[direction] = forces[direction : direction + 1]
    for copy in copies:
        copy.wait()


def call(kernel, shapes, in_specs, products, args, out_specs=None, scratch=(), aliases={}):
    moved = sum(4 * x.size for x in args) + sum(4 * x.size for x in shapes)
    return pl.pallas_call(
        kernel,
        out_shape=shapes,
        in_specs=in_specs,
        out_specs=out_specs or [vmem] * len(shapes),
        scratch_shapes=scratch,
        input_output_aliases=aliases,
        compiler_params=pltpu.CompilerParams(vmem_limit_bytes=32 * 2**20),
        cost_estimate=pl.CostEstimate(flops=products * 6 * B**3, bytes_accessed=moved, transcendentals=0),
    )(*args)


def local(hamiltonian, inverse_margin, density, cutoff, derivative, atom_of):
    def shape(*dims, kind=f32):
        return jax.ShapeDtypeStruct(dims, kind)

    dma = pltpu.SemaphoreType.DMA
    first = call(
        first_kernel,
        [shape(2, B, B)] * 2 + [shape(5, B, B)],
        [smem, vmem],
        0,
        (cutoff, hamiltonian),
    )
    ham_x = [shifted(first[offset - 1], offset) for offset in (1, 2)]
    send, send_three, send_four, left_high, left_low, start, members = call(
        second_kernel,
        [shape(3, B, B), shape(8, B, B), shape(8, B, B)]
        + [shape(3 * B, 5 * B, kind=bf16)] * 2
        + [shape(3 * B, 5 * B), shape(ATOMS, B)],
        [smem] + [vmem] * 4,
        15,
        (cutoff, inverse_margin, density, atom_of, first[2]),
        scratch=[pltpu.VMEM((B, 5 * B), bf16)] * 2,
    )
    near_y = [shifted(send_three, 3), shifted(send_four, 4)]
    zero_x = [shifted(send, offset) for offset in (1, 2)]
    pair = [shape(3 * B, 2 * B, kind=bf16)] * 2
    high_x, low_x, diagonal = call(
        third_kernel, pair + [shape(3 * B, B)], [vmem] * 5, 6000, (left_high, left_low, start, *ham_x)
    )
    send_one, send_two, high_y, low_y, base = call(
        fourth_kernel,
        [shape(3, B, B)] * 2 + pair + [shape(2, B, 5 * B)],
        [smem] + [vmem] * 8,
        32,
        (cutoff, inverse_margin, density, left_high, left_low, start, diagonal, *near_y),
    )
    back_x = [shifted(send_one, 1), shifted(send_two, 2)]
    fifth = call(
        fifth_kernel,
        [shape(*density.shape), shape(3, B)] + [shape(3, B)] * 4,
        [smem] + [vmem] * 11,
        16,
        (cutoff, density, derivative, base, high_x, low_x, high_y, low_y, *zero_x, *near_y),
        out_specs=[hbm] + [vmem] * 5,
        scratch=[pltpu.VMEM((2, 4, B, B), f32), dma((2, 4))],
    )
    columns = [shifted(fifth[offset + 1], opposite[offset]) for offset in range(1, 5)]
    args = (density, derivative, members, base, high_x, low_x, high_y, low_y, fifth[1], *back_x, *near_y, *columns, fifth[0])
    new_density, forces = call(
        sixth_kernel,
        [shape(*density.shape), shape(3, 1, ATOMS)],
        [vmem] * 17 + [hbm],
        16,
        args,
        out_specs=[hbm, vmem],
        scratch=[pltpu.VMEM((2, B, B), f32), dma((2,))],
        aliases={17: 0},
    )
    return new_density, forces.reshape(1, 1, 3, ATOMS)


def solution(mesh):
    placed = (
        P("gx", "gy", None, None, None),
        P("gx", "gy", None, None, None),
        P(None, "gx", "gy", None, None, None),
        P("gx", "gy", None),
        P(None, "gx", "gy", None, None, None),
        P("gx", "gy", None),
    )
    return jax.shard_map(
        local,
        mesh=mesh,
        in_specs=placed,
        out_specs=(P(None, "gx", "gy", None, None, None), P("gx", "gy", None, None)),
        check_vma=False,
    )
```

```python
import jax
import jax.numpy as jnp
from jax import lax
from jax.experimental import pallas as pl
from jax.experimental.pallas import tpu as pltpu
from jax.sharding import PartitionSpec as P

B = 128
ATOMS = 64

time_step = 0.25
vmem = pl.BlockSpec(memory_space=pltpu.VMEM)
hbm = pl.BlockSpec(memory_space=pltpu.HBM)
f32 = jnp.float32
bf16 = jnp.bfloat16
dma = pltpu.SemaphoreType.DMA


def swapped(cells, edge):
    axis = "gx" if edge < 3 else "gy"
    count = lax.axis_size(axis)
    assert count % 2 == 0
    first = 0 if edge in (1, 3) else 1
    pairs = []
    for i in range(first, count, 2):
        j = (i + 1) % count
        pairs += [(i, j), (j, i)]
    return lax.ppermute(cells, axis, pairs)


def order_of():
    odd_x = lax.rem(lax.axis_index("gx"), 2)
    odd_y = lax.rem(lax.axis_index("gy"), 2)
    return 0, 1 + odd_x, 2 - odd_x, 3 + odd_y, 4 - odd_y


def cols(place, count=1):
    return slice(place * B, (place + count) * B)


def split(values):
    high = values.astype(bf16)
    return high, (values - high.astype(f32)).astype(bf16)


def beside(*pairs):
    return tuple(jnp.concatenate(parts, axis=1) for parts in zip(*pairs))


def dot(left, right):
    def one(a, b):
        return jnp.dot(a, b, preferred_element_type=f32)

    return one(left[0], right[0]) + (one(left[0], right[1]) + one(left[1], right[0]))


def part(pair, rows, columns):
    return pair[0][rows, columns], pair[1][rows, columns]


def rows_of(pair):
    return (pair[0][:B], pair[1][:B]), (pair[0][B:], pair[1][B:])


def store(pair, columns, values):
    pair[0][:, columns], pair[1][:, columns] = values


def start_all(copies):
    for copy in copies:
        copy.start()
    return copies


def first_kernel(cutoff_hbm, ham_hbm, inv_hbm, rho_hbm, one, cutoff_ref, cutoff_sem, sems):
    flags = pltpu.make_async_copy(cutoff_hbm, cutoff_ref, cutoff_sem)
    flags.start()
    offset = order_of()[1]
    sources = (ham_hbm.at[0, 0, offset], ham_hbm.at[0, 0, 0], inv_hbm.at[0, 0, 0], rho_hbm.at[0, 0, 0, 0], rho_hbm.at[1, 0, 0, 0])
    copies = start_all(
        [pltpu.make_async_copy(source, one.at[(at + 4) % 5], sems.at[at]) for at, source in enumerate(sources)]
    )
    flags.wait()
    copies[0].wait()
    one[4] = one[4] * cutoff_ref[0, 0, offset].astype(f32)
    for copy in copies[1:]:
        copy.wait()


def second_kernel(
    cutoff_hbm, ham_hbm, inv_hbm, rho_hbm, atom_hbm, after, two, three, four, held, left_high, left_low, ham_high, ham_low, members,
    raw, cutoff_ref, atom_ref, cutoff_sem, atom_sem, sems
):
    flags = pltpu.make_async_copy(cutoff_hbm, cutoff_ref, cutoff_sem)
    flags.start()
    sources = (ham_hbm.at[0, 0], inv_hbm.at[0, 0], rho_hbm.at[0, 0, 0], rho_hbm.at[1, 0, 0])
    copies = start_all([pltpu.make_async_copy(source, raw.at[at], sems.at[at]) for at, source in enumerate(sources)])
    owners = pltpu.make_async_copy(atom_hbm, atom_ref, atom_sem)
    owners.start()
    order = order_of()
    flags.wait()
    keeps = [cutoff_ref[0, 0, offset].astype(f32) for offset in order]
    for kind, copy in enumerate(copies):
        copy.wait()
        for place, offset in enumerate(order):
            block = raw[kind, offset]
            if place == 0:
                for message in (two, three, four):
                    message[kind] = block
            else:
                block = block * keeps[place]
                if place > 2 or (place == 2 and kind == 0):
                    (two, three, four)[place - 2][4 + kind] = block
            if kind == 0:
                store((ham_high, ham_low), cols(place), split(block))
            else:
                held[kind - 1, place] = block
                rows = slice((kind - 1) * B, kind * B)
                left_high[rows, cols(place)], left_low[rows, cols(place)] = split(block)
    owners.wait()
    atoms = jnp.broadcast_to(atom_ref[0], (ATOMS, B))
    members[...] = -(lax.broadcasted_iota(jnp.int32, (ATOMS, B), 0) == atoms).astype(f32)


def edge(left, begun, near_zero, near_back):
    both = dot(left, beside(split(near_zero), split(near_back)))
    return split(begun + both[:, :B]), both[:, B:]


def commutators(mixed, invs, reals, imags):
    prop, inner = rows_of(mixed)
    count = len(reals)
    ahead = dot(prop, beside(*[split(x) for x in (*reals, *imags)]))
    behind = dot(inner, beside(*[split(x) for x in invs]))
    real = [ahead[:, cols(at)] - behind[:B, cols(at)] for at in range(count)]
    imag = [ahead[:, cols(count + at)] - behind[B:, cols(at)] for at in range(count)]
    return real, imag


def third_kernel(left_high, left_low, ham_high, ham_low, one, start, mixed_high, mixed_low, diagonal, other):
    left = (left_high, left_low)
    every = slice(0, 3 * B)
    begun = dot(part(left, every, cols(0)), part((ham_high, ham_low), slice(0, B), cols(0, 5)))
    start[...] = begun
    mixed, added = edge(part(left, every, cols(1)), begun[:, cols(1)], one[0], one[4])
    diagonal[...] = begun[:, cols(0)] + added
    mixed_high[...], mixed_low[...] = mixed
    (real,), (imag,) = commutators(mixed, (one[1],), (one[2],), (one[3],))
    other[0], other[1] = real, imag


def fourth_kernel(left_high, left_low, start, diagonal, held, three, four, one_more, two_more, diagonal_out, other):
    for kind in range(3):
        one_more[kind] = held[kind, 1]
        two_more[kind] = held[kind, 2]
    total = diagonal[...]
    for place, near in ((3, three), (4, four)):
        here = part((left_high, left_low), slice(0, 3 * B), cols(place))
        mixed, added = edge(here, start[:, cols(place)], near[0], near[4])
        total = total + added
        real, imag = commutators(mixed, (near[1], near[5]), (near[2], near[6]), (near[3], near[7]))
        other[0, place - 3], other[1, place - 3] = real[0], imag[0]
        if place == 3:
            other[0, 2], other[1, 2] = real[1], imag[1]
        else:
            other[0, 2] = other[0, 2] + real[1]
            other[1, 2] = other[1, 2] + imag[1]
    diagonal_out[...] = total


def fifth_kernel(
    left_high, left_low, start, diagonal, held, der_ref, other_one, other_y, two,
    out_hbm, mixed_high, mixed_low, comm, row_part, c1, c2, c3, c4, new, sems
):
    order = order_of()
    left = (left_high, left_low)
    mixed, added = edge(part(left, slice(0, 3 * B), cols(2)), start[:, cols(2)], two[0], two[4])
    mixed_high[...], mixed_low[...] = mixed
    (real_two,), (imag_two,) = commutators(mixed, (two[1],), (two[2],), (two[3],))
    total = diagonal[...] + added
    prop, inner = rows_of(split(total))
    whole = cols(0, 5)
    behind = dot(inner, part(left, slice(0, B), whole))
    imag_comm = dot(prop, part(left, slice(2 * B, 3 * B), whole)) - behind[B:]
    real_comm = dot(prop, part(left, slice(B, 2 * B), whole)) - behind[:B]
    others = [(other_one[0], other_one[1]), (real_two, imag_two)]
    others += [(other_y[0, at], other_y[1, at]) for at in range(2)]
    comm[0] = real_comm[:, cols(0)] + other_y[0, 2]
    comm[1] = imag_comm[:, cols(0)] + other_y[1, 2]
    weighted = [jnp.zeros((B, B), f32) for _ in range(3)]
    copies = []
    for place, column in enumerate((c1, c2, c3, c4), 1):
        real, imag = others[place - 1]
        real_new = held[1, place] + time_step * (imag_comm[:, cols(place)] + imag)
        new[0, place - 1] = real_new
        new[1, place - 1] = held[2, place] - time_step * (real_comm[:, cols(place)] + real)
        copies += start_all(
            [
                pltpu.make_async_copy(new.at[at, place - 1], out_hbm.at[at, 0, 0, order[place]], sems.at[at, place - 1])
                for at in range(2)
            ]
        )
        for direction in range(3):
            product = real_new * der_ref[direction, 0, 0, order[place]]
            weighted[direction] = weighted[direction] + product
            column[direction : direction + 1, :] = jnp.sum(product, axis=0, keepdims=True)
    for direction in range(3):
        row_part[direction : direction + 1, :] = jnp.sum(weighted[direction].T, axis=0, keepdims=True)
    for copy in copies:
        copy.wait()


def sixth_kernel(
    held, der_ref, members, high_one, low_one, high_two, low_two, comm, row_part, one, two, c1, c2, c3, c4, old_hbm, out_hbm, forces_ref, new, sems
):
    prop, inner = rows_of(beside((high_one[...], low_one[...]), (high_two[...], low_two[...])))
    near = [tuple(jnp.concatenate(x, axis=0) for x in zip(split(one[kind]), split(two[kind]))) for kind in range(3)]
    behind = dot(inner, near[0])
    ahead = dot(prop, beside(near[2], near[1]))
    real_new = held[1, 0] + time_step * (comm[1] + ahead[:, :B] - behind[B:])
    new[0] = real_new
    new[1] = held[2, 0] - time_step * (comm[0] + ahead[:, B:] - behind[:B])
    copies = start_all([pltpu.make_async_copy(new.at[at], out_hbm.at[at, 0, 0, 0], sems.at[at]) for at in range(2)])
    parts = []
    for direction in range(3):
        product = real_new * der_ref[direction, 0, 0, 0]
        parts.append(jnp.sum(product + product.T, axis=0, keepdims=True))
    orbital = jnp.concatenate(parts, axis=0) + row_part[...] + ((c1[...] + c2[...]) + (c3[...] + c4[...]))
    forces = lax.dot_general(
        orbital, members[...], (((1,), (1,)), ((), ())), precision=lax.Precision.HIGHEST, preferred_element_type=f32
    )
    for direction in range(3):
        forces_ref[direction] = forces[direction : direction + 1]
    for copy in copies:
        copy.wait()


def call(kernel, shapes, in_specs, products, args, out_specs=None, scratch=(), aliases={}):
    moved = sum(4 * x.size for x in args) + sum(4 * x.size for x in shapes)
    return pl.pallas_call(
        kernel,
        out_shape=shapes,
        in_specs=in_specs,
        out_specs=out_specs or [vmem] * len(shapes),
        scratch_shapes=scratch,
        input_output_aliases=aliases,
        compiler_params=pltpu.CompilerParams(vmem_limit_bytes=32 * 2**20),
        cost_estimate=pl.CostEstimate(flops=products * 6 * B**3, bytes_accessed=moved, transcendentals=0),
    )(*args)


def local(hamiltonian, inverse_margin, density, cutoff, derivative, atom_of):
    def shape(*dims, kind=f32):
        return jax.ShapeDtypeStruct(dims, kind)

    hamiltonian, inverse_margin, density, cutoff, atom_of = (
        pltpu.with_memory_space_constraint(x, pltpu.HBM) for x in (hamiltonian, inverse_margin, density, cutoff, atom_of)
    )
    flags = pltpu.SMEM((1, 1, 5), jnp.int32)
    (first,) = call(
        first_kernel,
        [shape(5, B, B)],
        [hbm] * 4,
        0,
        (cutoff, hamiltonian, inverse_margin, density),
        scratch=[flags, dma(()), dma((5,))],
    )
    near_one = swapped(first, 1)
    left = [shape(3 * B, 5 * B, kind=bf16)] * 2
    ham = [shape(B, 5 * B, kind=bf16)] * 2
    send_two, send_three, send_four, held, left_high, left_low, ham_high, ham_low, members = call(
        second_kernel,
        [shape(5, B, B), shape(8, B, B), shape(8, B, B), shape(3, 5, B, B)] + left + ham + [shape(ATOMS, B)],
        [hbm] * 6,
        0,
        (cutoff, hamiltonian, inverse_margin, density, atom_of, first),
        scratch=[pltpu.VMEM((4, 5, B, B), f32), flags, pltpu.VMEM((1, 1, B), jnp.int32), dma(()), dma(()), dma((4,))],
    )
    near_four = swapped(send_four, 4)
    near_three = swapped(send_three, 3)
    near_two = swapped(send_two, 2)
    mixed = [shape(3 * B, B, kind=bf16)] * 2
    start, high_one, low_one, diagonal, other_one = call(
        third_kernel,
        [shape(3 * B, 5 * B)] + mixed + [shape(3 * B, B), shape(2, B, B)],
        [vmem] * 5,
        8000,
        (left_high, left_low, ham_high, ham_low, near_one),
    )
    one_more, two_more, diagonal, other_y = call(
        fourth_kernel,
        [shape(3, B, B)] * 2 + [shape(3 * B, B), shape(2, 3, B, B)],
        [vmem] * 7,
        28,
        (left_high, left_low, start, diagonal, held, near_three, near_four),
    )
    near_one_more = swapped(one_more, 1)
    near_two_more = swapped(two_more, 2)
    args = (left_high, left_low, start, diagonal, held, derivative, other_one, other_y, near_two)
    out, high_two, low_two, comm, row_part, *columns = call(
        fifth_kernel,
        [shape(*density.shape)] + mixed + [shape(2, B, B)] + [shape(3, B)] * 5,
        [vmem] * 9,
        30,
        args,
        out_specs=[hbm] + [vmem] * 8,
        scratch=[pltpu.VMEM((2, 4, B, B), f32), dma((2, 4))],
    )
    columns = [swapped(column, at) for at, column in enumerate(columns, 1)]
    args = (held, derivative, members, high_one, low_one, high_two, low_two, comm, row_part)
    args += (near_one_more, near_two_more, *columns, out)
    new_density, forces = call(
        sixth_kernel,
        [shape(*density.shape), shape(3, 1, ATOMS)],
        [vmem] * 15 + [hbm],
        8,
        args,
        out_specs=[hbm, vmem],
        scratch=[pltpu.VMEM((2, B, B), f32), dma((2,))],
        aliases={15: 0},
    )
    return new_density, forces.reshape(1, 1, 3, ATOMS)


def solution(mesh):
    placed = (
        P("gx", "gy", None, None, None),
        P("gx", "gy", None, None, None),
        P(None, "gx", "gy", None, None, None),
        P("gx", "gy", None),
        P(None, "gx", "gy", None, None, None),
        P("gx", "gy", None),
    )
    return jax.shard_map(
        local,
        mesh=mesh,
        in_specs=placed,
        out_specs=(P(None, "gx", "gy", None, None, None), P("gx", "gy", None, None)),
        check_vma=False,
    )
```

```python
import jax
import jax.numpy as jnp
from jax import lax
from jax.experimental import pallas as pl
from jax.experimental.pallas import tpu as pltpu
from jax.sharding import PartitionSpec as P

B = 128
ATOMS = 64

time_step = 0.25
vmem = pl.BlockSpec(memory_space=pltpu.VMEM)
hbm = pl.BlockSpec(memory_space=pltpu.HBM)
f32 = jnp.float32
bf16 = jnp.bfloat16
dma = pltpu.SemaphoreType.DMA


def swapped(cells, edge):
    axis = "gx" if edge < 3 else "gy"
    count = lax.axis_size(axis)
    assert count % 2 == 0
    first = 0 if edge in (1, 3) else 1
    pairs = []
    for i in range(first, count, 2):
        j = (i + 1) % count
        pairs += [(i, j), (j, i)]
    return lax.ppermute(cells, axis, pairs)


def relayed(cells):
    count = lax.axis_size("gx")
    return lax.ppermute(cells, "gx", [(i, (i + (2 if i % 2 == 0 else count - 2)) % count) for i in range(count)])


def order_of():
    odd_x = lax.rem(lax.axis_index("gx"), 2)
    odd_y = lax.rem(lax.axis_index("gy"), 2)
    return 0, 1 + odd_x, 2 - odd_x, 3 + odd_y, 4 - odd_y


def cols(place, count=1):
    return slice(place * B, (place + count) * B)


def split(values):
    high = values.astype(bf16)
    return high, (values - high.astype(f32)).astype(bf16)


def beside(*pairs):
    return tuple(jnp.concatenate(parts, axis=1) for parts in zip(*pairs))


def dot(left, right):
    def one(a, b):
        return jnp.dot(a, b, preferred_element_type=f32)

    return one(left[0], right[0]) + (one(left[0], right[1]) + one(left[1], right[0]))


def part(pair, rows, columns):
    return pair[0][rows, columns], pair[1][rows, columns]


def rows_of(pair):
    return (pair[0][:B], pair[1][:B]), (pair[0][B:], pair[1][B:])


def store(pair, columns, values):
    pair[0][:, columns], pair[1][:, columns] = values


def start_all(copies):
    for copy in copies:
        copy.start()
    return copies


def first_kernel(cutoff_hbm, ham_hbm, inv_hbm, rho_hbm, one, cutoff_ref, cutoff_sem, sems):
    flags = pltpu.make_async_copy(cutoff_hbm, cutoff_ref, cutoff_sem)
    flags.start()
    order = order_of()
    sources = (ham_hbm.at[0, 0, 0], inv_hbm.at[0, 0, 0], rho_hbm.at[1, 0, 0, 0], ham_hbm.at[0, 0, order[2]], ham_hbm.at[0, 0, order[1]])
    copies = start_all([pltpu.make_async_copy(source, one.at[at], sems.at[at]) for at, source in enumerate(sources)])
    flags.wait()
    for copy in copies:
        copy.wait()
    for at, place in ((3, 2), (4, 1)):
        one[at] = one[at] * cutoff_ref[0, 0, order[place]].astype(f32)


def second_kernel(
    cutoff_hbm, ham_hbm, inv_hbm, rho_hbm, atom_hbm, after, three, four, held, left_high, left_low, ham_high, ham_low, members,
    raw, cutoff_ref, atom_ref, cutoff_sem, atom_sem, sems
):
    flags = pltpu.make_async_copy(cutoff_hbm, cutoff_ref, cutoff_sem)
    flags.start()
    sources = (ham_hbm.at[0, 0], inv_hbm.at[0, 0], rho_hbm.at[0, 0, 0], rho_hbm.at[1, 0, 0])
    copies = start_all([pltpu.make_async_copy(source, raw.at[at], sems.at[at]) for at, source in enumerate(sources)])
    owners = pltpu.make_async_copy(atom_hbm, atom_ref, atom_sem)
    owners.start()
    order = order_of()
    flags.wait()
    keeps = [cutoff_ref[0, 0, offset].astype(f32) for offset in order]
    for kind, copy in enumerate(copies):
        copy.wait()
        for place, offset in enumerate(order):
            block = raw[kind, offset]
            if place == 0:
                three[kind] = block
                four[kind] = block
            else:
                block = block * keeps[place]
                if place > 2:
                    (three, four)[place - 3][4 + kind] = block
            if kind == 0:
                store((ham_high, ham_low), cols(place), split(block))
            else:
                held[kind - 1, place] = block
                rows = slice((kind - 1) * B, kind * B)
                left_high[rows, cols(place)], left_low[rows, cols(place)] = split(block)
    owners.wait()
    atoms = jnp.broadcast_to(atom_ref[0], (ATOMS, B))
    members[...] = -(lax.broadcasted_iota(jnp.int32, (ATOMS, B), 0) == atoms).astype(f32)


def edge(left, begun, near_zero, near_back):
    both = dot(left, beside(split(near_zero), split(near_back)))
    return split(begun + both[:, :B]), both[:, B:]


def commutators(mixed, invs, reals, imags):
    prop, inner = rows_of(mixed)
    count = len(invs)
    ahead = dot(prop, beside(*[split(x) for x in (*imags, *reals)]))
    behind = dot(inner, beside(*[split(x) for x in invs]))
    imag = [ahead[:, cols(at)] - behind[B:, cols(at)] for at in range(count)]
    real = [-behind[:B, cols(at)] for at in range(count)]
    if len(reals) > 0:
        real = [ahead[:, cols(count + at)] + real[at] for at in range(count)]
    return real, imag


def more_kernel(near, held, relay, one_more, two_more):
    relay[...] = near[:4]
    for more, place in ((one_more, 1), (two_more, 2)):
        more[0] = held[1, 0]
        for kind in range(3):
            more[1 + kind] = held[kind, place]


def third_kernel(left_high, left_low, ham_high, ham_low, one, start, mixed_high, mixed_low, diagonal, other):
    left = (left_high, left_low)
    every = slice(0, 3 * B)
    begun = dot(part(left, every, cols(0)), part((ham_high, ham_low), slice(0, B), cols(0, 5)))
    start[...] = begun
    mixed, added = edge(part(left, every, cols(1)), begun[:, cols(1)], one[0], one[4])
    diagonal[...] = begun[:, cols(0)] + added
    mixed_high[...], mixed_low[...] = mixed
    (real,), (imag,) = commutators(mixed, (one[1],), (), (one[2],))
    other[0], other[1] = real, imag


def fourth_kernel(left_high, left_low, start, diagonal, three, four, diagonal_out, other):
    total = diagonal[...]
    for place, near in ((3, three), (4, four)):
        here = part((left_high, left_low), slice(0, 3 * B), cols(place))
        mixed, added = edge(here, start[:, cols(place)], near[0], near[4])
        total = total + added
        real, imag = commutators(mixed, (near[1], near[5]), (near[2], near[6]), (near[3], near[7]))
        other[0, place - 3], other[1, place - 3] = real[0], imag[0]
        if place == 3:
            other[0, 2], other[1, 2] = real[1], imag[1]
        else:
            other[0, 2] = other[0, 2] + real[1]
            other[1, 2] = other[1, 2] + imag[1]
    diagonal_out[...] = total


def fifth_kernel(
    left_high, left_low, start, diagonal, held, der_ref, other_one, other_y, two,
    out_hbm, mixed_high, mixed_low, self_high, self_low, real_two, comm, weighted, c1, c2, c3, c4, new, sems
):
    order = order_of()
    left = (left_high, left_low)
    mixed, added = edge(part(left, slice(0, 3 * B), cols(2)), start[:, cols(2)], two[0], two[3])
    mixed_high[...], mixed_low[...] = mixed
    (real_two[...],), (imag_two,) = commutators(mixed, (two[1],), (), (two[2],))
    at_self = split(diagonal[...] + added)
    self_high[...], self_low[...] = at_self
    whole = cols(0, 5)
    ahead = dot(part(at_self, slice(0, B), cols(0)), part(left, slice(2 * B, 3 * B), whole))
    behind = dot(part(at_self, slice(2 * B, 3 * B), cols(0)), part(left, slice(0, B), whole))
    imag_comm = ahead - behind
    comm[...] = imag_comm[:, cols(0)] + other_y[1, 2]
    sums = [None] * 3
    copies = []
    for place, column in enumerate((c1, c2, c3, c4), 1):
        imag = (other_one[1], imag_two, other_y[1, 0], other_y[1, 1])[place - 1]
        real_new = held[1, place] + time_step * (imag_comm[:, cols(place)] + imag)
        new[place - 1] = real_new
        copies += start_all(
            [pltpu.make_async_copy(new.at[place - 1], out_hbm.at[0, 0, 0, order[place]], sems.at[place - 1])]
        )
        for direction in range(3):
            product = real_new * der_ref[direction, 0, 0, order[place]]
            sums[direction] = product if place == 1 else sums[direction] + product
            column[direction : direction + 1, :] = jnp.sum(product, axis=0, keepdims=True)
    for direction in range(3):
        weighted[direction] = sums[direction]
    for copy in copies:
        copy.wait()


def real_kernel(left_high, left_low, self_high, self_low, other_one, real_two, other_y, weighted, comm, row_part):
    left = (left_high, left_low)
    whole = cols(0, 5)
    at_self = (self_high, self_low)
    ahead = dot(part(at_self, slice(0, B), cols(0)), part(left, slice(B, 2 * B), whole))
    behind = dot(part(at_self, slice(B, 2 * B), cols(0)), part(left, slice(0, B), whole))
    real_comm = ahead - behind
    for place, other in enumerate((other_y[0, 2], other_one[0], real_two[...], other_y[0, 0], other_y[0, 1])):
        comm[place] = real_comm[:, cols(place)] + other
    for direction in range(3):
        row_part[direction : direction + 1, :] = jnp.sum(weighted[direction].T, axis=0, keepdims=True)


def sixth_kernel(
    held, der_ref, members, high_one, low_one, high_two, low_two, imag_part, real_part, row_part, one, two, c1, c2, c3, c4, old_hbm,
    out_hbm, forces_ref, new, sems
):
    order = order_of()
    real_comm = [real_part[place] for place in range(5)]
    imag_comm = imag_part[...]
    for place, mixed, near in ((1, (high_one, low_one), one), (2, (high_two, low_two), two)):
        prop, inner = rows_of(mixed)
        ahead = dot(prop, beside(split(near[3]), split(near[2]), split(near[0])))
        behind = dot(inner, split(near[1]))
        imag_comm = imag_comm + ahead[:, cols(0)] - behind[B:]
        real_comm[0] = real_comm[0] + ahead[:, cols(1)] - behind[:B]
        real_comm[place] = real_comm[place] + ahead[:, cols(2)]
    real_new = held[1, 0] + time_step * imag_comm
    new[5] = real_new
    copies = start_all([pltpu.make_async_copy(new.at[5], out_hbm.at[0, 0, 0, 0], sems.at[5])])
    for place in range(5):
        new[place] = held[2, place] - time_step * real_comm[place]
        copies += start_all([pltpu.make_async_copy(new.at[place], out_hbm.at[1, 0, 0, order[place]], sems.at[place])])
    parts = []
    for direction in range(3):
        product = real_new * der_ref[direction, 0, 0, 0]
        parts.append(jnp.sum(product + product.T, axis=0, keepdims=True))
    orbital = jnp.concatenate(parts, axis=0) + row_part[...] + ((c1[...] + c2[...]) + (c3[...] + c4[...]))
    forces = lax.dot_general(
        orbital, members[...], (((1,), (1,)), ((), ())), precision=lax.Precision.HIGHEST, preferred_element_type=f32
    )
    for direction in range(3):
        forces_ref[direction] = forces[direction : direction + 1]
    for copy in copies:
        copy.wait()


def call(kernel, shapes, in_specs, products, args, out_specs=None, scratch=(), aliases={}):
    moved = sum(4 * x.size for x in args) + sum(4 * x.size for x in shapes)
    return pl.pallas_call(
        kernel,
        out_shape=shapes,
        in_specs=in_specs,
        out_specs=out_specs or [vmem] * len(shapes),
        scratch_shapes=scratch,
        input_output_aliases=aliases,
        compiler_params=pltpu.CompilerParams(vmem_limit_bytes=32 * 2**20),
        cost_estimate=pl.CostEstimate(flops=products * 6 * B**3, bytes_accessed=moved, transcendentals=0),
    )(*args)


def local(hamiltonian, inverse_margin, density, cutoff, derivative, atom_of):
    def shape(*dims, kind=f32):
        return jax.ShapeDtypeStruct(dims, kind)

    hamiltonian, inverse_margin, density, cutoff, atom_of = (
        pltpu.with_memory_space_constraint(x, pltpu.HBM) for x in (hamiltonian, inverse_margin, density, cutoff, atom_of)
    )
    flags = pltpu.SMEM((1, 1, 5), jnp.int32)
    (first,) = call(
        first_kernel,
        [shape(5, B, B)],
        [hbm] * 4,
        0,
        (cutoff, hamiltonian, inverse_margin, density),
        scratch=[flags, dma(()), dma((5,))],
    )
    near_one = swapped(first, 1)
    left = [shape(3 * B, 5 * B, kind=bf16)] * 2
    ham = [shape(B, 5 * B, kind=bf16)] * 2
    send_three, send_four, held, left_high, left_low, ham_high, ham_low, members = call(
        second_kernel,
        [shape(8, B, B), shape(8, B, B), shape(3, 5, B, B)] + left + ham + [shape(ATOMS, B)],
        [hbm] * 6,
        0,
        (cutoff, hamiltonian, inverse_margin, density, atom_of, first),
        scratch=[pltpu.VMEM((4, 5, B, B), f32), flags, pltpu.VMEM((1, 1, B), jnp.int32), dma(()), dma(()), dma((4,))],
    )
    near_four = swapped(send_four, 4)
    near_three = swapped(send_three, 3)
    relay, one_more, two_more = call(more_kernel, [shape(4, B, B)] * 3, [vmem] * 2, 0, (near_one, held))
    near_two = relayed(relay)
    near_one_more = swapped(one_more, 1)
    near_two_more = swapped(two_more, 2)
    mixed = [shape(3 * B, B, kind=bf16)] * 2
    start, high_one, low_one, diagonal, other_one = call(
        third_kernel,
        [shape(3 * B, 5 * B)] + mixed + [shape(3 * B, B), shape(2, B, B)],
        [vmem] * 5,
        8000,
        (left_high, left_low, ham_high, ham_low, near_one),
    )
    diagonal, other_y = call(
        fourth_kernel,
        [shape(3 * B, B), shape(2, 3, B, B)],
        [vmem] * 6,
        28,
        (left_high, left_low, start, diagonal, near_three, near_four),
    )
    out, high_two, low_two, self_high, self_low, real_two, imag_part, weighted, *columns = call(
        fifth_kernel,
        [shape(*density.shape)] + mixed * 2 + [shape(B, B), shape(B, B), shape(3, B, B)] + [shape(3, B)] * 4,
        [vmem] * 9,
        22,
        (left_high, left_low, start, diagonal, held, derivative, other_one, other_y, near_two),
        out_specs=[hbm] + [vmem] * 11,
        scratch=[pltpu.VMEM((4, B, B), f32), dma((4,))],
    )
    columns = [swapped(column, at) for at, column in enumerate(columns, 1)]
    real_part, row_part = call(
        real_kernel,
        [shape(5, B, B), shape(3, B)],
        [vmem] * 8,
        10,
        (left_high, left_low, self_high, self_low, other_one, real_two, other_y, weighted),
    )
    args = (held, derivative, members, high_one, low_one, high_two, low_two, imag_part, real_part, row_part)
    args += (near_one_more, near_two_more, *columns, out)
    new_density, forces = call(
        sixth_kernel,
        [shape(*density.shape), shape(3, 1, ATOMS)],
        [vmem] * 16 + [hbm],
        10,
        args,
        out_specs=[hbm, vmem],
        scratch=[pltpu.VMEM((6, B, B), f32), dma((6,))],
        aliases={16: 0},
    )
    return new_density, forces.reshape(1, 1, 3, ATOMS)


def solution(mesh):
    placed = (
        P("gx", "gy", None, None, None),
        P("gx", "gy", None, None, None),
        P(None, "gx", "gy", None, None, None),
        P("gx", "gy", None),
        P(None, "gx", "gy", None, None, None),
        P("gx", "gy", None),
    )
    return jax.shard_map(
        local,
        mesh=mesh,
        in_specs=placed,
        out_specs=(P(None, "gx", "gy", None, None, None), P("gx", "gy", None, None)),
        check_vma=False,
    )
```

```python
import jax
import jax.numpy as jnp
from jax import lax
from jax.experimental import pallas as pl
from jax.experimental.pallas import tpu as pltpu
from jax.sharding import PartitionSpec as P

B = 128
ATOMS = 64

time_step = 0.25
vmem = pl.BlockSpec(memory_space=pltpu.VMEM)
hbm = pl.BlockSpec(memory_space=pltpu.HBM)
f32 = jnp.float32
bf16 = jnp.bfloat16
dma = pltpu.SemaphoreType.DMA


def swapped(cells, edge):
    axis = "gx" if edge < 3 else "gy"
    count = lax.axis_size(axis)
    assert count % 2 == 0
    first = 0 if edge in (1, 3) else 1
    pairs = []
    for i in range(first, count, 2):
        j = (i + 1) % count
        pairs += [(i, j), (j, i)]
    return lax.ppermute(cells, axis, pairs)


def order_of():
    odd_x = lax.rem(lax.axis_index("gx"), 2)
    odd_y = lax.rem(lax.axis_index("gy"), 2)
    return 0, 1 + odd_x, 2 - odd_x, 3 + odd_y, 4 - odd_y


def cols(place, count=1):
    return slice(place * B, (place + count) * B)


def split(values):
    high = values.astype(bf16)
    return high, (values - high.astype(f32)).astype(bf16)


def beside(*pairs):
    return tuple(jnp.concatenate(parts, axis=1) for parts in zip(*pairs))


def dot(left, right):
    def one(a, b):
        return jnp.dot(a, b, preferred_element_type=f32)

    return one(left[0], right[0]) + (one(left[0], right[1]) + one(left[1], right[0]))


def part(pair, rows, columns):
    return pair[0][rows, columns], pair[1][rows, columns]


def rows_of(pair):
    return (pair[0][:B], pair[1][:B]), (pair[0][B:], pair[1][B:])


def store(pair, columns, values):
    pair[0][:, columns], pair[1][:, columns] = values


def start_all(copies):
    for copy in copies:
        copy.start()
    return copies


def first_kernel(cutoff_hbm, ham_hbm, inv_hbm, rho_hbm, one, two, cutoff_ref, cutoff_sem, sems):
    flags = pltpu.make_async_copy(cutoff_hbm, cutoff_ref, cutoff_sem)
    flags.start()
    order = order_of()
    copies = []
    for at, message in enumerate((one, two)):
        sources = (ham_hbm.at[0, 0, 0], inv_hbm.at[0, 0, 0], rho_hbm.at[1, 0, 0, 0], ham_hbm.at[0, 0, order[1 + at]])
        copies += start_all(
            [pltpu.make_async_copy(source, message.at[kind], sems.at[at, kind]) for kind, source in enumerate(sources)]
        )
    flags.wait()
    for copy in copies:
        copy.wait()
    for at, message in enumerate((one, two)):
        message[3] = message[3] * cutoff_ref[0, 0, order[1 + at]].astype(f32)


def second_kernel(
    cutoff_hbm, ham_hbm, inv_hbm, rho_hbm, atom_hbm, after, three, four, held, left_high, left_low, ham_high, ham_low, members,
    raw, cutoff_ref, atom_ref, cutoff_sem, atom_sem, sems
):
    flags = pltpu.make_async_copy(cutoff_hbm, cutoff_ref, cutoff_sem)
    flags.start()
    sources = (ham_hbm.at[0, 0], inv_hbm.at[0, 0], rho_hbm.at[0, 0, 0], rho_hbm.at[1, 0, 0])
    copies = start_all([pltpu.make_async_copy(source, raw.at[at], sems.at[at]) for at, source in enumerate(sources)])
    owners = pltpu.make_async_copy(atom_hbm, atom_ref, atom_sem)
    owners.start()
    order = order_of()
    flags.wait()
    keeps = [cutoff_ref[0, 0, offset].astype(f32) for offset in order]
    for kind, copy in enumerate(copies):
        copy.wait()
        for place, offset in enumerate(order):
            block = raw[kind, offset]
            if place == 0:
                three[(0, 1, 4, 2)[kind]] = block
                if kind != 2:
                    four[(0, 1, None, 2)[kind]] = block
            else:
                block = block * keeps[place]
                if place == 3:
                    three[(3, 5, 6, 7)[kind]] = block
                elif place == 4 and kind == 0:
                    four[3] = block
            if kind == 0:
                store((ham_high, ham_low), cols(place), split(block))
            else:
                held[kind - 1, place] = block
                rows = slice((kind - 1) * B, kind * B)
                left_high[rows, cols(place)], left_low[rows, cols(place)] = split(block)
    owners.wait()
    atoms = jnp.broadcast_to(atom_ref[0], (ATOMS, B))
    members[...] = -(lax.broadcasted_iota(jnp.int32, (ATOMS, B), 0) == atoms).astype(f32)


def first_half(left, place, start, near, diagonal):
    both = dot(part(left, slice(0, 3 * B), cols(place)), beside(split(near[0]), split(near[3])))
    mixed = split(start[:, cols(place)] + both[:, :B])
    prop, inner = rows_of(mixed)
    behind = dot(inner, split(near[1]))
    imag = dot(prop, split(near[2])) - behind[B:]
    return mixed, diagonal + both[:, B:], -behind[:B], imag


def second_half(mixed, near):
    prop, inner = rows_of(mixed)
    ahead = dot(prop, beside(split(near[0]), split(near[2]), split(near[3])))
    behind = dot(inner, split(near[1]))
    return ahead[:, cols(0)], ahead[:, cols(1)] - behind[:B], ahead[:, cols(2)] - behind[B:]


def send_more(more, held, place):
    more[0] = held[1, 0]
    for kind in range(3):
        more[1 + kind] = held[kind, place]


def third_kernel(
    left_high, left_low, ham_high, ham_low, held, one, one_more, two_more, start, mixed_high, mixed_low, diagonal, other
):
    send_more(one_more, held, 1)
    send_more(two_more, held, 2)
    left = (left_high, left_low)
    start[...] = dot(part(left, slice(0, 3 * B), cols(0)), part((ham_high, ham_low), slice(0, B), cols(0, 5)))
    mixed, diagonal[...], other[0], other[1] = first_half(left, 1, start, one, start[:, cols(0)])
    mixed_high[...], mixed_low[...] = mixed


def fourth_kernel(
    left_high, left_low, start, held, diagonal, three, four, four_more, mixed_high, mixed_low, diagonal_out, other
):
    send_more(four_more, held, 4)
    left = (left_high, left_low)
    mixed, total, real, other[1, 0] = first_half(left, 3, start, three, diagonal[...])
    added, other[0, 2], other[1, 2] = second_half(mixed, three[4:])
    other[0, 0] = real + added
    mixed, diagonal_out[...], other[0, 1], other[1, 1] = first_half(left, 4, start, four, total)
    mixed_high[...], mixed_low[...] = mixed


def fifth_kernel(
    left_high, left_low, start, diagonal, held, der_ref, other_one, other_y, two,
    out_hbm, mixed_high, mixed_low, self_high, self_low, real_two, comm, weighted, c1, c2, c3, c4, new, sems
):
    order = order_of()
    left = (left_high, left_low)
    mixed, total, real_two[...], imag_two = first_half(left, 2, start, two, diagonal[...])
    mixed_high[...], mixed_low[...] = mixed
    at_self = split(total)
    self_high[...], self_low[...] = at_self
    whole = cols(0, 5)
    ahead = dot(part(at_self, slice(0, B), cols(0)), part(left, slice(2 * B, 3 * B), whole))
    behind = dot(part(at_self, slice(2 * B, 3 * B), cols(0)), part(left, slice(0, B), whole))
    imag_comm = ahead - behind
    comm[...] = imag_comm[:, cols(0)] + other_y[1, 2]
    sums = [None] * 3
    copies = []
    for place, column in enumerate((c1, c2, c3, c4), 1):
        imag = (other_one[1], imag_two, other_y[1, 0], other_y[1, 1])[place - 1]
        real_new = held[1, place] + time_step * (imag_comm[:, cols(place)] + imag)
        new[place - 1] = real_new
        copies += start_all(
            [pltpu.make_async_copy(new.at[place - 1], out_hbm.at[0, 0, 0, order[place]], sems.at[place - 1])]
        )
        for direction in range(3):
            product = real_new * der_ref[direction, 0, 0, order[place]]
            sums[direction] = product if place == 1 else sums[direction] + product
            column[direction : direction + 1, :] = jnp.sum(product, axis=0, keepdims=True)
    for direction in range(3):
        weighted[direction] = sums[direction]
    for copy in copies:
        copy.wait()


def real_kernel(
    left_high, left_low, self_high, self_low, other_one, real_two, other_y, weighted, high_one, low_one, high_four, low_four,
    imag_part, one, four, comm, imag_out, row_part
):
    left = (left_high, left_low)
    whole = cols(0, 5)
    at_self = (self_high, self_low)
    ahead = dot(part(at_self, slice(0, B), cols(0)), part(left, slice(B, 2 * B), whole))
    behind = dot(part(at_self, slice(B, 2 * B), cols(0)), part(left, slice(0, B), whole))
    real_comm = ahead - behind
    added_one, real_one, imag_one = second_half((high_one[...], low_one[...]), one)
    added_four, real_four, imag_four = second_half((high_four[...], low_four[...]), four)
    comm[0] = real_comm[:, cols(0)] + other_y[0, 2] + real_one + real_four
    comm[1] = real_comm[:, cols(1)] + other_one[0] + added_one
    comm[2] = real_comm[:, cols(2)] + real_two[...]
    comm[3] = real_comm[:, cols(3)] + other_y[0, 0]
    comm[4] = real_comm[:, cols(4)] + other_y[0, 1] + added_four
    imag_out[...] = imag_part[...] + imag_one + imag_four
    for direction in range(3):
        row_part[direction : direction + 1, :] = jnp.sum(weighted[direction].T, axis=0, keepdims=True)


def sixth_kernel(
    held, der_ref, members, high_two, low_two, imag_part, real_part, row_part, two, c1, c2, c3, c4, old_hbm,
    out_hbm, forces_ref, new, sems
):
    order = order_of()
    added, real_two, imag_two = second_half((high_two[...], low_two[...]), two)
    real_new = held[1, 0] + time_step * (imag_part[...] + imag_two)
    new[5] = real_new
    copies = start_all([pltpu.make_async_copy(new.at[5], out_hbm.at[0, 0, 0, 0], sems.at[5])])
    for place in range(5):
        comm = real_part[place]
        if place in (0, 2):
            comm = comm + (real_two if place == 0 else added)
        new[place] = held[2, place] - time_step * comm
        copies += start_all([pltpu.make_async_copy(new.at[place], out_hbm.at[1, 0, 0, order[place]], sems.at[place])])
    parts = []
    for direction in range(3):
        product = real_new * der_ref[direction, 0, 0, 0]
        parts.append(jnp.sum(product + product.T, axis=0, keepdims=True))
    orbital = jnp.concatenate(parts, axis=0) + row_part[...] + ((c1[...] + c2[...]) + (c3[...] + c4[...]))
    forces = lax.dot_general(
        orbital, members[...], (((1,), (1,)), ((), ())), precision=lax.Precision.HIGHEST, preferred_element_type=f32
    )
    for direction in range(3):
        forces_ref[direction] = forces[direction : direction + 1]
    for copy in copies:
        copy.wait()


def call(kernel, shapes, in_specs, products, args, out_specs=None, scratch=(), aliases={}):
    moved = sum(4 * x.size for x in args) + sum(4 * x.size for x in shapes)
    return pl.pallas_call(
        kernel,
        out_shape=shapes,
        in_specs=in_specs,
        out_specs=out_specs or [vmem] * len(shapes),
        scratch_shapes=scratch,
        input_output_aliases=aliases,
        compiler_params=pltpu.CompilerParams(vmem_limit_bytes=32 * 2**20),
        cost_estimate=pl.CostEstimate(flops=products * 6 * B**3, bytes_accessed=moved, transcendentals=0),
    )(*args)


def local(hamiltonian, inverse_margin, density, cutoff, derivative, atom_of):
    def shape(*dims, kind=f32):
        return jax.ShapeDtypeStruct(dims, kind)

    hamiltonian, inverse_margin, density, cutoff, atom_of = (
        pltpu.with_memory_space_constraint(x, pltpu.HBM) for x in (hamiltonian, inverse_margin, density, cutoff, atom_of)
    )
    flags = pltpu.SMEM((1, 1, 5), jnp.int32)
    message = shape(4, B, B)
    first_one, first_two = call(
        first_kernel,
        [message] * 2,
        [hbm] * 4,
        0,
        (cutoff, hamiltonian, inverse_margin, density),
        scratch=[flags, dma(()), dma((2, 4))],
    )
    near_one = swapped(first_one, 1)
    near_two = swapped(first_two, 2)
    left = [shape(3 * B, 5 * B, kind=bf16)] * 2
    ham = [shape(B, 5 * B, kind=bf16)] * 2
    send_three, send_four, held, left_high, left_low, ham_high, ham_low, members = call(
        second_kernel,
        [shape(8, B, B), message, shape(3, 5, B, B)] + left + ham + [shape(ATOMS, B)],
        [hbm] * 6,
        0,
        (cutoff, hamiltonian, inverse_margin, density, atom_of, first_one),
        scratch=[pltpu.VMEM((4, 5, B, B), f32), flags, pltpu.VMEM((1, 1, B), jnp.int32), dma(()), dma(()), dma((4,))],
    )
    near_four = swapped(send_four, 4)
    near_three = swapped(send_three, 3)
    mixed = [shape(3 * B, B, kind=bf16)] * 2
    one_more, two_more, start, high_one, low_one, diagonal, other_one = call(
        third_kernel,
        [message] * 2 + [shape(3 * B, 5 * B)] + mixed + [shape(3 * B, B), shape(2, B, B)],
        [vmem] * 6,
        8000,
        (left_high, left_low, ham_high, ham_low, held, near_one),
    )
    near_one_more = swapped(one_more, 1)
    near_two_more = swapped(two_more, 2)
    four_more, high_four, low_four, diagonal, other_y = call(
        fourth_kernel,
        [message] + mixed + [shape(3 * B, B), shape(2, 3, B, B)],
        [vmem] * 7,
        28,
        (left_high, left_low, start, held, diagonal, near_three, near_four),
    )
    near_four_more = swapped(four_more, 4)
    out, high_two, low_two, self_high, self_low, real_two, imag_part, weighted, *columns = call(
        fifth_kernel,
        [shape(*density.shape)] + mixed * 2 + [shape(B, B), shape(B, B), shape(3, B, B)] + [shape(3, B)] * 4,
        [vmem] * 9,
        22,
        (left_high, left_low, start, diagonal, held, derivative, other_one, other_y, near_two),
        out_specs=[hbm] + [vmem] * 11,
        scratch=[pltpu.VMEM((4, B, B), f32), dma((4,))],
    )
    columns = [swapped(column, at) for at, column in enumerate(columns, 1)]
    args = (left_high, left_low, self_high, self_low, other_one, real_two, other_y, weighted, high_one, low_one)
    args += (high_four, low_four, imag_part, near_one_more, near_four_more)
    real_part, imag_part, row_part = call(
        real_kernel, [shape(5, B, B), shape(B, B), shape(3, B)], [vmem] * 15, 20, args
    )
    args = (held, derivative, members, high_two, low_two, imag_part, real_part, row_part, near_two_more, *columns, out)
    new_density, forces = call(
        sixth_kernel,
        [shape(*density.shape), shape(3, 1, ATOMS)],
        [vmem] * 13 + [hbm],
        10,
        args,
        out_specs=[hbm, vmem],
        scratch=[pltpu.VMEM((6, B, B), f32), dma((6,))],
        aliases={13: 0},
    )
    return new_density, forces.reshape(1, 1, 3, ATOMS)


def solution(mesh):
    placed = (
        P("gx", "gy", None, None, None),
        P("gx", "gy", None, None, None),
        P(None, "gx", "gy", None, None, None),
        P("gx", "gy", None),
        P(None, "gx", "gy", None, None, None),
        P("gx", "gy", None),
    )
    return jax.shard_map(
        local,
        mesh=mesh,
        in_specs=placed,
        out_specs=(P(None, "gx", "gy", None, None, None), P("gx", "gy", None, None)),
        check_vma=False,
    )
```

```python
import functools

import jax
import jax.numpy as jnp
from jax import lax
from jax.experimental import pallas as pl
from jax.experimental.pallas import tpu as pltpu
from jax.sharding import PartitionSpec as P

B = 128
ATOMS = 64

time_step = 0.25
vmem = pl.BlockSpec(memory_space=pltpu.VMEM)
hbm = pl.BlockSpec(memory_space=pltpu.HBM)
f32 = jnp.float32
bf16 = jnp.bfloat16
dma = pltpu.SemaphoreType.DMA


def swapped(cells, edge):
    axis = "gx" if edge < 3 else "gy"
    count = lax.axis_size(axis)
    assert count % 2 == 0
    first = 0 if edge in (1, 3) else 1
    pairs = []
    for i in range(first, count, 2):
        j = (i + 1) % count
        pairs += [(i, j), (j, i)]
    return lax.ppermute(cells, axis, pairs)


def order_of():
    odd_x = lax.rem(lax.axis_index("gx"), 2)
    odd_y = lax.rem(lax.axis_index("gy"), 2)
    return 0, 1 + odd_x, 2 - odd_x, 3 + odd_y, 4 - odd_y


def cols(place, count=1):
    return slice(place * B, (place + count) * B)


def split(values):
    high = values.astype(bf16)
    return high, (values - high.astype(f32)).astype(bf16)


def beside(*pairs):
    return tuple(jnp.concatenate(parts, axis=1) for parts in zip(*pairs))


def dot(left, right):
    def one(a, b):
        return jnp.dot(a, b, preferred_element_type=f32)

    return one(left[0], right[0]) + (one(left[0], right[1]) + one(left[1], right[0]))


def part(pair, rows, columns):
    return pair[0][rows, columns], pair[1][rows, columns]


def rows_of(pair):
    return (pair[0][:B], pair[1][:B]), (pair[0][B:], pair[1][B:])


def store(pair, columns, values):
    pair[0][:, columns], pair[1][:, columns] = values


def start_all(copies):
    for copy in copies:
        copy.start()
    return copies


def first_kernel(cutoff_hbm, ham_hbm, inv_hbm, rho_hbm, one, rest, cutoff_ref, cutoff_sem, sems):
    flags = pltpu.make_async_copy(cutoff_hbm, cutoff_ref, cutoff_sem)
    flags.start()
    order = order_of()
    sources = (ham_hbm.at[0, 0, 0], inv_hbm.at[0, 0, 0], rho_hbm.at[1, 0, 0, 0], ham_hbm.at[0, 0, order[1]])
    copies = [pltpu.make_async_copy(source, one.at[at], sems.at[at]) for at, source in enumerate(sources)]
    copies += [
        pltpu.make_async_copy(ham_hbm.at[0, 0, order[place]], rest.at[at], sems.at[4 + at]) for at, place in enumerate((4, 2))
    ]
    start_all(copies)
    flags.wait()
    for copy in copies:
        copy.wait()
    one[3] = one[3] * cutoff_ref[0, 0, order[1]].astype(f32)
    for at, place in enumerate((4, 2)):
        rest[at] = rest[at] * cutoff_ref[0, 0, order[place]].astype(f32)


def next_kernel(at, message, rest, out):
    out[:3] = message[:3]
    out[3] = rest[at]


def second_kernel(
    cutoff_hbm, ham_hbm, inv_hbm, rho_hbm, atom_hbm, after, three, held, left_high, left_low, ham_high, ham_low, members,
    raw, cutoff_ref, atom_ref, cutoff_sem, atom_sem, sems
):
    flags = pltpu.make_async_copy(cutoff_hbm, cutoff_ref, cutoff_sem)
    flags.start()
    sources = (ham_hbm.at[0, 0], inv_hbm.at[0, 0], rho_hbm.at[0, 0, 0], rho_hbm.at[1, 0, 0])
    copies = start_all([pltpu.make_async_copy(source, raw.at[at], sems.at[at]) for at, source in enumerate(sources)])
    owners = pltpu.make_async_copy(atom_hbm, atom_ref, atom_sem)
    owners.start()
    order = order_of()
    flags.wait()
    keeps = [cutoff_ref[0, 0, offset].astype(f32) for offset in order]
    for kind, copy in enumerate(copies):
        copy.wait()
        for place, offset in enumerate(order):
            block = raw[kind, offset]
            if place == 0:
                three[(0, 1, 4, 2)[kind]] = block
            else:
                block = block * keeps[place]
                if place == 3:
                    three[(3, 5, 6, 7)[kind]] = block
            if kind == 0:
                store((ham_high, ham_low), cols(place), split(block))
            else:
                held[kind - 1, place] = block
                rows = slice((kind - 1) * B, kind * B)
                left_high[rows, cols(place)], left_low[rows, cols(place)] = split(block)
    owners.wait()
    atoms = jnp.broadcast_to(atom_ref[0], (ATOMS, B))
    members[...] = -(lax.broadcasted_iota(jnp.int32, (ATOMS, B), 0) == atoms).astype(f32)


def first_half(left, place, start, near, diagonal):
    both = dot(part(left, slice(0, 3 * B), cols(place)), beside(split(near[0]), split(near[3])))
    mixed = split(start[:, cols(place)] + both[:, :B])
    prop, inner = rows_of(mixed)
    behind = dot(inner, split(near[1]))
    imag = dot(prop, split(near[2])) - behind[B:]
    return mixed, diagonal + both[:, B:], -behind[:B], imag


def second_half(mixed, near):
    prop, inner = rows_of(mixed)
    ahead = dot(prop, beside(split(near[0]), split(near[2]), split(near[3])))
    behind = dot(inner, split(near[1]))
    return ahead[:, cols(0)], ahead[:, cols(1)] - behind[:B], ahead[:, cols(2)] - behind[B:]


def send_more(more, held, place):
    more[0] = held[1, 0]
    for kind in range(3):
        more[1 + kind] = held[kind, place]


def third_kernel(
    left_high, left_low, ham_high, ham_low, held, four, one_more, four_more, start, mixed_high, mixed_low, diagonal, other
):
    send_more(one_more, held, 1)
    send_more(four_more, held, 4)
    left = (left_high, left_low)
    start[...] = dot(part(left, slice(0, 3 * B), cols(0)), part((ham_high, ham_low), slice(0, B), cols(0, 5)))
    mixed, diagonal[...], other[0], other[1] = first_half(left, 4, start, four, start[:, cols(0)])
    mixed_high[...], mixed_low[...] = mixed


def fourth_kernel(
    left_high, left_low, start, held, diagonal, one, three, two_more, mixed_high, mixed_low, diagonal_out, other
):
    send_more(two_more, held, 2)
    left = (left_high, left_low)
    mixed, total, real, other[1, 1] = first_half(left, 3, start, three, diagonal[...])
    added, other[0, 2], other[1, 2] = second_half(mixed, three[4:])
    other[0, 1] = real + added
    mixed, diagonal_out[...], other[0, 0], other[1, 0] = first_half(left, 1, start, one, total)
    mixed_high[...], mixed_low[...] = mixed


def fifth_kernel(
    left_high, left_low, start, diagonal, held, der_ref, other, other_four, two,
    out_hbm, mixed_high, mixed_low, self_high, self_low, real_two, comm, weighted, c1, c2, c3, c4, new, sems
):
    order = order_of()
    left = (left_high, left_low)
    mixed, total, real_two[...], imag_two = first_half(left, 2, start, two, diagonal[...])
    mixed_high[...], mixed_low[...] = mixed
    at_self = split(total)
    self_high[...], self_low[...] = at_self
    whole = cols(0, 5)
    ahead = dot(part(at_self, slice(0, B), cols(0)), part(left, slice(2 * B, 3 * B), whole))
    behind = dot(part(at_self, slice(2 * B, 3 * B), cols(0)), part(left, slice(0, B), whole))
    imag_comm = ahead - behind
    comm[...] = imag_comm[:, cols(0)] + other[1, 2]
    sums = [None] * 3
    copies = []
    for place, column in enumerate((c1, c2, c3, c4), 1):
        imag = (other[1, 0], imag_two, other[1, 1], other_four[1])[place - 1]
        real_new = held[1, place] + time_step * (imag_comm[:, cols(place)] + imag)
        new[place - 1] = real_new
        copies += start_all(
            [pltpu.make_async_copy(new.at[place - 1], out_hbm.at[0, 0, 0, order[place]], sems.at[place - 1])]
        )
        for direction in range(3):
            product = real_new * der_ref[direction, 0, 0, order[place]]
            sums[direction] = product if place == 1 else sums[direction] + product
            column[direction : direction + 1, :] = jnp.sum(product, axis=0, keepdims=True)
    for direction in range(3):
        weighted[direction] = sums[direction]
    for copy in copies:
        copy.wait()


def real_kernel(
    left_high, left_low, self_high, self_low, other, real_two, other_four, weighted, high_one, low_one, high_four, low_four,
    imag_part, one, four, comm, imag_out, row_part
):
    left = (left_high, left_low)
    whole = cols(0, 5)
    at_self = (self_high, self_low)
    ahead = dot(part(at_self, slice(0, B), cols(0)), part(left, slice(B, 2 * B), whole))
    behind = dot(part(at_self, slice(B, 2 * B), cols(0)), part(left, slice(0, B), whole))
    real_comm = ahead - behind
    added_one, real_one, imag_one = second_half((high_one[...], low_one[...]), one)
    added_four, real_four, imag_four = second_half((high_four[...], low_four[...]), four)
    comm[0] = real_comm[:, cols(0)] + other[0, 2] + real_one + real_four
    comm[1] = real_comm[:, cols(1)] + other[0, 0] + added_one
    comm[2] = real_comm[:, cols(2)] + real_two[...]
    comm[3] = real_comm[:, cols(3)] + other[0, 1]
    comm[4] = real_comm[:, cols(4)] + other_four[0] + added_four
    imag_out[...] = imag_part[...] + imag_one + imag_four
    for direction in range(3):
        row_part[direction : direction + 1, :] = jnp.sum(weighted[direction].T, axis=0, keepdims=True)


def sixth_kernel(
    held, der_ref, members, high_two, low_two, imag_part, real_part, row_part, two, c1, c2, c3, c4, old_hbm,
    out_hbm, forces_ref, new, sems
):
    order = order_of()
    added, real_two, imag_two = second_half((high_two[...], low_two[...]), two)
    real_new = held[1, 0] + time_step * (imag_part[...] + imag_two)
    new[5] = real_new
    copies = start_all([pltpu.make_async_copy(new.at[5], out_hbm.at[0, 0, 0, 0], sems.at[5])])
    for place in range(5):
        comm = real_part[place]
        if place in (0, 2):
            comm = comm + (real_two if place == 0 else added)
        new[place] = held[2, place] - time_step * comm
        copies += start_all([pltpu.make_async_copy(new.at[place], out_hbm.at[1, 0, 0, order[place]], sems.at[place])])
    parts = []
    for direction in range(3):
        product = real_new * der_ref[direction, 0, 0, 0]
        parts.append(jnp.sum(product + product.T, axis=0, keepdims=True))
    orbital = jnp.concatenate(parts, axis=0) + row_part[...] + ((c1[...] + c2[...]) + (c3[...] + c4[...]))
    forces = lax.dot_general(
        orbital, members[...], (((1,), (1,)), ((), ())), precision=lax.Precision.HIGHEST, preferred_element_type=f32
    )
    for direction in range(3):
        forces_ref[direction] = forces[direction : direction + 1]
    for copy in copies:
        copy.wait()


def call(kernel, shapes, in_specs, products, args, out_specs=None, scratch=(), aliases={}):
    moved = sum(4 * x.size for x in args) + sum(4 * x.size for x in shapes)
    return pl.pallas_call(
        kernel,
        out_shape=shapes,
        in_specs=in_specs,
        out_specs=out_specs or [vmem] * len(shapes),
        scratch_shapes=scratch,
        input_output_aliases=aliases,
        compiler_params=pltpu.CompilerParams(vmem_limit_bytes=32 * 2**20),
        cost_estimate=pl.CostEstimate(flops=products * 6 * B**3, bytes_accessed=moved, transcendentals=0),
    )(*args)


def local(hamiltonian, inverse_margin, density, cutoff, derivative, atom_of):
    def shape(*dims, kind=f32):
        return jax.ShapeDtypeStruct(dims, kind)

    hamiltonian, inverse_margin, density, cutoff, atom_of = (
        pltpu.with_memory_space_constraint(x, pltpu.HBM) for x in (hamiltonian, inverse_margin, density, cutoff, atom_of)
    )
    flags = pltpu.SMEM((1, 1, 5), jnp.int32)
    message = shape(4, B, B)
    first_one, rest = call(
        first_kernel,
        [message, shape(2, B, B)],
        [hbm] * 4,
        0,
        (cutoff, hamiltonian, inverse_margin, density),
        scratch=[flags, dma(()), dma((6,))],
    )
    near_one = swapped(first_one, 1)
    (first_four,) = call(functools.partial(next_kernel, 0), [message], [vmem] * 2, 0, (first_one, rest))
    near_four = swapped(first_four, 4)
    (first_two,) = call(functools.partial(next_kernel, 1), [message], [vmem] * 2, 0, (first_four, rest))
    near_two = swapped(first_two, 2)
    left = [shape(3 * B, 5 * B, kind=bf16)] * 2
    ham = [shape(B, 5 * B, kind=bf16)] * 2
    send_three, held, left_high, left_low, ham_high, ham_low, members = call(
        second_kernel,
        [shape(8, B, B), shape(3, 5, B, B)] + left + ham + [shape(ATOMS, B)],
        [hbm] * 6,
        0,
        (cutoff, hamiltonian, inverse_margin, density, atom_of, first_two),
        scratch=[pltpu.VMEM((4, 5, B, B), f32), flags, pltpu.VMEM((1, 1, B), jnp.int32), dma(()), dma(()), dma((4,))],
    )
    near_three = swapped(send_three, 3)
    mixed = [shape(3 * B, B, kind=bf16)] * 2
    one_more, four_more, start, high_four, low_four, diagonal, other_four = call(
        third_kernel,
        [message] * 2 + [shape(3 * B, 5 * B)] + mixed + [shape(3 * B, B), shape(2, B, B)],
        [vmem] * 6,
        8000,
        (left_high, left_low, ham_high, ham_low, held, near_four),
    )
    near_one_more = swapped(one_more, 1)
    near_four_more = swapped(four_more, 4)
    two_more, high_one, low_one, diagonal, other = call(
        fourth_kernel,
        [message] + mixed + [shape(3 * B, B), shape(2, 3, B, B)],
        [vmem] * 7,
        24,
        (left_high, left_low, start, held, diagonal, near_one, near_three),
    )
    near_two_more = swapped(two_more, 2)
    out, high_two, low_two, self_high, self_low, real_two, imag_part, weighted, *columns = call(
        fifth_kernel,
        [shape(*density.shape)] + mixed * 2 + [shape(B, B), shape(B, B), shape(3, B, B)] + [shape(3, B)] * 4,
        [vmem] * 9,
        22,
        (left_high, left_low, start, diagonal, held, derivative, other, other_four, near_two),
        out_specs=[hbm] + [vmem] * 11,
        scratch=[pltpu.VMEM((4, B, B), f32), dma((4,))],
    )
    columns = [swapped(column, at) for at, column in enumerate(columns, 1)]
    args = (left_high, left_low, self_high, self_low, other, real_two, other_four, weighted, high_one, low_one)
    args += (high_four, low_four, imag_part, near_one_more, near_four_more)
    real_part, imag_part, row_part = call(
        real_kernel, [shape(5, B, B), shape(B, B), shape(3, B)], [vmem] * 15, 20, args
    )
    args = (held, derivative, members, high_two, low_two, imag_part, real_part, row_part, near_two_more, *columns, out)
    new_density, forces = call(
        sixth_kernel,
        [shape(*density.shape), shape(3, 1, ATOMS)],
        [vmem] * 13 + [hbm],
        10,
        args,
        out_specs=[hbm, vmem],
        scratch=[pltpu.VMEM((6, B, B), f32), dma((6,))],
        aliases={13: 0},
    )
    return new_density, forces.reshape(1, 1, 3, ATOMS)


def solution(mesh):
    placed = (
        P("gx", "gy", None, None, None),
        P("gx", "gy", None, None, None),
        P(None, "gx", "gy", None, None, None),
        P("gx", "gy", None),
        P(None, "gx", "gy", None, None, None),
        P("gx", "gy", None),
    )
    return jax.shard_map(
        local,
        mesh=mesh,
        in_specs=placed,
        out_specs=(P(None, "gx", "gy", None, None, None), P("gx", "gy", None, None)),
        check_vma=False,
    )
```

```python
import functools

import jax
import jax.numpy as jnp
from jax import lax
from jax.experimental import pallas as pl
from jax.experimental.pallas import tpu as pltpu
from jax.sharding import PartitionSpec as P

B = 128
ATOMS = 64

time_step = 0.25
vmem = pl.BlockSpec(memory_space=pltpu.VMEM)
hbm = pl.BlockSpec(memory_space=pltpu.HBM)
f32 = jnp.float32
bf16 = jnp.bfloat16
dma = pltpu.SemaphoreType.DMA


def swapped(cells, edge):
    axis = "gx" if edge < 3 else "gy"
    count = lax.axis_size(axis)
    assert count % 2 == 0
    first = 0 if edge in (1, 3) else 1
    pairs = []
    for i in range(first, count, 2):
        j = (i + 1) % count
        pairs += [(i, j), (j, i)]
    return lax.ppermute(cells, axis, pairs)


def order_of():
    odd_x = lax.rem(lax.axis_index("gx"), 2)
    odd_y = lax.rem(lax.axis_index("gy"), 2)
    return 0, 1 + odd_x, 2 - odd_x, 3 + odd_y, 4 - odd_y


def cols(place, count=1):
    return slice(place * B, (place + count) * B)


def split(values):
    high = values.astype(bf16)
    return high, (values - high.astype(f32)).astype(bf16)


def beside(*pairs):
    return tuple(jnp.concatenate(parts, axis=1) for parts in zip(*pairs))


def dot(left, right):
    def one(a, b):
        return jnp.dot(a, b, preferred_element_type=f32)

    return one(left[0], right[0]) + (one(left[0], right[1]) + one(left[1], right[0]))


def part(pair, rows, columns):
    return pair[0][rows, columns], pair[1][rows, columns]


def rows_of(pair):
    return (pair[0][:B], pair[1][:B]), (pair[0][B:], pair[1][B:])


def store(pair, columns, values):
    pair[0][:, columns], pair[1][:, columns] = values


def start_all(copies):
    for copy in copies:
        copy.start()
    return copies


def first_kernel(cutoff_hbm, ham_hbm, inv_hbm, rho_hbm, one, rest, cutoff_ref, cutoff_sem, sems):
    flags = pltpu.make_async_copy(cutoff_hbm, cutoff_ref, cutoff_sem)
    flags.start()
    order = order_of()
    sources = (ham_hbm.at[0, 0, 0], inv_hbm.at[0, 0, 0], rho_hbm.at[1, 0, 0, 0], ham_hbm.at[0, 0, order[1]])
    copies = [pltpu.make_async_copy(source, one.at[at], sems.at[at]) for at, source in enumerate(sources)]
    copies += [
        pltpu.make_async_copy(ham_hbm.at[0, 0, order[place]], rest.at[at], sems.at[4 + at]) for at, place in enumerate((4, 2))
    ]
    start_all(copies)
    flags.wait()
    for copy in copies:
        copy.wait()
    one[3] = one[3] * cutoff_ref[0, 0, order[1]].astype(f32)
    for at, place in enumerate((4, 2)):
        rest[at] = rest[at] * cutoff_ref[0, 0, order[place]].astype(f32)


def next_kernel(at, message, rest, out):
    out[:3] = message[:3]
    out[3] = rest[at]


def second_kernel(
    cutoff_hbm, ham_hbm, inv_hbm, rho_hbm, atom_hbm, after, three, held, left_high, left_low, ham_high, ham_low, members,
    raw, cutoff_ref, atom_ref, cutoff_sem, atom_sem, sems
):
    flags = pltpu.make_async_copy(cutoff_hbm, cutoff_ref, cutoff_sem)
    flags.start()
    sources = (ham_hbm.at[0, 0], inv_hbm.at[0, 0], rho_hbm.at[0, 0, 0], rho_hbm.at[1, 0, 0])
    copies = start_all([pltpu.make_async_copy(source, raw.at[at], sems.at[at]) for at, source in enumerate(sources)])
    owners = pltpu.make_async_copy(atom_hbm, atom_ref, atom_sem)
    owners.start()
    order = order_of()
    flags.wait()
    keeps = [cutoff_ref[0, 0, offset].astype(f32) for offset in order]
    for kind, copy in enumerate(copies):
        copy.wait()
        for place, offset in enumerate(order):
            block = raw[kind, offset]
            if place == 0:
                three[(0, 1, 4, 2)[kind]] = block
            else:
                block = block * keeps[place]
                if place == 3:
                    three[(3, 5, 6, 7)[kind]] = block
            if kind == 0:
                store((ham_high, ham_low), cols(place), split(block))
            else:
                held[kind - 1, place] = block
                rows = slice((kind - 1) * B, kind * B)
                left_high[rows, cols(place)], left_low[rows, cols(place)] = split(block)
    owners.wait()
    atoms = jnp.broadcast_to(atom_ref[0], (ATOMS, B))
    members[...] = -(lax.broadcasted_iota(jnp.int32, (ATOMS, B), 0) == atoms).astype(f32)


def first_half(left, place, start, near, diagonal):
    both = dot(part(left, slice(0, 3 * B), cols(place)), beside(split(near[0]), split(near[3])))
    mixed = split(start[:, cols(place)] + both[:, :B])
    prop, inner = rows_of(mixed)
    behind = dot(inner, split(near[1]))
    imag = dot(prop, split(near[2])) - behind[B:]
    return mixed, diagonal + both[:, B:], -behind[:B], imag


def second_half(mixed, near):
    prop, inner = rows_of(mixed)
    ahead = dot(prop, beside(split(near[0]), split(near[2]), split(near[3])))
    behind = dot(inner, split(near[1]))
    return ahead[:, cols(0)], ahead[:, cols(1)] - behind[:B], ahead[:, cols(2)] - behind[B:]


def send_more(more, held, place):
    more[0] = held[1, 0]
    for kind in range(3):
        more[1 + kind] = held[kind, place]


def third_kernel(left_high, left_low, ham_high, ham_low, held, four, four_more, start, mixed_high, mixed_low, diagonal, other):
    send_more(four_more, held, 4)
    left = (left_high, left_low)
    start[...] = dot(part(left, slice(0, 3 * B), cols(0)), part((ham_high, ham_low), slice(0, B), cols(0, 5)))
    mixed, diagonal[...], other[0], other[1] = first_half(left, 4, start, four, start[:, cols(0)])
    mixed_high[...], mixed_low[...] = mixed


def whole_kernel(left_high, left_low, start, held, diagonal, three, one_more, diagonal_out, other):
    send_more(one_more, held, 1)
    mixed, diagonal_out[...], real, other[1, 0] = first_half((left_high, left_low), 3, start, three, diagonal[...])
    added, other[0, 1], other[1, 1] = second_half(mixed, three[4:])
    other[0, 0] = real + added


def fourth_kernel(left_high, left_low, start, diagonal, one, mixed_high, mixed_low, diagonal_out, other):
    mixed, diagonal_out[...], other[0], other[1] = first_half((left_high, left_low), 1, start, one, diagonal[...])
    mixed_high[...], mixed_low[...] = mixed


def fifth_kernel(
    left_high, left_low, start, diagonal, held, der_ref, other_one, other_three, other_four, two,
    two_more, new, mixed_high, mixed_low, self_high, self_low, real_two, comm, weighted, c1, c2, c3, c4
):
    send_more(two_more, held, 2)
    order = order_of()
    left = (left_high, left_low)
    mixed, total, real_two[...], imag_two = first_half(left, 2, start, two, diagonal[...])
    mixed_high[...], mixed_low[...] = mixed
    at_self = split(total)
    self_high[...], self_low[...] = at_self
    whole = cols(0, 5)
    ahead = dot(part(at_self, slice(0, B), cols(0)), part(left, slice(2 * B, 3 * B), whole))
    behind = dot(part(at_self, slice(2 * B, 3 * B), cols(0)), part(left, slice(0, B), whole))
    imag_comm = ahead - behind
    comm[...] = imag_comm[:, cols(0)] + other_three[1, 1]
    sums = [None] * 3
    for place, column in enumerate((c1, c2, c3, c4), 1):
        imag = (other_one[1], imag_two, other_three[1, 0], other_four[1])[place - 1]
        real_new = held[1, place] + time_step * (imag_comm[:, cols(place)] + imag)
        new[place - 1] = real_new
        for direction in range(3):
            product = real_new * der_ref[direction, 0, 0, order[place]]
            sums[direction] = product if place == 1 else sums[direction] + product
            column[direction : direction + 1, :] = jnp.sum(product, axis=0, keepdims=True)
    for direction in range(3):
        weighted[direction] = sums[direction]


def four_kernel(mixed_high, mixed_low, four, c3, c4, c3_out, c4_out, other):
    c3_out[...] = c3[...]
    c4_out[...] = c4[...]
    other[0], other[1], other[2] = second_half((mixed_high[...], mixed_low[...]), four)


def real_kernel(
    held, new, left_high, left_low, self_high, self_low, other_one, real_two, other_three, other_four, more_four, weighted,
    high_one, low_one, imag_part, one, out_hbm, comm, row_part, imag_new, sems
):
    order = order_of()
    copies = start_all(
        [pltpu.make_async_copy(new.at[at], out_hbm.at[0, 0, 0, order[1 + at]], sems.at[0, at]) for at in range(4)]
    )
    left = (left_high, left_low)
    whole = cols(0, 5)
    at_self = (self_high, self_low)
    ahead = dot(part(at_self, slice(0, B), cols(0)), part(left, slice(B, 2 * B), whole))
    behind = dot(part(at_self, slice(B, 2 * B), cols(0)), part(left, slice(0, B), whole))
    real_comm = ahead - behind
    added_one, real_one, imag_one = second_half((high_one[...], low_one[...]), one)
    others = ((1, other_one[0] + added_one), (3, other_three[0, 0]), (4, other_four[0] + more_four[0]))
    for at, (place, other) in enumerate(others):
        imag_new[at] = held[2, place] - time_step * (real_comm[:, cols(place)] + other)
        copies += start_all(
            [pltpu.make_async_copy(imag_new.at[at], out_hbm.at[1, 0, 0, order[place]], sems.at[1, at])]
        )
    comm[0] = real_comm[:, cols(0)] + other_three[0, 1] + real_one + more_four[1]
    comm[1] = imag_part[...] + imag_one + more_four[2]
    comm[2] = real_comm[:, cols(2)] + real_two[...]
    for direction in range(3):
        row_part[direction : direction + 1, :] = jnp.sum(weighted[direction].T, axis=0, keepdims=True)
    for copy in copies:
        copy.wait()


def sixth_kernel(
    held, der_ref, members, high_two, low_two, comm, row_part, two, c1, c2, c3, c4, old_hbm, out_hbm, forces_hbm, new, forces_ref, sems
):
    order = order_of()
    prop, inner = rows_of((high_two[...], low_two[...]))
    behind = dot(inner, split(two[1]))
    real_new = held[1, 0] + time_step * (comm[1] + dot(prop, split(two[3])) - behind[B:])
    new[0] = real_new
    copies = start_all([pltpu.make_async_copy(new.at[0], out_hbm.at[0, 0, 0, 0], sems.at[0])])
    parts = []
    for direction in range(3):
        product = real_new * der_ref[direction, 0, 0, 0]
        parts.append(jnp.sum(product + product.T, axis=0, keepdims=True))
    orbital = jnp.concatenate(parts, axis=0) + row_part[...] + ((c1[...] + c2[...]) + (c3[...] + c4[...]))
    forces = lax.dot_general(
        orbital, members[...], (((1,), (1,)), ((), ())), precision=lax.Precision.HIGHEST, preferred_element_type=f32
    )
    for direction in range(3):
        forces_ref[direction] = forces[direction : direction + 1]
    copies += start_all([pltpu.make_async_copy(forces_ref, forces_hbm, sems.at[3])])
    ahead = dot(prop, beside(split(two[2]), split(two[0])))
    new[1] = held[2, 0] - time_step * (comm[0] + ahead[:, cols(0)] - behind[:B])
    new[2] = held[2, 2] - time_step * (comm[2] + ahead[:, cols(1)])
    copies += start_all(
        [pltpu.make_async_copy(new.at[1 + at], out_hbm.at[1, 0, 0, order[2 * at]], sems.at[1 + at]) for at in range(2)]
    )
    for copy in copies:
        copy.wait()


def call(kernel, shapes, in_specs, products, args, out_specs=None, scratch=(), aliases={}):
    moved = sum(4 * x.size for x in args) + sum(4 * x.size for x in shapes)
    return pl.pallas_call(
        kernel,
        out_shape=shapes,
        in_specs=in_specs,
        out_specs=out_specs or [vmem] * len(shapes),
        scratch_shapes=scratch,
        input_output_aliases=aliases,
        compiler_params=pltpu.CompilerParams(vmem_limit_bytes=32 * 2**20),
        cost_estimate=pl.CostEstimate(flops=products * 6 * B**3, bytes_accessed=moved, transcendentals=0),
    )(*args)


def local(hamiltonian, inverse_margin, density, cutoff, derivative, atom_of):
    def shape(*dims, kind=f32):
        return jax.ShapeDtypeStruct(dims, kind)

    hamiltonian, inverse_margin, density, cutoff, atom_of = (
        pltpu.with_memory_space_constraint(x, pltpu.HBM) for x in (hamiltonian, inverse_margin, density, cutoff, atom_of)
    )
    flags = pltpu.SMEM((1, 1, 5), jnp.int32)
    message = shape(4, B, B)
    first_one, rest = call(
        first_kernel,
        [message, shape(2, B, B)],
        [hbm] * 4,
        0,
        (cutoff, hamiltonian, inverse_margin, density),
        scratch=[flags, dma(()), dma((6,))],
    )
    near_one = swapped(first_one, 1)
    (first_four,) = call(functools.partial(next_kernel, 0), [message], [vmem] * 2, 0, (first_one, rest))
    near_four = swapped(first_four, 4)
    (first_two,) = call(functools.partial(next_kernel, 1), [message], [vmem] * 2, 0, (first_four, rest))
    near_two = swapped(first_two, 2)
    left = [shape(3 * B, 5 * B, kind=bf16)] * 2
    ham = [shape(B, 5 * B, kind=bf16)] * 2
    send_three, held, left_high, left_low, ham_high, ham_low, members = call(
        second_kernel,
        [shape(8, B, B), shape(3, 5, B, B)] + left + ham + [shape(ATOMS, B)],
        [hbm] * 6,
        0,
        (cutoff, hamiltonian, inverse_margin, density, atom_of, first_two),
        scratch=[pltpu.VMEM((4, 5, B, B), f32), flags, pltpu.VMEM((1, 1, B), jnp.int32), dma(()), dma(()), dma((4,))],
    )
    near_three = swapped(send_three, 3)
    mixed = [shape(3 * B, B, kind=bf16)] * 2
    four_more, start, high_four, low_four, diagonal, other_four = call(
        third_kernel,
        [message, shape(3 * B, 5 * B)] + mixed + [shape(3 * B, B), shape(2, B, B)],
        [vmem] * 6,
        8000,
        (left_high, left_low, ham_high, ham_low, held, near_four),
    )
    near_four_more = swapped(four_more, 4)
    one_more, diagonal, other_three = call(
        whole_kernel,
        [message, shape(3 * B, B), shape(2, 2, B, B)],
        [vmem] * 6,
        14,
        (left_high, left_low, start, held, diagonal, near_three),
    )
    near_one_more = swapped(one_more, 1)
    high_one, low_one, diagonal, other_one = call(
        fourth_kernel,
        mixed + [shape(3 * B, B), shape(2, B, B)],
        [vmem] * 5,
        10,
        (left_high, left_low, start, diagonal, near_one),
    )
    block = shape(B, B)
    two_more, new, high_two, low_two, self_high, self_low, real_two, imag_part, weighted, *columns = call(
        fifth_kernel,
        [message, message] + mixed * 2 + [block, block, shape(3, B, B)] + [shape(3, B)] * 4,
        [vmem] * 10,
        22,
        (left_high, left_low, start, diagonal, held, derivative, other_one, other_three, other_four, near_two),
    )
    near_two_more = swapped(two_more, 2)
    c3, c4, more_four = call(
        four_kernel,
        [shape(3, B)] * 2 + [shape(3, B, B)],
        [vmem] * 5,
        5,
        (high_four, low_four, near_four_more, *columns[2:]),
    )
    columns = [swapped(column, at) for at, column in enumerate((*columns[:2], c3, c4), 1)]
    args = (held, new, left_high, left_low, self_high, self_low, other_one, real_two, other_three, other_four, more_four, weighted)
    args += (high_one, low_one, imag_part, near_one_more)
    out, comm, row_part = call(
        real_kernel,
        [shape(*density.shape), shape(3, B, B), shape(3, B)],
        [vmem] * 16,
        15,
        args,
        out_specs=[hbm] + [vmem] * 2,
        scratch=[pltpu.VMEM((3, B, B), f32), dma((2, 4))],
    )
    args = (held, derivative, members, high_two, low_two, comm, row_part, near_two_more, *columns, out)
    new_density, forces = call(
        sixth_kernel,
        [shape(*density.shape), shape(3, 1, ATOMS)],
        [vmem] * 12 + [hbm],
        10,
        args,
        out_specs=[hbm, hbm],
        scratch=[pltpu.VMEM((3, B, B), f32), pltpu.VMEM((3, 1, ATOMS), f32), dma((4,))],
        aliases={12: 0},
    )
    return new_density, forces.reshape(1, 1, 3, ATOMS)


def solution(mesh):
    placed = (
        P("gx", "gy", None, None, None),
        P("gx", "gy", None, None, None),
        P(None, "gx", "gy", None, None, None),
        P("gx", "gy", None),
        P(None, "gx", "gy", None, None, None),
        P("gx", "gy", None),
    )
    return jax.shard_map(
        local,
        mesh=mesh,
        in_specs=placed,
        out_specs=(P(None, "gx", "gy", None, None, None), P("gx", "gy", None, None)),
        check_vma=False,
    )
```

```python
import functools

import jax
import jax.numpy as jnp
from jax import lax
from jax.experimental import pallas as pl
from jax.experimental.pallas import tpu as pltpu
from jax.sharding import PartitionSpec as P

B = 128
ATOMS = 64

time_step = 0.25
vmem = pl.BlockSpec(memory_space=pltpu.VMEM)
hbm = pl.BlockSpec(memory_space=pltpu.HBM)
f32 = jnp.float32
bf16 = jnp.bfloat16
dma = pltpu.SemaphoreType.DMA


def swapped(cells, edge):
    axis = "gx" if edge < 3 else "gy"
    count = lax.axis_size(axis)
    assert count % 2 == 0
    first = 0 if edge in (1, 3) else 1
    pairs = []
    for i in range(first, count, 2):
        j = (i + 1) % count
        pairs += [(i, j), (j, i)]
    return lax.ppermute(cells, axis, pairs)


def order_of():
    odd_x = lax.rem(lax.axis_index("gx"), 2)
    odd_y = lax.rem(lax.axis_index("gy"), 2)
    return 0, 1 + odd_x, 2 - odd_x, 3 + odd_y, 4 - odd_y


def cols(place, count=1):
    return slice(place * B, (place + count) * B)


def split(values):
    high = values.astype(bf16)
    return high, (values - high.astype(f32)).astype(bf16)


def beside(*pairs):
    return tuple(jnp.concatenate(parts, axis=1) for parts in zip(*pairs))


def dot(left, right):
    def one(a, b):
        return jnp.dot(a, b, preferred_element_type=f32)

    return one(left[0], right[0]) + (one(left[0], right[1]) + one(left[1], right[0]))


def part(pair, rows, columns):
    return pair[0][rows, columns], pair[1][rows, columns]


def rows_of(pair):
    return (pair[0][:B], pair[1][:B]), (pair[0][B:], pair[1][B:])


def store(pair, columns, values):
    pair[0][:, columns], pair[1][:, columns] = values


def start_all(copies):
    for copy in copies:
        copy.start()
    return copies


def first_kernel(cutoff_hbm, ham_hbm, inv_hbm, rho_hbm, one, rest, cutoff_ref, cutoff_sem, sems):
    flags = pltpu.make_async_copy(cutoff_hbm, cutoff_ref, cutoff_sem)
    flags.start()
    order = order_of()
    sources = (ham_hbm.at[0, 0, 0], inv_hbm.at[0, 0, 0], rho_hbm.at[1, 0, 0, 0], ham_hbm.at[0, 0, order[1]])
    copies = [pltpu.make_async_copy(source, one.at[at], sems.at[at]) for at, source in enumerate(sources)]
    copies += [
        pltpu.make_async_copy(ham_hbm.at[0, 0, order[place]], rest.at[at], sems.at[4 + at]) for at, place in enumerate((4, 2))
    ]
    start_all(copies)
    flags.wait()
    for copy in copies:
        copy.wait()
    one[3] = one[3] * cutoff_ref[0, 0, order[1]].astype(f32)
    for at, place in enumerate((4, 2)):
        rest[at] = rest[at] * cutoff_ref[0, 0, order[place]].astype(f32)


def next_kernel(at, message, rest, out):
    out[:3] = message[:3]
    out[3] = rest[at]


def second_kernel(
    cutoff_hbm, ham_hbm, inv_hbm, rho_hbm, atom_hbm, after, three, held, left_high, left_low, ham_high, ham_low, members,
    raw, cutoff_ref, atom_ref, cutoff_sem, atom_sem, sems
):
    flags = pltpu.make_async_copy(cutoff_hbm, cutoff_ref, cutoff_sem)
    flags.start()
    sources = (ham_hbm.at[0, 0], inv_hbm.at[0, 0], rho_hbm.at[0, 0, 0], rho_hbm.at[1, 0, 0])
    copies = start_all([pltpu.make_async_copy(source, raw.at[at], sems.at[at]) for at, source in enumerate(sources)])
    owners = pltpu.make_async_copy(atom_hbm, atom_ref, atom_sem)
    owners.start()
    order = order_of()
    flags.wait()
    keeps = [cutoff_ref[0, 0, offset].astype(f32) for offset in order]
    for kind, copy in enumerate(copies):
        copy.wait()
        for place, offset in enumerate(order):
            block = raw[kind, offset]
            if place == 0:
                three[(0, 1, 4, 2)[kind]] = block
            else:
                block = block * keeps[place]
                if place == 3:
                    three[(3, 5, 6, 7)[kind]] = block
            if kind == 0:
                store((ham_high, ham_low), cols(place), split(block))
            else:
                held[kind - 1, place] = block
                rows = slice((kind - 1) * B, kind * B)
                left_high[rows, cols(place)], left_low[rows, cols(place)] = split(block)
    owners.wait()
    atoms = jnp.broadcast_to(atom_ref[0], (ATOMS, B))
    members[...] = -(lax.broadcasted_iota(jnp.int32, (ATOMS, B), 0) == atoms).astype(f32)


def first_half(left, place, start, near, diagonal):
    both = dot(part(left, slice(0, 3 * B), cols(place)), beside(split(near[0]), split(near[3])))
    mixed = split(start[:, cols(place)] + both[:, :B])
    prop, inner = rows_of(mixed)
    behind = dot(inner, split(near[1]))
    imag = dot(prop, split(near[2])) - behind[B:]
    return mixed, diagonal + both[:, B:], -behind[:B], imag


def second_half(mixed, near):
    prop, inner = rows_of(mixed)
    ahead = dot(prop, beside(split(near[0]), split(near[2]), split(near[3])))
    behind = dot(inner, split(near[1]))
    return ahead[:, cols(0)], ahead[:, cols(1)] - behind[:B], ahead[:, cols(2)] - behind[B:]


def send_more(more, held, place):
    more[0] = held[1, 0]
    for kind in range(3):
        more[1 + kind] = held[kind, place]


def third_kernel(left_high, left_low, ham_high, ham_low, held, four, four_more, start, mixed_high, mixed_low, diagonal, other):
    send_more(four_more, held, 4)
    left = (left_high, left_low)
    start[...] = dot(part(left, slice(0, 3 * B), cols(0)), part((ham_high, ham_low), slice(0, B), cols(0, 5)))
    mixed, diagonal[...], other[0], other[1] = first_half(left, 4, start, four, start[:, cols(0)])
    mixed_high[...], mixed_low[...] = mixed


def whole_kernel(left_high, left_low, start, held, diagonal, three, der_hbm, two_more, diagonal_out, other, der, sem):
    copy = pltpu.make_async_copy(der_hbm, der, sem)
    copy.start()
    send_more(two_more, held, 2)
    mixed, diagonal_out[...], real, other[1, 0] = first_half((left_high, left_low), 3, start, three, diagonal[...])
    added, other[0, 1], other[1, 1] = second_half(mixed, three[4:])
    other[0, 0] = real + added
    copy.wait()


def fourth_kernel(left_high, left_low, start, diagonal, one, mixed_high, mixed_low, diagonal_out, other):
    mixed, diagonal_out[...], other[0], other[1] = first_half((left_high, left_low), 1, start, one, diagonal[...])
    mixed_high[...], mixed_low[...] = mixed


def fifth_kernel(
    left_high, left_low, start, diagonal, held, der_ref, other_one, other_three, other_four, two,
    one_more, new, mixed_high, mixed_low, self_high, self_low, real_two, comm, weighted, c1, c2, c3, c4
):
    send_more(one_more, held, 1)
    order = order_of()
    left = (left_high, left_low)
    mixed, total, real_two[...], imag_two = first_half(left, 2, start, two, diagonal[...])
    mixed_high[...], mixed_low[...] = mixed
    at_self = split(total)
    self_high[...], self_low[...] = at_self
    whole = cols(0, 5)
    ahead = dot(part(at_self, slice(0, B), cols(0)), part(left, slice(2 * B, 3 * B), whole))
    behind = dot(part(at_self, slice(2 * B, 3 * B), cols(0)), part(left, slice(0, B), whole))
    imag_comm = ahead - behind
    comm[...] = imag_comm[:, cols(0)] + other_three[1, 1]
    sums = [None] * 3
    for place, column in enumerate((c1, c2, c3, c4), 1):
        imag = (other_one[1], imag_two, other_three[1, 0], other_four[1])[place - 1]
        real_new = held[1, place] + time_step * (imag_comm[:, cols(place)] + imag)
        new[place - 1] = real_new
        for direction in range(3):
            product = real_new * der_ref[direction, 0, 0, order[place]]
            sums[direction] = product if place == 1 else sums[direction] + product
            column[direction : direction + 1, :] = jnp.sum(product, axis=0, keepdims=True)
    for direction in range(3):
        weighted[direction] = sums[direction]


def pass_kernel(arrived, column, out):
    out[...] = column[...]


def four_kernel(mixed_high, mixed_low, four, column, out, other):
    out[...] = column[...]
    other[0], other[1], other[2] = second_half((mixed_high[...], mixed_low[...]), four)


def real_kernel(
    held, new, left_high, left_low, self_high, self_low, other_one, real_two, other_three, other_four, more_four, weighted,
    high_two, low_two, imag_part, two, out_hbm, comm, row_part, imag_new, sems
):
    order = order_of()
    copies = start_all(
        [pltpu.make_async_copy(new.at[at], out_hbm.at[0, 0, 0, order[1 + at]], sems.at[0, at]) for at in range(4)]
    )
    left = (left_high, left_low)
    whole = cols(0, 5)
    at_self = (self_high, self_low)
    ahead = dot(part(at_self, slice(0, B), cols(0)), part(left, slice(B, 2 * B), whole))
    behind = dot(part(at_self, slice(B, 2 * B), cols(0)), part(left, slice(0, B), whole))
    real_comm = ahead - behind
    added_two, real_self, imag_self = second_half((high_two[...], low_two[...]), two)
    others = ((2, real_two[...] + added_two), (3, other_three[0, 0]), (4, other_four[0] + more_four[0]))
    for at, (place, other) in enumerate(others):
        imag_new[at] = held[2, place] - time_step * (real_comm[:, cols(place)] + other)
        copies += start_all(
            [pltpu.make_async_copy(imag_new.at[at], out_hbm.at[1, 0, 0, order[place]], sems.at[1, at])]
        )
    comm[0] = real_comm[:, cols(0)] + other_three[0, 1] + real_self + more_four[1]
    comm[1] = imag_part[...] + imag_self + more_four[2]
    comm[2] = real_comm[:, cols(1)] + other_one[0]
    for direction in range(3):
        row_part[direction : direction + 1, :] = jnp.sum(weighted[direction].T, axis=0, keepdims=True)
    for copy in copies:
        copy.wait()


def sixth_kernel(
    held, der_ref, members, high_one, low_one, comm, row_part, one, c1, c2, c3, c4, old_hbm, out_hbm, forces_hbm, new, forces_ref, sems
):
    order = order_of()
    prop, inner = rows_of((high_one[...], low_one[...]))
    behind = dot(inner, split(one[1]))
    real_new = held[1, 0] + time_step * (comm[1] + dot(prop, split(one[3])) - behind[B:])
    new[0] = real_new
    copies = start_all([pltpu.make_async_copy(new.at[0], out_hbm.at[0, 0, 0, 0], sems.at[0])])
    parts = []
    for direction in range(3):
        product = real_new * der_ref[direction, 0, 0, 0]
        parts.append(jnp.sum(product + product.T, axis=0, keepdims=True))
    orbital = jnp.concatenate(parts, axis=0) + row_part[...] + ((c1[...] + c2[...]) + (c3[...] + c4[...]))
    forces = lax.dot_general(
        orbital, members[...], (((1,), (1,)), ((), ())), precision=lax.Precision.HIGHEST, preferred_element_type=f32
    )
    for direction in range(3):
        forces_ref[direction] = forces[direction : direction + 1]
    copies += start_all([pltpu.make_async_copy(forces_ref, forces_hbm, sems.at[3])])
    ahead = dot(prop, beside(split(one[2]), split(one[0])))
    new[1] = held[2, 0] - time_step * (comm[0] + ahead[:, cols(0)] - behind[:B])
    new[2] = held[2, 1] - time_step * (comm[2] + ahead[:, cols(1)])
    copies += start_all(
        [pltpu.make_async_copy(new.at[1 + at], out_hbm.at[1, 0, 0, order[at]], sems.at[1 + at]) for at in range(2)]
    )
    for copy in copies:
        copy.wait()


def call(kernel, shapes, in_specs, products, args, out_specs=None, scratch=(), aliases={}):
    moved = sum(4 * x.size for x in args) + sum(4 * x.size for x in shapes)
    return pl.pallas_call(
        kernel,
        out_shape=shapes,
        in_specs=in_specs,
        out_specs=out_specs or [vmem] * len(shapes),
        scratch_shapes=scratch,
        input_output_aliases=aliases,
        compiler_params=pltpu.CompilerParams(vmem_limit_bytes=32 * 2**20),
        cost_estimate=pl.CostEstimate(flops=products * 6 * B**3, bytes_accessed=moved, transcendentals=0),
    )(*args)


def local(hamiltonian, inverse_margin, density, cutoff, derivative, atom_of):
    def shape(*dims, kind=f32):
        return jax.ShapeDtypeStruct(dims, kind)

    args = (hamiltonian, inverse_margin, density, cutoff, derivative, atom_of)
    hamiltonian, inverse_margin, density, cutoff, derivative, atom_of = (
        pltpu.with_memory_space_constraint(x, pltpu.HBM) for x in args
    )
    flags = pltpu.SMEM((1, 1, 5), jnp.int32)
    message = shape(4, B, B)
    first_one, rest = call(
        first_kernel,
        [message, shape(2, B, B)],
        [hbm] * 4,
        0,
        (cutoff, hamiltonian, inverse_margin, density),
        scratch=[flags, dma(()), dma((6,))],
    )
    near_one = swapped(first_one, 1)
    (first_four,) = call(functools.partial(next_kernel, 0), [message], [vmem] * 2, 0, (first_one, rest))
    near_four = swapped(first_four, 4)
    (first_two,) = call(functools.partial(next_kernel, 1), [message], [vmem] * 2, 0, (first_four, rest))
    near_two = swapped(first_two, 2)
    left = [shape(3 * B, 5 * B, kind=bf16)] * 2
    ham = [shape(B, 5 * B, kind=bf16)] * 2
    send_three, held, left_high, left_low, ham_high, ham_low, members = call(
        second_kernel,
        [shape(8, B, B), shape(3, 5, B, B)] + left + ham + [shape(ATOMS, B)],
        [hbm] * 6,
        0,
        (cutoff, hamiltonian, inverse_margin, density, atom_of, first_two),
        scratch=[pltpu.VMEM((4, 5, B, B), f32), flags, pltpu.VMEM((1, 1, B), jnp.int32), dma(()), dma(()), dma((4,))],
    )
    near_three = swapped(send_three, 3)
    mixed = [shape(3 * B, B, kind=bf16)] * 2
    four_more, start, high_four, low_four, diagonal, other_four = call(
        third_kernel,
        [message, shape(3 * B, 5 * B)] + mixed + [shape(3 * B, B), shape(2, B, B)],
        [vmem] * 6,
        8000,
        (left_high, left_low, ham_high, ham_low, held, near_four),
    )
    near_four_more = swapped(four_more, 4)
    two_more, diagonal, other_three, derivative = call(
        whole_kernel,
        [message, shape(3 * B, B), shape(2, 2, B, B), shape(*derivative.shape)],
        [vmem] * 6 + [hbm],
        14,
        (left_high, left_low, start, held, diagonal, near_three, derivative),
        scratch=[dma(())],
    )
    near_two_more = swapped(two_more, 2)
    high_one, low_one, diagonal, other_one = call(
        fourth_kernel,
        mixed + [shape(3 * B, B), shape(2, B, B)],
        [vmem] * 5,
        10,
        (left_high, left_low, start, diagonal, near_one),
    )
    block = shape(B, B)
    one_more, new, high_two, low_two, self_high, self_low, real_two, imag_part, weighted, *columns = call(
        fifth_kernel,
        [message, message] + mixed * 2 + [block, block, shape(3, B, B)] + [shape(3, B)] * 4,
        [vmem] * 10,
        22,
        (left_high, left_low, start, diagonal, held, derivative, other_one, other_three, other_four, near_two),
    )
    near_one_more = swapped(one_more, 1)
    c4, more_four = call(
        four_kernel,
        [shape(3, B), shape(3, B, B)],
        [vmem] * 4,
        5,
        (high_four, low_four, near_four_more, columns[3]),
    )
    c1, c2, c3, _ = columns
    c2 = swapped(c2, 2)
    c1 = swapped(c1, 1)
    c4 = swapped(c4, 4)
    (c3,) = call(pass_kernel, [shape(3, B)], [vmem] * 2, 0, (c1, c3))
    columns = (c1, c2, swapped(c3, 3), c4)
    args = (held, new, left_high, left_low, self_high, self_low, other_one, real_two, other_three, other_four, more_four, weighted)
    args += (high_two, low_two, imag_part, near_two_more)
    out, comm, row_part = call(
        real_kernel,
        [shape(*density.shape), shape(3, B, B), shape(3, B)],
        [vmem] * 16,
        15,
        args,
        out_specs=[hbm] + [vmem] * 2,
        scratch=[pltpu.VMEM((3, B, B), f32), dma((2, 4))],
    )
    args = (held, derivative, members, high_one, low_one, comm, row_part, near_one_more, *columns, out)
    new_density, forces = call(
        sixth_kernel,
        [shape(*density.shape), shape(3, 1, ATOMS)],
        [vmem] * 12 + [hbm],
        10,
        args,
        out_specs=[hbm, hbm],
        scratch=[pltpu.VMEM((3, B, B), f32), pltpu.VMEM((3, 1, ATOMS), f32), dma((4,))],
        aliases={12: 0},
    )
    return new_density, forces.reshape(1, 1, 3, ATOMS)


def solution(mesh):
    placed = (
        P("gx", "gy", None, None, None),
        P("gx", "gy", None, None, None),
        P(None, "gx", "gy", None, None, None),
        P("gx", "gy", None),
        P(None, "gx", "gy", None, None, None),
        P("gx", "gy", None),
    )
    return jax.shard_map(
        local,
        mesh=mesh,
        in_specs=placed,
        out_specs=(P(None, "gx", "gy", None, None, None), P("gx", "gy", None, None)),
        check_vma=False,
    )
```

```python
import functools

import jax
import jax.numpy as jnp
from jax import lax
from jax.experimental import pallas as pl
from jax.experimental.pallas import tpu as pltpu
from jax.sharding import PartitionSpec as P

B = 128
ATOMS = 64

time_step = 0.25
vmem = pl.BlockSpec(memory_space=pltpu.VMEM)
hbm = pl.BlockSpec(memory_space=pltpu.HBM)
f32 = jnp.float32
bf16 = jnp.bfloat16
dma = pltpu.SemaphoreType.DMA


def swapped(cells, edge):
    axis = "gx" if edge < 3 else "gy"
    count = lax.axis_size(axis)
    assert count % 2 == 0
    first = 0 if edge in (1, 3) else 1
    pairs = []
    for i in range(first, count, 2):
        j = (i + 1) % count
        pairs += [(i, j), (j, i)]
    return lax.ppermute(cells, axis, pairs)


def order_of():
    odd_x = lax.rem(lax.axis_index("gx"), 2)
    odd_y = lax.rem(lax.axis_index("gy"), 2)
    return 0, 1 + odd_x, 2 - odd_x, 3 + odd_y, 4 - odd_y


def cols(place, count=1):
    return slice(place * B, (place + count) * B)


def split(values):
    high = values.astype(bf16)
    return high, (values - high.astype(f32)).astype(bf16)


def beside(*pairs):
    return tuple(jnp.concatenate(parts, axis=1) for parts in zip(*pairs))


def dot(left, right):
    def one(a, b):
        return jnp.dot(a, b, preferred_element_type=f32)

    return one(left[0], right[0]) + (one(left[0], right[1]) + one(left[1], right[0]))


def part(pair, rows, columns):
    return pair[0][rows, columns], pair[1][rows, columns]


def rows_of(pair):
    return (pair[0][:B], pair[1][:B]), (pair[0][B:], pair[1][B:])


def store(pair, columns, values):
    pair[0][:, columns], pair[1][:, columns] = values


def start_all(copies):
    for copy in copies:
        copy.start()
    return copies


def first_kernel(cutoff_hbm, ham_hbm, inv_hbm, rho_hbm, one, rest, cutoff_ref, cutoff_sem, sems):
    flags = pltpu.make_async_copy(cutoff_hbm, cutoff_ref, cutoff_sem)
    flags.start()
    order = order_of()
    sources = (ham_hbm.at[0, 0, 0], inv_hbm.at[0, 0, 0], rho_hbm.at[1, 0, 0, 0], ham_hbm.at[0, 0, order[1]])
    copies = [pltpu.make_async_copy(source, one.at[at], sems.at[at]) for at, source in enumerate(sources)]
    copies += [
        pltpu.make_async_copy(ham_hbm.at[0, 0, order[place]], rest.at[at], sems.at[4 + at]) for at, place in enumerate((4, 2))
    ]
    start_all(copies)
    flags.wait()
    for copy in copies:
        copy.wait()
    one[3] = one[3] * cutoff_ref[0, 0, order[1]].astype(f32)
    for at, place in enumerate((4, 2)):
        rest[at] = rest[at] * cutoff_ref[0, 0, order[place]].astype(f32)


def next_kernel(at, message, rest, out):
    out[:3] = message[:3]
    out[3] = rest[at]


def second_kernel(
    cutoff_hbm, ham_hbm, inv_hbm, rho_hbm, atom_hbm, after, three, held, left_high, left_low, ham_high, ham_low, members,
    raw, cutoff_ref, atom_ref, cutoff_sem, atom_sem, sems
):
    flags = pltpu.make_async_copy(cutoff_hbm, cutoff_ref, cutoff_sem)
    flags.start()
    sources = (ham_hbm.at[0, 0], inv_hbm.at[0, 0], rho_hbm.at[0, 0, 0], rho_hbm.at[1, 0, 0])
    copies = start_all([pltpu.make_async_copy(source, raw.at[at], sems.at[at]) for at, source in enumerate(sources)])
    owners = pltpu.make_async_copy(atom_hbm, atom_ref, atom_sem)
    owners.start()
    order = order_of()
    flags.wait()
    keeps = [cutoff_ref[0, 0, offset].astype(f32) for offset in order]
    for kind, copy in enumerate(copies):
        copy.wait()
        for place, offset in enumerate(order):
            block = raw[kind, offset]
            if place == 0:
                three[(0, 1, 4, 2)[kind]] = block
            else:
                block = block * keeps[place]
                if place == 3:
                    three[(3, 5, 6, 7)[kind]] = block
            if kind == 0:
                store((ham_high, ham_low), cols(place), split(block))
            else:
                held[kind - 1, place] = block
                rows = slice((kind - 1) * B, kind * B)
                left_high[rows, cols(place)], left_low[rows, cols(place)] = split(block)
    owners.wait()
    atoms = jnp.broadcast_to(atom_ref[0], (ATOMS, B))
    members[...] = -(lax.broadcasted_iota(jnp.int32, (ATOMS, B), 0) == atoms).astype(f32)


def first_half(left, place, start, near, diagonal):
    both = dot(part(left, slice(0, 3 * B), cols(place)), beside(split(near[0]), split(near[3])))
    mixed = split(start[:, cols(place)] + both[:, :B])
    prop, inner = rows_of(mixed)
    behind = dot(inner, split(near[1]))
    imag = dot(prop, split(near[2])) - behind[B:]
    return mixed, diagonal + both[:, B:], -behind[:B], imag


def second_half(mixed, near):
    prop, inner = rows_of(mixed)
    ahead = dot(prop, beside(split(near[0]), split(near[2]), split(near[3])))
    behind = dot(inner, split(near[1]))
    return ahead[:, cols(0)], ahead[:, cols(1)] - behind[:B], ahead[:, cols(2)] - behind[B:]


def send_more(more, held, place):
    more[0] = held[1, 0]
    for kind in range(3):
        more[1 + kind] = held[kind, place]


def third_kernel(left_high, left_low, ham_high, ham_low, held, four, four_more, start, mixed_high, mixed_low, diagonal, other):
    send_more(four_more, held, 4)
    left = (left_high, left_low)
    start[...] = dot(part(left, slice(0, 3 * B), cols(0)), part((ham_high, ham_low), slice(0, B), cols(0, 5)))
    mixed, diagonal[...], other[0], other[1] = first_half(left, 4, start, four, start[:, cols(0)])
    mixed_high[...], mixed_low[...] = mixed


def whole_kernel(left_high, left_low, start, held, diagonal, three, der_hbm, two_more, diagonal_out, other, der, sem):
    copy = pltpu.make_async_copy(der_hbm, der, sem)
    copy.start()
    send_more(two_more, held, 2)
    mixed, diagonal_out[...], real, other[1, 0] = first_half((left_high, left_low), 3, start, three, diagonal[...])
    added, other[0, 1], other[1, 1] = second_half(mixed, three[4:])
    other[0, 0] = real + added
    copy.wait()


def fourth_kernel(left_high, left_low, start, diagonal, one, mixed_high, mixed_low, diagonal_out, other):
    mixed, diagonal_out[...], other[0], other[1] = first_half((left_high, left_low), 1, start, one, diagonal[...])
    mixed_high[...], mixed_low[...] = mixed


def fifth_kernel(
    left_high, left_low, start, diagonal, held, der_ref, other_one, other_three, other_four, two,
    new, mixed_high, mixed_low, self_high, self_low, real_two, comm, weighted, c1, c2, c3, c4
):
    order = order_of()
    left = (left_high, left_low)
    mixed, total, real_two[...], imag_two = first_half(left, 2, start, two, diagonal[...])
    mixed_high[...], mixed_low[...] = mixed
    at_self = split(total)
    self_high[...], self_low[...] = at_self
    whole = cols(0, 5)
    ahead = dot(part(at_self, slice(0, B), cols(0)), part(left, slice(2 * B, 3 * B), whole))
    behind = dot(part(at_self, slice(2 * B, 3 * B), cols(0)), part(left, slice(0, B), whole))
    imag_comm = ahead - behind
    comm[...] = imag_comm[:, cols(0)] + other_three[1, 1]
    sums = [None] * 3
    for place, column in enumerate((c1, c2, c3, c4), 1):
        imag = (other_one[1], imag_two, other_three[1, 0], other_four[1])[place - 1]
        real_new = held[1, place] + time_step * (imag_comm[:, cols(place)] + imag)
        new[place - 1] = real_new
        for direction in range(3):
            product = real_new * der_ref[direction, 0, 0, order[place]]
            sums[direction] = product if place == 1 else sums[direction] + product
            column[direction : direction + 1, :] = jnp.sum(product, axis=0, keepdims=True)
    for direction in range(3):
        weighted[direction] = sums[direction]


def more_kernel(held, arrived, column, one_more, out):
    send_more(one_more, held, 1)
    out[...] = column[...]


def four_kernel(mixed_high, mixed_low, four, column, out, other):
    out[...] = column[...]
    other[0], other[1], other[2] = second_half((mixed_high[...], mixed_low[...]), four)


def real_kernel(
    held, new, left_high, left_low, self_high, self_low, other_one, real_two, other_three, other_four, more_four, weighted,
    high_two, low_two, imag_part, two, out_hbm, comm, row_part, imag_new, sems
):
    order = order_of()
    copies = start_all(
        [pltpu.make_async_copy(new.at[at], out_hbm.at[0, 0, 0, order[1 + at]], sems.at[0, at]) for at in range(4)]
    )
    left = (left_high, left_low)
    whole = cols(0, 5)
    at_self = (self_high, self_low)
    ahead = dot(part(at_self, slice(0, B), cols(0)), part(left, slice(B, 2 * B), whole))
    behind = dot(part(at_self, slice(B, 2 * B), cols(0)), part(left, slice(0, B), whole))
    real_comm = ahead - behind
    added_two, real_self, imag_self = second_half((high_two[...], low_two[...]), two)
    others = ((2, real_two[...] + added_two), (3, other_three[0, 0]), (4, other_four[0] + more_four[0]))
    for at, (place, other) in enumerate(others):
        imag_new[at] = held[2, place] - time_step * (real_comm[:, cols(place)] + other)
        copies += start_all(
            [pltpu.make_async_copy(imag_new.at[at], out_hbm.at[1, 0, 0, order[place]], sems.at[1, at])]
        )
    comm[0] = real_comm[:, cols(0)] + other_three[0, 1] + real_self + more_four[1]
    comm[1] = imag_part[...] + imag_self + more_four[2]
    comm[2] = real_comm[:, cols(1)] + other_one[0]
    for direction in range(3):
        row_part[direction : direction + 1, :] = jnp.sum(weighted[direction].T, axis=0, keepdims=True)
    for copy in copies:
        copy.wait()


def sixth_kernel(
    held, der_ref, members, high_one, low_one, comm, row_part, one, c1, c2, c3, c4, old_hbm, out_hbm, forces_hbm, new, forces_ref, sems
):
    order = order_of()
    prop, inner = rows_of((high_one[...], low_one[...]))
    behind = dot(inner, split(one[1]))
    real_new = held[1, 0] + time_step * (comm[1] + dot(prop, split(one[3])) - behind[B:])
    new[0] = real_new
    copies = start_all([pltpu.make_async_copy(new.at[0], out_hbm.at[0, 0, 0, 0], sems.at[0])])
    parts = []
    for direction in range(3):
        product = real_new * der_ref[direction, 0, 0, 0]
        parts.append(jnp.sum(product + product.T, axis=0, keepdims=True))
    orbital = jnp.concatenate(parts, axis=0) + row_part[...] + ((c1[...] + c2[...]) + (c3[...] + c4[...]))
    forces = lax.dot_general(
        orbital, members[...], (((1,), (1,)), ((), ())), precision=lax.Precision.HIGHEST, preferred_element_type=f32
    )
    for direction in range(3):
        forces_ref[direction] = forces[direction : direction + 1]
    copies += start_all([pltpu.make_async_copy(forces_ref, forces_hbm, sems.at[3])])
    ahead = dot(prop, beside(split(one[2]), split(one[0])))
    new[1] = held[2, 0] - time_step * (comm[0] + ahead[:, cols(0)] - behind[:B])
    new[2] = held[2, 1] - time_step * (comm[2] + ahead[:, cols(1)])
    copies += start_all(
        [pltpu.make_async_copy(new.at[1 + at], out_hbm.at[1, 0, 0, order[at]], sems.at[1 + at]) for at in range(2)]
    )
    for copy in copies:
        copy.wait()


def call(kernel, shapes, in_specs, products, args, out_specs=None, scratch=(), aliases={}):
    moved = sum(4 * x.size for x in args) + sum(4 * x.size for x in shapes)
    return pl.pallas_call(
        kernel,
        out_shape=shapes,
        in_specs=in_specs,
        out_specs=out_specs or [vmem] * len(shapes),
        scratch_shapes=scratch,
        input_output_aliases=aliases,
        compiler_params=pltpu.CompilerParams(vmem_limit_bytes=32 * 2**20),
        cost_estimate=pl.CostEstimate(flops=products * 6 * B**3, bytes_accessed=moved, transcendentals=0),
    )(*args)


def local(hamiltonian, inverse_margin, density, cutoff, derivative, atom_of):
    def shape(*dims, kind=f32):
        return jax.ShapeDtypeStruct(dims, kind)

    args = (hamiltonian, inverse_margin, density, cutoff, derivative, atom_of)
    hamiltonian, inverse_margin, density, cutoff, derivative, atom_of = (
        pltpu.with_memory_space_constraint(x, pltpu.HBM) for x in args
    )
    flags = pltpu.SMEM((1, 1, 5), jnp.int32)
    message = shape(4, B, B)
    first_one, rest = call(
        first_kernel,
        [message, shape(2, B, B)],
        [hbm] * 4,
        0,
        (cutoff, hamiltonian, inverse_margin, density),
        scratch=[flags, dma(()), dma((6,))],
    )
    near_one = swapped(first_one, 1)
    (first_four,) = call(functools.partial(next_kernel, 0), [message], [vmem] * 2, 0, (first_one, rest))
    near_four = swapped(first_four, 4)
    (first_two,) = call(functools.partial(next_kernel, 1), [message], [vmem] * 2, 500, (first_four, rest))
    near_two = swapped(first_two, 2)
    left = [shape(3 * B, 5 * B, kind=bf16)] * 2
    ham = [shape(B, 5 * B, kind=bf16)] * 2
    send_three, held, left_high, left_low, ham_high, ham_low, members = call(
        second_kernel,
        [shape(8, B, B), shape(3, 5, B, B)] + left + ham + [shape(ATOMS, B)],
        [hbm] * 6,
        0,
        (cutoff, hamiltonian, inverse_margin, density, atom_of, first_two),
        scratch=[pltpu.VMEM((4, 5, B, B), f32), flags, pltpu.VMEM((1, 1, B), jnp.int32), dma(()), dma(()), dma((4,))],
    )
    near_three = swapped(send_three, 3)
    mixed = [shape(3 * B, B, kind=bf16)] * 2
    four_more, start, high_four, low_four, diagonal, other_four = call(
        third_kernel,
        [message, shape(3 * B, 5 * B)] + mixed + [shape(3 * B, B), shape(2, B, B)],
        [vmem] * 6,
        8000,
        (left_high, left_low, ham_high, ham_low, held, near_four),
    )
    near_four_more = swapped(four_more, 4)
    two_more, diagonal, other_three, derivative = call(
        whole_kernel,
        [message, shape(3 * B, B), shape(2, 2, B, B), shape(*derivative.shape)],
        [vmem] * 6 + [hbm],
        14,
        (left_high, left_low, start, held, diagonal, near_three, derivative),
        scratch=[dma(())],
    )
    near_two_more = swapped(two_more, 2)
    high_one, low_one, diagonal, other_one = call(
        fourth_kernel,
        mixed + [shape(3 * B, B), shape(2, B, B)],
        [vmem] * 5,
        10,
        (left_high, left_low, start, diagonal, near_one),
    )
    block = shape(B, B)
    new, high_two, low_two, self_high, self_low, real_two, imag_part, weighted, *columns = call(
        fifth_kernel,
        [message] + mixed * 2 + [block, block, shape(3, B, B)] + [shape(3, B)] * 4,
        [vmem] * 10,
        22,
        (left_high, left_low, start, diagonal, held, derivative, other_one, other_three, other_four, near_two),
    )
    c1, c2, c3, c4 = columns
    c1 = swapped(c1, 1)
    c2 = swapped(c2, 2)
    one_more, c3 = call(more_kernel, [message, shape(3, B)], [vmem] * 3, 0, (held, c1, c3))
    near_one_more = swapped(one_more, 1)
    c4, more_four = call(
        four_kernel,
        [shape(3, B), shape(3, B, B)],
        [vmem] * 4,
        5,
        (high_four, low_four, near_four_more, c4),
    )
    columns = (c1, c2, swapped(c3, 3), swapped(c4, 4))
    args = (held, new, left_high, left_low, self_high, self_low, other_one, real_two, other_three, other_four, more_four, weighted)
    args += (high_two, low_two, imag_part, near_two_more)
    out, comm, row_part = call(
        real_kernel,
        [shape(*density.shape), shape(3, B, B), shape(3, B)],
        [vmem] * 16,
        15,
        args,
        out_specs=[hbm] + [vmem] * 2,
        scratch=[pltpu.VMEM((3, B, B), f32), dma((2, 4))],
    )
    args = (held, derivative, members, high_one, low_one, comm, row_part, near_one_more, *columns, out)
    new_density, forces = call(
        sixth_kernel,
        [shape(*density.shape), shape(3, 1, ATOMS)],
        [vmem] * 12 + [hbm],
        10,
        args,
        out_specs=[hbm, hbm],
        scratch=[pltpu.VMEM((3, B, B), f32), pltpu.VMEM((3, 1, ATOMS), f32), dma((4,))],
        aliases={12: 0},
    )
    return new_density, forces.reshape(1, 1, 3, ATOMS)


def solution(mesh):
    placed = (
        P("gx", "gy", None, None, None),
        P("gx", "gy", None, None, None),
        P(None, "gx", "gy", None, None, None),
        P("gx", "gy", None),
        P(None, "gx", "gy", None, None, None),
        P("gx", "gy", None),
    )
    return jax.shard_map(
        local,
        mesh=mesh,
        in_specs=placed,
        out_specs=(P(None, "gx", "gy", None, None, None), P("gx", "gy", None, None)),
        check_vma=False,
    )
```

```python
import functools

import jax
import jax.numpy as jnp
from jax import lax
from jax.experimental import pallas as pl
from jax.experimental.pallas import tpu as pltpu
from jax.sharding import PartitionSpec as P

B = 128
ATOMS = 64

time_step = 0.25
vmem = pl.BlockSpec(memory_space=pltpu.VMEM)
hbm = pl.BlockSpec(memory_space=pltpu.HBM)
f32 = jnp.float32
bf16 = jnp.bfloat16
dma = pltpu.SemaphoreType.DMA


def swapped(cells, edge):
    axis = "gx" if edge < 3 else "gy"
    count = lax.axis_size(axis)
    assert count % 2 == 0
    first = 0 if edge in (1, 3) else 1
    pairs = []
    for i in range(first, count, 2):
        j = (i + 1) % count
        pairs += [(i, j), (j, i)]
    return lax.ppermute(cells, axis, pairs)


def order_of():
    odd_x = lax.rem(lax.axis_index("gx"), 2)
    odd_y = lax.rem(lax.axis_index("gy"), 2)
    return 0, 1 + odd_x, 2 - odd_x, 3 + odd_y, 4 - odd_y


def cols(place, count=1):
    return slice(place * B, (place + count) * B)


def split(values):
    high = values.astype(bf16)
    return high, (values - high.astype(f32)).astype(bf16)


def beside(*pairs):
    return tuple(jnp.concatenate(parts, axis=1) for parts in zip(*pairs))


def dot(left, right):
    def one(a, b):
        return jnp.dot(a, b, preferred_element_type=f32)

    return one(left[0], right[0]) + (one(left[0], right[1]) + one(left[1], right[0]))


def part(pair, rows, columns):
    return pair[0][rows, columns], pair[1][rows, columns]


def rows_of(pair):
    return (pair[0][:B], pair[1][:B]), (pair[0][B:], pair[1][B:])


def store(pair, columns, values):
    pair[0][:, columns], pair[1][:, columns] = values


def start_all(copies):
    for copy in copies:
        copy.start()
    return copies


def first_kernel(cutoff_hbm, ham_hbm, inv_hbm, rho_hbm, one, rest, cutoff_ref, cutoff_sem, sems):
    flags = pltpu.make_async_copy(cutoff_hbm, cutoff_ref, cutoff_sem)
    flags.start()
    order = order_of()
    sources = (ham_hbm.at[0, 0, 0], inv_hbm.at[0, 0, 0], rho_hbm.at[1, 0, 0, 0], ham_hbm.at[0, 0, order[1]])
    copies = [pltpu.make_async_copy(source, one.at[at], sems.at[at]) for at, source in enumerate(sources)]
    copies += [
        pltpu.make_async_copy(ham_hbm.at[0, 0, order[place]], rest.at[at], sems.at[4 + at]) for at, place in enumerate((4, 2))
    ]
    start_all(copies)
    flags.wait()
    for copy in copies:
        copy.wait()
    one[3] = one[3] * cutoff_ref[0, 0, order[1]].astype(f32)
    for at, place in enumerate((4, 2)):
        rest[at] = rest[at] * cutoff_ref[0, 0, order[place]].astype(f32)


def next_kernel(at, message, rest, out):
    out[:3] = message[:3]
    out[3] = rest[at]


def second_kernel(
    cutoff_hbm, ham_hbm, inv_hbm, rho_hbm, atom_hbm, after, three, held, left_high, left_low, ham_high, ham_low, members,
    raw, cutoff_ref, atom_ref, cutoff_sem, atom_sem, sems
):
    flags = pltpu.make_async_copy(cutoff_hbm, cutoff_ref, cutoff_sem)
    flags.start()
    sources = (ham_hbm.at[0, 0], inv_hbm.at[0, 0], rho_hbm.at[0, 0, 0], rho_hbm.at[1, 0, 0])
    copies = start_all([pltpu.make_async_copy(source, raw.at[at], sems.at[at]) for at, source in enumerate(sources)])
    owners = pltpu.make_async_copy(atom_hbm, atom_ref, atom_sem)
    owners.start()
    order = order_of()
    flags.wait()
    keeps = [cutoff_ref[0, 0, offset].astype(f32) for offset in order]
    for kind, copy in enumerate(copies):
        copy.wait()
        for place, offset in enumerate(order):
            block = raw[kind, offset]
            if place == 0:
                three[(0, 1, 4, 2)[kind]] = block
            else:
                block = block * keeps[place]
                if place == 3:
                    three[(3, 5, 6, 7)[kind]] = block
            if kind == 0:
                store((ham_high, ham_low), cols(place), split(block))
            else:
                held[kind - 1, place] = block
                rows = slice((kind - 1) * B, kind * B)
                left_high[rows, cols(place)], left_low[rows, cols(place)] = split(block)
    owners.wait()
    atoms = jnp.broadcast_to(atom_ref[0], (ATOMS, B))
    members[...] = -(lax.broadcasted_iota(jnp.int32, (ATOMS, B), 0) == atoms).astype(f32)


def first_half(left, place, start, near, diagonal):
    both = dot(part(left, slice(0, 3 * B), cols(place)), beside(split(near[0]), split(near[3])))
    mixed = split(start[:, cols(place)] + both[:, :B])
    prop, inner = rows_of(mixed)
    behind = dot(inner, split(near[1]))
    imag = dot(prop, split(near[2])) - behind[B:]
    return mixed, diagonal + both[:, B:], -behind[:B], imag


def second_half(mixed, near):
    prop, inner = rows_of(mixed)
    ahead = dot(prop, beside(split(near[0]), split(near[2]), split(near[3])))
    behind = dot(inner, split(near[1]))
    return ahead[:, cols(0)], ahead[:, cols(1)] - behind[:B], ahead[:, cols(2)] - behind[B:]


def send_more(more, held, place):
    more[0] = held[1, 0]
    for kind in range(3):
        more[1 + kind] = held[kind, place]


def third_kernel(left_high, left_low, ham_high, ham_low, held, four, four_more, start, mixed_high, mixed_low, diagonal, other):
    send_more(four_more, held, 4)
    left = (left_high, left_low)
    start[...] = dot(part(left, slice(0, 3 * B), cols(0)), part((ham_high, ham_low), slice(0, B), cols(0, 5)))
    mixed, diagonal[...], other[0], other[1] = first_half(left, 4, start, four, start[:, cols(0)])
    mixed_high[...], mixed_low[...] = mixed


def whole_kernel(left_high, left_low, start, held, diagonal, three, der_hbm, one_more, two_more, diagonal_out, other, der, sem):
    copy = pltpu.make_async_copy(der_hbm, der, sem)
    copy.start()
    send_more(one_more, held, 1)
    send_more(two_more, held, 2)
    mixed, diagonal_out[...], real, other[1, 0] = first_half((left_high, left_low), 3, start, three, diagonal[...])
    added, other[0, 1], other[1, 1] = second_half(mixed, three[4:])
    other[0, 0] = real + added
    copy.wait()


def fourth_kernel(left_high, left_low, start, diagonal, one, mixed_high, mixed_low, diagonal_out, other):
    mixed, diagonal_out[...], other[0], other[1] = first_half((left_high, left_low), 1, start, one, diagonal[...])
    mixed_high[...], mixed_low[...] = mixed


def fifth_kernel(
    left_high, left_low, start, diagonal, held, der_ref, other_one, other_three, other_four, two,
    new, mixed_high, mixed_low, self_high, self_low, real_two, comm, weighted, c1, c2, c3, c4
):
    order = order_of()
    left = (left_high, left_low)
    mixed, total, real_two[...], imag_two = first_half(left, 2, start, two, diagonal[...])
    mixed_high[...], mixed_low[...] = mixed
    at_self = split(total)
    self_high[...], self_low[...] = at_self
    whole = cols(0, 5)
    ahead = dot(part(at_self, slice(0, B), cols(0)), part(left, slice(2 * B, 3 * B), whole))
    behind = dot(part(at_self, slice(2 * B, 3 * B), cols(0)), part(left, slice(0, B), whole))
    imag_comm = ahead - behind
    comm[...] = imag_comm[:, cols(0)] + other_three[1, 1]
    sums = [None] * 3
    for place, column in enumerate((c1, c2, c3, c4), 1):
        imag = (other_one[1], imag_two, other_three[1, 0], other_four[1])[place - 1]
        real_new = held[1, place] + time_step * (imag_comm[:, cols(place)] + imag)
        new[place - 1] = real_new
        for direction in range(3):
            product = real_new * der_ref[direction, 0, 0, order[place]]
            sums[direction] = product if place == 1 else sums[direction] + product
            column[direction : direction + 1, :] = jnp.sum(product, axis=0, keepdims=True)
    for direction in range(3):
        weighted[direction] = sums[direction]


def pass_kernel(arrived, column, out):
    out[...] = column[...]


def four_kernel(mixed_high, mixed_low, four, column, out, other):
    out[...] = column[...]
    other[0], other[1], other[2] = second_half((mixed_high[...], mixed_low[...]), four)


def real_kernel(
    held, new, left_high, left_low, self_high, self_low, other_one, real_two, other_three, other_four, more_four, weighted,
    high_one, low_one, imag_part, one, out_hbm, comm, row_part, imag_new, sems
):
    order = order_of()
    copies = start_all(
        [pltpu.make_async_copy(new.at[at], out_hbm.at[0, 0, 0, order[1 + at]], sems.at[0, at]) for at in range(4)]
    )
    left = (left_high, left_low)
    whole = cols(0, 5)
    at_self = (self_high, self_low)
    ahead = dot(part(at_self, slice(0, B), cols(0)), part(left, slice(B, 2 * B), whole))
    behind = dot(part(at_self, slice(B, 2 * B), cols(0)), part(left, slice(0, B), whole))
    real_comm = ahead - behind
    added_one, real_one, imag_one = second_half((high_one[...], low_one[...]), one)
    others = ((1, other_one[0] + added_one), (3, other_three[0, 0]), (4, other_four[0] + more_four[0]))
    for at, (place, other) in enumerate(others):
        imag_new[at] = held[2, place] - time_step * (real_comm[:, cols(place)] + other)
        copies += start_all(
            [pltpu.make_async_copy(imag_new.at[at], out_hbm.at[1, 0, 0, order[place]], sems.at[1, at])]
        )
    comm[0] = real_comm[:, cols(0)] + other_three[0, 1] + real_one + more_four[1]
    comm[1] = imag_part[...] + imag_one + more_four[2]
    comm[2] = real_comm[:, cols(2)] + real_two[...]
    for direction in range(3):
        row_part[direction : direction + 1, :] = jnp.sum(weighted[direction].T, axis=0, keepdims=True)
    for copy in copies:
        copy.wait()


def sixth_kernel(
    held, der_ref, members, high_two, low_two, comm, row_part, two, c1, c2, c3, c4, old_hbm, out_hbm, forces_hbm, new, forces_ref, sems
):
    order = order_of()
    prop, inner = rows_of((high_two[...], low_two[...]))
    behind = dot(inner, split(two[1]))
    real_new = held[1, 0] + time_step * (comm[1] + dot(prop, split(two[3])) - behind[B:])
    new[0] = real_new
    copies = start_all([pltpu.make_async_copy(new.at[0], out_hbm.at[0, 0, 0, 0], sems.at[0])])
    parts = []
    for direction in range(3):
        product = real_new * der_ref[direction, 0, 0, 0]
        parts.append(jnp.sum(product + product.T, axis=0, keepdims=True))
    orbital = jnp.concatenate(parts, axis=0) + row_part[...] + ((c1[...] + c2[...]) + (c3[...] + c4[...]))
    forces = lax.dot_general(
        orbital, members[...], (((1,), (1,)), ((), ())), precision=lax.Precision.HIGHEST, preferred_element_type=f32
    )
    for direction in range(3):
        forces_ref[direction] = forces[direction : direction + 1]
    copies += start_all([pltpu.make_async_copy(forces_ref, forces_hbm, sems.at[3])])
    ahead = dot(prop, beside(split(two[2]), split(two[0])))
    new[1] = held[2, 0] - time_step * (comm[0] + ahead[:, cols(0)] - behind[:B])
    new[2] = held[2, 2] - time_step * (comm[2] + ahead[:, cols(1)])
    copies += start_all(
        [pltpu.make_async_copy(new.at[1 + at], out_hbm.at[1, 0, 0, order[2 * at]], sems.at[1 + at]) for at in range(2)]
    )
    for copy in copies:
        copy.wait()


def call(kernel, shapes, in_specs, products, args, out_specs=None, scratch=(), aliases={}):
    moved = sum(4 * x.size for x in args) + sum(4 * x.size for x in shapes)
    return pl.pallas_call(
        kernel,
        out_shape=shapes,
        in_specs=in_specs,
        out_specs=out_specs or [vmem] * len(shapes),
        scratch_shapes=scratch,
        input_output_aliases=aliases,
        compiler_params=pltpu.CompilerParams(vmem_limit_bytes=32 * 2**20),
        cost_estimate=pl.CostEstimate(flops=products * 6 * B**3, bytes_accessed=moved, transcendentals=0),
    )(*args)


def local(hamiltonian, inverse_margin, density, cutoff, derivative, atom_of):
    def shape(*dims, kind=f32):
        return jax.ShapeDtypeStruct(dims, kind)

    args = (hamiltonian, inverse_margin, density, cutoff, derivative, atom_of)
    hamiltonian, inverse_margin, density, cutoff, derivative, atom_of = (
        pltpu.with_memory_space_constraint(x, pltpu.HBM) for x in args
    )
    flags = pltpu.SMEM((1, 1, 5), jnp.int32)
    message = shape(4, B, B)
    first_one, rest = call(
        first_kernel,
        [message, shape(2, B, B)],
        [hbm] * 4,
        0,
        (cutoff, hamiltonian, inverse_margin, density),
        scratch=[flags, dma(()), dma((6,))],
    )
    near_one = swapped(first_one, 1)
    (first_four,) = call(functools.partial(next_kernel, 0), [message], [vmem] * 2, 0, (first_one, rest))
    near_four = swapped(first_four, 4)
    (first_two,) = call(functools.partial(next_kernel, 1), [message], [vmem] * 2, 500, (first_four, rest))
    near_two = swapped(first_two, 2)
    left = [shape(3 * B, 5 * B, kind=bf16)] * 2
    ham = [shape(B, 5 * B, kind=bf16)] * 2
    send_three, held, left_high, left_low, ham_high, ham_low, members = call(
        second_kernel,
        [shape(8, B, B), shape(3, 5, B, B)] + left + ham + [shape(ATOMS, B)],
        [hbm] * 6,
        0,
        (cutoff, hamiltonian, inverse_margin, density, atom_of, first_two),
        scratch=[pltpu.VMEM((4, 5, B, B), f32), flags, pltpu.VMEM((1, 1, B), jnp.int32), dma(()), dma(()), dma((4,))],
    )
    near_three = swapped(send_three, 3)
    mixed = [shape(3 * B, B, kind=bf16)] * 2
    four_more, start, high_four, low_four, diagonal, other_four = call(
        third_kernel,
        [message, shape(3 * B, 5 * B)] + mixed + [shape(3 * B, B), shape(2, B, B)],
        [vmem] * 6,
        8000,
        (left_high, left_low, ham_high, ham_low, held, near_four),
    )
    near_four_more = swapped(four_more, 4)
    one_more, two_more, diagonal, other_three, derivative = call(
        whole_kernel,
        [message, message, shape(3 * B, B), shape(2, 2, B, B), shape(*derivative.shape)],
        [vmem] * 6 + [hbm],
        14,
        (left_high, left_low, start, held, diagonal, near_three, derivative),
        scratch=[dma(())],
    )
    near_one_more = swapped(one_more, 1)
    near_two_more = swapped(two_more, 2)
    high_one, low_one, diagonal, other_one = call(
        fourth_kernel,
        mixed + [shape(3 * B, B), shape(2, B, B)],
        [vmem] * 5,
        10,
        (left_high, left_low, start, diagonal, near_one),
    )
    block = shape(B, B)
    new, high_two, low_two, self_high, self_low, real_two, imag_part, weighted, *columns = call(
        fifth_kernel,
        [message] + mixed * 2 + [block, block, shape(3, B, B)] + [shape(3, B)] * 4,
        [vmem] * 10,
        22,
        (left_high, left_low, start, diagonal, held, derivative, other_one, other_three, other_four, near_two),
    )
    c1, c2, c3, c4 = columns
    c4, more_four = call(
        four_kernel,
        [shape(3, B), shape(3, B, B)],
        [vmem] * 4,
        5,
        (high_four, low_four, near_four_more, c4),
    )
    (c3,) = call(pass_kernel, [shape(3, B)], [vmem] * 2, 0, (near_one_more, c3))
    columns = [swapped(column, at) for at, column in enumerate((c1, c2, c3, c4), 1)]
    args = (held, new, left_high, left_low, self_high, self_low, other_one, real_two, other_three, other_four, more_four, weighted)
    args += (high_one, low_one, imag_part, near_one_more)
    out, comm, row_part = call(
        real_kernel,
        [shape(*density.shape), shape(3, B, B), shape(3, B)],
        [vmem] * 16,
        15,
        args,
        out_specs=[hbm] + [vmem] * 2,
        scratch=[pltpu.VMEM((3, B, B), f32), dma((2, 4))],
    )
    args = (held, derivative, members, high_two, low_two, comm, row_part, near_two_more, *columns, out)
    new_density, forces = call(
        sixth_kernel,
        [shape(*density.shape), shape(3, 1, ATOMS)],
        [vmem] * 12 + [hbm],
        10,
        args,
        out_specs=[hbm, hbm],
        scratch=[pltpu.VMEM((3, B, B), f32), pltpu.VMEM((3, 1, ATOMS), f32), dma((4,))],
        aliases={12: 0},
    )
    return new_density, forces.reshape(1, 1, 3, ATOMS)


def solution(mesh):
    placed = (
        P("gx", "gy", None, None, None),
        P("gx", "gy", None, None, None),
        P(None, "gx", "gy", None, None, None),
        P("gx", "gy", None),
        P(None, "gx", "gy", None, None, None),
        P("gx", "gy", None),
    )
    return jax.shard_map(
        local,
        mesh=mesh,
        in_specs=placed,
        out_specs=(P(None, "gx", "gy", None, None, None), P("gx", "gy", None, None)),
        check_vma=False,
    )
```

```python
import functools

import jax
import jax.numpy as jnp
from jax import lax
from jax.experimental import pallas as pl
from jax.experimental.pallas import tpu as pltpu
from jax.sharding import PartitionSpec as P

B = 128
ATOMS = 64

time_step = 0.25
vmem = pl.BlockSpec(memory_space=pltpu.VMEM)
hbm = pl.BlockSpec(memory_space=pltpu.HBM)
f32 = jnp.float32
bf16 = jnp.bfloat16
dma = pltpu.SemaphoreType.DMA


def swapped(cells, edge):
    axis = "gx" if edge < 3 else "gy"
    count = lax.axis_size(axis)
    assert count % 2 == 0
    first = 0 if edge in (1, 3) else 1
    pairs = []
    for i in range(first, count, 2):
        j = (i + 1) % count
        pairs += [(i, j), (j, i)]
    return lax.ppermute(cells, axis, pairs)


def order_of():
    odd_x = lax.rem(lax.axis_index("gx"), 2)
    odd_y = lax.rem(lax.axis_index("gy"), 2)
    return 0, 1 + odd_x, 2 - odd_x, 3 + odd_y, 4 - odd_y


def cols(place, count=1):
    return slice(place * B, (place + count) * B)


def split(values):
    high = values.astype(bf16)
    return high, (values - high.astype(f32)).astype(bf16)


def beside(*pairs):
    return tuple(jnp.concatenate(parts, axis=1) for parts in zip(*pairs))


def dot(left, right):
    def one(a, b):
        return jnp.dot(a, b, preferred_element_type=f32)

    return one(left[0], right[0]) + (one(left[0], right[1]) + one(left[1], right[0]))


def part(pair, rows, columns):
    return pair[0][rows, columns], pair[1][rows, columns]


def rows_of(pair):
    return (pair[0][:B], pair[1][:B]), (pair[0][B:], pair[1][B:])


def store(pair, columns, values):
    pair[0][:, columns], pair[1][:, columns] = values


def start_all(copies):
    for copy in copies:
        copy.start()
    return copies


def first_kernel(cutoff_hbm, ham_hbm, inv_hbm, rho_hbm, one, rest, cutoff_ref, cutoff_sem, sems):
    flags = pltpu.make_async_copy(cutoff_hbm, cutoff_ref, cutoff_sem)
    flags.start()
    order = order_of()
    sources = (ham_hbm.at[0, 0, 0], inv_hbm.at[0, 0, 0], rho_hbm.at[1, 0, 0, 0], ham_hbm.at[0, 0, order[1]])
    copies = [pltpu.make_async_copy(source, one.at[at], sems.at[at]) for at, source in enumerate(sources)]
    sources = (ham_hbm.at[0, 0, order[2]], rho_hbm.at[0, 0, 0, 0])
    for place in (3, 4):
        sources += (ham_hbm.at[0, 0, order[place]], inv_hbm.at[0, 0, order[place]])
        sources += (rho_hbm.at[0, 0, 0, order[place]], rho_hbm.at[1, 0, 0, order[place]])
    copies += [pltpu.make_async_copy(source, rest.at[at], sems.at[4 + at]) for at, source in enumerate(sources)]
    start_all(copies)
    flags.wait()
    for copy in copies:
        copy.wait()
    one[3] = one[3] * cutoff_ref[0, 0, order[1]].astype(f32)
    rest[0] = rest[0] * cutoff_ref[0, 0, order[2]].astype(f32)
    for place, first in ((3, 2), (4, 6)):
        keep = cutoff_ref[0, 0, order[place]].astype(f32)
        for at in range(first, first + 4):
            rest[at] = rest[at] * keep


def whole_first_kernel(first, after, message, rest, out):
    out[:3] = message[:3]
    out[3] = rest[first]
    out[4] = rest[1]
    out[5:] = rest[first + 1 : first + 4]


def two_first_kernel(message, rest, out):
    out[:3] = message[:3]
    out[3] = rest[0]


def second_kernel(
    cutoff_hbm, ham_hbm, inv_hbm, rho_hbm, atom_hbm, after, held, left_high, left_low, ham_high, ham_low, members,
    raw, cutoff_ref, atom_ref, cutoff_sem, atom_sem, sems
):
    flags = pltpu.make_async_copy(cutoff_hbm, cutoff_ref, cutoff_sem)
    flags.start()
    sources = (ham_hbm.at[0, 0], inv_hbm.at[0, 0], rho_hbm.at[0, 0, 0], rho_hbm.at[1, 0, 0])
    copies = start_all([pltpu.make_async_copy(source, raw.at[at], sems.at[at]) for at, source in enumerate(sources)])
    owners = pltpu.make_async_copy(atom_hbm, atom_ref, atom_sem)
    owners.start()
    order = order_of()
    flags.wait()
    keeps = [cutoff_ref[0, 0, offset].astype(f32) for offset in order]
    for kind, copy in enumerate(copies):
        copy.wait()
        for place, offset in enumerate(order):
            block = raw[kind, offset]
            if place > 0:
                block = block * keeps[place]
            if kind == 0:
                store((ham_high, ham_low), cols(place), split(block))
            else:
                held[kind - 1, place] = block
                rows = slice((kind - 1) * B, kind * B)
                left_high[rows, cols(place)], left_low[rows, cols(place)] = split(block)
    owners.wait()
    atoms = jnp.broadcast_to(atom_ref[0], (ATOMS, B))
    members[...] = -(lax.broadcasted_iota(jnp.int32, (ATOMS, B), 0) == atoms).astype(f32)


def first_half(left, place, start, near, diagonal):
    both = dot(part(left, slice(0, 3 * B), cols(place)), beside(split(near[0]), split(near[3])))
    mixed = split(start[:, cols(place)] + both[:, :B])
    prop, inner = rows_of(mixed)
    behind = dot(inner, split(near[1]))
    imag = dot(prop, split(near[2])) - behind[B:]
    return mixed, diagonal + both[:, B:], -behind[:B], imag


def second_half(mixed, near):
    prop, inner = rows_of(mixed)
    ahead = dot(prop, beside(split(near[0]), split(near[2]), split(near[3])))
    behind = dot(inner, split(near[1]))
    return ahead[:, cols(0)], ahead[:, cols(1)] - behind[:B], ahead[:, cols(2)] - behind[B:]


def send_more(more, held, place):
    more[0] = held[1, 0]
    for kind in range(3):
        more[1 + kind] = held[kind, place]


def whole_edge(left, place, start, near, diagonal, diagonal_out, other):
    mixed, diagonal_out[...], real, other[1, 0] = first_half(left, place, start, near, diagonal)
    added, other[0, 1], other[1, 1] = second_half(mixed, near[4:])
    other[0, 0] = real + added


def third_kernel(left_high, left_low, ham_high, ham_low, held, three, der_hbm, one_more, two_more, start, diagonal, other, der, sem):
    copy = pltpu.make_async_copy(der_hbm, der, sem)
    copy.start()
    send_more(one_more, held, 1)
    send_more(two_more, held, 2)
    left = (left_high, left_low)
    start[...] = dot(part(left, slice(0, 3 * B), cols(0)), part((ham_high, ham_low), slice(0, B), cols(0, 5)))
    whole_edge(left, 3, start, three, start[:, cols(0)], diagonal, other)
    copy.wait()


def four_kernel(left_high, left_low, start, diagonal, four, diagonal_out, other):
    whole_edge((left_high, left_low), 4, start, four, diagonal[...], diagonal_out, other)


def fourth_kernel(left_high, left_low, start, diagonal, one, mixed_high, mixed_low, diagonal_out, other):
    mixed, diagonal_out[...], other[0], other[1] = first_half((left_high, left_low), 1, start, one, diagonal[...])
    mixed_high[...], mixed_low[...] = mixed


def fifth_kernel(
    left_high, left_low, start, diagonal, held, der_ref, other_one, other_three, other_four, two,
    new, mixed_high, mixed_low, self_high, self_low, real_two, comm, weighted, c1, c2, c3, c4
):
    order = order_of()
    left = (left_high, left_low)
    mixed, total, real_two[...], imag_two = first_half(left, 2, start, two, diagonal[...])
    mixed_high[...], mixed_low[...] = mixed
    at_self = split(total)
    self_high[...], self_low[...] = at_self
    whole = cols(0, 5)
    ahead = dot(part(at_self, slice(0, B), cols(0)), part(left, slice(2 * B, 3 * B), whole))
    behind = dot(part(at_self, slice(2 * B, 3 * B), cols(0)), part(left, slice(0, B), whole))
    imag_comm = ahead - behind
    comm[...] = imag_comm[:, cols(0)] + other_three[1, 1] + other_four[1, 1]
    sums = [None] * 3
    for place, column in enumerate((c1, c2, c3, c4), 1):
        imag = (other_one[1], imag_two, other_three[1, 0], other_four[1, 0])[place - 1]
        real_new = held[1, place] + time_step * (imag_comm[:, cols(place)] + imag)
        new[place - 1] = real_new
        for direction in range(3):
            product = real_new * der_ref[direction, 0, 0, order[place]]
            sums[direction] = product if place == 1 else sums[direction] + product
            column[direction : direction + 1, :] = jnp.sum(product, axis=0, keepdims=True)
    for direction in range(3):
        weighted[direction] = sums[direction]


def pass_kernel(arrived, column, out):
    out[...] = column[...]


def real_kernel(
    held, new, left_high, left_low, self_high, self_low, other_one, real_two, other_three, other_four, weighted,
    out_hbm, comm, row_part, imag_new, sems
):
    order = order_of()
    copies = start_all(
        [pltpu.make_async_copy(new.at[at], out_hbm.at[0, 0, 0, order[1 + at]], sems.at[0, at]) for at in range(4)]
    )
    left = (left_high, left_low)
    whole = cols(0, 5)
    at_self = (self_high, self_low)
    ahead = dot(part(at_self, slice(0, B), cols(0)), part(left, slice(B, 2 * B), whole))
    behind = dot(part(at_self, slice(B, 2 * B), cols(0)), part(left, slice(0, B), whole))
    real_comm = ahead - behind
    for at, (place, other) in enumerate(((3, other_three), (4, other_four))):
        imag_new[at] = held[2, place] - time_step * (real_comm[:, cols(place)] + other[0, 0])
        copies += start_all(
            [pltpu.make_async_copy(imag_new.at[at], out_hbm.at[1, 0, 0, order[place]], sems.at[1, at])]
        )
    comm[0] = real_comm[:, cols(0)] + other_three[0, 1] + other_four[0, 1]
    comm[1] = real_comm[:, cols(1)] + other_one[0]
    comm[2] = real_comm[:, cols(2)] + real_two[...]
    for direction in range(3):
        row_part[direction : direction + 1, :] = jnp.sum(weighted[direction].T, axis=0, keepdims=True)
    for copy in copies:
        copy.wait()


def sixth_kernel(
    held, der_ref, members, high_one, low_one, high_two, low_two, imag_part, comm, row_part, one, two, c1, c2, c3, c4, old_hbm,
    out_hbm, forces_hbm, new, forces_ref, sems
):
    order = order_of()
    prop, inner = rows_of(beside((high_one[...], low_one[...]), (high_two[...], low_two[...])))
    near = [tuple(jnp.concatenate(x, axis=0) for x in zip(split(one[1 + kind]), split(two[1 + kind]))) for kind in range(3)]
    behind = dot(inner, near[0])
    real_new = held[1, 0] + time_step * (imag_part[...] + dot(prop, near[2]) - behind[B:])
    new[0] = real_new
    copies = start_all([pltpu.make_async_copy(new.at[0], out_hbm.at[0, 0, 0, 0], sems.at[0])])
    new[1] = held[2, 0] - time_step * (comm[0] + dot(prop, near[1]) - behind[:B])
    for place, message, mixed in ((1, one, (high_one, low_one)), (2, two, (high_two, low_two))):
        added = dot(rows_of((mixed[0][...], mixed[1][...]))[0], split(message[0]))
        new[1 + place] = held[2, place] - time_step * (comm[place] + added)
    copies += start_all(
        [pltpu.make_async_copy(new.at[1 + at], out_hbm.at[1, 0, 0, order[at]], sems.at[1 + at]) for at in range(3)]
    )
    parts = []
    for direction in range(3):
        product = real_new * der_ref[direction, 0, 0, 0]
        parts.append(jnp.sum(product + product.T, axis=0, keepdims=True))
    orbital = jnp.concatenate(parts, axis=0) + row_part[...] + ((c1[...] + c2[...]) + (c3[...] + c4[...]))
    forces = lax.dot_general(
        orbital, members[...], (((1,), (1,)), ((), ())), precision=lax.Precision.HIGHEST, preferred_element_type=f32
    )
    for direction in range(3):
        forces_ref[direction] = forces[direction : direction + 1]
    copies += start_all([pltpu.make_async_copy(forces_ref, forces_hbm, sems.at[4])])
    for copy in copies:
        copy.wait()


def call(kernel, shapes, in_specs, products, args, out_specs=None, scratch=(), aliases={}):
    moved = sum(4 * x.size for x in args) + sum(4 * x.size for x in shapes)
    return pl.pallas_call(
        kernel,
        out_shape=shapes,
        in_specs=in_specs,
        out_specs=out_specs or [vmem] * len(shapes),
        scratch_shapes=scratch,
        input_output_aliases=aliases,
        compiler_params=pltpu.CompilerParams(vmem_limit_bytes=32 * 2**20),
        cost_estimate=pl.CostEstimate(flops=products * 6 * B**3, bytes_accessed=moved, transcendentals=0),
    )(*args)


def local(hamiltonian, inverse_margin, density, cutoff, derivative, atom_of):
    def shape(*dims, kind=f32):
        return jax.ShapeDtypeStruct(dims, kind)

    args = (hamiltonian, inverse_margin, density, cutoff, derivative, atom_of)
    hamiltonian, inverse_margin, density, cutoff, derivative, atom_of = (
        pltpu.with_memory_space_constraint(x, pltpu.HBM) for x in args
    )
    flags = pltpu.SMEM((1, 1, 5), jnp.int32)
    message = shape(4, B, B)
    first_one, rest = call(
        first_kernel,
        [message, shape(10, B, B)],
        [hbm] * 4,
        0,
        (cutoff, hamiltonian, inverse_margin, density),
        scratch=[flags, dma(()), dma((14,))],
    )
    near_one = swapped(first_one, 1)
    whole = shape(8, B, B)
    kernel = functools.partial(whole_first_kernel, 6)
    (send_four,) = call(kernel, [whole], [vmem] * 3, 0, (first_one, first_one, rest))
    near_four = swapped(send_four, 4)
    (first_two,) = call(two_first_kernel, [message], [vmem] * 2, 500, (send_four, rest))
    near_two = swapped(first_two, 2)
    kernel = functools.partial(whole_first_kernel, 2)
    (send_three,) = call(kernel, [whole], [vmem] * 3, 500, (first_two, first_one, rest))
    near_three = swapped(send_three, 3)
    left = [shape(3 * B, 5 * B, kind=bf16)] * 2
    ham = [shape(B, 5 * B, kind=bf16)] * 2
    held, left_high, left_low, ham_high, ham_low, members = call(
        second_kernel,
        [shape(3, 5, B, B)] + left + ham + [shape(ATOMS, B)],
        [hbm] * 6,
        2000,
        (cutoff, hamiltonian, inverse_margin, density, atom_of, send_three),
        scratch=[pltpu.VMEM((4, 5, B, B), f32), flags, pltpu.VMEM((1, 1, B), jnp.int32), dma(()), dma(()), dma((4,))],
    )
    mixed = [shape(3 * B, B, kind=bf16)] * 2
    both = shape(2, 2, B, B)
    one_more, two_more, start, diagonal, other_three, derivative = call(
        third_kernel,
        [message, message, shape(3 * B, 5 * B), shape(3 * B, B), both, shape(*derivative.shape)],
        [vmem] * 6 + [hbm],
        8000,
        (left_high, left_low, ham_high, ham_low, held, near_three, derivative),
        scratch=[dma(())],
    )
    near_two_more = swapped(two_more, 2)
    near_one_more = swapped(one_more, 1)
    diagonal, other_four = call(
        four_kernel,
        [shape(3 * B, B), both],
        [vmem] * 5,
        14,
        (left_high, left_low, start, diagonal, near_four),
    )
    high_one, low_one, diagonal, other_one = call(
        fourth_kernel,
        mixed + [shape(3 * B, B), shape(2, B, B)],
        [vmem] * 5,
        10,
        (left_high, left_low, start, diagonal, near_one),
    )
    block = shape(B, B)
    new, high_two, low_two, self_high, self_low, real_two, imag_part, weighted, *columns = call(
        fifth_kernel,
        [message] + mixed * 2 + [block, block, shape(3, B, B)] + [shape(3, B)] * 4,
        [vmem] * 10,
        22,
        (left_high, left_low, start, diagonal, held, derivative, other_one, other_three, other_four, near_two),
    )
    c1, c2, c3, c4 = columns
    c1, c2, c4 = swapped(c1, 1), swapped(c2, 2), swapped(c4, 4)
    (c3,) = call(pass_kernel, [shape(3, B)], [vmem] * 2, 0, (c4, c3))
    columns = (c1, c2, swapped(c3, 3), c4)
    args = (held, new, left_high, left_low, self_high, self_low, other_one, real_two, other_three, other_four, weighted)
    out, comm, row_part = call(
        real_kernel,
        [shape(*density.shape), shape(3, B, B), shape(3, B)],
        [vmem] * 11,
        10,
        args,
        out_specs=[hbm] + [vmem] * 2,
        scratch=[pltpu.VMEM((2, B, B), f32), dma((2, 4))],
    )
    args = (held, derivative, members, high_one, low_one, high_two, low_two, imag_part, comm, row_part)
    args += (near_one_more, near_two_more, *columns, out)
    new_density, forces = call(
        sixth_kernel,
        [shape(*density.shape), shape(3, 1, ATOMS)],
        [vmem] * 16 + [hbm],
        10,
        args,
        out_specs=[hbm, hbm],
        scratch=[pltpu.VMEM((4, B, B), f32), pltpu.VMEM((3, 1, ATOMS), f32), dma((5,))],
        aliases={16: 0},
    )
    return new_density, forces.reshape(1, 1, 3, ATOMS)


def solution(mesh):
    placed = (
        P("gx", "gy", None, None, None),
        P("gx", "gy", None, None, None),
        P(None, "gx", "gy", None, None, None),
        P("gx", "gy", None),
        P(None, "gx", "gy", None, None, None),
        P("gx", "gy", None),
    )
    return jax.shard_map(
        local,
        mesh=mesh,
        in_specs=placed,
        out_specs=(P(None, "gx", "gy", None, None, None), P("gx", "gy", None, None)),
        check_vma=False,
    )
```

```python
import functools

import jax
import jax.numpy as jnp
from jax import lax
from jax.experimental import pallas as pl
from jax.experimental.pallas import tpu as pltpu
from jax.sharding import PartitionSpec as P

B = 128
ATOMS = 64

time_step = 0.25
vmem = pl.BlockSpec(memory_space=pltpu.VMEM)
hbm = pl.BlockSpec(memory_space=pltpu.HBM)
f32 = jnp.float32
bf16 = jnp.bfloat16
dma = pltpu.SemaphoreType.DMA


def swapped(cells, edge):
    axis = "gx" if edge < 3 else "gy"
    count = lax.axis_size(axis)
    assert count % 2 == 0
    first = 0 if edge in (1, 3) else 1
    pairs = []
    for i in range(first, count, 2):
        j = (i + 1) % count
        pairs += [(i, j), (j, i)]
    return lax.ppermute(cells, axis, pairs)


def order_of():
    odd_x = lax.rem(lax.axis_index("gx"), 2)
    odd_y = lax.rem(lax.axis_index("gy"), 2)
    return 0, 1 + odd_x, 2 - odd_x, 3 + odd_y, 4 - odd_y


def cols(place, count=1):
    return slice(place * B, (place + count) * B)


def split(values):
    high = values.astype(bf16)
    return high, (values - high.astype(f32)).astype(bf16)


def beside(*pairs):
    return tuple(jnp.concatenate(parts, axis=1) for parts in zip(*pairs))


def dot(left, right):
    def one(a, b):
        return jnp.dot(a, b, preferred_element_type=f32)

    return one(left[0], right[0]) + (one(left[0], right[1]) + one(left[1], right[0]))


def part(pair, rows, columns):
    return pair[0][rows, columns], pair[1][rows, columns]


def rows_of(pair):
    return (pair[0][:B], pair[1][:B]), (pair[0][B:], pair[1][B:])


def store(pair, columns, values):
    pair[0][:, columns], pair[1][:, columns] = values


def start_all(copies):
    for copy in copies:
        copy.start()
    return copies


def first_kernel(cutoff_hbm, ham_hbm, inv_hbm, rho_hbm, one, rest, cutoff_ref, cutoff_sem, sems):
    flags = pltpu.make_async_copy(cutoff_hbm, cutoff_ref, cutoff_sem)
    flags.start()
    order = order_of()
    sources = (ham_hbm.at[0, 0, 0], inv_hbm.at[0, 0, 0], rho_hbm.at[1, 0, 0, 0], ham_hbm.at[0, 0, order[1]])
    copies = [pltpu.make_async_copy(source, one.at[at], sems.at[at]) for at, source in enumerate(sources)]
    copies += [
        pltpu.make_async_copy(ham_hbm.at[0, 0, order[place]], rest.at[at], sems.at[4 + at]) for at, place in enumerate((4, 2))
    ]
    start_all(copies)
    flags.wait()
    for copy in copies:
        copy.wait()
    one[3] = one[3] * cutoff_ref[0, 0, order[1]].astype(f32)
    for at, place in enumerate((4, 2)):
        rest[at] = rest[at] * cutoff_ref[0, 0, order[place]].astype(f32)


def next_kernel(at, message, rest, out):
    out[:3] = message[:3]
    out[3] = rest[at]


def whole_first_kernel(cutoff_hbm, ham_hbm, inv_hbm, rho_hbm, message, out, cutoff_ref, cutoff_sem, sems):
    flags = pltpu.make_async_copy(cutoff_hbm, cutoff_ref, cutoff_sem)
    flags.start()
    offset = order_of()[3]
    sources = (ham_hbm.at[0, 0, offset], rho_hbm.at[0, 0, 0, 0], inv_hbm.at[0, 0, offset], rho_hbm.at[0, 0, 0, offset])
    sources += (rho_hbm.at[1, 0, 0, offset],)
    copies = start_all([pltpu.make_async_copy(source, out.at[3 + at], sems.at[at]) for at, source in enumerate(sources)])
    out[:3] = message[:3]
    flags.wait()
    keep = cutoff_ref[0, 0, offset].astype(f32)
    for copy in copies:
        copy.wait()
    for at in (3, 5, 6, 7):
        out[at] = out[at] * keep


def second_kernel(
    cutoff_hbm, ham_hbm, inv_hbm, rho_hbm, atom_hbm, after, held, left_high, left_low, ham_high, ham_low, members,
    raw, cutoff_ref, atom_ref, cutoff_sem, atom_sem, sems
):
    flags = pltpu.make_async_copy(cutoff_hbm, cutoff_ref, cutoff_sem)
    flags.start()
    sources = (ham_hbm.at[0, 0], inv_hbm.at[0, 0], rho_hbm.at[0, 0, 0], rho_hbm.at[1, 0, 0])
    copies = start_all([pltpu.make_async_copy(source, raw.at[at], sems.at[at]) for at, source in enumerate(sources)])
    owners = pltpu.make_async_copy(atom_hbm, atom_ref, atom_sem)
    owners.start()
    order = order_of()
    flags.wait()
    keeps = [cutoff_ref[0, 0, offset].astype(f32) for offset in order]
    for kind, copy in enumerate(copies):
        copy.wait()
        for place, offset in enumerate(order):
            block = raw[kind, offset]
            if place > 0:
                block = block * keeps[place]
            if kind == 0:
                store((ham_high, ham_low), cols(place), split(block))
            else:
                held[kind - 1, place] = block
                rows = slice((kind - 1) * B, kind * B)
                left_high[rows, cols(place)], left_low[rows, cols(place)] = split(block)
    owners.wait()
    atoms = jnp.broadcast_to(atom_ref[0], (ATOMS, B))
    members[...] = -(lax.broadcasted_iota(jnp.int32, (ATOMS, B), 0) == atoms).astype(f32)


def first_half(left, place, start, near, diagonal):
    both = dot(part(left, slice(0, 3 * B), cols(place)), beside(split(near[0]), split(near[3])))
    mixed = split(start[:, cols(place)] + both[:, :B])
    prop, inner = rows_of(mixed)
    behind = dot(inner, split(near[1]))
    imag = dot(prop, split(near[2])) - behind[B:]
    return mixed, diagonal + both[:, B:], -behind[:B], imag


def second_half(mixed, near):
    prop, inner = rows_of(mixed)
    ahead = dot(prop, beside(split(near[0]), split(near[2]), split(near[3])))
    behind = dot(inner, split(near[1]))
    return ahead[:, cols(0)], ahead[:, cols(1)] - behind[:B], ahead[:, cols(2)] - behind[B:]


def send_more(more, held, place):
    more[0] = held[1, 0]
    for kind in range(3):
        more[1 + kind] = held[kind, place]


def third_kernel(left_high, left_low, ham_high, ham_low, held, three, der_hbm, start, diagonal, other, der, sem):
    copy = pltpu.make_async_copy(der_hbm, der, sem)
    copy.start()
    left = (left_high, left_low)
    start[...] = dot(part(left, slice(0, 3 * B), cols(0)), part((ham_high, ham_low), slice(0, B), cols(0, 5)))
    mixed, diagonal[...], real, other[1, 0] = first_half(left, 3, start, three, start[:, cols(0)])
    added, other[0, 1], other[1, 1] = second_half(mixed, three[4:])
    other[0, 0] = real + added
    copy.wait()


def four_kernel(
    left_high, left_low, start, held, diagonal, four, one_more, mixed_high, mixed_low, diagonal_out, other
):
    send_more(one_more, held, 1)
    mixed, diagonal_out[...], other[0], other[1] = first_half((left_high, left_low), 4, start, four, diagonal[...])
    mixed_high[...], mixed_low[...] = mixed


def more_kernel(after, held, two_more, four_more):
    send_more(two_more, held, 2)
    send_more(four_more, held, 4)


def fourth_kernel(left_high, left_low, start, diagonal, one, mixed_high, mixed_low, diagonal_out, other):
    mixed, diagonal_out[...], other[0], other[1] = first_half((left_high, left_low), 1, start, one, diagonal[...])
    mixed_high[...], mixed_low[...] = mixed


def fifth_kernel(
    left_high, left_low, start, diagonal, held, der_ref, other_one, other_three, other_four, two,
    new, mixed_high, mixed_low, self_high, self_low, real_two, comm, weighted, c1, c2, c3, c4
):
    order = order_of()
    left = (left_high, left_low)
    mixed, total, real_two[...], imag_two = first_half(left, 2, start, two, diagonal[...])
    mixed_high[...], mixed_low[...] = mixed
    at_self = split(total)
    self_high[...], self_low[...] = at_self
    whole = cols(0, 5)
    ahead = dot(part(at_self, slice(0, B), cols(0)), part(left, slice(2 * B, 3 * B), whole))
    behind = dot(part(at_self, slice(2 * B, 3 * B), cols(0)), part(left, slice(0, B), whole))
    imag_comm = ahead - behind
    comm[...] = imag_comm[:, cols(0)] + other_three[1, 1]
    sums = [None] * 3
    for place, column in enumerate((c1, c2, c3, c4), 1):
        imag = (other_one[1], imag_two, other_three[1, 0], other_four[1])[place - 1]
        real_new = held[1, place] + time_step * (imag_comm[:, cols(place)] + imag)
        new[place - 1] = real_new
        for direction in range(3):
            product = real_new * der_ref[direction, 0, 0, order[place]]
            sums[direction] = product if place == 1 else sums[direction] + product
            column[direction : direction + 1, :] = jnp.sum(product, axis=0, keepdims=True)
    for direction in range(3):
        weighted[direction] = sums[direction]


def pass_kernel(arrived, column, out):
    out[...] = column[...]


def real_kernel(
    held, new, left_high, left_low, self_high, self_low, other_one, real_two, other_three, other_four, weighted,
    imag_part, high_four, low_four, four, out_hbm, comm, imag_out, row_part, imag_new, sems
):
    order = order_of()
    copies = start_all(
        [pltpu.make_async_copy(new.at[at], out_hbm.at[0, 0, 0, order[1 + at]], sems.at[0, at]) for at in range(4)]
    )
    left = (left_high, left_low)
    whole = cols(0, 5)
    at_self = (self_high, self_low)
    ahead = dot(part(at_self, slice(0, B), cols(0)), part(left, slice(B, 2 * B), whole))
    behind = dot(part(at_self, slice(B, 2 * B), cols(0)), part(left, slice(0, B), whole))
    real_comm = ahead - behind
    added, real_four, imag_four = second_half((high_four[...], low_four[...]), four)
    imag_out[...] = imag_part[...] + imag_four
    for at, (place, other) in enumerate(((3, other_three[0, 0]), (4, other_four[0] + added))):
        imag_new[at] = held[2, place] - time_step * (real_comm[:, cols(place)] + other)
        copies += start_all(
            [pltpu.make_async_copy(imag_new.at[at], out_hbm.at[1, 0, 0, order[place]], sems.at[1, at])]
        )
    comm[0] = real_comm[:, cols(0)] + other_three[0, 1] + real_four
    comm[1] = real_comm[:, cols(1)] + other_one[0]
    comm[2] = real_comm[:, cols(2)] + real_two[...]
    for direction in range(3):
        row_part[direction : direction + 1, :] = jnp.sum(weighted[direction].T, axis=0, keepdims=True)
    for copy in copies:
        copy.wait()


def sixth_kernel(
    held, der_ref, members, high_one, low_one, high_two, low_two, imag_part, comm, row_part, one, two, c1, c2, c3, c4, old_hbm,
    out_hbm, forces_hbm, new, forces_ref, sems
):
    order = order_of()
    prop, inner = rows_of(beside((high_one[...], low_one[...]), (high_two[...], low_two[...])))
    near = [tuple(jnp.concatenate(x, axis=0) for x in zip(split(one[1 + kind]), split(two[1 + kind]))) for kind in range(3)]
    behind = dot(inner, near[0])
    real_new = held[1, 0] + time_step * (imag_part[...] + dot(prop, near[2]) - behind[B:])
    new[0] = real_new
    copies = start_all([pltpu.make_async_copy(new.at[0], out_hbm.at[0, 0, 0, 0], sems.at[0])])
    new[1] = held[2, 0] - time_step * (comm[0] + dot(prop, near[1]) - behind[:B])
    for place, message, mixed in ((1, one, (high_one, low_one)), (2, two, (high_two, low_two))):
        added = dot(rows_of((mixed[0][...], mixed[1][...]))[0], split(message[0]))
        new[1 + place] = held[2, place] - time_step * (comm[place] + added)
    copies += start_all(
        [pltpu.make_async_copy(new.at[1 + at], out_hbm.at[1, 0, 0, order[at]], sems.at[1 + at]) for at in range(3)]
    )
    parts = []
    for direction in range(3):
        product = real_new * der_ref[direction, 0, 0, 0]
        parts.append(jnp.sum(product + product.T, axis=0, keepdims=True))
    orbital = jnp.concatenate(parts, axis=0) + row_part[...] + ((c1[...] + c2[...]) + (c3[...] + c4[...]))
    forces = lax.dot_general(
        orbital, members[...], (((1,), (1,)), ((), ())), precision=lax.Precision.HIGHEST, preferred_element_type=f32
    )
    for direction in range(3):
        forces_ref[direction] = forces[direction : direction + 1]
    copies += start_all([pltpu.make_async_copy(forces_ref, forces_hbm, sems.at[4])])
    for copy in copies:
        copy.wait()


def call(kernel, shapes, in_specs, products, args, out_specs=None, scratch=(), aliases={}):
    moved = sum(4 * x.size for x in args) + sum(4 * x.size for x in shapes)
    return pl.pallas_call(
        kernel,
        out_shape=shapes,
        in_specs=in_specs,
        out_specs=out_specs or [vmem] * len(shapes),
        scratch_shapes=scratch,
        input_output_aliases=aliases,
        compiler_params=pltpu.CompilerParams(vmem_limit_bytes=32 * 2**20),
        cost_estimate=pl.CostEstimate(flops=products * 6 * B**3, bytes_accessed=moved, transcendentals=0),
    )(*args)


def local(hamiltonian, inverse_margin, density, cutoff, derivative, atom_of):
    def shape(*dims, kind=f32):
        return jax.ShapeDtypeStruct(dims, kind)

    args = (hamiltonian, inverse_margin, density, cutoff, derivative, atom_of)
    hamiltonian, inverse_margin, density, cutoff, derivative, atom_of = (
        pltpu.with_memory_space_constraint(x, pltpu.HBM) for x in args
    )
    flags = pltpu.SMEM((1, 1, 5), jnp.int32)
    message = shape(4, B, B)
    first_one, rest = call(
        first_kernel,
        [message, shape(2, B, B)],
        [hbm] * 4,
        0,
        (cutoff, hamiltonian, inverse_margin, density),
        scratch=[flags, dma(()), dma((6,))],
    )
    near_one = swapped(first_one, 1)
    (first_four,) = call(functools.partial(next_kernel, 0), [message], [vmem] * 2, 0, (first_one, rest))
    near_four = swapped(first_four, 4)
    (first_two,) = call(functools.partial(next_kernel, 1), [message], [vmem] * 2, 500, (first_four, rest))
    near_two = swapped(first_two, 2)
    (send_three,) = call(
        whole_first_kernel,
        [shape(8, B, B)],
        [hbm] * 4 + [vmem],
        500,
        (cutoff, hamiltonian, inverse_margin, density, first_two),
        scratch=[flags, dma(()), dma((5,))],
    )
    near_three = swapped(send_three, 3)
    left = [shape(3 * B, 5 * B, kind=bf16)] * 2
    ham = [shape(B, 5 * B, kind=bf16)] * 2
    held, left_high, left_low, ham_high, ham_low, members = call(
        second_kernel,
        [shape(3, 5, B, B)] + left + ham + [shape(ATOMS, B)],
        [hbm] * 6,
        2000,
        (cutoff, hamiltonian, inverse_margin, density, atom_of, send_three),
        scratch=[pltpu.VMEM((4, 5, B, B), f32), flags, pltpu.VMEM((1, 1, B), jnp.int32), dma(()), dma(()), dma((4,))],
    )
    mixed = [shape(3 * B, B, kind=bf16)] * 2
    both = shape(2, 2, B, B)
    start, diagonal, other_three, derivative = call(
        third_kernel,
        [shape(3 * B, 5 * B), shape(3 * B, B), shape(2, 2, B, B), shape(*derivative.shape)],
        [vmem] * 6 + [hbm],
        8000,
        (left_high, left_low, ham_high, ham_low, held, near_three, derivative),
        scratch=[dma(())],
    )
    one_more, high_four, low_four, diagonal, other_four = call(
        four_kernel,
        [message] + mixed + [shape(3 * B, B), shape(2, B, B)],
        [vmem] * 6,
        8,
        (left_high, left_low, start, held, diagonal, near_four),
    )
    near_one_more = swapped(one_more, 1)
    two_more, four_more = call(more_kernel, [message] * 2, [vmem] * 2, 300, (one_more, held))
    near_four_more = swapped(four_more, 4)
    near_two_more = swapped(two_more, 2)
    high_one, low_one, diagonal, other_one = call(
        fourth_kernel,
        mixed + [shape(3 * B, B), shape(2, B, B)],
        [vmem] * 5,
        10,
        (left_high, left_low, start, diagonal, near_one),
    )
    block = shape(B, B)
    new, high_two, low_two, self_high, self_low, real_two, imag_part, weighted, *columns = call(
        fifth_kernel,
        [message] + mixed * 2 + [block, block, shape(3, B, B)] + [shape(3, B)] * 4,
        [vmem] * 10,
        22,
        (left_high, left_low, start, diagonal, held, derivative, other_one, other_three, other_four, near_two),
    )
    c1, c2, c3, c4 = columns
    c1, c2 = swapped(c1, 1), swapped(c2, 2)
    (c4,) = call(pass_kernel, [shape(3, B)], [vmem] * 2, 0, (near_four_more, c4))
    c4 = swapped(c4, 4)
    (c3,) = call(pass_kernel, [shape(3, B)], [vmem] * 2, 0, (c4, c3))
    columns = (c1, c2, swapped(c3, 3), c4)
    args = (held, new, left_high, left_low, self_high, self_low, other_one, real_two, other_three, other_four, weighted)
    args += (imag_part, high_four, low_four, near_four_more)
    out, comm, imag_part, row_part = call(
        real_kernel,
        [shape(*density.shape), shape(3, B, B), shape(B, B), shape(3, B)],
        [vmem] * 15,
        10,
        args,
        out_specs=[hbm] + [vmem] * 3,
        scratch=[pltpu.VMEM((2, B, B), f32), dma((2, 4))],
    )
    args = (held, derivative, members, high_one, low_one, high_two, low_two, imag_part, comm, row_part)
    args += (near_one_more, near_two_more, *columns, out)
    new_density, forces = call(
        sixth_kernel,
        [shape(*density.shape), shape(3, 1, ATOMS)],
        [vmem] * 16 + [hbm],
        10,
        args,
        out_specs=[hbm, hbm],
        scratch=[pltpu.VMEM((4, B, B), f32), pltpu.VMEM((3, 1, ATOMS), f32), dma((5,))],
        aliases={16: 0},
    )
    return new_density, forces.reshape(1, 1, 3, ATOMS)


def solution(mesh):
    placed = (
        P("gx", "gy", None, None, None),
        P("gx", "gy", None, None, None),
        P(None, "gx", "gy", None, None, None),
        P("gx", "gy", None),
        P(None, "gx", "gy", None, None, None),
        P("gx", "gy", None),
    )
    return jax.shard_map(
        local,
        mesh=mesh,
        in_specs=placed,
        out_specs=(P(None, "gx", "gy", None, None, None), P("gx", "gy", None, None)),
        check_vma=False,
    )
```

```python
import functools

import jax
import jax.numpy as jnp
from jax import lax
from jax.experimental import pallas as pl
from jax.experimental.pallas import tpu as pltpu
from jax.sharding import PartitionSpec as P

B = 128
ATOMS = 64

time_step = 0.25
vmem = pl.BlockSpec(memory_space=pltpu.VMEM)
hbm = pl.BlockSpec(memory_space=pltpu.HBM)
f32 = jnp.float32
bf16 = jnp.bfloat16
dma = pltpu.SemaphoreType.DMA


def swapped(cells, edge):
    axis = "gx" if edge < 3 else "gy"
    count = lax.axis_size(axis)
    assert count % 2 == 0
    first = 0 if edge in (1, 3) else 1
    pairs = []
    for i in range(first, count, 2):
        j = (i + 1) % count
        pairs += [(i, j), (j, i)]
    return lax.ppermute(cells, axis, pairs)


def order_of():
    odd_x = lax.rem(lax.axis_index("gx"), 2)
    odd_y = lax.rem(lax.axis_index("gy"), 2)
    return 0, 1 + odd_x, 2 - odd_x, 3 + odd_y, 4 - odd_y


def cols(place, count=1):
    return slice(place * B, (place + count) * B)


def split(values):
    high = values.astype(bf16)
    return high, (values - high.astype(f32)).astype(bf16)


def beside(*pairs):
    return tuple(jnp.concatenate(parts, axis=1) for parts in zip(*pairs))


def dot(left, right):
    def one(a, b):
        return jnp.dot(a, b, preferred_element_type=f32)

    return one(left[0], right[0]) + (one(left[0], right[1]) + one(left[1], right[0]))


def part(pair, rows, columns):
    return pair[0][rows, columns], pair[1][rows, columns]


def rows_of(pair):
    return (pair[0][:B], pair[1][:B]), (pair[0][B:], pair[1][B:])


def store(pair, columns, values):
    pair[0][:, columns], pair[1][:, columns] = values


def start_all(copies):
    for copy in copies:
        copy.start()
    return copies


def first_kernel(cutoff_hbm, ham_hbm, inv_hbm, rho_hbm, one, rest, cutoff_ref, cutoff_sem, sems):
    flags = pltpu.make_async_copy(cutoff_hbm, cutoff_ref, cutoff_sem)
    flags.start()
    order = order_of()
    sources = (ham_hbm.at[0, 0, 0], inv_hbm.at[0, 0, 0], rho_hbm.at[1, 0, 0, 0], ham_hbm.at[0, 0, order[1]])
    copies = [pltpu.make_async_copy(source, one.at[at], sems.at[at]) for at, source in enumerate(sources)]
    copies += [
        pltpu.make_async_copy(ham_hbm.at[0, 0, order[place]], rest.at[at], sems.at[4 + at]) for at, place in enumerate((4, 2))
    ]
    start_all(copies)
    flags.wait()
    for copy in copies:
        copy.wait()
    one[3] = one[3] * cutoff_ref[0, 0, order[1]].astype(f32)
    for at, place in enumerate((4, 2)):
        rest[at] = rest[at] * cutoff_ref[0, 0, order[place]].astype(f32)


def next_kernel(at, message, rest, out):
    out[:3] = message[:3]
    out[3] = rest[at]


def whole_first_kernel(cutoff_hbm, ham_hbm, inv_hbm, rho_hbm, message, out, cutoff_ref, cutoff_sem, sems):
    flags = pltpu.make_async_copy(cutoff_hbm, cutoff_ref, cutoff_sem)
    flags.start()
    offset = order_of()[3]
    sources = (ham_hbm.at[0, 0, offset], rho_hbm.at[0, 0, 0, 0], inv_hbm.at[0, 0, offset], rho_hbm.at[0, 0, 0, offset])
    sources += (rho_hbm.at[1, 0, 0, offset],)
    copies = start_all([pltpu.make_async_copy(source, out.at[3 + at], sems.at[at]) for at, source in enumerate(sources)])
    out[:3] = message[:3]
    flags.wait()
    keep = cutoff_ref[0, 0, offset].astype(f32)
    for copy in copies:
        copy.wait()
    for at in (3, 5, 6, 7):
        out[at] = out[at] * keep


def second_kernel(
    cutoff_hbm, ham_hbm, inv_hbm, rho_hbm, atom_hbm, after, held, left_high, left_low, ham_high, ham_low, members,
    raw, cutoff_ref, atom_ref, cutoff_sem, atom_sem, sems
):
    flags = pltpu.make_async_copy(cutoff_hbm, cutoff_ref, cutoff_sem)
    flags.start()
    sources = (ham_hbm.at[0, 0], inv_hbm.at[0, 0], rho_hbm.at[0, 0, 0], rho_hbm.at[1, 0, 0])
    copies = start_all([pltpu.make_async_copy(source, raw.at[at], sems.at[at]) for at, source in enumerate(sources)])
    owners = pltpu.make_async_copy(atom_hbm, atom_ref, atom_sem)
    owners.start()
    order = order_of()
    flags.wait()
    keeps = [cutoff_ref[0, 0, offset].astype(f32) for offset in order]
    for kind, copy in enumerate(copies):
        copy.wait()
        for place, offset in enumerate(order):
            block = raw[kind, offset]
            if place > 0:
                block = block * keeps[place]
            if kind == 0:
                store((ham_high, ham_low), cols(place), split(block))
            else:
                held[kind - 1, place] = block
                rows = slice((kind - 1) * B, kind * B)
                left_high[rows, cols(place)], left_low[rows, cols(place)] = split(block)
    owners.wait()
    atoms = jnp.broadcast_to(atom_ref[0], (ATOMS, B))
    members[...] = -(lax.broadcasted_iota(jnp.int32, (ATOMS, B), 0) == atoms).astype(f32)


def first_half(left, place, start, near, diagonal):
    both = dot(part(left, slice(0, 3 * B), cols(place)), beside(split(near[0]), split(near[3])))
    mixed = split(start[:, cols(place)] + both[:, :B])
    prop, inner = rows_of(mixed)
    behind = dot(inner, split(near[1]))
    imag = dot(prop, split(near[2])) - behind[B:]
    return mixed, diagonal + both[:, B:], -behind[:B], imag


def second_half(mixed, near):
    prop, inner = rows_of(mixed)
    ahead = dot(prop, beside(split(near[0]), split(near[2]), split(near[3])))
    behind = dot(inner, split(near[1]))
    return ahead[:, cols(0)], ahead[:, cols(1)] - behind[:B], ahead[:, cols(2)] - behind[B:]


def send_more(more, held, place):
    more[0] = held[1, 0]
    for kind in range(3):
        more[1 + kind] = held[kind, place]


def third_kernel(left_high, left_low, ham_high, ham_low, held, three, der_hbm, start, diagonal, other, der, sem):
    copy = pltpu.make_async_copy(der_hbm, der, sem)
    copy.start()
    left = (left_high, left_low)
    start[...] = dot(part(left, slice(0, 3 * B), cols(0)), part((ham_high, ham_low), slice(0, B), cols(0, 5)))
    mixed, diagonal[...], real, other[1, 0] = first_half(left, 3, start, three, start[:, cols(0)])
    added, other[0, 1], other[1, 1] = second_half(mixed, three[4:])
    other[0, 0] = real + added
    copy.wait()


def four_kernel(
    left_high, left_low, start, held, diagonal, four, one_more, mixed_high, mixed_low, diagonal_out, other
):
    send_more(one_more, held, 1)
    mixed, diagonal_out[...], other[0], other[1] = first_half((left_high, left_low), 4, start, four, diagonal[...])
    mixed_high[...], mixed_low[...] = mixed


def more_kernel(after, held, two_more, four_more):
    send_more(two_more, held, 2)
    send_more(four_more, held, 4)


def fourth_kernel(left_high, left_low, start, diagonal, one, mixed_high, mixed_low, diagonal_out, other):
    mixed, diagonal_out[...], other[0], other[1] = first_half((left_high, left_low), 1, start, one, diagonal[...])
    mixed_high[...], mixed_low[...] = mixed


def fifth_kernel(
    left_high, left_low, start, diagonal, held, der_ref, other_one, other_three, other_four, two,
    new, mixed_high, mixed_low, self_high, self_low, real_two, comm, weighted, c1, c2, c3, c4
):
    order = order_of()
    left = (left_high, left_low)
    mixed, total, real_two[...], imag_two = first_half(left, 2, start, two, diagonal[...])
    mixed_high[...], mixed_low[...] = mixed
    at_self = split(total)
    self_high[...], self_low[...] = at_self
    whole = cols(0, 5)
    ahead = dot(part(at_self, slice(0, B), cols(0)), part(left, slice(2 * B, 3 * B), whole))
    behind = dot(part(at_self, slice(2 * B, 3 * B), cols(0)), part(left, slice(0, B), whole))
    imag_comm = ahead - behind
    comm[...] = imag_comm[:, cols(0)] + other_three[1, 1]
    sums = [None] * 3
    for place, column in enumerate((c1, c2, c3, c4), 1):
        imag = (other_one[1], imag_two, other_three[1, 0], other_four[1])[place - 1]
        real_new = held[1, place] + time_step * (imag_comm[:, cols(place)] + imag)
        new[place - 1] = real_new
        for direction in range(3):
            product = real_new * der_ref[direction, 0, 0, order[place]]
            sums[direction] = product if place == 1 else sums[direction] + product
            column[direction : direction + 1, :] = jnp.sum(product, axis=0, keepdims=True)
    for direction in range(3):
        weighted[direction] = sums[direction]


def later_kernel(arrived, column, out):
    out[...] = column[...]


def real_kernel(
    held, new, left_high, left_low, self_high, self_low, other_one, real_two, other_three, other_four, weighted,
    imag_part, high_four, low_four, four, out_hbm, comm, imag_out, row_part, imag_new, sems
):
    order = order_of()
    copies = start_all(
        [pltpu.make_async_copy(new.at[at], out_hbm.at[0, 0, 0, order[1 + at]], sems.at[0, at]) for at in range(4)]
    )
    left = (left_high, left_low)
    whole = cols(0, 5)
    at_self = (self_high, self_low)
    ahead = dot(part(at_self, slice(0, B), cols(0)), part(left, slice(B, 2 * B), whole))
    behind = dot(part(at_self, slice(B, 2 * B), cols(0)), part(left, slice(0, B), whole))
    real_comm = ahead - behind
    added, real_four, imag_four = second_half((high_four[...], low_four[...]), four)
    imag_out[...] = imag_part[...] + imag_four
    for at, (place, other) in enumerate(((3, other_three[0, 0]), (4, other_four[0] + added))):
        imag_new[at] = held[2, place] - time_step * (real_comm[:, cols(place)] + other)
        copies += start_all(
            [pltpu.make_async_copy(imag_new.at[at], out_hbm.at[1, 0, 0, order[place]], sems.at[1, at])]
        )
    comm[0] = real_comm[:, cols(0)] + other_three[0, 1] + real_four
    comm[1] = real_comm[:, cols(1)] + other_one[0]
    comm[2] = real_comm[:, cols(2)] + real_two[...]
    for direction in range(3):
        row_part[direction : direction + 1, :] = jnp.sum(weighted[direction].T, axis=0, keepdims=True)
    for copy in copies:
        copy.wait()


def sixth_kernel(
    held, der_ref, members, high_one, low_one, high_two, low_two, imag_part, comm, row_part, one, two, c1, c2, c3, c4, old_hbm,
    out_hbm, forces_hbm, new, forces_ref, sems
):
    order = order_of()
    prop, inner = rows_of(beside((high_one[...], low_one[...]), (high_two[...], low_two[...])))
    near = [tuple(jnp.concatenate(x, axis=0) for x in zip(split(one[1 + kind]), split(two[1 + kind]))) for kind in range(3)]
    behind = dot(inner, near[0])
    real_new = held[1, 0] + time_step * (imag_part[...] + dot(prop, near[2]) - behind[B:])
    new[0] = real_new
    copies = start_all([pltpu.make_async_copy(new.at[0], out_hbm.at[0, 0, 0, 0], sems.at[0])])
    new[1] = held[2, 0] - time_step * (comm[0] + dot(prop, near[1]) - behind[:B])
    for place, message, mixed in ((1, one, (high_one, low_one)), (2, two, (high_two, low_two))):
        added = dot(rows_of((mixed[0][...], mixed[1][...]))[0], split(message[0]))
        new[1 + place] = held[2, place] - time_step * (comm[place] + added)
    copies += start_all(
        [pltpu.make_async_copy(new.at[1 + at], out_hbm.at[1, 0, 0, order[at]], sems.at[1 + at]) for at in range(3)]
    )
    parts = []
    for direction in range(3):
        product = real_new * der_ref[direction, 0, 0, 0]
        parts.append(jnp.sum(product + product.T, axis=0, keepdims=True))
    orbital = jnp.concatenate(parts, axis=0) + row_part[...] + ((c1[...] + c2[...]) + (c3[...] + c4[...]))
    forces = lax.dot_general(
        orbital, members[...], (((1,), (1,)), ((), ())), precision=lax.Precision.HIGHEST, preferred_element_type=f32
    )
    for direction in range(3):
        forces_ref[direction] = forces[direction : direction + 1]
    copies += start_all([pltpu.make_async_copy(forces_ref, forces_hbm, sems.at[4])])
    for copy in copies:
        copy.wait()


def call(kernel, shapes, in_specs, products, args, out_specs=None, scratch=(), aliases={}):
    moved = sum(4 * x.size for x in args) + sum(4 * x.size for x in shapes)
    return pl.pallas_call(
        kernel,
        out_shape=shapes,
        in_specs=in_specs,
        out_specs=out_specs or [vmem] * len(shapes),
        scratch_shapes=scratch,
        input_output_aliases=aliases,
        compiler_params=pltpu.CompilerParams(vmem_limit_bytes=32 * 2**20),
        cost_estimate=pl.CostEstimate(flops=products * 6 * B**3, bytes_accessed=moved, transcendentals=0),
    )(*args)


def local(hamiltonian, inverse_margin, density, cutoff, derivative, atom_of):
    def shape(*dims, kind=f32):
        return jax.ShapeDtypeStruct(dims, kind)

    args = (hamiltonian, inverse_margin, density, cutoff, derivative, atom_of)
    hamiltonian, inverse_margin, density, cutoff, derivative, atom_of = (
        pltpu.with_memory_space_constraint(x, pltpu.HBM) for x in args
    )
    flags = pltpu.SMEM((1, 1, 5), jnp.int32)
    message = shape(4, B, B)
    first_one, rest = call(
        first_kernel,
        [message, shape(2, B, B)],
        [hbm] * 4,
        0,
        (cutoff, hamiltonian, inverse_margin, density),
        scratch=[flags, dma(()), dma((6,))],
    )
    near_one = swapped(first_one, 1)
    (first_four,) = call(functools.partial(next_kernel, 0), [message], [vmem] * 2, 0, (first_one, rest))
    near_four = swapped(first_four, 4)
    (first_two,) = call(functools.partial(next_kernel, 1), [message], [vmem] * 2, 500, (first_four, rest))
    near_two = swapped(first_two, 2)
    (send_three,) = call(
        whole_first_kernel,
        [shape(8, B, B)],
        [hbm] * 4 + [vmem],
        500,
        (cutoff, hamiltonian, inverse_margin, density, first_two),
        scratch=[flags, dma(()), dma((5,))],
    )
    near_three = swapped(send_three, 3)
    left = [shape(3 * B, 5 * B, kind=bf16)] * 2
    ham = [shape(B, 5 * B, kind=bf16)] * 2
    held, left_high, left_low, ham_high, ham_low, members = call(
        second_kernel,
        [shape(3, 5, B, B)] + left + ham + [shape(ATOMS, B)],
        [hbm] * 6,
        2000,
        (cutoff, hamiltonian, inverse_margin, density, atom_of, send_three),
        scratch=[pltpu.VMEM((4, 5, B, B), f32), flags, pltpu.VMEM((1, 1, B), jnp.int32), dma(()), dma(()), dma((4,))],
    )
    mixed = [shape(3 * B, B, kind=bf16)] * 2
    both = shape(2, 2, B, B)
    start, diagonal, other_three, derivative = call(
        third_kernel,
        [shape(3 * B, 5 * B), shape(3 * B, B), shape(2, 2, B, B), shape(*derivative.shape)],
        [vmem] * 6 + [hbm],
        8000,
        (left_high, left_low, ham_high, ham_low, held, near_three, derivative),
        scratch=[dma(())],
    )
    one_more, high_four, low_four, diagonal, other_four = call(
        four_kernel,
        [message] + mixed + [shape(3 * B, B), shape(2, B, B)],
        [vmem] * 6,
        8,
        (left_high, left_low, start, held, diagonal, near_four),
    )
    near_one_more = swapped(one_more, 1)
    two_more, four_more = call(more_kernel, [message] * 2, [vmem] * 2, 300, (one_more, held))
    near_four_more = swapped(four_more, 4)
    near_two_more = swapped(two_more, 2)
    high_one, low_one, diagonal, other_one = call(
        fourth_kernel,
        mixed + [shape(3 * B, B), shape(2, B, B)],
        [vmem] * 5,
        10,
        (left_high, left_low, start, diagonal, near_one),
    )
    block = shape(B, B)
    new, high_two, low_two, self_high, self_low, real_two, imag_part, weighted, *columns = call(
        fifth_kernel,
        [message] + mixed * 2 + [block, block, shape(3, B, B)] + [shape(3, B)] * 4,
        [vmem] * 10,
        22,
        (left_high, left_low, start, diagonal, held, derivative, other_one, other_three, other_four, near_two),
    )
    c1, c2, c3, c4 = columns
    c1, c2 = swapped(c1, 1), swapped(c2, 2)
    (c3,) = call(later_kernel, [shape(3, B)], [vmem] * 2, 0, (near_four_more, c3))
    columns = (c1, c2, swapped(c3, 3), swapped(c4, 4))
    args = (held, new, left_high, left_low, self_high, self_low, other_one, real_two, other_three, other_four, weighted)
    args += (imag_part, high_four, low_four, near_four_more)
    out, comm, imag_part, row_part = call(
        real_kernel,
        [shape(*density.shape), shape(3, B, B), shape(B, B), shape(3, B)],
        [vmem] * 15,
        10,
        args,
        out_specs=[hbm] + [vmem] * 3,
        scratch=[pltpu.VMEM((2, B, B), f32), dma((2, 4))],
    )
    args = (held, derivative, members, high_one, low_one, high_two, low_two, imag_part, comm, row_part)
    args += (near_one_more, near_two_more, *columns, out)
    new_density, forces = call(
        sixth_kernel,
        [shape(*density.shape), shape(3, 1, ATOMS)],
        [vmem] * 16 + [hbm],
        10,
        args,
        out_specs=[hbm, hbm],
        scratch=[pltpu.VMEM((4, B, B), f32), pltpu.VMEM((3, 1, ATOMS), f32), dma((5,))],
        aliases={16: 0},
    )
    return new_density, forces.reshape(1, 1, 3, ATOMS)


def solution(mesh):
    placed = (
        P("gx", "gy", None, None, None),
        P("gx", "gy", None, None, None),
        P(None, "gx", "gy", None, None, None),
        P("gx", "gy", None),
        P(None, "gx", "gy", None, None, None),
        P("gx", "gy", None),
    )
    return jax.shard_map(
        local,
        mesh=mesh,
        in_specs=placed,
        out_specs=(P(None, "gx", "gy", None, None, None), P("gx", "gy", None, None)),
        check_vma=False,
    )
```

```python
import functools

import jax
import jax.numpy as jnp
from jax import lax
from jax.experimental import pallas as pl
from jax.experimental.pallas import tpu as pltpu
from jax.sharding import PartitionSpec as P

B = 128
ATOMS = 64

time_step = 0.25
vmem = pl.BlockSpec(memory_space=pltpu.VMEM)
hbm = pl.BlockSpec(memory_space=pltpu.HBM)
f32 = jnp.float32
bf16 = jnp.bfloat16
dma = pltpu.SemaphoreType.DMA


def swapped(cells, edge):
    axis = "gx" if edge < 3 else "gy"
    count = lax.axis_size(axis)
    assert count % 2 == 0
    first = 0 if edge in (1, 3) else 1
    pairs = []
    for i in range(first, count, 2):
        j = (i + 1) % count
        pairs += [(i, j), (j, i)]
    return lax.ppermute(cells, axis, pairs)


def order_of():
    odd_x = lax.rem(lax.axis_index("gx"), 2)
    odd_y = lax.rem(lax.axis_index("gy"), 2)
    return 0, 1 + odd_x, 2 - odd_x, 3 + odd_y, 4 - odd_y


def cols(place, count=1):
    return slice(place * B, (place + count) * B)


def split(values):
    high = values.astype(bf16)
    return high, (values - high.astype(f32)).astype(bf16)


def beside(*pairs):
    return tuple(jnp.concatenate(parts, axis=1) for parts in zip(*pairs))


def dot(left, right):
    def one(a, b):
        return jnp.dot(a, b, preferred_element_type=f32)

    return one(left[0], right[0]) + (one(left[0], right[1]) + one(left[1], right[0]))


def part(pair, rows, columns):
    return pair[0][rows, columns], pair[1][rows, columns]


def rows_of(pair):
    return (pair[0][:B], pair[1][:B]), (pair[0][B:], pair[1][B:])


def store(pair, columns, values):
    pair[0][:, columns], pair[1][:, columns] = values


def start_all(copies):
    for copy in copies:
        copy.start()
    return copies


def first_kernel(cutoff_hbm, ham_hbm, inv_hbm, rho_hbm, one, rest, cutoff_ref, cutoff_sem, sems):
    flags = pltpu.make_async_copy(cutoff_hbm, cutoff_ref, cutoff_sem)
    flags.start()
    order = order_of()
    sources = (ham_hbm.at[0, 0, 0], inv_hbm.at[0, 0, 0], rho_hbm.at[1, 0, 0, 0], ham_hbm.at[0, 0, order[1]])
    copies = [pltpu.make_async_copy(source, one.at[at], sems.at[at]) for at, source in enumerate(sources)]
    copies += [
        pltpu.make_async_copy(ham_hbm.at[0, 0, order[place]], rest.at[at], sems.at[4 + at]) for at, place in enumerate((4, 2))
    ]
    start_all(copies)
    flags.wait()
    for copy in copies:
        copy.wait()
    one[3] = one[3] * cutoff_ref[0, 0, order[1]].astype(f32)
    for at, place in enumerate((4, 2)):
        rest[at] = rest[at] * cutoff_ref[0, 0, order[place]].astype(f32)


def next_kernel(at, message, rest, out):
    out[:3] = message[:3]
    out[3] = rest[at]


def whole_first_kernel(cutoff_hbm, ham_hbm, inv_hbm, rho_hbm, message, out, cutoff_ref, cutoff_sem, sems):
    flags = pltpu.make_async_copy(cutoff_hbm, cutoff_ref, cutoff_sem)
    flags.start()
    offset = order_of()[3]
    sources = (ham_hbm.at[0, 0, offset], rho_hbm.at[0, 0, 0, 0], inv_hbm.at[0, 0, offset], rho_hbm.at[0, 0, 0, offset])
    sources += (rho_hbm.at[1, 0, 0, offset],)
    copies = start_all([pltpu.make_async_copy(source, out.at[3 + at], sems.at[at]) for at, source in enumerate(sources)])
    out[:3] = message[:3]
    flags.wait()
    keep = cutoff_ref[0, 0, offset].astype(f32)
    for copy in copies:
        copy.wait()
    for at in (3, 5, 6, 7):
        out[at] = out[at] * keep


def second_kernel(
    cutoff_hbm, ham_hbm, inv_hbm, rho_hbm, atom_hbm, after, held, left_high, left_low, ham_high, ham_low, members,
    raw, cutoff_ref, atom_ref, cutoff_sem, atom_sem, sems
):
    flags = pltpu.make_async_copy(cutoff_hbm, cutoff_ref, cutoff_sem)
    flags.start()
    sources = (ham_hbm.at[0, 0], inv_hbm.at[0, 0], rho_hbm.at[0, 0, 0], rho_hbm.at[1, 0, 0])
    copies = start_all([pltpu.make_async_copy(source, raw.at[at], sems.at[at]) for at, source in enumerate(sources)])
    owners = pltpu.make_async_copy(atom_hbm, atom_ref, atom_sem)
    owners.start()
    order = order_of()
    flags.wait()
    keeps = [cutoff_ref[0, 0, offset].astype(f32) for offset in order]
    for kind, copy in enumerate(copies):
        copy.wait()
        for place, offset in enumerate(order):
            block = raw[kind, offset]
            if place > 0:
                block = block * keeps[place]
            if kind == 0:
                store((ham_high, ham_low), cols(place), split(block))
            else:
                held[kind - 1, place] = block
                rows = slice((kind - 1) * B, kind * B)
                left_high[rows, cols(place)], left_low[rows, cols(place)] = split(block)
    owners.wait()
    atoms = jnp.broadcast_to(atom_ref[0], (ATOMS, B))
    members[...] = -(lax.broadcasted_iota(jnp.int32, (ATOMS, B), 0) == atoms).astype(f32)


def first_half(left, place, start, near, diagonal):
    both = dot(part(left, slice(0, 3 * B), cols(place)), beside(split(near[0]), split(near[3])))
    mixed = split(start[:, cols(place)] + both[:, :B])
    prop, inner = rows_of(mixed)
    behind = dot(inner, split(near[1]))
    imag = dot(prop, split(near[2])) - behind[B:]
    return mixed, diagonal + both[:, B:], -behind[:B], imag


def second_half(mixed, near):
    prop, inner = rows_of(mixed)
    ahead = dot(prop, beside(split(near[0]), split(near[2]), split(near[3])))
    behind = dot(inner, split(near[1]))
    return ahead[:, cols(0)], ahead[:, cols(1)] - behind[:B], ahead[:, cols(2)] - behind[B:]


def send_more(more, held, place):
    more[0] = held[1, 0]
    for kind in range(3):
        more[1 + kind] = held[kind, place]


def third_kernel(left_high, left_low, ham_high, ham_low, held, three, der_hbm, start, diagonal, other, der, sem):
    copy = pltpu.make_async_copy(der_hbm, der, sem)
    copy.start()
    left = (left_high, left_low)
    start[...] = dot(part(left, slice(0, 3 * B), cols(0)), part((ham_high, ham_low), slice(0, B), cols(0, 5)))
    mixed, diagonal[...], real, other[1, 0] = first_half(left, 3, start, three, start[:, cols(0)])
    added, other[0, 1], other[1, 1] = second_half(mixed, three[4:])
    other[0, 0] = real + added
    copy.wait()


def four_kernel(
    left_high, left_low, start, held, diagonal, four, one_more, mixed_high, mixed_low, diagonal_out, other
):
    send_more(one_more, held, 1)
    mixed, diagonal_out[...], other[0], other[1] = first_half((left_high, left_low), 4, start, four, diagonal[...])
    mixed_high[...], mixed_low[...] = mixed


def more_kernel(after, held, two_more, four_more):
    send_more(two_more, held, 2)
    send_more(four_more, held, 4)


def fourth_kernel(left_high, left_low, start, diagonal, one, mixed_high, mixed_low, diagonal_out, other):
    mixed, diagonal_out[...], other[0], other[1] = first_half((left_high, left_low), 1, start, one, diagonal[...])
    mixed_high[...], mixed_low[...] = mixed


def fifth_kernel(
    left_high, left_low, start, diagonal, held, der_ref, other_one, other_three, other_four, two,
    new, mixed_high, mixed_low, self_high, self_low, real_two, comm, weighted, c1, c2, c3, c4
):
    order = order_of()
    left = (left_high, left_low)
    mixed, total, real_two[...], imag_two = first_half(left, 2, start, two, diagonal[...])
    mixed_high[...], mixed_low[...] = mixed
    at_self = split(total)
    self_high[...], self_low[...] = at_self
    whole = cols(0, 5)
    ahead = dot(part(at_self, slice(0, B), cols(0)), part(left, slice(2 * B, 3 * B), whole))
    behind = dot(part(at_self, slice(2 * B, 3 * B), cols(0)), part(left, slice(0, B), whole))
    imag_comm = ahead - behind
    comm[...] = imag_comm[:, cols(0)] + other_three[1, 1]
    sums = [None] * 3
    for place, column in enumerate((c1, c2, c3, c4), 1):
        imag = (other_one[1], imag_two, other_three[1, 0], other_four[1])[place - 1]
        real_new = held[1, place] + time_step * (imag_comm[:, cols(place)] + imag)
        new[place - 1] = real_new
        for direction in range(3):
            product = real_new * der_ref[direction, 0, 0, order[place]]
            sums[direction] = product if place == 1 else sums[direction] + product
            column[direction : direction + 1, :] = jnp.sum(product, axis=0, keepdims=True)
    for direction in range(3):
        weighted[direction] = sums[direction]


def later_kernel(arrived, column, out):
    out[...] = column[...]


def real_kernel(
    held, new, left_high, left_low, self_high, self_low, other_one, real_two, other_three, other_four, weighted,
    imag_part, high_four, low_four, four, out_hbm, comm, imag_out, row_part, imag_new, sems
):
    order = order_of()
    copies = start_all(
        [pltpu.make_async_copy(new.at[at], out_hbm.at[0, 0, 0, order[1 + at]], sems.at[0, at]) for at in range(4)]
    )
    left = (left_high, left_low)
    whole = cols(0, 5)
    at_self = (self_high, self_low)
    ahead = dot(part(at_self, slice(0, B), cols(0)), part(left, slice(B, 2 * B), whole))
    behind = dot(part(at_self, slice(B, 2 * B), cols(0)), part(left, slice(0, B), whole))
    real_comm = ahead - behind
    added, real_four, imag_four = second_half((high_four[...], low_four[...]), four)
    imag_out[...] = imag_part[...] + imag_four
    for at, (place, other) in enumerate(((3, other_three[0, 0]), (4, other_four[0] + added))):
        imag_new[at] = held[2, place] - time_step * (real_comm[:, cols(place)] + other)
        copies += start_all(
            [pltpu.make_async_copy(imag_new.at[at], out_hbm.at[1, 0, 0, order[place]], sems.at[1, at])]
        )
    comm[0] = real_comm[:, cols(0)] + other_three[0, 1] + real_four
    comm[1] = real_comm[:, cols(1)] + other_one[0]
    comm[2] = real_comm[:, cols(2)] + real_two[...]
    for direction in range(3):
        row_part[direction : direction + 1, :] = jnp.sum(weighted[direction].T, axis=0, keepdims=True)
    for copy in copies:
        copy.wait()


def sixth_kernel(
    held, der_ref, members, high_one, low_one, high_two, low_two, imag_part, comm, row_part, one, two, c1, c2, c3, c4, old_hbm,
    out_hbm, forces_hbm, new, forces_ref, sems
):
    order = order_of()
    prop, inner = rows_of(beside((high_one[...], low_one[...]), (high_two[...], low_two[...])))
    near = [tuple(jnp.concatenate(x, axis=0) for x in zip(split(one[1 + kind]), split(two[1 + kind]))) for kind in range(3)]
    behind = dot(inner, near[0])
    real_new = held[1, 0] + time_step * (imag_part[...] + dot(prop, near[2]) - behind[B:])
    new[0] = real_new
    copies = start_all([pltpu.make_async_copy(new.at[0], out_hbm.at[0, 0, 0, 0], sems.at[0])])
    new[1] = held[2, 0] - time_step * (comm[0] + dot(prop, near[1]) - behind[:B])
    for place, message, mixed in ((1, one, (high_one, low_one)), (2, two, (high_two, low_two))):
        added = dot(rows_of((mixed[0][...], mixed[1][...]))[0], split(message[0]))
        new[1 + place] = held[2, place] - time_step * (comm[place] + added)
    copies += start_all(
        [pltpu.make_async_copy(new.at[1 + at], out_hbm.at[1, 0, 0, order[at]], sems.at[1 + at]) for at in range(3)]
    )
    parts = []
    for direction in range(3):
        product = real_new * der_ref[direction, 0, 0, 0]
        parts.append(jnp.sum(product + product.T, axis=0, keepdims=True))
    orbital = jnp.concatenate(parts, axis=0) + row_part[...] + ((c1[...] + c2[...]) + (c3[...] + c4[...]))
    forces = lax.dot_general(
        orbital, members[...], (((1,), (1,)), ((), ())), precision=lax.Precision.HIGHEST, preferred_element_type=f32
    )
    for direction in range(3):
        forces_ref[direction] = forces[direction : direction + 1]
    copies += start_all([pltpu.make_async_copy(forces_ref, forces_hbm, sems.at[4])])
    for copy in copies:
        copy.wait()


def call(kernel, shapes, in_specs, products, args, out_specs=None, scratch=(), aliases={}):
    moved = sum(4 * x.size for x in args) + sum(4 * x.size for x in shapes)
    return pl.pallas_call(
        kernel,
        out_shape=shapes,
        in_specs=in_specs,
        out_specs=out_specs or [vmem] * len(shapes),
        scratch_shapes=scratch,
        input_output_aliases=aliases,
        compiler_params=pltpu.CompilerParams(vmem_limit_bytes=32 * 2**20),
        cost_estimate=pl.CostEstimate(flops=products * 6 * B**3, bytes_accessed=moved, transcendentals=0),
    )(*args)


def local(hamiltonian, inverse_margin, density, cutoff, derivative, atom_of):
    def shape(*dims, kind=f32):
        return jax.ShapeDtypeStruct(dims, kind)

    args = (hamiltonian, inverse_margin, density, cutoff, derivative, atom_of)
    hamiltonian, inverse_margin, density, cutoff, derivative, atom_of = (
        pltpu.with_memory_space_constraint(x, pltpu.HBM) for x in args
    )
    flags = pltpu.SMEM((1, 1, 5), jnp.int32)
    message = shape(4, B, B)
    first_one, rest = call(
        first_kernel,
        [message, shape(2, B, B)],
        [hbm] * 4,
        0,
        (cutoff, hamiltonian, inverse_margin, density),
        scratch=[flags, dma(()), dma((6,))],
    )
    near_one = swapped(first_one, 1)
    (first_four,) = call(functools.partial(next_kernel, 0), [message], [vmem] * 2, 0, (first_one, rest))
    near_four = swapped(first_four, 4)
    (first_two,) = call(functools.partial(next_kernel, 1), [message], [vmem] * 2, 500, (first_four, rest))
    near_two = swapped(first_two, 2)
    (send_three,) = call(
        whole_first_kernel,
        [shape(8, B, B)],
        [hbm] * 4 + [vmem],
        500,
        (cutoff, hamiltonian, inverse_margin, density, first_two),
        scratch=[flags, dma(()), dma((5,))],
    )
    near_three = swapped(send_three, 3)
    left = [shape(3 * B, 5 * B, kind=bf16)] * 2
    ham = [shape(B, 5 * B, kind=bf16)] * 2
    held, left_high, left_low, ham_high, ham_low, members = call(
        second_kernel,
        [shape(3, 5, B, B)] + left + ham + [shape(ATOMS, B)],
        [hbm] * 6,
        2000,
        (cutoff, hamiltonian, inverse_margin, density, atom_of, send_three),
        scratch=[pltpu.VMEM((4, 5, B, B), f32), flags, pltpu.VMEM((1, 1, B), jnp.int32), dma(()), dma(()), dma((4,))],
    )
    mixed = [shape(3 * B, B, kind=bf16)] * 2
    both = shape(2, 2, B, B)
    start, diagonal, other_three, derivative = call(
        third_kernel,
        [shape(3 * B, 5 * B), shape(3 * B, B), shape(2, 2, B, B), shape(*derivative.shape)],
        [vmem] * 6 + [hbm],
        8000,
        (left_high, left_low, ham_high, ham_low, held, near_three, derivative),
        scratch=[dma(())],
    )
    one_more, high_four, low_four, diagonal, other_four = call(
        four_kernel,
        [message] + mixed + [shape(3 * B, B), shape(2, B, B)],
        [vmem] * 6,
        8,
        (left_high, left_low, start, held, diagonal, near_four),
    )
    near_one_more = swapped(one_more, 1)
    two_more, four_more = call(more_kernel, [message] * 2, [vmem] * 2, 300, (one_more, held))
    near_four_more = swapped(four_more, 4)
    near_two_more = swapped(two_more, 2)
    high_one, low_one, diagonal, other_one = call(
        fourth_kernel,
        mixed + [shape(3 * B, B), shape(2, B, B)],
        [vmem] * 5,
        10,
        (left_high, left_low, start, diagonal, near_one),
    )
    block = shape(B, B)
    new, high_two, low_two, self_high, self_low, real_two, imag_part, weighted, *columns = call(
        fifth_kernel,
        [message] + mixed * 2 + [block, block, shape(3, B, B)] + [shape(3, B)] * 4,
        [vmem] * 10,
        22,
        (left_high, left_low, start, diagonal, held, derivative, other_one, other_three, other_four, near_two),
    )
    c1, c2, c3, c4 = columns
    c1, c2, c3 = swapped(c1, 1), swapped(c2, 2), swapped(c3, 3)
    (c4,) = call(later_kernel, [shape(3, B)], [vmem] * 2, 0, (c3, c4))
    columns = (c1, c2, c3, swapped(c4, 4))
    args = (held, new, left_high, left_low, self_high, self_low, other_one, real_two, other_three, other_four, weighted)
    args += (imag_part, high_four, low_four, near_four_more)
    out, comm, imag_part, row_part = call(
        real_kernel,
        [shape(*density.shape), shape(3, B, B), shape(B, B), shape(3, B)],
        [vmem] * 15,
        10,
        args,
        out_specs=[hbm] + [vmem] * 3,
        scratch=[pltpu.VMEM((2, B, B), f32), dma((2, 4))],
    )
    args = (held, derivative, members, high_one, low_one, high_two, low_two, imag_part, comm, row_part)
    args += (near_one_more, near_two_more, *columns, out)
    new_density, forces = call(
        sixth_kernel,
        [shape(*density.shape), shape(3, 1, ATOMS)],
        [vmem] * 16 + [hbm],
        10,
        args,
        out_specs=[hbm, hbm],
        scratch=[pltpu.VMEM((4, B, B), f32), pltpu.VMEM((3, 1, ATOMS), f32), dma((5,))],
        aliases={16: 0},
    )
    return new_density, forces.reshape(1, 1, 3, ATOMS)


def solution(mesh):
    placed = (
        P("gx", "gy", None, None, None),
        P("gx", "gy", None, None, None),
        P(None, "gx", "gy", None, None, None),
        P("gx", "gy", None),
        P(None, "gx", "gy", None, None, None),
        P("gx", "gy", None),
    )
    return jax.shard_map(
        local,
        mesh=mesh,
        in_specs=placed,
        out_specs=(P(None, "gx", "gy", None, None, None), P("gx", "gy", None, None)),
        check_vma=False,
    )
```

```python
import functools

import jax
import jax.numpy as jnp
from jax import lax
from jax.experimental import pallas as pl
from jax.experimental.pallas import tpu as pltpu
from jax.sharding import PartitionSpec as P

B = 128
ATOMS = 64

time_step = 0.25
vmem = pl.BlockSpec(memory_space=pltpu.VMEM)
hbm = pl.BlockSpec(memory_space=pltpu.HBM)
f32 = jnp.float32
bf16 = jnp.bfloat16
dma = pltpu.SemaphoreType.DMA


def swapped(cells, edge):
    axis = "gx" if edge < 3 else "gy"
    count = lax.axis_size(axis)
    assert count % 2 == 0
    first = 0 if edge in (1, 3) else 1
    pairs = []
    for i in range(first, count, 2):
        j = (i + 1) % count
        pairs += [(i, j), (j, i)]
    return lax.ppermute(cells, axis, pairs)


def relayed(cells):
    count = lax.axis_size("gx")
    return lax.ppermute(cells, "gx", [(i, (i + (2 if i % 2 == 0 else count - 2)) % count) for i in range(count)])


def order_of():
    odd_x = lax.rem(lax.axis_index("gx"), 2)
    odd_y = lax.rem(lax.axis_index("gy"), 2)
    return 0, 1 + odd_x, 2 - odd_x, 3 + odd_y, 4 - odd_y


def cols(place, count=1):
    return slice(place * B, (place + count) * B)


def split(values):
    high = values.astype(bf16)
    return high, (values - high.astype(f32)).astype(bf16)


def beside(*pairs):
    return tuple(jnp.concatenate(parts, axis=1) for parts in zip(*pairs))


def dot(left, right):
    def one(a, b):
        return jnp.dot(a, b, preferred_element_type=f32)

    return one(left[0], right[0]) + (one(left[0], right[1]) + one(left[1], right[0]))


def part(pair, rows, columns):
    return pair[0][rows, columns], pair[1][rows, columns]


def rows_of(pair):
    return (pair[0][:B], pair[1][:B]), (pair[0][B:], pair[1][B:])


def store(pair, columns, values):
    pair[0][:, columns], pair[1][:, columns] = values


def start_all(copies):
    for copy in copies:
        copy.start()
    return copies


def first_kernel(cutoff_hbm, ham_hbm, inv_hbm, rho_hbm, one, rest, cutoff_ref, cutoff_sem, sems):
    flags = pltpu.make_async_copy(cutoff_hbm, cutoff_ref, cutoff_sem)
    flags.start()
    order = order_of()
    sources = (ham_hbm.at[0, 0, 0], inv_hbm.at[0, 0, 0], rho_hbm.at[1, 0, 0, 0], ham_hbm.at[0, 0, order[1]], rho_hbm.at[0, 0, 0, 0])
    copies = [pltpu.make_async_copy(source, one.at[at], sems.at[at]) for at, source in enumerate(sources)]
    sources = (ham_hbm.at[0, 0, order[2]], ham_hbm.at[0, 0, order[4]], inv_hbm.at[0, 0, order[4]])
    sources += (rho_hbm.at[0, 0, 0, order[4]], rho_hbm.at[1, 0, 0, order[4]])
    copies += [pltpu.make_async_copy(source, rest.at[at], sems.at[5 + at]) for at, source in enumerate(sources)]
    start_all(copies)
    flags.wait()
    for copy in copies:
        copy.wait()
    one[3] = one[3] * cutoff_ref[0, 0, order[1]].astype(f32)
    rest[0] = rest[0] * cutoff_ref[0, 0, order[2]].astype(f32)
    for at in range(1, 5):
        rest[at] = rest[at] * cutoff_ref[0, 0, order[4]].astype(f32)


def four_first_kernel(message, rest, out):
    out[:3] = message[:3]
    out[3] = rest[1]
    out[4] = message[4]
    out[5:] = rest[2:]


def two_first_kernel(after, message, rest, out):
    out[:3] = message[:3]
    out[3] = rest[0]


def gate_kernel(rest, out):
    out[...] = rest[0, :8]


def whole_first_kernel(after, message, held, ham, out):
    out[:3] = message[:3]
    out[3] = ham[...]
    out[4] = message[4]
    for kind in range(3):
        out[5 + kind] = held[kind, 3]


def second_kernel(
    cutoff_hbm, ham_hbm, inv_hbm, rho_hbm, atom_hbm, after, held, ham_three, left_high, left_low, ham_high, ham_low, members,
    raw, cutoff_ref, atom_ref, cutoff_sem, atom_sem, sems
):
    flags = pltpu.make_async_copy(cutoff_hbm, cutoff_ref, cutoff_sem)
    flags.start()
    sources = (ham_hbm.at[0, 0], inv_hbm.at[0, 0], rho_hbm.at[0, 0, 0], rho_hbm.at[1, 0, 0])
    copies = start_all([pltpu.make_async_copy(source, raw.at[at], sems.at[at]) for at, source in enumerate(sources)])
    owners = pltpu.make_async_copy(atom_hbm, atom_ref, atom_sem)
    owners.start()
    order = order_of()
    flags.wait()
    keeps = [cutoff_ref[0, 0, offset].astype(f32) for offset in order]
    for kind, copy in enumerate(copies):
        copy.wait()
        for place, offset in enumerate(order):
            block = raw[kind, offset]
            if place > 0:
                block = block * keeps[place]
            if kind == 0:
                if place == 3:
                    ham_three[...] = block
                store((ham_high, ham_low), cols(place), split(block))
            else:
                held[kind - 1, place] = block
                rows = slice((kind - 1) * B, kind * B)
                left_high[rows, cols(place)], left_low[rows, cols(place)] = split(block)
    owners.wait()
    atoms = jnp.broadcast_to(atom_ref[0], (ATOMS, B))
    members[...] = -(lax.broadcasted_iota(jnp.int32, (ATOMS, B), 0) == atoms).astype(f32)


def first_half(left, place, start, near, diagonal):
    both = dot(part(left, slice(0, 3 * B), cols(place)), beside(split(near[0]), split(near[3])))
    mixed = split(start[:, cols(place)] + both[:, :B])
    prop, inner = rows_of(mixed)
    behind = dot(inner, split(near[1]))
    imag = dot(prop, split(near[2])) - behind[B:]
    return mixed, diagonal + both[:, B:], -behind[:B], imag


def second_half(mixed, near):
    prop, inner = rows_of(mixed)
    ahead = dot(prop, beside(split(near[0]), split(near[2]), split(near[3])))
    behind = dot(inner, split(near[1]))
    return ahead[:, cols(0)], ahead[:, cols(1)] - behind[:B], ahead[:, cols(2)] - behind[B:]


def send_more(more, held, place):
    for kind in range(3):
        more[kind] = held[kind, place]


def whole_edge(left, place, start, near, diagonal, diagonal_out, other):
    mixed, diagonal_out[...], real, other[1, 0] = first_half(left, place, start, near, diagonal)
    added, other[0, 1], other[1, 1] = second_half(mixed, near[4:])
    other[0, 0] = real + added


def third_kernel(left_high, left_low, ham_high, ham_low, held, three, gate, der_hbm, one_more, two_more, start, diagonal, other, der, sem):
    copy = pltpu.make_async_copy(der_hbm, der, sem)
    copy.start()
    send_more(one_more, held, 1)
    send_more(two_more, held, 2)
    left = (left_high, left_low)
    start[...] = dot(part(left, slice(0, 3 * B), cols(0)), part((ham_high, ham_low), slice(0, B), cols(0, 5)))
    whole_edge(left, 3, start, three, start[:, cols(0)], diagonal, other)
    copy.wait()


def four_kernel(left_high, left_low, start, diagonal, four, diagonal_out, other):
    whole_edge((left_high, left_low), 4, start, four, diagonal[...], diagonal_out, other)


def fourth_kernel(left_high, left_low, start, diagonal, one, mixed_high, mixed_low, diagonal_out, other):
    mixed, diagonal_out[...], real, other[1] = first_half((left_high, left_low), 1, start, one, diagonal[...])
    mixed_high[...], mixed_low[...] = mixed
    other[0] = real + dot(rows_of(mixed)[0], split(one[4]))


def fifth_kernel(
    left_high, left_low, start, diagonal, held, der_ref, other_one, other_three, other_four, two,
    new, mixed_high, mixed_low, self_high, self_low, real_two, comm, weighted, c1, c2, c3, c4
):
    order = order_of()
    left = (left_high, left_low)
    mixed, total, real_two[...], imag_two = first_half(left, 2, start, two, diagonal[...])
    mixed_high[...], mixed_low[...] = mixed
    at_self = split(total)
    self_high[...], self_low[...] = at_self
    whole = cols(0, 5)
    ahead = dot(part(at_self, slice(0, B), cols(0)), part(left, slice(2 * B, 3 * B), whole))
    behind = dot(part(at_self, slice(2 * B, 3 * B), cols(0)), part(left, slice(0, B), whole))
    imag_comm = ahead - behind
    comm[...] = imag_comm[:, cols(0)] + other_three[1, 1] + other_four[1, 1]
    sums = [None] * 3
    for place, column in enumerate((c1, c2, c3, c4), 1):
        imag = (other_one[1], imag_two, other_three[1, 0], other_four[1, 0])[place - 1]
        real_new = held[1, place] + time_step * (imag_comm[:, cols(place)] + imag)
        new[place - 1] = real_new
        for direction in range(3):
            product = real_new * der_ref[direction, 0, 0, order[place]]
            sums[direction] = product if place == 1 else sums[direction] + product
            column[direction : direction + 1, :] = jnp.sum(product, axis=0, keepdims=True)
    for direction in range(3):
        weighted[direction] = sums[direction]


def later_kernel(arrived, column, out):
    out[...] = column[...]


def real_kernel(
    held, new, left_high, left_low, self_high, self_low, other_one, real_two, other_three, other_four, weighted,
    out_hbm, comm, row_part, imag_new, sems
):
    order = order_of()
    copies = start_all(
        [pltpu.make_async_copy(new.at[at], out_hbm.at[0, 0, 0, order[1 + at]], sems.at[0, at]) for at in range(4)]
    )
    left = (left_high, left_low)
    whole = cols(0, 5)
    at_self = (self_high, self_low)
    ahead = dot(part(at_self, slice(0, B), cols(0)), part(left, slice(B, 2 * B), whole))
    behind = dot(part(at_self, slice(B, 2 * B), cols(0)), part(left, slice(0, B), whole))
    real_comm = ahead - behind
    others = ((3, other_three[0, 0]), (4, other_four[0, 0]), (1, other_one[0]))
    for at, (place, other) in enumerate(others):
        imag_new[at] = held[2, place] - time_step * (real_comm[:, cols(place)] + other)
        copies += start_all(
            [pltpu.make_async_copy(imag_new.at[at], out_hbm.at[1, 0, 0, order[place]], sems.at[1, at])]
        )
    comm[0] = real_comm[:, cols(0)] + other_three[0, 1] + other_four[0, 1]
    comm[1] = real_comm[:, cols(2)] + real_two[...]
    for direction in range(3):
        row_part[direction : direction + 1, :] = jnp.sum(weighted[direction].T, axis=0, keepdims=True)
    for copy in copies:
        copy.wait()


def sixth_kernel(
    held, der_ref, members, high_one, low_one, high_two, low_two, imag_part, comm, row_part, one, two, zero, c1, c2, c3, c4, old_hbm,
    out_hbm, forces_hbm, new, forces_ref, sems
):
    order = order_of()
    prop, inner = rows_of(beside((high_one[...], low_one[...]), (high_two[...], low_two[...])))
    near = [tuple(jnp.concatenate(x, axis=0) for x in zip(split(one[kind]), split(two[kind]))) for kind in range(3)]
    behind = dot(inner, near[0])
    real_new = held[1, 0] + time_step * (imag_part[...] + dot(prop, near[2]) - behind[B:])
    new[0] = real_new
    copies = start_all([pltpu.make_async_copy(new.at[0], out_hbm.at[0, 0, 0, 0], sems.at[0])])
    new[1] = held[2, 0] - time_step * (comm[0] + dot(prop, near[1]) - behind[:B])
    added = dot(rows_of((high_two[...], low_two[...]))[0], split(zero[0]))
    new[2] = held[2, 2] - time_step * (comm[1] + added)
    copies += start_all(
        [pltpu.make_async_copy(new.at[1 + at], out_hbm.at[1, 0, 0, order[2 * at]], sems.at[1 + at]) for at in range(2)]
    )
    parts = []
    for direction in range(3):
        product = real_new * der_ref[direction, 0, 0, 0]
        parts.append(jnp.sum(product + product.T, axis=0, keepdims=True))
    orbital = jnp.concatenate(parts, axis=0) + row_part[...] + ((c1[...] + c2[...]) + (c3[...] + c4[...]))
    forces = lax.dot_general(
        orbital, members[...], (((1,), (1,)), ((), ())), precision=lax.Precision.HIGHEST, preferred_element_type=f32
    )
    for direction in range(3):
        forces_ref[direction] = forces[direction : direction + 1]
    copies += start_all([pltpu.make_async_copy(forces_ref, forces_hbm, sems.at[3])])
    for copy in copies:
        copy.wait()


def call(kernel, shapes, in_specs, products, args, out_specs=None, scratch=(), aliases={}):
    moved = sum(4 * x.size for x in args) + sum(4 * x.size for x in shapes)
    return pl.pallas_call(
        kernel,
        out_shape=shapes,
        in_specs=in_specs,
        out_specs=out_specs or [vmem] * len(shapes),
        scratch_shapes=scratch,
        input_output_aliases=aliases,
        compiler_params=pltpu.CompilerParams(vmem_limit_bytes=32 * 2**20),
        cost_estimate=pl.CostEstimate(flops=products * 6 * B**3, bytes_accessed=moved, transcendentals=0),
    )(*args)


def local(hamiltonian, inverse_margin, density, cutoff, derivative, atom_of):
    def shape(*dims, kind=f32):
        return jax.ShapeDtypeStruct(dims, kind)

    args = (hamiltonian, inverse_margin, density, cutoff, derivative, atom_of)
    hamiltonian, inverse_margin, density, cutoff, derivative, atom_of = (
        pltpu.with_memory_space_constraint(x, pltpu.HBM) for x in args
    )
    flags = pltpu.SMEM((1, 1, 5), jnp.int32)
    message = shape(4, B, B)
    first_one, rest = call(
        first_kernel,
        [shape(5, B, B), shape(5, B, B)],
        [hbm] * 4,
        0,
        (cutoff, hamiltonian, inverse_margin, density),
        scratch=[flags, dma(()), dma((10,))],
    )
    near_one = swapped(first_one, 1)
    (send_four,) = call(four_first_kernel, [shape(8, B, B)], [vmem] * 2, 0, (first_one, rest))
    near_four = swapped(send_four, 4)
    (first_two,) = call(two_first_kernel, [message], [vmem] * 3, 500, (send_four, first_one, rest))
    near_two = swapped(first_two, 2)
    left = [shape(3 * B, 5 * B, kind=bf16)] * 2
    ham = [shape(B, 5 * B, kind=bf16)] * 2
    held, ham_three, left_high, left_low, ham_high, ham_low, members = call(
        second_kernel,
        [shape(3, 5, B, B), shape(B, B)] + left + ham + [shape(ATOMS, B)],
        [hbm] * 6,
        0,
        (cutoff, hamiltonian, inverse_margin, density, atom_of, first_two),
        scratch=[pltpu.VMEM((4, 5, B, B), f32), flags, pltpu.VMEM((1, 1, B), jnp.int32), dma(()), dma(()), dma((4,))],
    )
    (send_three,) = call(whole_first_kernel, [shape(8, B, B)], [vmem] * 4, 0, (held, first_one, held, ham_three))
    near_three = swapped(send_three, 3)
    (gate,) = call(gate_kernel, [shape(8, B)], [vmem], 500, (rest,))
    mixed = [shape(3 * B, B, kind=bf16)] * 2
    both = shape(2, 2, B, B)
    both = shape(2, 2, B, B)
    one_more, two_more, start, diagonal, other_three, derivative = call(
        third_kernel,
        [shape(3, B, B)] * 2 + [shape(3 * B, 5 * B), shape(3 * B, B), both, shape(*derivative.shape)],
        [vmem] * 7 + [hbm],
        14,
        (left_high, left_low, ham_high, ham_low, held, near_three, gate, derivative),
        scratch=[dma(())],
    )
    near_one_more = swapped(one_more, 1)
    near_two_more = swapped(two_more, 2)
    diagonal, other_four = call(
        four_kernel,
        [shape(3 * B, B), both],
        [vmem] * 5,
        14,
        (left_high, left_low, start, diagonal, near_four),
    )
    near_two_zero = relayed(near_one[4:])
    high_one, low_one, diagonal, other_one = call(
        fourth_kernel,
        mixed + [shape(3 * B, B), shape(2, B, B)],
        [vmem] * 5,
        10,
        (left_high, left_low, start, diagonal, near_one),
    )
    block = shape(B, B)
    new, high_two, low_two, self_high, self_low, real_two, imag_part, weighted, *columns = call(
        fifth_kernel,
        [message] + mixed * 2 + [block, block, shape(3, B, B)] + [shape(3, B)] * 4,
        [vmem] * 10,
        22,
        (left_high, left_low, start, diagonal, held, derivative, other_one, other_three, other_four, near_two),
    )
    c1, c2, c3, c4 = columns
    c1, c2, c3 = swapped(c1, 1), swapped(c2, 2), swapped(c3, 3)
    (c4,) = call(later_kernel, [shape(3, B)], [vmem] * 2, 0, (c3, c4))
    columns = (c1, c2, c3, swapped(c4, 4))
    args = (held, new, left_high, left_low, self_high, self_low, other_one, real_two, other_three, other_four, weighted)
    out, comm, row_part = call(
        real_kernel,
        [shape(*density.shape), shape(2, B, B), shape(3, B)],
        [vmem] * 11,
        10,
        args,
        out_specs=[hbm] + [vmem] * 2,
        scratch=[pltpu.VMEM((3, B, B), f32), dma((2, 4))],
    )
    args = (held, derivative, members, high_one, low_one, high_two, low_two, imag_part, comm, row_part)
    args += (near_one_more, near_two_more, near_two_zero, *columns, out)
    new_density, forces = call(
        sixth_kernel,
        [shape(*density.shape), shape(3, 1, ATOMS)],
        [vmem] * 17 + [hbm],
        10,
        args,
        out_specs=[hbm, hbm],
        scratch=[pltpu.VMEM((3, B, B), f32), pltpu.VMEM((3, 1, ATOMS), f32), dma((4,))],
        aliases={17: 0},
    )
    return new_density, forces.reshape(1, 1, 3, ATOMS)


def solution(mesh):
    placed = (
        P("gx", "gy", None, None, None),
        P("gx", "gy", None, None, None),
        P(None, "gx", "gy", None, None, None),
        P("gx", "gy", None),
        P(None, "gx", "gy", None, None, None),
        P("gx", "gy", None),
    )
    return jax.shard_map(
        local,
        mesh=mesh,
        in_specs=placed,
        out_specs=(P(None, "gx", "gy", None, None, None), P("gx", "gy", None, None)),
        check_vma=False,
    )
```

```python
import functools

import jax
import jax.numpy as jnp
from jax import lax
from jax.experimental import pallas as pl
from jax.experimental.pallas import tpu as pltpu
from jax.sharding import PartitionSpec as P

B = 128
ATOMS = 64

time_step = 0.25
vmem = pl.BlockSpec(memory_space=pltpu.VMEM)
hbm = pl.BlockSpec(memory_space=pltpu.HBM)
f32 = jnp.float32
bf16 = jnp.bfloat16
dma = pltpu.SemaphoreType.DMA


def swapped(cells, edge):
    axis = "gx" if edge < 3 else "gy"
    count = lax.axis_size(axis)
    assert count % 2 == 0
    first = 0 if edge in (1, 3) else 1
    pairs = []
    for i in range(first, count, 2):
        j = (i + 1) % count
        pairs += [(i, j), (j, i)]
    return lax.ppermute(cells, axis, pairs)


def order_of():
    odd_x = lax.rem(lax.axis_index("gx"), 2)
    odd_y = lax.rem(lax.axis_index("gy"), 2)
    return 0, 1 + odd_x, 2 - odd_x, 3 + odd_y, 4 - odd_y


def cols(place, count=1):
    return slice(place * B, (place + count) * B)


def split(values):
    high = values.astype(bf16)
    return high, (values - high.astype(f32)).astype(bf16)


def beside(*pairs):
    return tuple(jnp.concatenate(parts, axis=1) for parts in zip(*pairs))


def dot(left, right):
    def one(a, b):
        return jnp.dot(a, b, preferred_element_type=f32)

    return one(left[0], right[0]) + (one(left[0], right[1]) + one(left[1], right[0]))


def part(pair, rows, columns):
    return pair[0][rows, columns], pair[1][rows, columns]


def rows_of(pair):
    return (pair[0][:B], pair[1][:B]), (pair[0][B:], pair[1][B:])


def store(pair, columns, values):
    pair[0][:, columns], pair[1][:, columns] = values


def start_all(copies):
    for copy in copies:
        copy.start()
    return copies


def first_kernel(cutoff_hbm, ham_hbm, inv_hbm, rho_hbm, one, rest, cutoff_ref, cutoff_sem, sems):
    flags = pltpu.make_async_copy(cutoff_hbm, cutoff_ref, cutoff_sem)
    flags.start()
    order = order_of()
    sources = (ham_hbm.at[0, 0, 0], inv_hbm.at[0, 0, 0], rho_hbm.at[1, 0, 0, 0], ham_hbm.at[0, 0, order[1]])
    copies = [pltpu.make_async_copy(source, one.at[at], sems.at[at]) for at, source in enumerate(sources)]
    copies += [
        pltpu.make_async_copy(ham_hbm.at[0, 0, order[place]], rest.at[at], sems.at[4 + at]) for at, place in enumerate((4, 2))
    ]
    start_all(copies)
    flags.wait()
    for copy in copies:
        copy.wait()
    one[3] = one[3] * cutoff_ref[0, 0, order[1]].astype(f32)
    for at, place in enumerate((4, 2)):
        rest[at] = rest[at] * cutoff_ref[0, 0, order[place]].astype(f32)


def next_kernel(at, message, rest, out):
    out[:3] = message[:3]
    out[3] = rest[at]


def second_kernel(
    cutoff_hbm, ham_hbm, inv_hbm, rho_hbm, atom_hbm, after, three, held, left_high, left_low, ham_high, ham_low, members,
    raw, cutoff_ref, atom_ref, cutoff_sem, atom_sem, sems
):
    flags = pltpu.make_async_copy(cutoff_hbm, cutoff_ref, cutoff_sem)
    flags.start()
    sources = (ham_hbm.at[0, 0], inv_hbm.at[0, 0], rho_hbm.at[0, 0, 0], rho_hbm.at[1, 0, 0])
    copies = start_all([pltpu.make_async_copy(source, raw.at[at], sems.at[at]) for at, source in enumerate(sources)])
    owners = pltpu.make_async_copy(atom_hbm, atom_ref, atom_sem)
    owners.start()
    order = order_of()
    flags.wait()
    keeps = [cutoff_ref[0, 0, offset].astype(f32) for offset in order]
    for kind, copy in enumerate(copies):
        copy.wait()
        for place, offset in enumerate(order):
            block = raw[kind, offset]
            if place == 0:
                three[(0, 1, 4, 2)[kind]] = block
            else:
                block = block * keeps[place]
                if place == 3:
                    three[(3, 5, 6, 7)[kind]] = block
            if kind == 0:
                store((ham_high, ham_low), cols(place), split(block))
            else:
                held[kind - 1, place] = block
                rows = slice((kind - 1) * B, kind * B)
                left_high[rows, cols(place)], left_low[rows, cols(place)] = split(block)
    owners.wait()
    atoms = jnp.broadcast_to(atom_ref[0], (ATOMS, B))
    members[...] = -(lax.broadcasted_iota(jnp.int32, (ATOMS, B), 0) == atoms).astype(f32)


def first_half(left, place, start, near, diagonal):
    both = dot(part(left, slice(0, 3 * B), cols(place)), beside(split(near[0]), split(near[3])))
    mixed = split(start[:, cols(place)] + both[:, :B])
    prop, inner = rows_of(mixed)
    behind = dot(inner, split(near[1]))
    imag = dot(prop, split(near[2])) - behind[B:]
    return mixed, diagonal + both[:, B:], -behind[:B], imag


def second_half(mixed, near):
    prop, inner = rows_of(mixed)
    ahead = dot(prop, beside(split(near[0]), split(near[2]), split(near[3])))
    behind = dot(inner, split(near[1]))
    return ahead[:, cols(0)], ahead[:, cols(1)] - behind[:B], ahead[:, cols(2)] - behind[B:]


def send_more(more, held, place):
    more[0] = held[1, 0]
    for kind in range(3):
        more[1 + kind] = held[kind, place]


def third_kernel(left_high, left_low, ham_high, ham_low, held, four, one_more, start, mixed_high, mixed_low, diagonal, other):
    send_more(one_more, held, 1)
    left = (left_high, left_low)
    start[...] = dot(part(left, slice(0, 3 * B), cols(0)), part((ham_high, ham_low), slice(0, B), cols(0, 5)))
    mixed, diagonal[...], other[0], other[1] = first_half(left, 4, start, four, start[:, cols(0)])
    mixed_high[...], mixed_low[...] = mixed


def whole_kernel(left_high, left_low, start, diagonal, three, der_hbm, diagonal_out, other, der, sem):
    copy = pltpu.make_async_copy(der_hbm, der, sem)
    copy.start()
    mixed, diagonal_out[...], real, other[1, 0] = first_half((left_high, left_low), 3, start, three, diagonal[...])
    added, other[0, 1], other[1, 1] = second_half(mixed, three[4:])
    other[0, 0] = real + added
    copy.wait()


def more_kernel(after, held, two_more, four_more):
    send_more(two_more, held, 2)
    send_more(four_more, held, 4)


def fourth_kernel(left_high, left_low, start, diagonal, one, mixed_high, mixed_low, diagonal_out, other):
    mixed, diagonal_out[...], other[0], other[1] = first_half((left_high, left_low), 1, start, one, diagonal[...])
    mixed_high[...], mixed_low[...] = mixed


def fifth_kernel(
    left_high, left_low, start, diagonal, held, der_ref, other_one, other_three, other_four, two,
    new, mixed_high, mixed_low, self_high, self_low, real_two, comm, weighted, c1, c2, c3, c4
):
    order = order_of()
    left = (left_high, left_low)
    mixed, total, real_two[...], imag_two = first_half(left, 2, start, two, diagonal[...])
    mixed_high[...], mixed_low[...] = mixed
    at_self = split(total)
    self_high[...], self_low[...] = at_self
    whole = cols(0, 5)
    ahead = dot(part(at_self, slice(0, B), cols(0)), part(left, slice(2 * B, 3 * B), whole))
    behind = dot(part(at_self, slice(2 * B, 3 * B), cols(0)), part(left, slice(0, B), whole))
    imag_comm = ahead - behind
    comm[...] = imag_comm[:, cols(0)] + other_three[1, 1]
    sums = [None] * 3
    for place, column in enumerate((c1, c2, c3, c4), 1):
        imag = (other_one[1], imag_two, other_three[1, 0], other_four[1])[place - 1]
        real_new = held[1, place] + time_step * (imag_comm[:, cols(place)] + imag)
        new[place - 1] = real_new
        for direction in range(3):
            product = real_new * der_ref[direction, 0, 0, order[place]]
            sums[direction] = product if place == 1 else sums[direction] + product
            column[direction : direction + 1, :] = jnp.sum(product, axis=0, keepdims=True)
    for direction in range(3):
        weighted[direction] = sums[direction]


def later_kernel(arrived, column, out):
    out[...] = column[...]


def real_kernel(
    held, new, left_high, left_low, self_high, self_low, other_one, real_two, other_three, other_four, weighted,
    imag_part, high_four, low_four, four, out_hbm, comm, imag_out, row_part, imag_new, sems
):
    order = order_of()
    copies = start_all(
        [pltpu.make_async_copy(new.at[at], out_hbm.at[0, 0, 0, order[1 + at]], sems.at[0, at]) for at in range(4)]
    )
    left = (left_high, left_low)
    whole = cols(0, 5)
    at_self = (self_high, self_low)
    ahead = dot(part(at_self, slice(0, B), cols(0)), part(left, slice(B, 2 * B), whole))
    behind = dot(part(at_self, slice(B, 2 * B), cols(0)), part(left, slice(0, B), whole))
    real_comm = ahead - behind
    added, real_four, imag_four = second_half((high_four[...], low_four[...]), four)
    imag_out[...] = imag_part[...] + imag_four
    for at, (place, other) in enumerate(((3, other_three[0, 0]), (4, other_four[0] + added))):
        imag_new[at] = held[2, place] - time_step * (real_comm[:, cols(place)] + other)
        copies += start_all(
            [pltpu.make_async_copy(imag_new.at[at], out_hbm.at[1, 0, 0, order[place]], sems.at[1, at])]
        )
    comm[0] = real_comm[:, cols(0)] + other_three[0, 1] + real_four
    comm[1] = real_comm[:, cols(1)] + other_one[0]
    comm[2] = real_comm[:, cols(2)] + real_two[...]
    for direction in range(3):
        row_part[direction : direction + 1, :] = jnp.sum(weighted[direction].T, axis=0, keepdims=True)
    for copy in copies:
        copy.wait()


def sixth_kernel(
    held, der_ref, members, high_one, low_one, high_two, low_two, imag_part, comm, row_part, one, two, c1, c2, c3, c4, old_hbm,
    out_hbm, forces_hbm, new, forces_ref, sems
):
    order = order_of()
    prop, inner = rows_of(beside((high_one[...], low_one[...]), (high_two[...], low_two[...])))
    near = [tuple(jnp.concatenate(x, axis=0) for x in zip(split(one[1 + kind]), split(two[1 + kind]))) for kind in range(3)]
    behind = dot(inner, near[0])
    real_new = held[1, 0] + time_step * (imag_part[...] + dot(prop, near[2]) - behind[B:])
    new[0] = real_new
    copies = start_all([pltpu.make_async_copy(new.at[0], out_hbm.at[0, 0, 0, 0], sems.at[0])])
    new[1] = held[2, 0] - time_step * (comm[0] + dot(prop, near[1]) - behind[:B])
    for place, message, mixed in ((1, one, (high_one, low_one)), (2, two, (high_two, low_two))):
        added = dot(rows_of((mixed[0][...], mixed[1][...]))[0], split(message[0]))
        new[1 + place] = held[2, place] - time_step * (comm[place] + added)
    copies += start_all(
        [pltpu.make_async_copy(new.at[1 + at], out_hbm.at[1, 0, 0, order[at]], sems.at[1 + at]) for at in range(3)]
    )
    parts = []
    for direction in range(3):
        product = real_new * der_ref[direction, 0, 0, 0]
        parts.append(jnp.sum(product + product.T, axis=0, keepdims=True))
    orbital = jnp.concatenate(parts, axis=0) + row_part[...] + ((c1[...] + c2[...]) + (c3[...] + c4[...]))
    forces = lax.dot_general(
        orbital, members[...], (((1,), (1,)), ((), ())), precision=lax.Precision.HIGHEST, preferred_element_type=f32
    )
    for direction in range(3):
        forces_ref[direction] = forces[direction : direction + 1]
    copies += start_all([pltpu.make_async_copy(forces_ref, forces_hbm, sems.at[4])])
    for copy in copies:
        copy.wait()


def call(kernel, shapes, in_specs, products, args, out_specs=None, scratch=(), aliases={}):
    moved = sum(4 * x.size for x in args) + sum(4 * x.size for x in shapes)
    return pl.pallas_call(
        kernel,
        out_shape=shapes,
        in_specs=in_specs,
        out_specs=out_specs or [vmem] * len(shapes),
        scratch_shapes=scratch,
        input_output_aliases=aliases,
        compiler_params=pltpu.CompilerParams(vmem_limit_bytes=32 * 2**20),
        cost_estimate=pl.CostEstimate(flops=products * 6 * B**3, bytes_accessed=moved, transcendentals=0),
    )(*args)


def local(hamiltonian, inverse_margin, density, cutoff, derivative, atom_of):
    def shape(*dims, kind=f32):
        return jax.ShapeDtypeStruct(dims, kind)

    args = (hamiltonian, inverse_margin, density, cutoff, derivative, atom_of)
    hamiltonian, inverse_margin, density, cutoff, derivative, atom_of = (
        pltpu.with_memory_space_constraint(x, pltpu.HBM) for x in args
    )
    flags = pltpu.SMEM((1, 1, 5), jnp.int32)
    message = shape(4, B, B)
    first_one, rest = call(
        first_kernel,
        [message, shape(2, B, B)],
        [hbm] * 4,
        0,
        (cutoff, hamiltonian, inverse_margin, density),
        scratch=[flags, dma(()), dma((6,))],
    )
    near_one = swapped(first_one, 1)
    (first_four,) = call(functools.partial(next_kernel, 0), [message], [vmem] * 2, 0, (first_one, rest))
    near_four = swapped(first_four, 4)
    (first_two,) = call(functools.partial(next_kernel, 1), [message], [vmem] * 2, 500, (first_four, rest))
    near_two = swapped(first_two, 2)
    left = [shape(3 * B, 5 * B, kind=bf16)] * 2
    ham = [shape(B, 5 * B, kind=bf16)] * 2
    send_three, held, left_high, left_low, ham_high, ham_low, members = call(
        second_kernel,
        [shape(8, B, B), shape(3, 5, B, B)] + left + ham + [shape(ATOMS, B)],
        [hbm] * 6,
        0,
        (cutoff, hamiltonian, inverse_margin, density, atom_of, first_two),
        scratch=[pltpu.VMEM((4, 5, B, B), f32), flags, pltpu.VMEM((1, 1, B), jnp.int32), dma(()), dma(()), dma((4,))],
    )
    near_three = swapped(send_three, 3)
    mixed = [shape(3 * B, B, kind=bf16)] * 2
    both = shape(2, 2, B, B)
    one_more, start, high_four, low_four, diagonal, other_four = call(
        third_kernel,
        [message, shape(3 * B, 5 * B)] + mixed + [shape(3 * B, B), shape(2, B, B)],
        [vmem] * 6,
        8000,
        (left_high, left_low, ham_high, ham_low, held, near_four),
    )
    near_one_more = swapped(one_more, 1)
    two_more, four_more = call(more_kernel, [message] * 2, [vmem] * 2, 300, (one_more, held))
    near_four_more = swapped(four_more, 4)
    near_two_more = swapped(two_more, 2)
    diagonal, other_three, derivative = call(
        whole_kernel,
        [shape(3 * B, B), shape(2, 2, B, B), shape(*derivative.shape)],
        [vmem] * 5 + [hbm],
        14,
        (left_high, left_low, start, diagonal, near_three, derivative),
        scratch=[dma(())],
    )
    high_one, low_one, diagonal, other_one = call(
        fourth_kernel,
        mixed + [shape(3 * B, B), shape(2, B, B)],
        [vmem] * 5,
        10,
        (left_high, left_low, start, diagonal, near_one),
    )
    block = shape(B, B)
    new, high_two, low_two, self_high, self_low, real_two, imag_part, weighted, *columns = call(
        fifth_kernel,
        [message] + mixed * 2 + [block, block, shape(3, B, B)] + [shape(3, B)] * 4,
        [vmem] * 10,
        22,
        (left_high, left_low, start, diagonal, held, derivative, other_one, other_three, other_four, near_two),
    )
    c1, c2, c3, c4 = columns
    c1, c2, c3 = swapped(c1, 1), swapped(c2, 2), swapped(c3, 3)
    (c4,) = call(later_kernel, [shape(3, B)], [vmem] * 2, 0, (c3, c4))
    columns = (c1, c2, c3, swapped(c4, 4))
    args = (held, new, left_high, left_low, self_high, self_low, other_one, real_two, other_three, other_four, weighted)
    args += (imag_part, high_four, low_four, near_four_more)
    out, comm, imag_part, row_part = call(
        real_kernel,
        [shape(*density.shape), shape(3, B, B), shape(B, B), shape(3, B)],
        [vmem] * 15,
        10,
        args,
        out_specs=[hbm] + [vmem] * 3,
        scratch=[pltpu.VMEM((2, B, B), f32), dma((2, 4))],
    )
    args = (held, derivative, members, high_one, low_one, high_two, low_two, imag_part, comm, row_part)
    args += (near_one_more, near_two_more, *columns, out)
    new_density, forces = call(
        sixth_kernel,
        [shape(*density.shape), shape(3, 1, ATOMS)],
        [vmem] * 16 + [hbm],
        10,
        args,
        out_specs=[hbm, hbm],
        scratch=[pltpu.VMEM((4, B, B), f32), pltpu.VMEM((3, 1, ATOMS), f32), dma((5,))],
        aliases={16: 0},
    )
    return new_density, forces.reshape(1, 1, 3, ATOMS)


def solution(mesh):
    placed = (
        P("gx", "gy", None, None, None),
        P("gx", "gy", None, None, None),
        P(None, "gx", "gy", None, None, None),
        P("gx", "gy", None),
        P(None, "gx", "gy", None, None, None),
        P("gx", "gy", None),
    )
    return jax.shard_map(
        local,
        mesh=mesh,
        in_specs=placed,
        out_specs=(P(None, "gx", "gy", None, None, None), P("gx", "gy", None, None)),
        check_vma=False,
    )
```

```python
import functools

import jax
import jax.numpy as jnp
from jax import lax
from jax.experimental import pallas as pl
from jax.experimental.pallas import tpu as pltpu
from jax.sharding import PartitionSpec as P

B = 128
ATOMS = 64

time_step = 0.25
vmem = pl.BlockSpec(memory_space=pltpu.VMEM)
hbm = pl.BlockSpec(memory_space=pltpu.HBM)
f32 = jnp.float32
bf16 = jnp.bfloat16
dma = pltpu.SemaphoreType.DMA


def swapped(cells, edge):
    axis = "gx" if edge < 3 else "gy"
    count = lax.axis_size(axis)
    assert count % 2 == 0
    first = 0 if edge in (1, 3) else 1
    pairs = []
    for i in range(first, count, 2):
        j = (i + 1) % count
        pairs += [(i, j), (j, i)]
    return lax.ppermute(cells, axis, pairs)


def order_of():
    odd_x = lax.rem(lax.axis_index("gx"), 2)
    odd_y = lax.rem(lax.axis_index("gy"), 2)
    return 0, 1 + odd_x, 2 - odd_x, 3 + odd_y, 4 - odd_y


def cols(place, count=1):
    return slice(place * B, (place + count) * B)


def split(values):
    high = values.astype(bf16)
    return high, (values - high.astype(f32)).astype(bf16)


def beside(*pairs):
    return tuple(jnp.concatenate(parts, axis=1) for parts in zip(*pairs))


def dot(left, right):
    def one(a, b):
        return jnp.dot(a, b, preferred_element_type=f32)

    return one(left[0], right[0]) + (one(left[0], right[1]) + one(left[1], right[0]))


def part(pair, rows, columns):
    return pair[0][rows, columns], pair[1][rows, columns]


def rows_of(pair):
    return (pair[0][:B], pair[1][:B]), (pair[0][B:], pair[1][B:])


def store(pair, columns, values):
    pair[0][:, columns], pair[1][:, columns] = values


def start_all(copies):
    for copy in copies:
        copy.start()
    return copies


def first_kernel(cutoff_hbm, ham_hbm, inv_hbm, rho_hbm, one, rest, cutoff_ref, cutoff_sem, sems):
    flags = pltpu.make_async_copy(cutoff_hbm, cutoff_ref, cutoff_sem)
    flags.start()
    order = order_of()
    sources = (ham_hbm.at[0, 0, 0], inv_hbm.at[0, 0, 0], rho_hbm.at[1, 0, 0, 0], ham_hbm.at[0, 0, order[1]])
    copies = [pltpu.make_async_copy(source, one.at[at], sems.at[at]) for at, source in enumerate(sources)]
    copies += [
        pltpu.make_async_copy(ham_hbm.at[0, 0, order[place]], rest.at[at], sems.at[4 + at]) for at, place in enumerate((4, 2))
    ]
    start_all(copies)
    flags.wait()
    for copy in copies:
        copy.wait()
    one[3] = one[3] * cutoff_ref[0, 0, order[1]].astype(f32)
    for at, place in enumerate((4, 2)):
        rest[at] = rest[at] * cutoff_ref[0, 0, order[place]].astype(f32)


def next_kernel(at, message, rest, out):
    out[:3] = message[:3]
    out[3] = rest[at]


def whole_first_kernel(cutoff_hbm, ham_hbm, inv_hbm, rho_hbm, message, out, cutoff_ref, cutoff_sem, sems):
    flags = pltpu.make_async_copy(cutoff_hbm, cutoff_ref, cutoff_sem)
    flags.start()
    offset = order_of()[3]
    sources = (ham_hbm.at[0, 0, offset], rho_hbm.at[0, 0, 0, 0], inv_hbm.at[0, 0, offset], rho_hbm.at[0, 0, 0, offset])
    sources += (rho_hbm.at[1, 0, 0, offset],)
    copies = start_all([pltpu.make_async_copy(source, out.at[3 + at], sems.at[at]) for at, source in enumerate(sources)])
    out[:3] = message[:3]
    flags.wait()
    keep = cutoff_ref[0, 0, offset].astype(f32)
    for copy in copies:
        copy.wait()
    for at in (3, 5, 6, 7):
        out[at] = out[at] * keep


def second_kernel(
    cutoff_hbm, ham_hbm, inv_hbm, rho_hbm, atom_hbm, after, held, left_high, left_low, ham_high, ham_low, members,
    raw, cutoff_ref, atom_ref, cutoff_sem, atom_sem, sems
):
    flags = pltpu.make_async_copy(cutoff_hbm, cutoff_ref, cutoff_sem)
    flags.start()
    sources = (ham_hbm.at[0, 0], inv_hbm.at[0, 0], rho_hbm.at[0, 0, 0], rho_hbm.at[1, 0, 0])
    copies = start_all([pltpu.make_async_copy(source, raw.at[at], sems.at[at]) for at, source in enumerate(sources)])
    owners = pltpu.make_async_copy(atom_hbm, atom_ref, atom_sem)
    owners.start()
    order = order_of()
    flags.wait()
    keeps = [cutoff_ref[0, 0, offset].astype(f32) for offset in order]
    for kind, copy in enumerate(copies):
        copy.wait()
        for place, offset in enumerate(order):
            block = raw[kind, offset]
            if place > 0:
                block = block * keeps[place]
            if kind == 0:
                store((ham_high, ham_low), cols(place), split(block))
            else:
                held[kind - 1, place] = block
                rows = slice((kind - 1) * B, kind * B)
                left_high[rows, cols(place)], left_low[rows, cols(place)] = split(block)
    owners.wait()
    atoms = jnp.broadcast_to(atom_ref[0], (ATOMS, B))
    members[...] = (-(lax.broadcasted_iota(jnp.int32, (ATOMS, B), 0) == atoms).astype(f32)).astype(bf16)


def first_half(left, place, start, near, diagonal):
    both = dot(part(left, slice(0, 3 * B), cols(place)), beside(split(near[0]), split(near[3])))
    mixed = split(start[:, cols(place)] + both[:, :B])
    prop, inner = rows_of(mixed)
    behind = dot(inner, split(near[1]))
    imag = dot(prop, split(near[2])) - behind[B:]
    return mixed, diagonal + both[:, B:], -behind[:B], imag


def second_half(mixed, near):
    prop, inner = rows_of(mixed)
    ahead = dot(prop, beside(split(near[0]), split(near[2]), split(near[3])))
    behind = dot(inner, split(near[1]))
    return ahead[:, cols(0)], ahead[:, cols(1)] - behind[:B], ahead[:, cols(2)] - behind[B:]


def send_more(more, held, place):
    more[0] = held[1, 0]
    for kind in range(3):
        more[1 + kind] = held[kind, place]


def third_kernel(left_high, left_low, ham_high, ham_low, held, three, der_hbm, start, diagonal, other, der, sem):
    copy = pltpu.make_async_copy(der_hbm, der, sem)
    copy.start()
    left = (left_high, left_low)
    start[...] = dot(part(left, slice(0, 3 * B), cols(0)), part((ham_high, ham_low), slice(0, B), cols(0, 5)))
    mixed, diagonal[...], real, other[1, 0] = first_half(left, 3, start, three, start[:, cols(0)])
    added, other[0, 1], other[1, 1] = second_half(mixed, three[4:])
    other[0, 0] = real + added
    copy.wait()


def four_kernel(
    left_high, left_low, start, held, diagonal, four, one_more, mixed_high, mixed_low, diagonal_out, other
):
    send_more(one_more, held, 1)
    mixed, diagonal_out[...], other[0], other[1] = first_half((left_high, left_low), 4, start, four, diagonal[...])
    mixed_high[...], mixed_low[...] = mixed


def more_kernel(after, held, two_more, four_more):
    send_more(two_more, held, 2)
    send_more(four_more, held, 4)


def fourth_kernel(left_high, left_low, start, diagonal, one, mixed_high, mixed_low, diagonal_out, other):
    mixed, diagonal_out[...], other[0], other[1] = first_half((left_high, left_low), 1, start, one, diagonal[...])
    mixed_high[...], mixed_low[...] = mixed


def fifth_kernel(
    left_high, left_low, start, diagonal, held, der_ref, other_one, other_three, other_four, two,
    new, mixed_high, mixed_low, self_high, self_low, real_two, comm, weighted, c1, c2, c3, c4
):
    order = order_of()
    left = (left_high, left_low)
    mixed, total, real_two[...], imag_two = first_half(left, 2, start, two, diagonal[...])
    mixed_high[...], mixed_low[...] = mixed
    at_self = split(total)
    self_high[...], self_low[...] = at_self
    whole = cols(0, 5)
    ahead = dot(part(at_self, slice(0, B), cols(0)), part(left, slice(2 * B, 3 * B), whole))
    behind = dot(part(at_self, slice(2 * B, 3 * B), cols(0)), part(left, slice(0, B), whole))
    imag_comm = ahead - behind
    comm[...] = imag_comm[:, cols(0)] + other_three[1, 1]
    sums = [None] * 3
    for place, column in enumerate((c1, c2, c3, c4), 1):
        imag = (other_one[1], imag_two, other_three[1, 0], other_four[1])[place - 1]
        real_new = held[1, place] + time_step * (imag_comm[:, cols(place)] + imag)
        new[place - 1] = real_new
        for direction in range(3):
            product = real_new * der_ref[direction, 0, 0, order[place]]
            sums[direction] = product if place == 1 else sums[direction] + product
            column[direction : direction + 1, :] = jnp.sum(product, axis=0, keepdims=True)
    for direction in range(3):
        weighted[direction] = sums[direction]


def later_kernel(arrived, column, out):
    out[...] = column[...]


def real_kernel(
    held, new, left_high, left_low, self_high, self_low, other_one, real_two, other_three, other_four, weighted,
    imag_part, high_four, low_four, four, out_hbm, comm, imag_out, row_part, imag_new, sems
):
    order = order_of()
    copies = start_all(
        [pltpu.make_async_copy(new.at[at], out_hbm.at[0, 0, 0, order[1 + at]], sems.at[0, at]) for at in range(4)]
    )
    left = (left_high, left_low)
    whole = cols(0, 5)
    at_self = (self_high, self_low)
    ahead = dot(part(at_self, slice(0, B), cols(0)), part(left, slice(B, 2 * B), whole))
    behind = dot(part(at_self, slice(B, 2 * B), cols(0)), part(left, slice(0, B), whole))
    real_comm = ahead - behind
    added, real_four, imag_four = second_half((high_four[...], low_four[...]), four)
    imag_out[...] = imag_part[...] + imag_four
    for at, (place, other) in enumerate(((3, other_three[0, 0]), (4, other_four[0] + added))):
        imag_new[at] = held[2, place] - time_step * (real_comm[:, cols(place)] + other)
        copies += start_all(
            [pltpu.make_async_copy(imag_new.at[at], out_hbm.at[1, 0, 0, order[place]], sems.at[1, at])]
        )
    comm[0] = real_comm[:, cols(0)] + other_three[0, 1] + real_four
    comm[1] = real_comm[:, cols(1)] + other_one[0]
    comm[2] = real_comm[:, cols(2)] + real_two[...]
    for direction in range(3):
        row_part[direction : direction + 1, :] = jnp.sum(weighted[direction].T, axis=0, keepdims=True)
    for copy in copies:
        copy.wait()


def sixth_kernel(
    held, der_ref, members, high_one, low_one, high_two, low_two, imag_part, comm, row_part, one, two, c1, c2, c3, c4, old_hbm,
    out_hbm, forces_hbm, new, forces_ref, sems
):
    order = order_of()
    prop, inner = rows_of(beside((high_one[...], low_one[...]), (high_two[...], low_two[...])))
    near = [tuple(jnp.concatenate(x, axis=0) for x in zip(split(one[1 + kind]), split(two[1 + kind]))) for kind in range(3)]
    behind = dot(inner, near[0])
    ahead = dot(prop, beside(near[2], near[1]))
    real_new = held[1, 0] + time_step * (imag_part[...] + ahead[:, :B] - behind[B:])
    new[0] = real_new
    new[1] = held[2, 0] - time_step * (comm[0] + ahead[:, B:] - behind[:B])
    copies = start_all([pltpu.make_async_copy(new.at[at], out_hbm.at[at, 0, 0, 0], sems.at[at]) for at in range(2)])
    parts = []
    for direction in range(3):
        product = real_new * der_ref[direction, 0, 0, 0]
        parts.append(jnp.sum(product + product.T, axis=0, keepdims=True))
    orbital = jnp.concatenate(parts, axis=0) + row_part[...] + ((c1[...] + c2[...]) + (c3[...] + c4[...]))
    forces = jnp.zeros((3, ATOMS), f32)
    for some in split(orbital):
        forces = forces + lax.dot_general(some, members[...], (((1,), (1,)), ((), ())), preferred_element_type=f32)
    for direction in range(3):
        forces_ref[direction] = forces[direction : direction + 1]
    copies += start_all([pltpu.make_async_copy(forces_ref, forces_hbm, sems.at[4])])
    for place, message, mixed in ((1, one, (high_one, low_one)), (2, two, (high_two, low_two))):
        added = dot(rows_of((mixed[0][...], mixed[1][...]))[0], split(message[0]))
        new[1 + place] = held[2, place] - time_step * (comm[place] + added)
        copies += start_all(
            [pltpu.make_async_copy(new.at[1 + place], out_hbm.at[1, 0, 0, order[place]], sems.at[1 + place])]
        )
    for copy in copies:
        copy.wait()


def call(kernel, shapes, in_specs, products, args, out_specs=None, scratch=(), aliases={}):
    moved = sum(4 * x.size for x in args) + sum(4 * x.size for x in shapes)
    return pl.pallas_call(
        kernel,
        out_shape=shapes,
        in_specs=in_specs,
        out_specs=out_specs or [vmem] * len(shapes),
        scratch_shapes=scratch,
        input_output_aliases=aliases,
        compiler_params=pltpu.CompilerParams(vmem_limit_bytes=32 * 2**20),
        cost_estimate=pl.CostEstimate(flops=products * 6 * B**3, bytes_accessed=moved, transcendentals=0),
    )(*args)


def local(hamiltonian, inverse_margin, density, cutoff, derivative, atom_of):
    def shape(*dims, kind=f32):
        return jax.ShapeDtypeStruct(dims, kind)

    args = (hamiltonian, inverse_margin, density, cutoff, derivative, atom_of)
    hamiltonian, inverse_margin, density, cutoff, derivative, atom_of = (
        pltpu.with_memory_space_constraint(x, pltpu.HBM) for x in args
    )
    flags = pltpu.SMEM((1, 1, 5), jnp.int32)
    message = shape(4, B, B)
    first_one, rest = call(
        first_kernel,
        [message, shape(2, B, B)],
        [hbm] * 4,
        0,
        (cutoff, hamiltonian, inverse_margin, density),
        scratch=[flags, dma(()), dma((6,))],
    )
    near_one = swapped(first_one, 1)
    (first_four,) = call(functools.partial(next_kernel, 0), [message], [vmem] * 2, 0, (first_one, rest))
    near_four = swapped(first_four, 4)
    (first_two,) = call(functools.partial(next_kernel, 1), [message], [vmem] * 2, 500, (first_four, rest))
    near_two = swapped(first_two, 2)
    (send_three,) = call(
        whole_first_kernel,
        [shape(8, B, B)],
        [hbm] * 4 + [vmem],
        500,
        (cutoff, hamiltonian, inverse_margin, density, first_two),
        scratch=[flags, dma(()), dma((5,))],
    )
    near_three = swapped(send_three, 3)
    left = [shape(3 * B, 5 * B, kind=bf16)] * 2
    ham = [shape(B, 5 * B, kind=bf16)] * 2
    held, left_high, left_low, ham_high, ham_low, members = call(
        second_kernel,
        [shape(3, 5, B, B)] + left + ham + [shape(ATOMS, B, kind=bf16)],
        [hbm] * 6,
        2000,
        (cutoff, hamiltonian, inverse_margin, density, atom_of, send_three),
        scratch=[pltpu.VMEM((4, 5, B, B), f32), flags, pltpu.VMEM((1, 1, B), jnp.int32), dma(()), dma(()), dma((4,))],
    )
    mixed = [shape(3 * B, B, kind=bf16)] * 2
    both = shape(2, 2, B, B)
    start, diagonal, other_three, derivative = call(
        third_kernel,
        [shape(3 * B, 5 * B), shape(3 * B, B), shape(2, 2, B, B), shape(*derivative.shape)],
        [vmem] * 6 + [hbm],
        8000,
        (left_high, left_low, ham_high, ham_low, held, near_three, derivative),
        scratch=[dma(())],
    )
    one_more, high_four, low_four, diagonal, other_four = call(
        four_kernel,
        [message] + mixed + [shape(3 * B, B), shape(2, B, B)],
        [vmem] * 6,
        8,
        (left_high, left_low, start, held, diagonal, near_four),
    )
    near_one_more = swapped(one_more, 1)
    two_more, four_more = call(more_kernel, [message] * 2, [vmem] * 2, 300, (one_more, held))
    near_four_more = swapped(four_more, 4)
    near_two_more = swapped(two_more, 2)
    high_one, low_one, diagonal, other_one = call(
        fourth_kernel,
        mixed + [shape(3 * B, B), shape(2, B, B)],
        [vmem] * 5,
        10,
        (left_high, left_low, start, diagonal, near_one),
    )
    block = shape(B, B)
    new, high_two, low_two, self_high, self_low, real_two, imag_part, weighted, *columns = call(
        fifth_kernel,
        [message] + mixed * 2 + [block, block, shape(3, B, B)] + [shape(3, B)] * 4,
        [vmem] * 10,
        22,
        (left_high, left_low, start, diagonal, held, derivative, other_one, other_three, other_four, near_two),
    )
    c1, c2, c3, c4 = columns
    c1, c2, c3 = swapped(c1, 1), swapped(c2, 2), swapped(c3, 3)
    (c4,) = call(later_kernel, [shape(3, B)], [vmem] * 2, 0, (c3, c4))
    columns = (c1, c2, c3, swapped(c4, 4))
    args = (held, new, left_high, left_low, self_high, self_low, other_one, real_two, other_three, other_four, weighted)
    args += (imag_part, high_four, low_four, near_four_more)
    out, comm, imag_part, row_part = call(
        real_kernel,
        [shape(*density.shape), shape(3, B, B), shape(B, B), shape(3, B)],
        [vmem] * 15,
        10,
        args,
        out_specs=[hbm] + [vmem] * 3,
        scratch=[pltpu.VMEM((2, B, B), f32), dma((2, 4))],
    )
    args = (held, derivative, members, high_one, low_one, high_two, low_two, imag_part, comm, row_part)
    args += (near_one_more, near_two_more, *columns, out)
    new_density, forces = call(
        sixth_kernel,
        [shape(*density.shape), shape(3, 1, ATOMS)],
        [vmem] * 16 + [hbm],
        10,
        args,
        out_specs=[hbm, hbm],
        scratch=[pltpu.VMEM((4, B, B), f32), pltpu.VMEM((3, 1, ATOMS), f32), dma((5,))],
        aliases={16: 0},
    )
    return new_density, forces.reshape(1, 1, 3, ATOMS)


def solution(mesh):
    placed = (
        P("gx", "gy", None, None, None),
        P("gx", "gy", None, None, None),
        P(None, "gx", "gy", None, None, None),
        P("gx", "gy", None),
        P(None, "gx", "gy", None, None, None),
        P("gx", "gy", None),
    )
    return jax.shard_map(
        local,
        mesh=mesh,
        in_specs=placed,
        out_specs=(P(None, "gx", "gy", None, None, None), P("gx", "gy", None, None)),
        check_vma=False,
    )
```

```python
import functools

import jax
import jax.numpy as jnp
from jax import lax
from jax.experimental import pallas as pl
from jax.experimental.pallas import tpu as pltpu
from jax.sharding import PartitionSpec as P

B = 128
ATOMS = 64

time_step = 0.25
vmem = pl.BlockSpec(memory_space=pltpu.VMEM)
hbm = pl.BlockSpec(memory_space=pltpu.HBM)
f32 = jnp.float32
bf16 = jnp.bfloat16
dma = pltpu.SemaphoreType.DMA


def swapped(cells, edge):
    axis = "gx" if edge < 3 else "gy"
    count = lax.axis_size(axis)
    assert count % 2 == 0
    first = 0 if edge in (1, 3) else 1
    pairs = []
    for i in range(first, count, 2):
        j = (i + 1) % count
        pairs += [(i, j), (j, i)]
    return lax.ppermute(cells, axis, pairs)


def one_way(cells, first):
    count = lax.axis_size("gy")
    assert count % 2 == 0
    return lax.ppermute(cells, "gy", [(i + first, i + 1 - first) for i in range(0, count, 2)])


def order_of():
    odd_x = lax.rem(lax.axis_index("gx"), 2)
    odd_y = lax.rem(lax.axis_index("gy"), 2)
    return 0, 1 + odd_x, 2 - odd_x, 3 + odd_y, 4 - odd_y


def cols(place, count=1):
    return slice(place * B, (place + count) * B)


def split(values):
    high = values.astype(bf16)
    return high, (values - high.astype(f32)).astype(bf16)


def beside(*pairs):
    return tuple(jnp.concatenate(parts, axis=1) for parts in zip(*pairs))


def dot(left, right):
    def one(a, b):
        return jnp.dot(a, b, preferred_element_type=f32)

    return one(left[0], right[0]) + (one(left[0], right[1]) + one(left[1], right[0]))


def part(pair, rows, columns):
    return pair[0][rows, columns], pair[1][rows, columns]


def rows_of(pair):
    return (pair[0][:B], pair[1][:B]), (pair[0][B:], pair[1][B:])


def store(pair, columns, values):
    pair[0][:, columns], pair[1][:, columns] = values


def start_all(copies):
    for copy in copies:
        copy.start()
    return copies


def first_kernel(cutoff_hbm, ham_hbm, inv_hbm, rho_hbm, one, rest, cutoff_ref, cutoff_sem, sems):
    flags = pltpu.make_async_copy(cutoff_hbm, cutoff_ref, cutoff_sem)
    flags.start()
    order = order_of()
    sources = (ham_hbm.at[0, 0, 0], inv_hbm.at[0, 0, 0], rho_hbm.at[1, 0, 0, 0], ham_hbm.at[0, 0, order[1]])
    copies = [pltpu.make_async_copy(source, one.at[at], sems.at[at]) for at, source in enumerate(sources)]
    copies += [
        pltpu.make_async_copy(ham_hbm.at[0, 0, order[place]], rest.at[at], sems.at[4 + at]) for at, place in enumerate((4, 2))
    ]
    start_all(copies)
    flags.wait()
    for copy in copies:
        copy.wait()
    one[3] = one[3] * cutoff_ref[0, 0, order[1]].astype(f32)
    for at, place in enumerate((4, 2)):
        rest[at] = rest[at] * cutoff_ref[0, 0, order[place]].astype(f32)


def next_kernel(at, message, rest, out):
    out[:3] = message[:3]
    out[3] = rest[at]


def whole_first_kernel(cutoff_hbm, ham_hbm, inv_hbm, rho_hbm, message, out, cutoff_ref, cutoff_sem, sems):
    flags = pltpu.make_async_copy(cutoff_hbm, cutoff_ref, cutoff_sem)
    flags.start()
    offset = order_of()[3]
    sources = (ham_hbm.at[0, 0, offset], rho_hbm.at[0, 0, 0, 0], inv_hbm.at[0, 0, offset], rho_hbm.at[0, 0, 0, offset])
    sources += (rho_hbm.at[1, 0, 0, offset],)
    copies = start_all([pltpu.make_async_copy(source, out.at[3 + at], sems.at[at]) for at, source in enumerate(sources)])
    out[:3] = message[:3]
    flags.wait()
    keep = cutoff_ref[0, 0, offset].astype(f32)
    for copy in copies:
        copy.wait()
    for at in (3, 5, 6, 7):
        out[at] = out[at] * keep


def second_kernel(
    cutoff_hbm, ham_hbm, inv_hbm, rho_hbm, atom_hbm, after, held, left_high, left_low, ham_high, ham_low, members,
    raw, cutoff_ref, atom_ref, cutoff_sem, atom_sem, sems
):
    flags = pltpu.make_async_copy(cutoff_hbm, cutoff_ref, cutoff_sem)
    flags.start()
    sources = (ham_hbm.at[0, 0], inv_hbm.at[0, 0], rho_hbm.at[0, 0, 0], rho_hbm.at[1, 0, 0])
    copies = start_all([pltpu.make_async_copy(source, raw.at[at], sems.at[at]) for at, source in enumerate(sources)])
    owners = pltpu.make_async_copy(atom_hbm, atom_ref, atom_sem)
    owners.start()
    order = order_of()
    flags.wait()
    keeps = [cutoff_ref[0, 0, offset].astype(f32) for offset in order]
    for kind, copy in enumerate(copies):
        copy.wait()
        for place, offset in enumerate(order):
            block = raw[kind, offset]
            if place > 0:
                block = block * keeps[place]
            if kind == 0:
                store((ham_high, ham_low), cols(place), split(block))
            else:
                held[kind - 1, place] = block
                rows = slice((kind - 1) * B, kind * B)
                left_high[rows, cols(place)], left_low[rows, cols(place)] = split(block)
    owners.wait()
    atoms = jnp.broadcast_to(atom_ref[0], (ATOMS, B))
    members[...] = -(lax.broadcasted_iota(jnp.int32, (ATOMS, B), 0) == atoms).astype(f32)


def first_half(left, place, start, near, diagonal):
    both = dot(part(left, slice(0, 3 * B), cols(place)), beside(split(near[0]), split(near[3])))
    mixed = split(start[:, cols(place)] + both[:, :B])
    prop, inner = rows_of(mixed)
    behind = dot(inner, split(near[1]))
    imag = dot(prop, split(near[2])) - behind[B:]
    return mixed, diagonal + both[:, B:], -behind[:B], imag


def second_half(mixed, near):
    prop, inner = rows_of(mixed)
    ahead = dot(prop, beside(split(near[0]), split(near[2]), split(near[3])))
    behind = dot(inner, split(near[1]))
    return ahead[:, cols(0)], ahead[:, cols(1)] - behind[:B], ahead[:, cols(2)] - behind[B:]


def send_more(more, held, place):
    more[0] = held[1, 0]
    for kind in range(3):
        more[1 + kind] = held[kind, place]


def third_kernel(left_high, left_low, ham_high, ham_low, held, up, down, der_hbm, start, diagonal, other, der, three, sem):
    three[...] = up[...] + down[...]
    copy = pltpu.make_async_copy(der_hbm, der, sem)
    copy.start()
    left = (left_high, left_low)
    start[...] = dot(part(left, slice(0, 3 * B), cols(0)), part((ham_high, ham_low), slice(0, B), cols(0, 5)))
    mixed, diagonal[...], real, other[1, 0] = first_half(left, 3, start, three, start[:, cols(0)])
    added, other[0, 1], other[1, 1] = second_half(mixed, three[4:])
    other[0, 0] = real + added
    copy.wait()


def four_kernel(
    left_high, left_low, start, held, diagonal, four, one_more, mixed_high, mixed_low, diagonal_out, other
):
    send_more(one_more, held, 1)
    mixed, diagonal_out[...], other[0], other[1] = first_half((left_high, left_low), 4, start, four, diagonal[...])
    mixed_high[...], mixed_low[...] = mixed


def more_kernel(after, held, two_more, four_more):
    send_more(two_more, held, 2)
    send_more(four_more, held, 4)


def fourth_kernel(left_high, left_low, start, diagonal, one, mixed_high, mixed_low, diagonal_out, other):
    mixed, diagonal_out[...], other[0], other[1] = first_half((left_high, left_low), 1, start, one, diagonal[...])
    mixed_high[...], mixed_low[...] = mixed


def fifth_kernel(
    left_high, left_low, start, diagonal, held, der_ref, other_one, other_three, other_four, two,
    new, mixed_high, mixed_low, self_high, self_low, real_two, comm, weighted, c1, c2, c3, c4
):
    order = order_of()
    left = (left_high, left_low)
    mixed, total, real_two[...], imag_two = first_half(left, 2, start, two, diagonal[...])
    mixed_high[...], mixed_low[...] = mixed
    at_self = split(total)
    self_high[...], self_low[...] = at_self
    whole = cols(0, 5)
    ahead = dot(part(at_self, slice(0, B), cols(0)), part(left, slice(2 * B, 3 * B), whole))
    behind = dot(part(at_self, slice(2 * B, 3 * B), cols(0)), part(left, slice(0, B), whole))
    imag_comm = ahead - behind
    comm[...] = imag_comm[:, cols(0)] + other_three[1, 1]
    sums = [None] * 3
    for place, column in enumerate((c1, c2, c3, c4), 1):
        imag = (other_one[1], imag_two, other_three[1, 0], other_four[1])[place - 1]
        real_new = held[1, place] + time_step * (imag_comm[:, cols(place)] + imag)
        new[place - 1] = real_new
        for direction in range(3):
            product = real_new * der_ref[direction, 0, 0, order[place]]
            sums[direction] = product if place == 1 else sums[direction] + product
            column[direction : direction + 1, :] = jnp.sum(product, axis=0, keepdims=True)
    for direction in range(3):
        weighted[direction] = sums[direction]


def later_kernel(arrived, column, out):
    out[...] = column[...]


def real_kernel(
    held, new, left_high, left_low, self_high, self_low, other_one, real_two, other_three, other_four, weighted,
    imag_part, high_four, low_four, four, out_hbm, comm, imag_out, row_part, imag_new, sems
):
    order = order_of()
    copies = start_all(
        [pltpu.make_async_copy(new.at[at], out_hbm.at[0, 0, 0, order[1 + at]], sems.at[0, at]) for at in range(4)]
    )
    left = (left_high, left_low)
    whole = cols(0, 5)
    at_self = (self_high, self_low)
    ahead = dot(part(at_self, slice(0, B), cols(0)), part(left, slice(B, 2 * B), whole))
    behind = dot(part(at_self, slice(B, 2 * B), cols(0)), part(left, slice(0, B), whole))
    real_comm = ahead - behind
    added, real_four, imag_four = second_half((high_four[...], low_four[...]), four)
    imag_out[...] = imag_part[...] + imag_four
    for at, (place, other) in enumerate(((3, other_three[0, 0]), (4, other_four[0] + added))):
        imag_new[at] = held[2, place] - time_step * (real_comm[:, cols(place)] + other)
        copies += start_all(
            [pltpu.make_async_copy(imag_new.at[at], out_hbm.at[1, 0, 0, order[place]], sems.at[1, at])]
        )
    comm[0] = real_comm[:, cols(0)] + other_three[0, 1] + real_four
    comm[1] = real_comm[:, cols(1)] + other_one[0]
    comm[2] = real_comm[:, cols(2)] + real_two[...]
    for direction in range(3):
        row_part[direction : direction + 1, :] = jnp.sum(weighted[direction].T, axis=0, keepdims=True)
    for copy in copies:
        copy.wait()


def sixth_kernel(
    held, der_ref, members, high_one, low_one, high_two, low_two, imag_part, comm, row_part, one, two, c1, c2, c3, c4, old_hbm,
    out_hbm, forces_hbm, new, forces_ref, sems
):
    order = order_of()
    prop, inner = rows_of(beside((high_one[...], low_one[...]), (high_two[...], low_two[...])))
    near = [tuple(jnp.concatenate(x, axis=0) for x in zip(split(one[1 + kind]), split(two[1 + kind]))) for kind in range(3)]
    behind = dot(inner, near[0])
    real_new = held[1, 0] + time_step * (imag_part[...] + dot(prop, near[2]) - behind[B:])
    new[0] = real_new
    copies = start_all([pltpu.make_async_copy(new.at[0], out_hbm.at[0, 0, 0, 0], sems.at[0])])
    new[1] = held[2, 0] - time_step * (comm[0] + dot(prop, near[1]) - behind[:B])
    for place, message, mixed in ((1, one, (high_one, low_one)), (2, two, (high_two, low_two))):
        added = dot(rows_of((mixed[0][...], mixed[1][...]))[0], split(message[0]))
        new[1 + place] = held[2, place] - time_step * (comm[place] + added)
    copies += start_all(
        [pltpu.make_async_copy(new.at[1 + at], out_hbm.at[1, 0, 0, order[at]], sems.at[1 + at]) for at in range(3)]
    )
    parts = []
    for direction in range(3):
        product = real_new * der_ref[direction, 0, 0, 0]
        parts.append(jnp.sum(product + product.T, axis=0, keepdims=True))
    orbital = jnp.concatenate(parts, axis=0) + row_part[...] + ((c1[...] + c2[...]) + (c3[...] + c4[...]))
    forces = lax.dot_general(
        orbital, members[...], (((1,), (1,)), ((), ())), precision=lax.Precision.HIGHEST, preferred_element_type=f32
    )
    for direction in range(3):
        forces_ref[direction] = forces[direction : direction + 1]
    copies += start_all([pltpu.make_async_copy(forces_ref, forces_hbm, sems.at[4])])
    for copy in copies:
        copy.wait()


def call(kernel, shapes, in_specs, products, args, out_specs=None, scratch=(), aliases={}):
    moved = sum(4 * x.size for x in args) + sum(4 * x.size for x in shapes)
    return pl.pallas_call(
        kernel,
        out_shape=shapes,
        in_specs=in_specs,
        out_specs=out_specs or [vmem] * len(shapes),
        scratch_shapes=scratch,
        input_output_aliases=aliases,
        compiler_params=pltpu.CompilerParams(vmem_limit_bytes=32 * 2**20),
        cost_estimate=pl.CostEstimate(flops=products * 6 * B**3, bytes_accessed=moved, transcendentals=0),
    )(*args)


def local(hamiltonian, inverse_margin, density, cutoff, derivative, atom_of):
    def shape(*dims, kind=f32):
        return jax.ShapeDtypeStruct(dims, kind)

    args = (hamiltonian, inverse_margin, density, cutoff, derivative, atom_of)
    hamiltonian, inverse_margin, density, cutoff, derivative, atom_of = (
        pltpu.with_memory_space_constraint(x, pltpu.HBM) for x in args
    )
    flags = pltpu.SMEM((1, 1, 5), jnp.int32)
    message = shape(4, B, B)
    first_one, rest = call(
        first_kernel,
        [message, shape(2, B, B)],
        [hbm] * 4,
        0,
        (cutoff, hamiltonian, inverse_margin, density),
        scratch=[flags, dma(()), dma((6,))],
    )
    near_one = swapped(first_one, 1)
    (first_four,) = call(functools.partial(next_kernel, 0), [message], [vmem] * 2, 0, (first_one, rest))
    near_four = swapped(first_four, 4)
    (first_two,) = call(functools.partial(next_kernel, 1), [message], [vmem] * 2, 500, (first_four, rest))
    near_two = swapped(first_two, 2)
    (send_three,) = call(
        whole_first_kernel,
        [shape(8, B, B)],
        [hbm] * 4 + [vmem],
        500,
        (cutoff, hamiltonian, inverse_margin, density, first_two),
        scratch=[flags, dma(()), dma((5,))],
    )
    near_three = (one_way(send_three, 0), one_way(send_three, 1))
    left = [shape(3 * B, 5 * B, kind=bf16)] * 2
    ham = [shape(B, 5 * B, kind=bf16)] * 2
    held, left_high, left_low, ham_high, ham_low, members = call(
        second_kernel,
        [shape(3, 5, B, B)] + left + ham + [shape(ATOMS, B)],
        [hbm] * 6,
        2000,
        (cutoff, hamiltonian, inverse_margin, density, atom_of, send_three),
        scratch=[pltpu.VMEM((4, 5, B, B), f32), flags, pltpu.VMEM((1, 1, B), jnp.int32), dma(()), dma(()), dma((4,))],
    )
    mixed = [shape(3 * B, B, kind=bf16)] * 2
    both = shape(2, 2, B, B)
    start, diagonal, other_three, derivative = call(
        third_kernel,
        [shape(3 * B, 5 * B), shape(3 * B, B), shape(2, 2, B, B), shape(*derivative.shape)],
        [vmem] * 7 + [hbm],
        8000,
        (left_high, left_low, ham_high, ham_low, held, *near_three, derivative),
        scratch=[pltpu.VMEM((8, B, B), f32), dma(())],
    )
    one_more, high_four, low_four, diagonal, other_four = call(
        four_kernel,
        [message] + mixed + [shape(3 * B, B), shape(2, B, B)],
        [vmem] * 6,
        8,
        (left_high, left_low, start, held, diagonal, near_four),
    )
    near_one_more = swapped(one_more, 1)
    two_more, four_more = call(more_kernel, [message] * 2, [vmem] * 2, 300, (one_more, held))
    near_four_more = swapped(four_more, 4)
    near_two_more = swapped(two_more, 2)
    high_one, low_one, diagonal, other_one = call(
        fourth_kernel,
        mixed + [shape(3 * B, B), shape(2, B, B)],
        [vmem] * 5,
        10,
        (left_high, left_low, start, diagonal, near_one),
    )
    block = shape(B, B)
    new, high_two, low_two, self_high, self_low, real_two, imag_part, weighted, *columns = call(
        fifth_kernel,
        [message] + mixed * 2 + [block, block, shape(3, B, B)] + [shape(3, B)] * 4,
        [vmem] * 10,
        22,
        (left_high, left_low, start, diagonal, held, derivative, other_one, other_three, other_four, near_two),
    )
    c1, c2, c3, c4 = columns
    c1, c2, c3 = swapped(c1, 1), swapped(c2, 2), swapped(c3, 3)
    (c4,) = call(later_kernel, [shape(3, B)], [vmem] * 2, 0, (c3, c4))
    columns = (c1, c2, c3, swapped(c4, 4))
    args = (held, new, left_high, left_low, self_high, self_low, other_one, real_two, other_three, other_four, weighted)
    args += (imag_part, high_four, low_four, near_four_more)
    out, comm, imag_part, row_part = call(
        real_kernel,
        [shape(*density.shape), shape(3, B, B), shape(B, B), shape(3, B)],
        [vmem] * 15,
        10,
        args,
        out_specs=[hbm] + [vmem] * 3,
        scratch=[pltpu.VMEM((2, B, B), f32), dma((2, 4))],
    )
    args = (held, derivative, members, high_one, low_one, high_two, low_two, imag_part, comm, row_part)
    args += (near_one_more, near_two_more, *columns, out)
    new_density, forces = call(
        sixth_kernel,
        [shape(*density.shape), shape(3, 1, ATOMS)],
        [vmem] * 16 + [hbm],
        10,
        args,
        out_specs=[hbm, hbm],
        scratch=[pltpu.VMEM((4, B, B), f32), pltpu.VMEM((3, 1, ATOMS), f32), dma((5,))],
        aliases={16: 0},
    )
    return new_density, forces.reshape(1, 1, 3, ATOMS)


def solution(mesh):
    placed = (
        P("gx", "gy", None, None, None),
        P("gx", "gy", None, None, None),
        P(None, "gx", "gy", None, None, None),
        P("gx", "gy", None),
        P(None, "gx", "gy", None, None, None),
        P("gx", "gy", None),
    )
    return jax.shard_map(
        local,
        mesh=mesh,
        in_specs=placed,
        out_specs=(P(None, "gx", "gy", None, None, None), P("gx", "gy", None, None)),
        check_vma=False,
    )
```

```python
import functools

import jax
import jax.numpy as jnp
from jax import lax
from jax.experimental import pallas as pl
from jax.experimental.pallas import tpu as pltpu
from jax.sharding import PartitionSpec as P

B = 128
ATOMS = 64

time_step = 0.25
vmem = pl.BlockSpec(memory_space=pltpu.VMEM)
hbm = pl.BlockSpec(memory_space=pltpu.HBM)
f32 = jnp.float32
bf16 = jnp.bfloat16
dma = pltpu.SemaphoreType.DMA


def swapped(cells, edge):
    axis = "gx" if edge < 3 else "gy"
    count = lax.axis_size(axis)
    assert count % 2 == 0
    first = 0 if edge in (1, 3) else 1
    pairs = []
    for i in range(first, count, 2):
        j = (i + 1) % count
        pairs += [(i, j), (j, i)]
    return lax.ppermute(cells, axis, pairs)


def order_of():
    odd_x = lax.rem(lax.axis_index("gx"), 2)
    odd_y = lax.rem(lax.axis_index("gy"), 2)
    return 0, 1 + odd_x, 2 - odd_x, 3 + odd_y, 4 - odd_y


def cols(place, count=1):
    return slice(place * B, (place + count) * B)


def split(values):
    high = values.astype(bf16)
    return high, (values - high.astype(f32)).astype(bf16)


def beside(*pairs):
    return tuple(jnp.concatenate(parts, axis=1) for parts in zip(*pairs))


def dot(left, right):
    def one(a, b):
        return jnp.dot(a, b, preferred_element_type=f32)

    return one(left[0], right[0]) + (one(left[0], right[1]) + one(left[1], right[0]))


def part(pair, rows, columns):
    return pair[0][rows, columns], pair[1][rows, columns]


def rows_of(pair):
    return (pair[0][:B], pair[1][:B]), (pair[0][B:], pair[1][B:])


def store(pair, columns, values):
    pair[0][:, columns], pair[1][:, columns] = values


def start_all(copies):
    for copy in copies:
        copy.start()
    return copies


def first_kernel(cutoff_hbm, ham_hbm, inv_hbm, rho_hbm, one, rest, cutoff_ref, cutoff_sem, sems):
    flags = pltpu.make_async_copy(cutoff_hbm, cutoff_ref, cutoff_sem)
    flags.start()
    order = order_of()
    sources = (ham_hbm.at[0, 0, 0], inv_hbm.at[0, 0, 0], rho_hbm.at[1, 0, 0, 0], ham_hbm.at[0, 0, order[1]])
    copies = [pltpu.make_async_copy(source, one.at[at], sems.at[at]) for at, source in enumerate(sources)]
    copies += [
        pltpu.make_async_copy(ham_hbm.at[0, 0, order[place]], rest.at[at], sems.at[4 + at]) for at, place in enumerate((4, 2))
    ]
    start_all(copies)
    flags.wait()
    for copy in copies:
        copy.wait()
    one[3] = one[3] * cutoff_ref[0, 0, order[1]].astype(f32)
    for at, place in enumerate((4, 2)):
        rest[at] = rest[at] * cutoff_ref[0, 0, order[place]].astype(f32)


def next_kernel(at, message, rest, out):
    out[:3] = message[:3]
    out[3] = rest[at]


def whole_first_kernel(cutoff_hbm, ham_hbm, inv_hbm, rho_hbm, message, out, cutoff_ref, cutoff_sem, sems):
    flags = pltpu.make_async_copy(cutoff_hbm, cutoff_ref, cutoff_sem)
    flags.start()
    offset = order_of()[3]
    sources = (ham_hbm.at[0, 0, offset], rho_hbm.at[0, 0, 0, 0], inv_hbm.at[0, 0, offset], rho_hbm.at[0, 0, 0, offset])
    sources += (rho_hbm.at[1, 0, 0, offset],)
    copies = start_all([pltpu.make_async_copy(source, out.at[3 + at], sems.at[at]) for at, source in enumerate(sources)])
    out[:3] = message[:3]
    flags.wait()
    keep = cutoff_ref[0, 0, offset].astype(f32)
    for copy in copies:
        copy.wait()
    for at in (3, 5, 6, 7):
        out[at] = out[at] * keep


def second_kernel(
    cutoff_hbm, ham_hbm, inv_hbm, rho_hbm, atom_hbm, after, held, left_high, left_low, ham_high, ham_low, members,
    raw, cutoff_ref, atom_ref, cutoff_sem, atom_sem, sems
):
    flags = pltpu.make_async_copy(cutoff_hbm, cutoff_ref, cutoff_sem)
    flags.start()
    sources = (ham_hbm.at[0, 0], inv_hbm.at[0, 0], rho_hbm.at[0, 0, 0], rho_hbm.at[1, 0, 0])
    copies = start_all([pltpu.make_async_copy(source, raw.at[at], sems.at[at]) for at, source in enumerate(sources)])
    owners = pltpu.make_async_copy(atom_hbm, atom_ref, atom_sem)
    owners.start()
    order = order_of()
    flags.wait()
    keeps = [cutoff_ref[0, 0, offset].astype(f32) for offset in order]
    for kind, copy in enumerate(copies):
        copy.wait()
        for place, offset in enumerate(order):
            block = raw[kind, offset]
            if place > 0:
                block = block * keeps[place]
            if kind == 0:
                store((ham_high, ham_low), cols(place), split(block))
            else:
                held[kind - 1, place] = block
                rows = slice((kind - 1) * B, kind * B)
                left_high[rows, cols(place)], left_low[rows, cols(place)] = split(block)
    owners.wait()
    atoms = jnp.broadcast_to(atom_ref[0], (ATOMS, B))
    members[...] = -(lax.broadcasted_iota(jnp.int32, (ATOMS, B), 0) == atoms).astype(f32)


def first_half(left, place, start, near, diagonal):
    both = dot(part(left, slice(0, 3 * B), cols(place)), beside(split(near[0]), split(near[3])))
    mixed = split(start[:, cols(place)] + both[:, :B])
    prop, inner = rows_of(mixed)
    behind = dot(inner, split(near[1]))
    imag = dot(prop, split(near[2])) - behind[B:]
    return mixed, diagonal + both[:, B:], -behind[:B], imag


def second_half(mixed, near):
    prop, inner = rows_of(mixed)
    ahead = dot(prop, beside(split(near[0]), split(near[2]), split(near[3])))
    behind = dot(inner, split(near[1]))
    return ahead[:, cols(0)], ahead[:, cols(1)] - behind[:B], ahead[:, cols(2)] - behind[B:]


def send_more(more, held, place):
    more[0] = held[1, 0]
    for kind in range(3):
        more[1 + kind] = held[kind, place]


def third_kernel(left_high, left_low, ham_high, ham_low, held, three, der_hbm, start, diagonal, other, der, sem):
    copy = pltpu.make_async_copy(der_hbm, der, sem)
    copy.start()
    left = (left_high, left_low)
    start[...] = dot(part(left, slice(0, 3 * B), cols(0)), part((ham_high, ham_low), slice(0, B), cols(0, 5)))
    mixed, diagonal[...], real, other[1, 0] = first_half(left, 3, start, three, start[:, cols(0)])
    added, other[0, 1], other[1, 1] = second_half(mixed, three[4:])
    other[0, 0] = real + added
    copy.wait()


def four_kernel(
    left_high, left_low, start, held, diagonal, four, one_more, two_more, mixed_high, mixed_low, diagonal_out, other
):
    send_more(one_more, held, 1)
    send_more(two_more, held, 2)
    mixed, diagonal_out[...], other[0], other[1] = first_half((left_high, left_low), 4, start, four, diagonal[...])
    mixed_high[...], mixed_low[...] = mixed


def fourth_kernel(left_high, left_low, start, held, diagonal, one, four_more, mixed_high, mixed_low, diagonal_out, other):
    send_more(four_more, held, 4)
    mixed, diagonal_out[...], other[0], other[1] = first_half((left_high, left_low), 1, start, one, diagonal[...])
    mixed_high[...], mixed_low[...] = mixed


def fifth_kernel(
    left_high, left_low, start, diagonal, held, der_ref, other_one, other_three, other_four, two,
    new, mixed_high, mixed_low, self_high, self_low, real_two, comm, weighted, c1, c2, c3, c4
):
    order = order_of()
    left = (left_high, left_low)
    mixed, total, real_two[...], imag_two = first_half(left, 2, start, two, diagonal[...])
    mixed_high[...], mixed_low[...] = mixed
    at_self = split(total)
    self_high[...], self_low[...] = at_self
    whole = cols(0, 5)
    ahead = dot(part(at_self, slice(0, B), cols(0)), part(left, slice(2 * B, 3 * B), whole))
    behind = dot(part(at_self, slice(2 * B, 3 * B), cols(0)), part(left, slice(0, B), whole))
    imag_comm = ahead - behind
    comm[...] = imag_comm[:, cols(0)] + other_three[1, 1]
    sums = [None] * 3
    for place, column in enumerate((c1, c2, c3, c4), 1):
        imag = (other_one[1], imag_two, other_three[1, 0], other_four[1])[place - 1]
        real_new = held[1, place] + time_step * (imag_comm[:, cols(place)] + imag)
        new[place - 1] = real_new
        for direction in range(3):
            product = real_new * der_ref[direction, 0, 0, order[place]]
            sums[direction] = product if place == 1 else sums[direction] + product
            column[direction : direction + 1, :] = jnp.sum(product, axis=0, keepdims=True)
    for direction in range(3):
        weighted[direction] = sums[direction]


def later_kernel(arrived, column, out):
    out[...] = column[...]


def real_kernel(
    held, new, left_high, left_low, self_high, self_low, other_one, real_two, other_three, other_four, weighted,
    out_hbm, comm, row_part, imag_new, sems
):
    order = order_of()
    copies = start_all(
        [pltpu.make_async_copy(new.at[at], out_hbm.at[0, 0, 0, order[1 + at]], sems.at[0, at]) for at in range(4)]
    )
    left = (left_high, left_low)
    whole = cols(0, 5)
    at_self = (self_high, self_low)
    ahead = dot(part(at_self, slice(0, B), cols(0)), part(left, slice(B, 2 * B), whole))
    behind = dot(part(at_self, slice(B, 2 * B), cols(0)), part(left, slice(0, B), whole))
    real_comm = ahead - behind
    for at, (place, other) in enumerate(((3, other_three[0, 0]),)):
        imag_new[at] = held[2, place] - time_step * (real_comm[:, cols(place)] + other)
        copies += start_all(
            [pltpu.make_async_copy(imag_new.at[at], out_hbm.at[1, 0, 0, order[place]], sems.at[1, at])]
        )
    comm[0] = real_comm[:, cols(0)] + other_three[0, 1]
    comm[1] = real_comm[:, cols(1)] + other_one[0]
    comm[2] = real_comm[:, cols(2)] + real_two[...]
    comm[3] = real_comm[:, cols(4)] + other_four[0]
    for direction in range(3):
        row_part[direction : direction + 1, :] = jnp.sum(weighted[direction].T, axis=0, keepdims=True)
    for copy in copies:
        copy.wait()


def sixth_kernel(
    held, der_ref, members, high_one, low_one, high_two, low_two, high_four, low_four, imag_part, comm, row_part, one, two, four, c1, c2, c3, c4, old_hbm,
    out_hbm, forces_hbm, new, forces_ref, sems
):
    order = order_of()
    added_four, real_four, imag_four = second_half((high_four[...], low_four[...]), four)
    prop, inner = rows_of(beside((high_one[...], low_one[...]), (high_two[...], low_two[...])))
    near = [tuple(jnp.concatenate(x, axis=0) for x in zip(split(one[1 + kind]), split(two[1 + kind]))) for kind in range(3)]
    behind = dot(inner, near[0])
    real_new = held[1, 0] + time_step * (imag_part[...] + imag_four + dot(prop, near[2]) - behind[B:])
    new[0] = real_new
    copies = start_all([pltpu.make_async_copy(new.at[0], out_hbm.at[0, 0, 0, 0], sems.at[0])])
    new[1] = held[2, 0] - time_step * (comm[0] + real_four + dot(prop, near[1]) - behind[:B])
    for place, message, mixed in ((1, one, (high_one, low_one)), (2, two, (high_two, low_two))):
        added = dot(rows_of((mixed[0][...], mixed[1][...]))[0], split(message[0]))
        new[1 + place] = held[2, place] - time_step * (comm[place] + added)
    new[4] = held[2, 4] - time_step * (comm[3] + added_four)
    places = (0, 1, 2, 4)
    copies += start_all(
        [pltpu.make_async_copy(new.at[1 + at], out_hbm.at[1, 0, 0, order[x]], sems.at[1 + at]) for at, x in enumerate(places)]
    )
    parts = []
    for direction in range(3):
        product = real_new * der_ref[direction, 0, 0, 0]
        parts.append(jnp.sum(product + product.T, axis=0, keepdims=True))
    orbital = jnp.concatenate(parts, axis=0) + row_part[...] + ((c1[...] + c2[...]) + (c3[...] + c4[...]))
    forces = lax.dot_general(
        orbital, members[...], (((1,), (1,)), ((), ())), precision=lax.Precision.HIGHEST, preferred_element_type=f32
    )
    for direction in range(3):
        forces_ref[direction] = forces[direction : direction + 1]
    copies += start_all([pltpu.make_async_copy(forces_ref, forces_hbm, sems.at[5])])
    for copy in copies:
        copy.wait()


def call(kernel, shapes, in_specs, products, args, out_specs=None, scratch=(), aliases={}):
    moved = sum(4 * x.size for x in args) + sum(4 * x.size for x in shapes)
    return pl.pallas_call(
        kernel,
        out_shape=shapes,
        in_specs=in_specs,
        out_specs=out_specs or [vmem] * len(shapes),
        scratch_shapes=scratch,
        input_output_aliases=aliases,
        compiler_params=pltpu.CompilerParams(vmem_limit_bytes=32 * 2**20),
        cost_estimate=pl.CostEstimate(flops=products * 6 * B**3, bytes_accessed=moved, transcendentals=0),
    )(*args)


def local(hamiltonian, inverse_margin, density, cutoff, derivative, atom_of):
    def shape(*dims, kind=f32):
        return jax.ShapeDtypeStruct(dims, kind)

    args = (hamiltonian, inverse_margin, density, cutoff, derivative, atom_of)
    hamiltonian, inverse_margin, density, cutoff, derivative, atom_of = (
        pltpu.with_memory_space_constraint(x, pltpu.HBM) for x in args
    )
    flags = pltpu.SMEM((1, 1, 5), jnp.int32)
    message = shape(4, B, B)
    first_one, rest = call(
        first_kernel,
        [message, shape(2, B, B)],
        [hbm] * 4,
        0,
        (cutoff, hamiltonian, inverse_margin, density),
        scratch=[flags, dma(()), dma((6,))],
    )
    near_one = swapped(first_one, 1)
    (first_four,) = call(functools.partial(next_kernel, 0), [message], [vmem] * 2, 0, (first_one, rest))
    near_four = swapped(first_four, 4)
    (first_two,) = call(functools.partial(next_kernel, 1), [message], [vmem] * 2, 500, (first_four, rest))
    near_two = swapped(first_two, 2)
    (send_three,) = call(
        whole_first_kernel,
        [shape(8, B, B)],
        [hbm] * 4 + [vmem],
        500,
        (cutoff, hamiltonian, inverse_margin, density, first_two),
        scratch=[flags, dma(()), dma((5,))],
    )
    near_three = swapped(send_three, 3)
    left = [shape(3 * B, 5 * B, kind=bf16)] * 2
    ham = [shape(B, 5 * B, kind=bf16)] * 2
    held, left_high, left_low, ham_high, ham_low, members = call(
        second_kernel,
        [shape(3, 5, B, B)] + left + ham + [shape(ATOMS, B)],
        [hbm] * 6,
        2000,
        (cutoff, hamiltonian, inverse_margin, density, atom_of, send_three),
        scratch=[pltpu.VMEM((4, 5, B, B), f32), flags, pltpu.VMEM((1, 1, B), jnp.int32), dma(()), dma(()), dma((4,))],
    )
    mixed = [shape(3 * B, B, kind=bf16)] * 2
    both = shape(2, 2, B, B)
    start, diagonal, other_three, derivative = call(
        third_kernel,
        [shape(3 * B, 5 * B), shape(3 * B, B), shape(2, 2, B, B), shape(*derivative.shape)],
        [vmem] * 6 + [hbm],
        8000,
        (left_high, left_low, ham_high, ham_low, held, near_three, derivative),
        scratch=[dma(())],
    )
    one_more, two_more, high_four, low_four, diagonal, other_four = call(
        four_kernel,
        [message] * 2 + mixed + [shape(3 * B, B), shape(2, B, B)],
        [vmem] * 6,
        8,
        (left_high, left_low, start, held, diagonal, near_four),
    )
    near_one_more = swapped(one_more, 1)
    near_two_more = swapped(two_more, 2)
    four_more, high_one, low_one, diagonal, other_one = call(
        fourth_kernel,
        [message] + mixed + [shape(3 * B, B), shape(2, B, B)],
        [vmem] * 6,
        10,
        (left_high, left_low, start, held, diagonal, near_one),
    )
    near_four_more = swapped(four_more, 4)
    block = shape(B, B)
    new, high_two, low_two, self_high, self_low, real_two, imag_part, weighted, *columns = call(
        fifth_kernel,
        [message] + mixed * 2 + [block, block, shape(3, B, B)] + [shape(3, B)] * 4,
        [vmem] * 10,
        22,
        (left_high, left_low, start, diagonal, held, derivative, other_one, other_three, other_four, near_two),
    )
    c1, c2, c3, c4 = columns
    c3, c4 = swapped(c3, 3), swapped(c4, 4)
    (c1,) = call(later_kernel, [shape(3, B)], [vmem] * 2, 0, (c3, c1))
    (c2,) = call(later_kernel, [shape(3, B)], [vmem] * 2, 0, (c4, c2))
    columns = (swapped(c1, 1), swapped(c2, 2), c3, c4)
    args = (held, new, left_high, left_low, self_high, self_low, other_one, real_two, other_three, other_four, weighted)
    out, comm, row_part = call(
        real_kernel,
        [shape(*density.shape), shape(4, B, B), shape(3, B)],
        [vmem] * 11,
        10,
        args,
        out_specs=[hbm] + [vmem] * 2,
        scratch=[pltpu.VMEM((1, B, B), f32), dma((2, 4))],
    )
    args = (held, derivative, members, high_one, low_one, high_two, low_two, high_four, low_four, imag_part, comm, row_part)
    args += (near_one_more, near_two_more, near_four_more, *columns, out)
    new_density, forces = call(
        sixth_kernel,
        [shape(*density.shape), shape(3, 1, ATOMS)],
        [vmem] * 19 + [hbm],
        10,
        args,
        out_specs=[hbm, hbm],
        scratch=[pltpu.VMEM((5, B, B), f32), pltpu.VMEM((3, 1, ATOMS), f32), dma((6,))],
        aliases={19: 0},
    )
    return new_density, forces.reshape(1, 1, 3, ATOMS)


def solution(mesh):
    placed = (
        P("gx", "gy", None, None, None),
        P("gx", "gy", None, None, None),
        P(None, "gx", "gy", None, None, None),
        P("gx", "gy", None),
        P(None, "gx", "gy", None, None, None),
        P("gx", "gy", None),
    )
    return jax.shard_map(
        local,
        mesh=mesh,
        in_specs=placed,
        out_specs=(P(None, "gx", "gy", None, None, None), P("gx", "gy", None, None)),
        check_vma=False,
    )
```

```python
import functools

import jax
import jax.numpy as jnp
from jax import lax
from jax.experimental import pallas as pl
from jax.experimental.pallas import tpu as pltpu
from jax.sharding import PartitionSpec as P

B = 128
ATOMS = 64

time_step = 0.25
vmem = pl.BlockSpec(memory_space=pltpu.VMEM)
hbm = pl.BlockSpec(memory_space=pltpu.HBM)
f32 = jnp.float32
bf16 = jnp.bfloat16
dma = pltpu.SemaphoreType.DMA


def swapped(cells, edge):
    axis = "gx" if edge < 3 else "gy"
    count = lax.axis_size(axis)
    assert count % 2 == 0
    first = 0 if edge in (1, 3) else 1
    pairs = []
    for i in range(first, count, 2):
        j = (i + 1) % count
        pairs += [(i, j), (j, i)]
    return lax.ppermute(cells, axis, pairs)


def order_of():
    odd_x = lax.rem(lax.axis_index("gx"), 2)
    odd_y = lax.rem(lax.axis_index("gy"), 2)
    return 0, 1 + odd_x, 2 - odd_x, 3 + odd_y, 4 - odd_y


def cols(place, count=1):
    return slice(place * B, (place + count) * B)


def split(values):
    high = values.astype(bf16)
    return high, (values - high.astype(f32)).astype(bf16)


def beside(*pairs):
    return tuple(jnp.concatenate(parts, axis=1) for parts in zip(*pairs))


def dot(left, right):
    def one(a, b):
        return jnp.dot(a, b, preferred_element_type=f32)

    return one(left[0], right[0]) + (one(left[0], right[1]) + one(left[1], right[0]))


def part(pair, rows, columns):
    return pair[0][rows, columns], pair[1][rows, columns]


def rows_of(pair):
    return (pair[0][:B], pair[1][:B]), (pair[0][B:], pair[1][B:])


def store(pair, columns, values):
    pair[0][:, columns], pair[1][:, columns] = values


def start_all(copies):
    for copy in copies:
        copy.start()
    return copies


def first_kernel(cutoff_hbm, ham_hbm, inv_hbm, rho_hbm, one, rest, cutoff_ref, cutoff_sem, sems):
    flags = pltpu.make_async_copy(cutoff_hbm, cutoff_ref, cutoff_sem)
    flags.start()
    order = order_of()
    sources = (ham_hbm.at[0, 0, 0], inv_hbm.at[0, 0, 0], rho_hbm.at[1, 0, 0, 0], ham_hbm.at[0, 0, order[1]])
    copies = [pltpu.make_async_copy(source, one.at[at], sems.at[at]) for at, source in enumerate(sources)]
    copies += [
        pltpu.make_async_copy(ham_hbm.at[0, 0, order[place]], rest.at[at], sems.at[4 + at]) for at, place in enumerate((4, 2))
    ]
    start_all(copies)
    flags.wait()
    for copy in copies:
        copy.wait()
    one[3] = one[3] * cutoff_ref[0, 0, order[1]].astype(f32)
    for at, place in enumerate((4, 2)):
        rest[at] = rest[at] * cutoff_ref[0, 0, order[place]].astype(f32)


def next_kernel(at, message, rest, out):
    out[:3] = message[:3]
    out[3] = rest[at]


def whole_first_kernel(cutoff_hbm, ham_hbm, inv_hbm, rho_hbm, message, out, cutoff_ref, cutoff_sem, sems):
    flags = pltpu.make_async_copy(cutoff_hbm, cutoff_ref, cutoff_sem)
    flags.start()
    offset = order_of()[3]
    sources = (ham_hbm.at[0, 0, offset], rho_hbm.at[0, 0, 0, 0], inv_hbm.at[0, 0, offset], rho_hbm.at[0, 0, 0, offset])
    sources += (rho_hbm.at[1, 0, 0, offset],)
    copies = start_all([pltpu.make_async_copy(source, out.at[3 + at], sems.at[at]) for at, source in enumerate(sources)])
    out[:3] = message[:3]
    flags.wait()
    keep = cutoff_ref[0, 0, offset].astype(f32)
    for copy in copies:
        copy.wait()
    for at in (3, 5, 6, 7):
        out[at] = out[at] * keep


def second_kernel(
    cutoff_hbm, ham_hbm, inv_hbm, rho_hbm, atom_hbm, after, held, left_high, left_low, ham_high, ham_low, members,
    raw, cutoff_ref, atom_ref, cutoff_sem, atom_sem, sems
):
    flags = pltpu.make_async_copy(cutoff_hbm, cutoff_ref, cutoff_sem)
    flags.start()
    sources = (ham_hbm.at[0, 0], inv_hbm.at[0, 0], rho_hbm.at[0, 0, 0], rho_hbm.at[1, 0, 0])
    copies = start_all([pltpu.make_async_copy(source, raw.at[at], sems.at[at]) for at, source in enumerate(sources)])
    owners = pltpu.make_async_copy(atom_hbm, atom_ref, atom_sem)
    owners.start()
    order = order_of()
    flags.wait()
    keeps = [cutoff_ref[0, 0, offset].astype(f32) for offset in order]
    for kind, copy in enumerate(copies):
        copy.wait()
        for place, offset in enumerate(order):
            block = raw[kind, offset]
            if place > 0:
                block = block * keeps[place]
            if kind == 0:
                store((ham_high, ham_low), cols(place), split(block))
            else:
                held[kind - 1, place] = block
                rows = slice((kind - 1) * B, kind * B)
                left_high[rows, cols(place)], left_low[rows, cols(place)] = split(block)
    owners.wait()
    atoms = jnp.broadcast_to(atom_ref[0], (ATOMS, B))
    members[...] = -(lax.broadcasted_iota(jnp.int32, (ATOMS, B), 0) == atoms).astype(f32)


def first_half(left, place, start, near, diagonal):
    both = dot(part(left, slice(0, 3 * B), cols(place)), beside(split(near[0]), split(near[3])))
    mixed = split(start[:, cols(place)] + both[:, :B])
    prop, inner = rows_of(mixed)
    behind = dot(inner, split(near[1]))
    imag = dot(prop, split(near[2])) - behind[B:]
    return mixed, diagonal + both[:, B:], -behind[:B], imag


def second_half(mixed, near):
    prop, inner = rows_of(mixed)
    ahead = dot(prop, beside(split(near[0]), split(near[2]), split(near[3])))
    behind = dot(inner, split(near[1]))
    return ahead[:, cols(0)], ahead[:, cols(1)] - behind[:B], ahead[:, cols(2)] - behind[B:]


def send_more(more, held, place):
    more[0] = held[1, 0]
    for kind in range(3):
        more[1 + kind] = held[kind, place]


def third_kernel(left_high, left_low, ham_high, ham_low, held, three, der_hbm, start, diagonal, other, der, sem):
    copy = pltpu.make_async_copy(der_hbm, der, sem)
    copy.start()
    left = (left_high, left_low)
    start[...] = dot(part(left, slice(0, 3 * B), cols(0)), part((ham_high, ham_low), slice(0, B), cols(0, 5)))
    mixed, diagonal[...], real, other[1, 0] = first_half(left, 3, start, three, start[:, cols(0)])
    added, other[0, 1], other[1, 1] = second_half(mixed, three[4:])
    other[0, 0] = real + added
    copy.wait()


def four_kernel(
    left_high, left_low, start, diagonal, four, mixed_high, mixed_low, diagonal_out, other
):
    mixed, diagonal_out[...], other[0], other[1] = first_half((left_high, left_low), 4, start, four, diagonal[...])
    mixed_high[...], mixed_low[...] = mixed


def more_kernel(arrived, after, held, one_more, two_more, four_more):
    send_more(one_more, held, 1)
    send_more(two_more, held, 2)
    send_more(four_more, held, 4)


def fourth_kernel(left_high, left_low, start, diagonal, one, mixed_high, mixed_low, diagonal_out, other):
    mixed, diagonal_out[...], other[0], other[1] = first_half((left_high, left_low), 1, start, one, diagonal[...])
    mixed_high[...], mixed_low[...] = mixed


def fifth_kernel(
    left_high, left_low, start, diagonal, held, der_ref, other_one, other_three, other_four, two,
    new, mixed_high, mixed_low, self_high, self_low, real_two, comm, weighted, c1, c2, c3, c4
):
    order = order_of()
    left = (left_high, left_low)
    mixed, total, real_two[...], imag_two = first_half(left, 2, start, two, diagonal[...])
    mixed_high[...], mixed_low[...] = mixed
    at_self = split(total)
    self_high[...], self_low[...] = at_self
    whole = cols(0, 5)
    ahead = dot(part(at_self, slice(0, B), cols(0)), part(left, slice(2 * B, 3 * B), whole))
    behind = dot(part(at_self, slice(2 * B, 3 * B), cols(0)), part(left, slice(0, B), whole))
    imag_comm = ahead - behind
    comm[...] = imag_comm[:, cols(0)] + other_three[1, 1]
    sums = [None] * 3
    for place, column in enumerate((c1, c2, c3, c4), 1):
        imag = (other_one[1], imag_two, other_three[1, 0], other_four[1])[place - 1]
        real_new = held[1, place] + time_step * (imag_comm[:, cols(place)] + imag)
        new[place - 1] = real_new
        for direction in range(3):
            product = real_new * der_ref[direction, 0, 0, order[place]]
            sums[direction] = product if place == 1 else sums[direction] + product
            column[direction : direction + 1, :] = jnp.sum(product, axis=0, keepdims=True)
    for direction in range(3):
        weighted[direction] = sums[direction]


def later_kernel(arrived, column, out):
    out[...] = column[...]


def real_kernel(
    held, new, left_high, left_low, self_high, self_low, other_one, real_two, other_three, other_four, weighted,
    imag_part, high_four, low_four, four, out_hbm, comm, imag_out, row_part, imag_new, sems
):
    order = order_of()
    copies = start_all(
        [pltpu.make_async_copy(new.at[at], out_hbm.at[0, 0, 0, order[1 + at]], sems.at[0, at]) for at in range(4)]
    )
    left = (left_high, left_low)
    whole = cols(0, 5)
    at_self = (self_high, self_low)
    ahead = dot(part(at_self, slice(0, B), cols(0)), part(left, slice(B, 2 * B), whole))
    behind = dot(part(at_self, slice(B, 2 * B), cols(0)), part(left, slice(0, B), whole))
    real_comm = ahead - behind
    added, real_four, imag_four = second_half((high_four[...], low_four[...]), four)
    imag_out[...] = imag_part[...] + imag_four
    for at, (place, other) in enumerate(((3, other_three[0, 0]), (4, other_four[0] + added))):
        imag_new[at] = held[2, place] - time_step * (real_comm[:, cols(place)] + other)
        copies += start_all(
            [pltpu.make_async_copy(imag_new.at[at], out_hbm.at[1, 0, 0, order[place]], sems.at[1, at])]
        )
    comm[0] = real_comm[:, cols(0)] + other_three[0, 1] + real_four
    comm[1] = real_comm[:, cols(1)] + other_one[0]
    comm[2] = real_comm[:, cols(2)] + real_two[...]
    for direction in range(3):
        row_part[direction : direction + 1, :] = jnp.sum(weighted[direction].T, axis=0, keepdims=True)
    for copy in copies:
        copy.wait()


def sixth_kernel(
    held, der_ref, members, high_one, low_one, high_two, low_two, imag_part, comm, row_part, one, two, c1, c2, c3, c4, old_hbm,
    out_hbm, forces_hbm, new, forces_ref, sems
):
    order = order_of()
    prop, inner = rows_of(beside((high_one[...], low_one[...]), (high_two[...], low_two[...])))
    near = [tuple(jnp.concatenate(x, axis=0) for x in zip(split(one[1 + kind]), split(two[1 + kind]))) for kind in range(3)]
    behind = dot(inner, near[0])
    real_new = held[1, 0] + time_step * (imag_part[...] + dot(prop, near[2]) - behind[B:])
    new[0] = real_new
    copies = start_all([pltpu.make_async_copy(new.at[0], out_hbm.at[0, 0, 0, 0], sems.at[0])])
    new[1] = held[2, 0] - time_step * (comm[0] + dot(prop, near[1]) - behind[:B])
    for place, message, mixed in ((1, one, (high_one, low_one)), (2, two, (high_two, low_two))):
        added = dot(rows_of((mixed[0][...], mixed[1][...]))[0], split(message[0]))
        new[1 + place] = held[2, place] - time_step * (comm[place] + added)
    copies += start_all(
        [pltpu.make_async_copy(new.at[1 + at], out_hbm.at[1, 0, 0, order[at]], sems.at[1 + at]) for at in range(3)]
    )
    parts = []
    for direction in range(3):
        product = real_new * der_ref[direction, 0, 0, 0]
        parts.append(jnp.sum(product + product.T, axis=0, keepdims=True))
    orbital = jnp.concatenate(parts, axis=0) + row_part[...] + ((c1[...] + c2[...]) + (c3[...] + c4[...]))
    forces = lax.dot_general(
        orbital, members[...], (((1,), (1,)), ((), ())), precision=lax.Precision.HIGHEST, preferred_element_type=f32
    )
    for direction in range(3):
        forces_ref[direction] = forces[direction : direction + 1]
    copies += start_all([pltpu.make_async_copy(forces_ref, forces_hbm, sems.at[4])])
    for copy in copies:
        copy.wait()


def call(kernel, shapes, in_specs, products, args, out_specs=None, scratch=(), aliases={}):
    moved = sum(4 * x.size for x in args) + sum(4 * x.size for x in shapes)
    return pl.pallas_call(
        kernel,
        out_shape=shapes,
        in_specs=in_specs,
        out_specs=out_specs or [vmem] * len(shapes),
        scratch_shapes=scratch,
        input_output_aliases=aliases,
        compiler_params=pltpu.CompilerParams(vmem_limit_bytes=32 * 2**20),
        cost_estimate=pl.CostEstimate(flops=products * 6 * B**3, bytes_accessed=moved, transcendentals=0),
    )(*args)


def local(hamiltonian, inverse_margin, density, cutoff, derivative, atom_of):
    def shape(*dims, kind=f32):
        return jax.ShapeDtypeStruct(dims, kind)

    args = (hamiltonian, inverse_margin, density, cutoff, derivative, atom_of)
    hamiltonian, inverse_margin, density, cutoff, derivative, atom_of = (
        pltpu.with_memory_space_constraint(x, pltpu.HBM) for x in args
    )
    flags = pltpu.SMEM((1, 1, 5), jnp.int32)
    message = shape(4, B, B)
    first_one, rest = call(
        first_kernel,
        [message, shape(2, B, B)],
        [hbm] * 4,
        0,
        (cutoff, hamiltonian, inverse_margin, density),
        scratch=[flags, dma(()), dma((6,))],
    )
    near_one = swapped(first_one, 1)
    (first_four,) = call(functools.partial(next_kernel, 0), [message], [vmem] * 2, 0, (first_one, rest))
    near_four = swapped(first_four, 4)
    (first_two,) = call(functools.partial(next_kernel, 1), [message], [vmem] * 2, 500, (first_four, rest))
    near_two = swapped(first_two, 2)
    (send_three,) = call(
        whole_first_kernel,
        [shape(8, B, B)],
        [hbm] * 4 + [vmem],
        500,
        (cutoff, hamiltonian, inverse_margin, density, first_two),
        scratch=[flags, dma(()), dma((5,))],
    )
    near_three = swapped(send_three, 3)
    left = [shape(3 * B, 5 * B, kind=bf16)] * 2
    ham = [shape(B, 5 * B, kind=bf16)] * 2
    held, left_high, left_low, ham_high, ham_low, members = call(
        second_kernel,
        [shape(3, 5, B, B)] + left + ham + [shape(ATOMS, B)],
        [hbm] * 6,
        2000,
        (cutoff, hamiltonian, inverse_margin, density, atom_of, send_three),
        scratch=[pltpu.VMEM((4, 5, B, B), f32), flags, pltpu.VMEM((1, 1, B), jnp.int32), dma(()), dma(()), dma((4,))],
    )
    mixed = [shape(3 * B, B, kind=bf16)] * 2
    both = shape(2, 2, B, B)
    start, diagonal, other_three, derivative = call(
        third_kernel,
        [shape(3 * B, 5 * B), shape(3 * B, B), shape(2, 2, B, B), shape(*derivative.shape)],
        [vmem] * 6 + [hbm],
        8000,
        (left_high, left_low, ham_high, ham_low, held, near_three, derivative),
        scratch=[dma(())],
    )
    one_more, two_more, four_more = call(more_kernel, [message] * 3, [vmem] * 3, 300, (near_four, other_three, held))
    near_four_more = swapped(four_more, 4)
    near_one_more = swapped(one_more, 1)
    near_two_more = swapped(two_more, 2)
    high_four, low_four, diagonal, other_four = call(
        four_kernel,
        mixed + [shape(3 * B, B), shape(2, B, B)],
        [vmem] * 5,
        8,
        (left_high, left_low, start, diagonal, near_four),
    )
    high_one, low_one, diagonal, other_one = call(
        fourth_kernel,
        mixed + [shape(3 * B, B), shape(2, B, B)],
        [vmem] * 5,
        10,
        (left_high, left_low, start, diagonal, near_one),
    )
    block = shape(B, B)
    new, high_two, low_two, self_high, self_low, real_two, imag_part, weighted, *columns = call(
        fifth_kernel,
        [message] + mixed * 2 + [block, block, shape(3, B, B)] + [shape(3, B)] * 4,
        [vmem] * 10,
        22,
        (left_high, left_low, start, diagonal, held, derivative, other_one, other_three, other_four, near_two),
    )
    c1, c2, c3, c4 = columns
    c1, c2, c3 = swapped(c1, 1), swapped(c2, 2), swapped(c3, 3)
    (c4,) = call(later_kernel, [shape(3, B)], [vmem] * 2, 0, (c3, c4))
    columns = (c1, c2, c3, swapped(c4, 4))
    args = (held, new, left_high, left_low, self_high, self_low, other_one, real_two, other_three, other_four, weighted)
    args += (imag_part, high_four, low_four, near_four_more)
    out, comm, imag_part, row_part = call(
        real_kernel,
        [shape(*density.shape), shape(3, B, B), shape(B, B), shape(3, B)],
        [vmem] * 15,
        10,
        args,
        out_specs=[hbm] + [vmem] * 3,
        scratch=[pltpu.VMEM((2, B, B), f32), dma((2, 4))],
    )
    args = (held, derivative, members, high_one, low_one, high_two, low_two, imag_part, comm, row_part)
    args += (near_one_more, near_two_more, *columns, out)
    new_density, forces = call(
        sixth_kernel,
        [shape(*density.shape), shape(3, 1, ATOMS)],
        [vmem] * 16 + [hbm],
        10,
        args,
        out_specs=[hbm, hbm],
        scratch=[pltpu.VMEM((4, B, B), f32), pltpu.VMEM((3, 1, ATOMS), f32), dma((5,))],
        aliases={16: 0},
    )
    return new_density, forces.reshape(1, 1, 3, ATOMS)


def solution(mesh):
    placed = (
        P("gx", "gy", None, None, None),
        P("gx", "gy", None, None, None),
        P(None, "gx", "gy", None, None, None),
        P("gx", "gy", None),
        P(None, "gx", "gy", None, None, None),
        P("gx", "gy", None),
    )
    return jax.shard_map(
        local,
        mesh=mesh,
        in_specs=placed,
        out_specs=(P(None, "gx", "gy", None, None, None), P("gx", "gy", None, None)),
        check_vma=False,
    )
```

```python
import functools

import jax
import jax.numpy as jnp
from jax import lax
from jax.experimental import pallas as pl
from jax.experimental.pallas import tpu as pltpu
from jax.sharding import PartitionSpec as P

B = 128
ATOMS = 64

time_step = 0.25
vmem = pl.BlockSpec(memory_space=pltpu.VMEM)
hbm = pl.BlockSpec(memory_space=pltpu.HBM)
f32 = jnp.float32
bf16 = jnp.bfloat16
dma = pltpu.SemaphoreType.DMA


def swapped(cells, edge):
    axis = "gx" if edge < 3 else "gy"
    count = lax.axis_size(axis)
    assert count % 2 == 0
    first = 0 if edge in (1, 3) else 1
    pairs = []
    for i in range(first, count, 2):
        j = (i + 1) % count
        pairs += [(i, j), (j, i)]
    return lax.ppermute(cells, axis, pairs)


def order_of():
    odd_x = lax.rem(lax.axis_index("gx"), 2)
    odd_y = lax.rem(lax.axis_index("gy"), 2)
    return 0, 1 + odd_x, 2 - odd_x, 3 + odd_y, 4 - odd_y


def cols(place, count=1):
    return slice(place * B, (place + count) * B)


def split(values):
    high = values.astype(bf16)
    return high, (values - high.astype(f32)).astype(bf16)


def beside(*pairs):
    return tuple(jnp.concatenate(parts, axis=1) for parts in zip(*pairs))


def dot(left, right):
    def one(a, b):
        return jnp.dot(a, b, preferred_element_type=f32)

    return one(left[0], right[0]) + (one(left[0], right[1]) + one(left[1], right[0]))


def part(pair, rows, columns):
    return pair[0][rows, columns], pair[1][rows, columns]


def rows_of(pair):
    return (pair[0][:B], pair[1][:B]), (pair[0][B:], pair[1][B:])


def store(pair, columns, values):
    pair[0][:, columns], pair[1][:, columns] = values


def start_all(copies):
    for copy in copies:
        copy.start()
    return copies


def first_kernel(cutoff_hbm, ham_hbm, inv_hbm, rho_hbm, one, rest, cutoff_ref, cutoff_sem, sems):
    flags = pltpu.make_async_copy(cutoff_hbm, cutoff_ref, cutoff_sem)
    flags.start()
    order = order_of()
    sources = (ham_hbm.at[0, 0, 0], inv_hbm.at[0, 0, 0], rho_hbm.at[1, 0, 0, 0], ham_hbm.at[0, 0, order[1]])
    copies = [pltpu.make_async_copy(source, one.at[at], sems.at[at]) for at, source in enumerate(sources)]
    copies += [
        pltpu.make_async_copy(ham_hbm.at[0, 0, order[place]], rest.at[at], sems.at[4 + at]) for at, place in enumerate((4, 2))
    ]
    start_all(copies)
    flags.wait()
    for copy in copies:
        copy.wait()
    one[3] = one[3] * cutoff_ref[0, 0, order[1]].astype(f32)
    for at, place in enumerate((4, 2)):
        rest[at] = rest[at] * cutoff_ref[0, 0, order[place]].astype(f32)


def next_kernel(at, message, rest, out):
    out[:3] = message[:3]
    out[3] = rest[at]


def whole_first_kernel(cutoff_hbm, ham_hbm, inv_hbm, rho_hbm, message, out, cutoff_ref, cutoff_sem, sems):
    flags = pltpu.make_async_copy(cutoff_hbm, cutoff_ref, cutoff_sem)
    flags.start()
    offset = order_of()[3]
    sources = (ham_hbm.at[0, 0, offset], rho_hbm.at[0, 0, 0, 0], inv_hbm.at[0, 0, offset], rho_hbm.at[0, 0, 0, offset])
    sources += (rho_hbm.at[1, 0, 0, offset],)
    copies = start_all([pltpu.make_async_copy(source, out.at[3 + at], sems.at[at]) for at, source in enumerate(sources)])
    out[:3] = message[:3]
    flags.wait()
    keep = cutoff_ref[0, 0, offset].astype(f32)
    for copy in copies:
        copy.wait()
    for at in (3, 5, 6, 7):
        out[at] = out[at] * keep


def second_kernel(
    cutoff_hbm, ham_hbm, inv_hbm, rho_hbm, atom_hbm, after, held, left_high, left_low, ham_high, ham_low, members,
    raw, cutoff_ref, atom_ref, cutoff_sem, atom_sem, sems
):
    flags = pltpu.make_async_copy(cutoff_hbm, cutoff_ref, cutoff_sem)
    flags.start()
    sources = (ham_hbm.at[0, 0], inv_hbm.at[0, 0], rho_hbm.at[0, 0, 0], rho_hbm.at[1, 0, 0])
    copies = start_all([pltpu.make_async_copy(source, raw.at[at], sems.at[at]) for at, source in enumerate(sources)])
    owners = pltpu.make_async_copy(atom_hbm, atom_ref, atom_sem)
    owners.start()
    order = order_of()
    flags.wait()
    keeps = [cutoff_ref[0, 0, offset].astype(f32) for offset in order]
    for kind, copy in enumerate(copies):
        copy.wait()
        for place, offset in enumerate(order):
            block = raw[kind, offset]
            if place > 0:
                block = block * keeps[place]
            if kind == 0:
                store((ham_high, ham_low), cols(place), split(block))
            else:
                held[kind - 1, place] = block
                rows = slice((kind - 1) * B, kind * B)
                left_high[rows, cols(place)], left_low[rows, cols(place)] = split(block)
    owners.wait()
    atoms = jnp.broadcast_to(atom_ref[0], (ATOMS, B))
    members[...] = -(lax.broadcasted_iota(jnp.int32, (ATOMS, B), 0) == atoms).astype(f32)


def first_half(left, place, start, near, diagonal):
    both = dot(part(left, slice(0, 3 * B), cols(place)), beside(split(near[0]), split(near[3])))
    mixed = split(start[:, cols(place)] + both[:, :B])
    prop, inner = rows_of(mixed)
    behind = dot(inner, split(near[1]))
    imag = dot(prop, split(near[2])) - behind[B:]
    return mixed, diagonal + both[:, B:], -behind[:B], imag


def second_half(mixed, near):
    prop, inner = rows_of(mixed)
    ahead = dot(prop, beside(split(near[0]), split(near[2]), split(near[3])))
    behind = dot(inner, split(near[1]))
    return ahead[:, cols(0)], ahead[:, cols(1)] - behind[:B], ahead[:, cols(2)] - behind[B:]


def send_more(more, held, place):
    more[0] = held[1, 0]
    for kind in range(3):
        more[1 + kind] = held[kind, place]


def third_kernel(left_high, left_low, ham_high, ham_low, held, three, der_hbm, start, diagonal, other, der, sem):
    copy = pltpu.make_async_copy(der_hbm, der, sem)
    copy.start()
    left = (left_high, left_low)
    start[...] = dot(part(left, slice(0, 3 * B), cols(0)), part((ham_high, ham_low), slice(0, B), cols(0, 5)))
    mixed, diagonal[...], real, other[1, 0] = first_half(left, 3, start, three, start[:, cols(0)])
    added, other[0, 1], other[1, 1] = second_half(mixed, three[4:])
    other[0, 0] = real + added
    copy.wait()


def four_kernel(
    left_high, left_low, start, diagonal, four, mixed_high, mixed_low, diagonal_out, other
):
    mixed, diagonal_out[...], other[0], other[1] = first_half((left_high, left_low), 4, start, four, diagonal[...])
    mixed_high[...], mixed_low[...] = mixed


def four_more_kernel(after, held, four_more):
    send_more(four_more, held, 4)


def more_kernel(arrived, after, held, one_more, two_more):
    send_more(one_more, held, 1)
    send_more(two_more, held, 2)


def fourth_kernel(left_high, left_low, start, diagonal, one, mixed_high, mixed_low, diagonal_out, other):
    mixed, diagonal_out[...], other[0], other[1] = first_half((left_high, left_low), 1, start, one, diagonal[...])
    mixed_high[...], mixed_low[...] = mixed


def fifth_kernel(
    left_high, left_low, start, diagonal, held, der_ref, other_one, other_three, other_four, two,
    new, mixed_high, mixed_low, self_high, self_low, real_two, comm, weighted, c1, c2, c3, c4
):
    order = order_of()
    left = (left_high, left_low)
    mixed, total, real_two[...], imag_two = first_half(left, 2, start, two, diagonal[...])
    mixed_high[...], mixed_low[...] = mixed
    at_self = split(total)
    self_high[...], self_low[...] = at_self
    whole = cols(0, 5)
    ahead = dot(part(at_self, slice(0, B), cols(0)), part(left, slice(2 * B, 3 * B), whole))
    behind = dot(part(at_self, slice(2 * B, 3 * B), cols(0)), part(left, slice(0, B), whole))
    imag_comm = ahead - behind
    comm[...] = imag_comm[:, cols(0)] + other_three[1, 1]
    sums = [None] * 3
    for place, column in enumerate((c1, c2, c3, c4), 1):
        imag = (other_one[1], imag_two, other_three[1, 0], other_four[1])[place - 1]
        real_new = held[1, place] + time_step * (imag_comm[:, cols(place)] + imag)
        new[place - 1] = real_new
        for direction in range(3):
            product = real_new * der_ref[direction, 0, 0, order[place]]
            sums[direction] = product if place == 1 else sums[direction] + product
            column[direction : direction + 1, :] = jnp.sum(product, axis=0, keepdims=True)
    for direction in range(3):
        weighted[direction] = sums[direction]


def later_kernel(arrived, column, out):
    out[...] = column[...]


def real_kernel(
    held, new, left_high, left_low, self_high, self_low, other_one, real_two, other_three, other_four, weighted,
    imag_part, high_four, low_four, four, out_hbm, comm, imag_out, row_part, imag_new, sems
):
    order = order_of()
    copies = start_all(
        [pltpu.make_async_copy(new.at[at], out_hbm.at[0, 0, 0, order[1 + at]], sems.at[0, at]) for at in range(4)]
    )
    left = (left_high, left_low)
    whole = cols(0, 5)
    at_self = (self_high, self_low)
    ahead = dot(part(at_self, slice(0, B), cols(0)), part(left, slice(B, 2 * B), whole))
    behind = dot(part(at_self, slice(B, 2 * B), cols(0)), part(left, slice(0, B), whole))
    real_comm = ahead - behind
    added, real_four, imag_four = second_half((high_four[...], low_four[...]), four)
    imag_out[...] = imag_part[...] + imag_four
    for at, (place, other) in enumerate(((3, other_three[0, 0]), (4, other_four[0] + added))):
        imag_new[at] = held[2, place] - time_step * (real_comm[:, cols(place)] + other)
        copies += start_all(
            [pltpu.make_async_copy(imag_new.at[at], out_hbm.at[1, 0, 0, order[place]], sems.at[1, at])]
        )
    comm[0] = real_comm[:, cols(0)] + other_three[0, 1] + real_four
    comm[1] = real_comm[:, cols(1)] + other_one[0]
    comm[2] = real_comm[:, cols(2)] + real_two[...]
    for direction in range(3):
        row_part[direction : direction + 1, :] = jnp.sum(weighted[direction].T, axis=0, keepdims=True)
    for copy in copies:
        copy.wait()


def sixth_kernel(
    held, der_ref, members, high_one, low_one, high_two, low_two, imag_part, comm, row_part, one, two, c1, c2, c3, c4, old_hbm,
    out_hbm, forces_hbm, new, forces_ref, sems
):
    order = order_of()
    prop, inner = rows_of(beside((high_one[...], low_one[...]), (high_two[...], low_two[...])))
    near = [tuple(jnp.concatenate(x, axis=0) for x in zip(split(one[1 + kind]), split(two[1 + kind]))) for kind in range(3)]
    behind = dot(inner, near[0])
    real_new = held[1, 0] + time_step * (imag_part[...] + dot(prop, near[2]) - behind[B:])
    new[0] = real_new
    copies = start_all([pltpu.make_async_copy(new.at[0], out_hbm.at[0, 0, 0, 0], sems.at[0])])
    new[1] = held[2, 0] - time_step * (comm[0] + dot(prop, near[1]) - behind[:B])
    for place, message, mixed in ((1, one, (high_one, low_one)), (2, two, (high_two, low_two))):
        added = dot(rows_of((mixed[0][...], mixed[1][...]))[0], split(message[0]))
        new[1 + place] = held[2, place] - time_step * (comm[place] + added)
    copies += start_all(
        [pltpu.make_async_copy(new.at[1 + at], out_hbm.at[1, 0, 0, order[at]], sems.at[1 + at]) for at in range(3)]
    )
    parts = []
    for direction in range(3):
        product = real_new * der_ref[direction, 0, 0, 0]
        parts.append(jnp.sum(product + product.T, axis=0, keepdims=True))
    orbital = jnp.concatenate(parts, axis=0) + row_part[...] + ((c1[...] + c2[...]) + (c3[...] + c4[...]))
    forces = lax.dot_general(
        orbital, members[...], (((1,), (1,)), ((), ())), precision=lax.Precision.HIGHEST, preferred_element_type=f32
    )
    for direction in range(3):
        forces_ref[direction] = forces[direction : direction + 1]
    copies += start_all([pltpu.make_async_copy(forces_ref, forces_hbm, sems.at[4])])
    for copy in copies:
        copy.wait()


def call(kernel, shapes, in_specs, products, args, out_specs=None, scratch=(), aliases={}):
    moved = sum(4 * x.size for x in args) + sum(4 * x.size for x in shapes)
    return pl.pallas_call(
        kernel,
        out_shape=shapes,
        in_specs=in_specs,
        out_specs=out_specs or [vmem] * len(shapes),
        scratch_shapes=scratch,
        input_output_aliases=aliases,
        compiler_params=pltpu.CompilerParams(vmem_limit_bytes=32 * 2**20),
        cost_estimate=pl.CostEstimate(flops=products * 6 * B**3, bytes_accessed=moved, transcendentals=0),
    )(*args)


def local(hamiltonian, inverse_margin, density, cutoff, derivative, atom_of):
    def shape(*dims, kind=f32):
        return jax.ShapeDtypeStruct(dims, kind)

    args = (hamiltonian, inverse_margin, density, cutoff, derivative, atom_of)
    hamiltonian, inverse_margin, density, cutoff, derivative, atom_of = (
        pltpu.with_memory_space_constraint(x, pltpu.HBM) for x in args
    )
    flags = pltpu.SMEM((1, 1, 5), jnp.int32)
    message = shape(4, B, B)
    first_one, rest = call(
        first_kernel,
        [message, shape(2, B, B)],
        [hbm] * 4,
        0,
        (cutoff, hamiltonian, inverse_margin, density),
        scratch=[flags, dma(()), dma((6,))],
    )
    near_one = swapped(first_one, 1)
    (first_four,) = call(functools.partial(next_kernel, 0), [message], [vmem] * 2, 0, (first_one, rest))
    near_four = swapped(first_four, 4)
    (first_two,) = call(functools.partial(next_kernel, 1), [message], [vmem] * 2, 500, (first_four, rest))
    near_two = swapped(first_two, 2)
    (send_three,) = call(
        whole_first_kernel,
        [shape(8, B, B)],
        [hbm] * 4 + [vmem],
        500,
        (cutoff, hamiltonian, inverse_margin, density, first_two),
        scratch=[flags, dma(()), dma((5,))],
    )
    near_three = swapped(send_three, 3)
    left = [shape(3 * B, 5 * B, kind=bf16)] * 2
    ham = [shape(B, 5 * B, kind=bf16)] * 2
    held, left_high, left_low, ham_high, ham_low, members = call(
        second_kernel,
        [shape(3, 5, B, B)] + left + ham + [shape(ATOMS, B)],
        [hbm] * 6,
        2000,
        (cutoff, hamiltonian, inverse_margin, density, atom_of, send_three),
        scratch=[pltpu.VMEM((4, 5, B, B), f32), flags, pltpu.VMEM((1, 1, B), jnp.int32), dma(()), dma(()), dma((4,))],
    )
    mixed = [shape(3 * B, B, kind=bf16)] * 2
    both = shape(2, 2, B, B)
    start, diagonal, other_three, derivative = call(
        third_kernel,
        [shape(3 * B, 5 * B), shape(3 * B, B), shape(2, 2, B, B), shape(*derivative.shape)],
        [vmem] * 6 + [hbm],
        8000,
        (left_high, left_low, ham_high, ham_low, held, near_three, derivative),
        scratch=[dma(())],
    )
    (four_more,) = call(four_more_kernel, [message], [vmem] * 2, 7, (other_three, held))
    one_more, two_more = call(more_kernel, [message] * 2, [vmem] * 3, 300, (near_four, four_more, held))
    near_four_more = swapped(four_more, 4)
    near_one_more = swapped(one_more, 1)
    near_two_more = swapped(two_more, 2)
    high_four, low_four, diagonal, other_four = call(
        four_kernel,
        mixed + [shape(3 * B, B), shape(2, B, B)],
        [vmem] * 5,
        8,
        (left_high, left_low, start, diagonal, near_four),
    )
    high_one, low_one, diagonal, other_one = call(
        fourth_kernel,
        mixed + [shape(3 * B, B), shape(2, B, B)],
        [vmem] * 5,
        10,
        (left_high, left_low, start, diagonal, near_one),
    )
    block = shape(B, B)
    new, high_two, low_two, self_high, self_low, real_two, imag_part, weighted, *columns = call(
        fifth_kernel,
        [message] + mixed * 2 + [block, block, shape(3, B, B)] + [shape(3, B)] * 4,
        [vmem] * 10,
        22,
        (left_high, left_low, start, diagonal, held, derivative, other_one, other_three, other_four, near_two),
    )
    c1, c2, c3, c4 = columns
    c1, c2, c3 = swapped(c1, 1), swapped(c2, 2), swapped(c3, 3)
    (c4,) = call(later_kernel, [shape(3, B)], [vmem] * 2, 0, (c3, c4))
    columns = (c1, c2, c3, swapped(c4, 4))
    args = (held, new, left_high, left_low, self_high, self_low, other_one, real_two, other_three, other_four, weighted)
    args += (imag_part, high_four, low_four, near_four_more)
    out, comm, imag_part, row_part = call(
        real_kernel,
        [shape(*density.shape), shape(3, B, B), shape(B, B), shape(3, B)],
        [vmem] * 15,
        10,
        args,
        out_specs=[hbm] + [vmem] * 3,
        scratch=[pltpu.VMEM((2, B, B), f32), dma((2, 4))],
    )
    args = (held, derivative, members, high_one, low_one, high_two, low_two, imag_part, comm, row_part)
    args += (near_one_more, near_two_more, *columns, out)
    new_density, forces = call(
        sixth_kernel,
        [shape(*density.shape), shape(3, 1, ATOMS)],
        [vmem] * 16 + [hbm],
        10,
        args,
        out_specs=[hbm, hbm],
        scratch=[pltpu.VMEM((4, B, B), f32), pltpu.VMEM((3, 1, ATOMS), f32), dma((5,))],
        aliases={16: 0},
    )
    return new_density, forces.reshape(1, 1, 3, ATOMS)


def solution(mesh):
    placed = (
        P("gx", "gy", None, None, None),
        P("gx", "gy", None, None, None),
        P(None, "gx", "gy", None, None, None),
        P("gx", "gy", None),
        P(None, "gx", "gy", None, None, None),
        P("gx", "gy", None),
    )
    return jax.shard_map(
        local,
        mesh=mesh,
        in_specs=placed,
        out_specs=(P(None, "gx", "gy", None, None, None), P("gx", "gy", None, None)),
        check_vma=False,
    )
```

```python
import functools

import jax
import jax.numpy as jnp
from jax import lax
from jax.experimental import pallas as pl
from jax.experimental.pallas import tpu as pltpu
from jax.sharding import PartitionSpec as P

B = 128
ATOMS = 64

time_step = 0.25
vmem = pl.BlockSpec(memory_space=pltpu.VMEM)
hbm = pl.BlockSpec(memory_space=pltpu.HBM)
f32 = jnp.float32
bf16 = jnp.bfloat16
dma = pltpu.SemaphoreType.DMA


def swapped(cells, edge):
    axis = "gx" if edge < 3 else "gy"
    count = lax.axis_size(axis)
    assert count % 2 == 0
    first = 0 if edge in (1, 3) else 1
    pairs = []
    for i in range(first, count, 2):
        j = (i + 1) % count
        pairs += [(i, j), (j, i)]
    return lax.ppermute(cells, axis, pairs)


def order_of():
    odd_x = lax.rem(lax.axis_index("gx"), 2)
    odd_y = lax.rem(lax.axis_index("gy"), 2)
    return 0, 1 + odd_x, 2 - odd_x, 3 + odd_y, 4 - odd_y


def cols(place, count=1):
    return slice(place * B, (place + count) * B)


def split(values):
    high = values.astype(bf16)
    return high, (values - high.astype(f32)).astype(bf16)


def beside(*pairs):
    return tuple(jnp.concatenate(parts, axis=1) for parts in zip(*pairs))


def dot(left, right):
    def one(a, b):
        return jnp.dot(a, b, preferred_element_type=f32)

    return one(left[0], right[0]) + (one(left[0], right[1]) + one(left[1], right[0]))


def part(pair, rows, columns):
    return pair[0][rows, columns], pair[1][rows, columns]


def rows_of(pair):
    return (pair[0][:B], pair[1][:B]), (pair[0][B:], pair[1][B:])


def store(pair, columns, values):
    pair[0][:, columns], pair[1][:, columns] = values


def start_all(copies):
    for copy in copies:
        copy.start()
    return copies


def first_kernel(cutoff_hbm, ham_hbm, inv_hbm, rho_hbm, one, rest, ham, cutoff_ref, cutoff_sem, sems):
    flags = pltpu.make_async_copy(cutoff_hbm, cutoff_ref, cutoff_sem)
    flags.start()
    copies = start_all(
        [
            pltpu.make_async_copy(ham_hbm.at[0, 0], ham, sems.at[0]),
            pltpu.make_async_copy(inv_hbm.at[0, 0, 0], one.at[1], sems.at[1]),
            pltpu.make_async_copy(rho_hbm.at[1, 0, 0, 0], one.at[2], sems.at[2]),
        ]
    )
    order = order_of()
    flags.wait()
    for copy in copies:
        copy.wait()
    one[0] = ham[0]
    for target, at, place in ((one, 3, 1), (rest, 0, 4), (rest, 1, 2)):
        target[at] = ham[order[place]] * cutoff_ref[0, 0, order[place]].astype(f32)


def next_kernel(at, message, rest, out):
    out[:3] = message[:3]
    out[3] = rest[at]


def whole_first_kernel(cutoff_hbm, ham_hbm, inv_hbm, rho_hbm, message, out, cutoff_ref, cutoff_sem, sems):
    flags = pltpu.make_async_copy(cutoff_hbm, cutoff_ref, cutoff_sem)
    flags.start()
    offset = order_of()[3]
    sources = (ham_hbm.at[0, 0, offset], rho_hbm.at[0, 0, 0, 0], inv_hbm.at[0, 0, offset], rho_hbm.at[0, 0, 0, offset])
    sources += (rho_hbm.at[1, 0, 0, offset],)
    copies = start_all([pltpu.make_async_copy(source, out.at[3 + at], sems.at[at]) for at, source in enumerate(sources)])
    out[:3] = message[:3]
    flags.wait()
    keep = cutoff_ref[0, 0, offset].astype(f32)
    for copy in copies:
        copy.wait()
    for at in (3, 5, 6, 7):
        out[at] = out[at] * keep


def second_kernel(
    cutoff_hbm, ham_hbm, inv_hbm, rho_hbm, atom_hbm, after, held, left_high, left_low, ham_high, ham_low, members,
    raw, cutoff_ref, atom_ref, cutoff_sem, atom_sem, sems
):
    flags = pltpu.make_async_copy(cutoff_hbm, cutoff_ref, cutoff_sem)
    flags.start()
    sources = (ham_hbm.at[0, 0], inv_hbm.at[0, 0], rho_hbm.at[0, 0, 0], rho_hbm.at[1, 0, 0])
    copies = start_all([pltpu.make_async_copy(source, raw.at[at], sems.at[at]) for at, source in enumerate(sources)])
    owners = pltpu.make_async_copy(atom_hbm, atom_ref, atom_sem)
    owners.start()
    order = order_of()
    flags.wait()
    keeps = [cutoff_ref[0, 0, offset].astype(f32) for offset in order]
    for kind, copy in enumerate(copies):
        copy.wait()
        for place, offset in enumerate(order):
            block = raw[kind, offset]
            if place > 0:
                block = block * keeps[place]
            if kind == 0:
                store((ham_high, ham_low), cols(place), split(block))
            else:
                held[kind - 1, place] = block
                rows = slice((kind - 1) * B, kind * B)
                left_high[rows, cols(place)], left_low[rows, cols(place)] = split(block)
    owners.wait()
    atoms = jnp.broadcast_to(atom_ref[0], (ATOMS, B))
    members[...] = -(lax.broadcasted_iota(jnp.int32, (ATOMS, B), 0) == atoms).astype(f32)


def first_half(left, place, start, near, diagonal):
    both = dot(part(left, slice(0, 3 * B), cols(place)), beside(split(near[0]), split(near[3])))
    mixed = split(start[:, cols(place)] + both[:, :B])
    prop, inner = rows_of(mixed)
    behind = dot(inner, split(near[1]))
    imag = dot(prop, split(near[2])) - behind[B:]
    return mixed, diagonal + both[:, B:], -behind[:B], imag


def second_half(mixed, near):
    prop, inner = rows_of(mixed)
    ahead = dot(prop, beside(split(near[0]), split(near[2]), split(near[3])))
    behind = dot(inner, split(near[1]))
    return ahead[:, cols(0)], ahead[:, cols(1)] - behind[:B], ahead[:, cols(2)] - behind[B:]


def send_more(more, held, place):
    more[0] = held[1, 0]
    for kind in range(3):
        more[1 + kind] = held[kind, place]


def third_kernel(left_high, left_low, ham_high, ham_low, held, three, der_hbm, start, diagonal, other, der, sem):
    copy = pltpu.make_async_copy(der_hbm, der, sem)
    copy.start()
    left = (left_high, left_low)
    start[...] = dot(part(left, slice(0, 3 * B), cols(0)), part((ham_high, ham_low), slice(0, B), cols(0, 5)))
    mixed, diagonal[...], real, other[1, 0] = first_half(left, 3, start, three, start[:, cols(0)])
    added, other[0, 1], other[1, 1] = second_half(mixed, three[4:])
    other[0, 0] = real + added
    copy.wait()


def four_kernel(
    left_high, left_low, start, diagonal, four, mixed_high, mixed_low, diagonal_out, other
):
    mixed, diagonal_out[...], other[0], other[1] = first_half((left_high, left_low), 4, start, four, diagonal[...])
    mixed_high[...], mixed_low[...] = mixed


def more_kernel(arrived, after, held, one_more, two_more, four_more):
    send_more(one_more, held, 1)
    send_more(two_more, held, 2)
    send_more(four_more, held, 4)


def fourth_kernel(left_high, left_low, start, diagonal, one, mixed_high, mixed_low, diagonal_out, other):
    mixed, diagonal_out[...], other[0], other[1] = first_half((left_high, left_low), 1, start, one, diagonal[...])
    mixed_high[...], mixed_low[...] = mixed


def fifth_kernel(
    left_high, left_low, start, diagonal, held, der_ref, other_one, other_three, other_four, two,
    new, mixed_high, mixed_low, self_high, self_low, real_two, comm, weighted, c1, c2, c3, c4
):
    order = order_of()
    left = (left_high, left_low)
    mixed, total, real_two[...], imag_two = first_half(left, 2, start, two, diagonal[...])
    mixed_high[...], mixed_low[...] = mixed
    at_self = split(total)
    self_high[...], self_low[...] = at_self
    whole = cols(0, 5)
    ahead = dot(part(at_self, slice(0, B), cols(0)), part(left, slice(2 * B, 3 * B), whole))
    behind = dot(part(at_self, slice(2 * B, 3 * B), cols(0)), part(left, slice(0, B), whole))
    imag_comm = ahead - behind
    comm[...] = imag_comm[:, cols(0)] + other_three[1, 1]
    sums = [None] * 3
    for place, column in enumerate((c1, c2, c3, c4), 1):
        imag = (other_one[1], imag_two, other_three[1, 0], other_four[1])[place - 1]
        real_new = held[1, place] + time_step * (imag_comm[:, cols(place)] + imag)
        new[place - 1] = real_new
        for direction in range(3):
            product = real_new * der_ref[direction, 0, 0, order[place]]
            sums[direction] = product if place == 1 else sums[direction] + product
            column[direction : direction + 1, :] = jnp.sum(product, axis=0, keepdims=True)
    for direction in range(3):
        weighted[direction] = sums[direction]


def later_kernel(arrived, column, out):
    out[...] = column[...]


def real_kernel(
    held, new, left_high, left_low, self_high, self_low, other_one, real_two, other_three, other_four, weighted,
    imag_part, high_four, low_four, four, out_hbm, comm, imag_out, row_part, imag_new, sems
):
    order = order_of()
    copies = start_all(
        [pltpu.make_async_copy(new.at[at], out_hbm.at[0, 0, 0, order[1 + at]], sems.at[0, at]) for at in range(4)]
    )
    left = (left_high, left_low)
    whole = cols(0, 5)
    at_self = (self_high, self_low)
    ahead = dot(part(at_self, slice(0, B), cols(0)), part(left, slice(B, 2 * B), whole))
    behind = dot(part(at_self, slice(B, 2 * B), cols(0)), part(left, slice(0, B), whole))
    real_comm = ahead - behind
    added, real_four, imag_four = second_half((high_four[...], low_four[...]), four)
    imag_out[...] = imag_part[...] + imag_four
    for at, (place, other) in enumerate(((3, other_three[0, 0]), (4, other_four[0] + added))):
        imag_new[at] = held[2, place] - time_step * (real_comm[:, cols(place)] + other)
        copies += start_all(
            [pltpu.make_async_copy(imag_new.at[at], out_hbm.at[1, 0, 0, order[place]], sems.at[1, at])]
        )
    comm[0] = real_comm[:, cols(0)] + other_three[0, 1] + real_four
    comm[1] = real_comm[:, cols(1)] + other_one[0]
    comm[2] = real_comm[:, cols(2)] + real_two[...]
    for direction in range(3):
        row_part[direction : direction + 1, :] = jnp.sum(weighted[direction].T, axis=0, keepdims=True)
    for copy in copies:
        copy.wait()


def sixth_kernel(
    held, der_ref, members, high_one, low_one, high_two, low_two, imag_part, comm, row_part, one, two, c1, c2, c3, c4, old_hbm,
    out_hbm, forces_hbm, new, forces_ref, sems
):
    order = order_of()
    prop, inner = rows_of(beside((high_one[...], low_one[...]), (high_two[...], low_two[...])))
    near = [tuple(jnp.concatenate(x, axis=0) for x in zip(split(one[1 + kind]), split(two[1 + kind]))) for kind in range(3)]
    behind = dot(inner, near[0])
    real_new = held[1, 0] + time_step * (imag_part[...] + dot(prop, near[2]) - behind[B:])
    new[0] = real_new
    copies = start_all([pltpu.make_async_copy(new.at[0], out_hbm.at[0, 0, 0, 0], sems.at[0])])
    new[1] = held[2, 0] - time_step * (comm[0] + dot(prop, near[1]) - behind[:B])
    for place, message, mixed in ((1, one, (high_one, low_one)), (2, two, (high_two, low_two))):
        added = dot(rows_of((mixed[0][...], mixed[1][...]))[0], split(message[0]))
        new[1 + place] = held[2, place] - time_step * (comm[place] + added)
    copies += start_all(
        [pltpu.make_async_copy(new.at[1 + at], out_hbm.at[1, 0, 0, order[at]], sems.at[1 + at]) for at in range(3)]
    )
    parts = []
    for direction in range(3):
        product = real_new * der_ref[direction, 0, 0, 0]
        parts.append(jnp.sum(product + product.T, axis=0, keepdims=True))
    orbital = jnp.concatenate(parts, axis=0) + row_part[...] + ((c1[...] + c2[...]) + (c3[...] + c4[...]))
    forces = lax.dot_general(
        orbital, members[...], (((1,), (1,)), ((), ())), precision=lax.Precision.HIGHEST, preferred_element_type=f32
    )
    for direction in range(3):
        forces_ref[direction] = forces[direction : direction + 1]
    copies += start_all([pltpu.make_async_copy(forces_ref, forces_hbm, sems.at[4])])
    for copy in copies:
        copy.wait()


def call(kernel, shapes, in_specs, products, args, out_specs=None, scratch=(), aliases={}):
    moved = sum(4 * x.size for x in args) + sum(4 * x.size for x in shapes)
    return pl.pallas_call(
        kernel,
        out_shape=shapes,
        in_specs=in_specs,
        out_specs=out_specs or [vmem] * len(shapes),
        scratch_shapes=scratch,
        input_output_aliases=aliases,
        compiler_params=pltpu.CompilerParams(vmem_limit_bytes=32 * 2**20),
        cost_estimate=pl.CostEstimate(flops=products * 6 * B**3, bytes_accessed=moved, transcendentals=0),
    )(*args)


def local(hamiltonian, inverse_margin, density, cutoff, derivative, atom_of):
    def shape(*dims, kind=f32):
        return jax.ShapeDtypeStruct(dims, kind)

    args = (hamiltonian, inverse_margin, density, cutoff, derivative, atom_of)
    hamiltonian, inverse_margin, density, cutoff, derivative, atom_of = (
        pltpu.with_memory_space_constraint(x, pltpu.HBM) for x in args
    )
    flags = pltpu.SMEM((1, 1, 5), jnp.int32)
    message = shape(4, B, B)
    first_one, rest = call(
        first_kernel,
        [message, shape(2, B, B)],
        [hbm] * 4,
        0,
        (cutoff, hamiltonian, inverse_margin, density),
        scratch=[pltpu.VMEM((5, B, B), f32), flags, dma(()), dma((3,))],
    )
    near_one = swapped(first_one, 1)
    (first_four,) = call(functools.partial(next_kernel, 0), [message], [vmem] * 2, 0, (first_one, rest))
    near_four = swapped(first_four, 4)
    (first_two,) = call(functools.partial(next_kernel, 1), [message], [vmem] * 2, 500, (first_four, rest))
    near_two = swapped(first_two, 2)
    (send_three,) = call(
        whole_first_kernel,
        [shape(8, B, B)],
        [hbm] * 4 + [vmem],
        500,
        (cutoff, hamiltonian, inverse_margin, density, first_two),
        scratch=[flags, dma(()), dma((5,))],
    )
    near_three = swapped(send_three, 3)
    left = [shape(3 * B, 5 * B, kind=bf16)] * 2
    ham = [shape(B, 5 * B, kind=bf16)] * 2
    held, left_high, left_low, ham_high, ham_low, members = call(
        second_kernel,
        [shape(3, 5, B, B)] + left + ham + [shape(ATOMS, B)],
        [hbm] * 6,
        2000,
        (cutoff, hamiltonian, inverse_margin, density, atom_of, send_three),
        scratch=[pltpu.VMEM((4, 5, B, B), f32), flags, pltpu.VMEM((1, 1, B), jnp.int32), dma(()), dma(()), dma((4,))],
    )
    mixed = [shape(3 * B, B, kind=bf16)] * 2
    both = shape(2, 2, B, B)
    start, diagonal, other_three, derivative = call(
        third_kernel,
        [shape(3 * B, 5 * B), shape(3 * B, B), shape(2, 2, B, B), shape(*derivative.shape)],
        [vmem] * 6 + [hbm],
        8000,
        (left_high, left_low, ham_high, ham_low, held, near_three, derivative),
        scratch=[dma(())],
    )
    one_more, two_more, four_more = call(more_kernel, [message] * 3, [vmem] * 3, 300, (near_four, other_three, held))
    near_four_more = swapped(four_more, 4)
    near_one_more = swapped(one_more, 1)
    near_two_more = swapped(two_more, 2)
    high_four, low_four, diagonal, other_four = call(
        four_kernel,
        mixed + [shape(3 * B, B), shape(2, B, B)],
        [vmem] * 5,
        8,
        (left_high, left_low, start, diagonal, near_four),
    )
    high_one, low_one, diagonal, other_one = call(
        fourth_kernel,
        mixed + [shape(3 * B, B), shape(2, B, B)],
        [vmem] * 5,
        10,
        (left_high, left_low, start, diagonal, near_one),
    )
    block = shape(B, B)
    new, high_two, low_two, self_high, self_low, real_two, imag_part, weighted, *columns = call(
        fifth_kernel,
        [message] + mixed * 2 + [block, block, shape(3, B, B)] + [shape(3, B)] * 4,
        [vmem] * 10,
        22,
        (left_high, left_low, start, diagonal, held, derivative, other_one, other_three, other_four, near_two),
    )
    c1, c2, c3, c4 = columns
    c1, c2, c3 = swapped(c1, 1), swapped(c2, 2), swapped(c3, 3)
    (c4,) = call(later_kernel, [shape(3, B)], [vmem] * 2, 0, (c3, c4))
    columns = (c1, c2, c3, swapped(c4, 4))
    args = (held, new, left_high, left_low, self_high, self_low, other_one, real_two, other_three, other_four, weighted)
    args += (imag_part, high_four, low_four, near_four_more)
    out, comm, imag_part, row_part = call(
        real_kernel,
        [shape(*density.shape), shape(3, B, B), shape(B, B), shape(3, B)],
        [vmem] * 15,
        10,
        args,
        out_specs=[hbm] + [vmem] * 3,
        scratch=[pltpu.VMEM((2, B, B), f32), dma((2, 4))],
    )
    args = (held, derivative, members, high_one, low_one, high_two, low_two, imag_part, comm, row_part)
    args += (near_one_more, near_two_more, *columns, out)
    new_density, forces = call(
        sixth_kernel,
        [shape(*density.shape), shape(3, 1, ATOMS)],
        [vmem] * 16 + [hbm],
        10,
        args,
        out_specs=[hbm, hbm],
        scratch=[pltpu.VMEM((4, B, B), f32), pltpu.VMEM((3, 1, ATOMS), f32), dma((5,))],
        aliases={16: 0},
    )
    return new_density, forces.reshape(1, 1, 3, ATOMS)


def solution(mesh):
    placed = (
        P("gx", "gy", None, None, None),
        P("gx", "gy", None, None, None),
        P(None, "gx", "gy", None, None, None),
        P("gx", "gy", None),
        P(None, "gx", "gy", None, None, None),
        P("gx", "gy", None),
    )
    return jax.shard_map(
        local,
        mesh=mesh,
        in_specs=placed,
        out_specs=(P(None, "gx", "gy", None, None, None), P("gx", "gy", None, None)),
        check_vma=False,
    )
```

```python
import functools

import jax
import jax.numpy as jnp
from jax import lax
from jax.experimental import pallas as pl
from jax.experimental.pallas import tpu as pltpu
from jax.sharding import PartitionSpec as P

B = 128
ATOMS = 64

time_step = 0.25
vmem = pl.BlockSpec(memory_space=pltpu.VMEM)
hbm = pl.BlockSpec(memory_space=pltpu.HBM)
f32 = jnp.float32
bf16 = jnp.bfloat16
dma = pltpu.SemaphoreType.DMA


def swapped(cells, edge):
    axis = "gx" if edge < 3 else "gy"
    count = lax.axis_size(axis)
    assert count % 2 == 0
    first = 0 if edge in (1, 3) else 1
    pairs = []
    for i in range(first, count, 2):
        j = (i + 1) % count
        pairs += [(i, j), (j, i)]
    return lax.ppermute(cells, axis, pairs)


def order_of():
    odd_x = lax.rem(lax.axis_index("gx"), 2)
    odd_y = lax.rem(lax.axis_index("gy"), 2)
    return 0, 1 + odd_x, 2 - odd_x, 3 + odd_y, 4 - odd_y


def cols(place, count=1):
    return slice(place * B, (place + count) * B)


def split(values):
    high = values.astype(bf16)
    return high, (values - high.astype(f32)).astype(bf16)


def beside(*pairs):
    return tuple(jnp.concatenate(parts, axis=1) for parts in zip(*pairs))


def dot(left, right):
    def one(a, b):
        return jnp.dot(a, b, preferred_element_type=f32)

    return one(left[0], right[0]) + (one(left[0], right[1]) + one(left[1], right[0]))


def part(pair, rows, columns):
    return pair[0][rows, columns], pair[1][rows, columns]


def rows_of(pair):
    return (pair[0][:B], pair[1][:B]), (pair[0][B:], pair[1][B:])


def store(pair, columns, values):
    pair[0][:, columns], pair[1][:, columns] = values


def start_all(copies):
    for copy in copies:
        copy.start()
    return copies


def first_kernel(cutoff_hbm, ham_hbm, inv_hbm, rho_hbm, one, rest, ham, cutoff_ref, cutoff_sem, sems):
    flags = pltpu.make_async_copy(cutoff_hbm, cutoff_ref, cutoff_sem)
    flags.start()
    copies = start_all(
        [
            pltpu.make_async_copy(ham_hbm.at[0, 0], ham, sems.at[0]),
            pltpu.make_async_copy(inv_hbm.at[0, 0, 0], one.at[1], sems.at[1]),
            pltpu.make_async_copy(rho_hbm.at[1, 0, 0, 0], one.at[2], sems.at[2]),
        ]
    )
    order = order_of()
    flags.wait()
    for copy in copies:
        copy.wait()
    one[0] = ham[0]
    for target, at, place in ((one, 3, 1), (rest, 0, 4), (rest, 1, 2)):
        target[at] = ham[order[place]] * cutoff_ref[0, 0, order[place]].astype(f32)


def next_kernel(at, message, rest, out):
    out[:3] = message[:3]
    out[3] = rest[at]


def whole_first_kernel(cutoff_hbm, row, inv_hbm, rho_hbm, message, out, cutoff_ref, cutoff_sem, sems):
    flags = pltpu.make_async_copy(cutoff_hbm, cutoff_ref, cutoff_sem)
    flags.start()
    offset = order_of()[3]
    sources = (rho_hbm.at[0, 0, 0, 0], inv_hbm.at[0, 0, offset], rho_hbm.at[0, 0, 0, offset], rho_hbm.at[1, 0, 0, offset])
    copies = start_all([pltpu.make_async_copy(source, out.at[4 + at], sems.at[at]) for at, source in enumerate(sources)])
    out[:3] = message[:3]
    out[3] = row[offset]
    flags.wait()
    keep = cutoff_ref[0, 0, offset].astype(f32)
    for copy in copies:
        copy.wait()
    for at in (3, 5, 6, 7):
        out[at] = out[at] * keep


def second_kernel(
    cutoff_hbm, row, inv_hbm, rho_hbm, atom_hbm, after, held, left_high, left_low, ham_high, ham_low, members,
    raw, cutoff_ref, atom_ref, cutoff_sem, atom_sem, sems
):
    flags = pltpu.make_async_copy(cutoff_hbm, cutoff_ref, cutoff_sem)
    flags.start()
    sources = (inv_hbm.at[0, 0], rho_hbm.at[0, 0, 0], rho_hbm.at[1, 0, 0])
    copies = start_all([pltpu.make_async_copy(source, raw.at[at], sems.at[at]) for at, source in enumerate(sources)])
    owners = pltpu.make_async_copy(atom_hbm, atom_ref, atom_sem)
    owners.start()
    order = order_of()
    flags.wait()
    keeps = [cutoff_ref[0, 0, offset].astype(f32) for offset in order]
    for kind in range(4):
        if kind > 0:
            copies[kind - 1].wait()
        for place, offset in enumerate(order):
            block = row[offset] if kind == 0 else raw[kind - 1, offset]
            if place > 0:
                block = block * keeps[place]
            if kind == 0:
                store((ham_high, ham_low), cols(place), split(block))
            else:
                held[kind - 1, place] = block
                rows = slice((kind - 1) * B, kind * B)
                left_high[rows, cols(place)], left_low[rows, cols(place)] = split(block)
    owners.wait()
    atoms = jnp.broadcast_to(atom_ref[0], (ATOMS, B))
    members[...] = -(lax.broadcasted_iota(jnp.int32, (ATOMS, B), 0) == atoms).astype(f32)


def first_half(left, place, start, near, diagonal):
    both = dot(part(left, slice(0, 3 * B), cols(place)), beside(split(near[0]), split(near[3])))
    mixed = split(start[:, cols(place)] + both[:, :B])
    prop, inner = rows_of(mixed)
    behind = dot(inner, split(near[1]))
    imag = dot(prop, split(near[2])) - behind[B:]
    return mixed, diagonal + both[:, B:], -behind[:B], imag


def second_half(mixed, near):
    prop, inner = rows_of(mixed)
    ahead = dot(prop, beside(split(near[0]), split(near[2]), split(near[3])))
    behind = dot(inner, split(near[1]))
    return ahead[:, cols(0)], ahead[:, cols(1)] - behind[:B], ahead[:, cols(2)] - behind[B:]


def send_more(more, held, place):
    more[0] = held[1, 0]
    for kind in range(3):
        more[1 + kind] = held[kind, place]


def third_kernel(left_high, left_low, ham_high, ham_low, held, three, der_hbm, start, diagonal, other, der, sem):
    copy = pltpu.make_async_copy(der_hbm, der, sem)
    copy.start()
    left = (left_high, left_low)
    start[...] = dot(part(left, slice(0, 3 * B), cols(0)), part((ham_high, ham_low), slice(0, B), cols(0, 5)))
    mixed, diagonal[...], real, other[1, 0] = first_half(left, 3, start, three, start[:, cols(0)])
    added, other[0, 1], other[1, 1] = second_half(mixed, three[4:])
    other[0, 0] = real + added
    copy.wait()


def four_kernel(
    left_high, left_low, start, diagonal, four, mixed_high, mixed_low, diagonal_out, other
):
    mixed, diagonal_out[...], other[0], other[1] = first_half((left_high, left_low), 4, start, four, diagonal[...])
    mixed_high[...], mixed_low[...] = mixed


def more_kernel(arrived, after, held, one_more, two_more, four_more):
    send_more(one_more, held, 1)
    send_more(two_more, held, 2)
    send_more(four_more, held, 4)


def fourth_kernel(left_high, left_low, start, diagonal, one, mixed_high, mixed_low, diagonal_out, other):
    mixed, diagonal_out[...], other[0], other[1] = first_half((left_high, left_low), 1, start, one, diagonal[...])
    mixed_high[...], mixed_low[...] = mixed


def fifth_kernel(
    left_high, left_low, start, diagonal, held, der_ref, other_one, other_three, other_four, two,
    new, mixed_high, mixed_low, self_high, self_low, real_two, comm, weighted, c1, c2, c3, c4
):
    order = order_of()
    left = (left_high, left_low)
    mixed, total, real_two[...], imag_two = first_half(left, 2, start, two, diagonal[...])
    mixed_high[...], mixed_low[...] = mixed
    at_self = split(total)
    self_high[...], self_low[...] = at_self
    whole = cols(0, 5)
    ahead = dot(part(at_self, slice(0, B), cols(0)), part(left, slice(2 * B, 3 * B), whole))
    behind = dot(part(at_self, slice(2 * B, 3 * B), cols(0)), part(left, slice(0, B), whole))
    imag_comm = ahead - behind
    comm[...] = imag_comm[:, cols(0)] + other_three[1, 1]
    sums = [None] * 3
    for place, column in enumerate((c1, c2, c3, c4), 1):
        imag = (other_one[1], imag_two, other_three[1, 0], other_four[1])[place - 1]
        real_new = held[1, place] + time_step * (imag_comm[:, cols(place)] + imag)
        new[place - 1] = real_new
        for direction in range(3):
            product = real_new * der_ref[direction, 0, 0, order[place]]
            sums[direction] = product if place == 1 else sums[direction] + product
            column[direction : direction + 1, :] = jnp.sum(product, axis=0, keepdims=True)
    for direction in range(3):
        weighted[direction] = sums[direction]


def later_kernel(arrived, column, out):
    out[...] = column[...]


def real_kernel(
    held, new, left_high, left_low, self_high, self_low, other_one, real_two, other_three, other_four, weighted,
    imag_part, high_four, low_four, four, out_hbm, comm, imag_out, row_part, imag_new, sems
):
    order = order_of()
    copies = start_all(
        [pltpu.make_async_copy(new.at[at], out_hbm.at[0, 0, 0, order[1 + at]], sems.at[0, at]) for at in range(4)]
    )
    left = (left_high, left_low)
    whole = cols(0, 5)
    at_self = (self_high, self_low)
    ahead = dot(part(at_self, slice(0, B), cols(0)), part(left, slice(B, 2 * B), whole))
    behind = dot(part(at_self, slice(B, 2 * B), cols(0)), part(left, slice(0, B), whole))
    real_comm = ahead - behind
    added, real_four, imag_four = second_half((high_four[...], low_four[...]), four)
    imag_out[...] = imag_part[...] + imag_four
    for at, (place, other) in enumerate(((3, other_three[0, 0]), (4, other_four[0] + added))):
        imag_new[at] = held[2, place] - time_step * (real_comm[:, cols(place)] + other)
        copies += start_all(
            [pltpu.make_async_copy(imag_new.at[at], out_hbm.at[1, 0, 0, order[place]], sems.at[1, at])]
        )
    comm[0] = real_comm[:, cols(0)] + other_three[0, 1] + real_four
    comm[1] = real_comm[:, cols(1)] + other_one[0]
    comm[2] = real_comm[:, cols(2)] + real_two[...]
    for direction in range(3):
        row_part[direction : direction + 1, :] = jnp.sum(weighted[direction].T, axis=0, keepdims=True)
    for copy in copies:
        copy.wait()


def sixth_kernel(
    held, der_ref, members, high_one, low_one, high_two, low_two, imag_part, comm, row_part, one, two, c1, c2, c3, c4, old_hbm,
    out_hbm, forces_hbm, new, forces_ref, sems
):
    order = order_of()
    prop, inner = rows_of(beside((high_one[...], low_one[...]), (high_two[...], low_two[...])))
    near = [tuple(jnp.concatenate(x, axis=0) for x in zip(split(one[1 + kind]), split(two[1 + kind]))) for kind in range(3)]
    behind = dot(inner, near[0])
    real_new = held[1, 0] + time_step * (imag_part[...] + dot(prop, near[2]) - behind[B:])
    new[0] = real_new
    copies = start_all([pltpu.make_async_copy(new.at[0], out_hbm.at[0, 0, 0, 0], sems.at[0])])
    new[1] = held[2, 0] - time_step * (comm[0] + dot(prop, near[1]) - behind[:B])
    for place, message, mixed in ((1, one, (high_one, low_one)), (2, two, (high_two, low_two))):
        added = dot(rows_of((mixed[0][...], mixed[1][...]))[0], split(message[0]))
        new[1 + place] = held[2, place] - time_step * (comm[place] + added)
    copies += start_all(
        [pltpu.make_async_copy(new.at[1 + at], out_hbm.at[1, 0, 0, order[at]], sems.at[1 + at]) for at in range(3)]
    )
    parts = []
    for direction in range(3):
        product = real_new * der_ref[direction, 0, 0, 0]
        parts.append(jnp.sum(product + product.T, axis=0, keepdims=True))
    orbital = jnp.concatenate(parts, axis=0) + row_part[...] + ((c1[...] + c2[...]) + (c3[...] + c4[...]))
    forces = lax.dot_general(
        orbital, members[...], (((1,), (1,)), ((), ())), precision=lax.Precision.HIGHEST, preferred_element_type=f32
    )
    for direction in range(3):
        forces_ref[direction] = forces[direction : direction + 1]
    copies += start_all([pltpu.make_async_copy(forces_ref, forces_hbm, sems.at[4])])
    for copy in copies:
        copy.wait()


def call(kernel, shapes, in_specs, products, args, out_specs=None, scratch=(), aliases={}):
    moved = sum(4 * x.size for x in args) + sum(4 * x.size for x in shapes)
    return pl.pallas_call(
        kernel,
        out_shape=shapes,
        in_specs=in_specs,
        out_specs=out_specs or [vmem] * len(shapes),
        scratch_shapes=scratch,
        input_output_aliases=aliases,
        compiler_params=pltpu.CompilerParams(vmem_limit_bytes=32 * 2**20),
        cost_estimate=pl.CostEstimate(flops=products * 6 * B**3, bytes_accessed=moved, transcendentals=0),
    )(*args)


def local(hamiltonian, inverse_margin, density, cutoff, derivative, atom_of):
    def shape(*dims, kind=f32):
        return jax.ShapeDtypeStruct(dims, kind)

    args = (hamiltonian, inverse_margin, density, cutoff, derivative, atom_of)
    hamiltonian, inverse_margin, density, cutoff, derivative, atom_of = (
        pltpu.with_memory_space_constraint(x, pltpu.HBM) for x in args
    )
    flags = pltpu.SMEM((1, 1, 5), jnp.int32)
    message = shape(4, B, B)
    first_one, rest, row = call(
        first_kernel,
        [message, shape(2, B, B), shape(5, B, B)],
        [hbm] * 4,
        0,
        (cutoff, hamiltonian, inverse_margin, density),
        scratch=[flags, dma(()), dma((3,))],
    )
    near_one = swapped(first_one, 1)
    (first_four,) = call(functools.partial(next_kernel, 0), [message], [vmem] * 2, 0, (first_one, rest))
    near_four = swapped(first_four, 4)
    (first_two,) = call(functools.partial(next_kernel, 1), [message], [vmem] * 2, 500, (first_four, rest))
    near_two = swapped(first_two, 2)
    (send_three,) = call(
        whole_first_kernel,
        [shape(8, B, B)],
        [hbm, vmem, hbm, hbm, vmem],
        500,
        (cutoff, row, inverse_margin, density, first_two),
        scratch=[flags, dma(()), dma((4,))],
    )
    near_three = swapped(send_three, 3)
    left = [shape(3 * B, 5 * B, kind=bf16)] * 2
    ham = [shape(B, 5 * B, kind=bf16)] * 2
    held, left_high, left_low, ham_high, ham_low, members = call(
        second_kernel,
        [shape(3, 5, B, B)] + left + ham + [shape(ATOMS, B)],
        [hbm, vmem] + [hbm] * 4,
        2000,
        (cutoff, row, inverse_margin, density, atom_of, send_three),
        scratch=[pltpu.VMEM((3, 5, B, B), f32), flags, pltpu.VMEM((1, 1, B), jnp.int32), dma(()), dma(()), dma((3,))],
    )
    mixed = [shape(3 * B, B, kind=bf16)] * 2
    both = shape(2, 2, B, B)
    start, diagonal, other_three, derivative = call(
        third_kernel,
        [shape(3 * B, 5 * B), shape(3 * B, B), shape(2, 2, B, B), shape(*derivative.shape)],
        [vmem] * 6 + [hbm],
        8000,
        (left_high, left_low, ham_high, ham_low, held, near_three, derivative),
        scratch=[dma(())],
    )
    one_more, two_more, four_more = call(more_kernel, [message] * 3, [vmem] * 3, 300, (near_four, other_three, held))
    near_four_more = swapped(four_more, 4)
    near_one_more = swapped(one_more, 1)
    near_two_more = swapped(two_more, 2)
    high_four, low_four, diagonal, other_four = call(
        four_kernel,
        mixed + [shape(3 * B, B), shape(2, B, B)],
        [vmem] * 5,
        8,
        (left_high, left_low, start, diagonal, near_four),
    )
    high_one, low_one, diagonal, other_one = call(
        fourth_kernel,
        mixed + [shape(3 * B, B), shape(2, B, B)],
        [vmem] * 5,
        10,
        (left_high, left_low, start, diagonal, near_one),
    )
    block = shape(B, B)
    new, high_two, low_two, self_high, self_low, real_two, imag_part, weighted, *columns = call(
        fifth_kernel,
        [message] + mixed * 2 + [block, block, shape(3, B, B)] + [shape(3, B)] * 4,
        [vmem] * 10,
        22,
        (left_high, left_low, start, diagonal, held, derivative, other_one, other_three, other_four, near_two),
    )
    c1, c2, c3, c4 = columns
    c1, c2, c3 = swapped(c1, 1), swapped(c2, 2), swapped(c3, 3)
    (c4,) = call(later_kernel, [shape(3, B)], [vmem] * 2, 0, (c3, c4))
    columns = (c1, c2, c3, swapped(c4, 4))
    args = (held, new, left_high, left_low, self_high, self_low, other_one, real_two, other_three, other_four, weighted)
    args += (imag_part, high_four, low_four, near_four_more)
    out, comm, imag_part, row_part = call(
        real_kernel,
        [shape(*density.shape), shape(3, B, B), shape(B, B), shape(3, B)],
        [vmem] * 15,
        10,
        args,
        out_specs=[hbm] + [vmem] * 3,
        scratch=[pltpu.VMEM((2, B, B), f32), dma((2, 4))],
    )
    args = (held, derivative, members, high_one, low_one, high_two, low_two, imag_part, comm, row_part)
    args += (near_one_more, near_two_more, *columns, out)
    new_density, forces = call(
        sixth_kernel,
        [shape(*density.shape), shape(3, 1, ATOMS)],
        [vmem] * 16 + [hbm],
        10,
        args,
        out_specs=[hbm, hbm],
        scratch=[pltpu.VMEM((4, B, B), f32), pltpu.VMEM((3, 1, ATOMS), f32), dma((5,))],
        aliases={16: 0},
    )
    return new_density, forces.reshape(1, 1, 3, ATOMS)


def solution(mesh):
    placed = (
        P("gx", "gy", None, None, None),
        P("gx", "gy", None, None, None),
        P(None, "gx", "gy", None, None, None),
        P("gx", "gy", None),
        P(None, "gx", "gy", None, None, None),
        P("gx", "gy", None),
    )
    return jax.shard_map(
        local,
        mesh=mesh,
        in_specs=placed,
        out_specs=(P(None, "gx", "gy", None, None, None), P("gx", "gy", None, None)),
        check_vma=False,
    )
```

```python
import functools

import jax
import jax.numpy as jnp
from jax import lax
from jax.experimental import pallas as pl
from jax.experimental.pallas import tpu as pltpu
from jax.sharding import PartitionSpec as P

B = 128
ATOMS = 64

time_step = 0.25
vmem = pl.BlockSpec(memory_space=pltpu.VMEM)
hbm = pl.BlockSpec(memory_space=pltpu.HBM)
f32 = jnp.float32
bf16 = jnp.bfloat16
dma = pltpu.SemaphoreType.DMA


def swapped(cells, edge):
    axis = "gx" if edge < 3 else "gy"
    count = lax.axis_size(axis)
    assert count % 2 == 0
    first = 0 if edge in (1, 3) else 1
    pairs = []
    for i in range(first, count, 2):
        j = (i + 1) % count
        pairs += [(i, j), (j, i)]
    return lax.ppermute(cells, axis, pairs)


def order_of():
    odd_x = lax.rem(lax.axis_index("gx"), 2)
    odd_y = lax.rem(lax.axis_index("gy"), 2)
    return 0, 1 + odd_x, 2 - odd_x, 3 + odd_y, 4 - odd_y


def cols(place, count=1):
    return slice(place * B, (place + count) * B)


def split(values):
    high = values.astype(bf16)
    return high, (values - high.astype(f32)).astype(bf16)


def beside(*pairs):
    return tuple(jnp.concatenate(parts, axis=1) for parts in zip(*pairs))


def dot(left, right):
    def one(a, b):
        return jnp.dot(a, b, preferred_element_type=f32)

    return one(left[0], right[0]) + (one(left[0], right[1]) + one(left[1], right[0]))


def part(pair, rows, columns):
    return pair[0][rows, columns], pair[1][rows, columns]


def rows_of(pair):
    return (pair[0][:B], pair[1][:B]), (pair[0][B:], pair[1][B:])


def store(pair, columns, values):
    pair[0][:, columns], pair[1][:, columns] = values


def start_all(copies):
    for copy in copies:
        copy.start()
    return copies


def first_kernel(cutoff_hbm, ham_hbm, inv_hbm, rho_hbm, one, rest, ham, cutoff_ref, cutoff_sem, sems):
    flags = pltpu.make_async_copy(cutoff_hbm, cutoff_ref, cutoff_sem)
    flags.start()
    copies = start_all(
        [
            pltpu.make_async_copy(ham_hbm.at[0, 0], ham, sems.at[0]),
            pltpu.make_async_copy(inv_hbm.at[0, 0, 0], one.at[1], sems.at[1]),
            pltpu.make_async_copy(rho_hbm.at[1, 0, 0, 0], one.at[2], sems.at[2]),
        ]
    )
    order = order_of()
    flags.wait()
    for copy in copies:
        copy.wait()
    one[0] = ham[0]
    for target, at, place in ((one, 3, 1), (rest, 0, 4), (rest, 1, 2)):
        target[at] = ham[order[place]] * cutoff_ref[0, 0, order[place]].astype(f32)


def next_kernel(at, message, rest, out):
    out[:3] = message[:3]
    out[3] = rest[at]


def whole_first_kernel(cutoff_hbm, ham_hbm, inv_hbm, rho_hbm, message, out, cutoff_ref, cutoff_sem, sems):
    flags = pltpu.make_async_copy(cutoff_hbm, cutoff_ref, cutoff_sem)
    flags.start()
    offset = order_of()[3]
    sources = (ham_hbm.at[0, 0, offset], rho_hbm.at[0, 0, 0, 0], inv_hbm.at[0, 0, offset], rho_hbm.at[0, 0, 0, offset])
    sources += (rho_hbm.at[1, 0, 0, offset],)
    copies = start_all([pltpu.make_async_copy(source, out.at[3 + at], sems.at[at]) for at, source in enumerate(sources)])
    out[:3] = message[:3]
    flags.wait()
    keep = cutoff_ref[0, 0, offset].astype(f32)
    for copy in copies:
        copy.wait()
    for at in (3, 5, 6, 7):
        out[at] = out[at] * keep


def second_kernel(
    cutoff_hbm, ham_hbm, inv_hbm, rho_hbm, atom_hbm, after, held, left_high, left_low, ham_high, ham_low, members,
    raw, cutoff_ref, atom_ref, cutoff_sem, atom_sem, sems
):
    flags = pltpu.make_async_copy(cutoff_hbm, cutoff_ref, cutoff_sem)
    flags.start()
    sources = (ham_hbm.at[0, 0], inv_hbm.at[0, 0], rho_hbm.at[0, 0, 0], rho_hbm.at[1, 0, 0])
    copies = start_all([pltpu.make_async_copy(source, raw.at[at], sems.at[at]) for at, source in enumerate(sources)])
    owners = pltpu.make_async_copy(atom_hbm, atom_ref, atom_sem)
    owners.start()
    order = order_of()
    flags.wait()
    keeps = [cutoff_ref[0, 0, offset].astype(f32) for offset in order]
    for kind, copy in enumerate(copies):
        copy.wait()
        for place, offset in enumerate(order):
            block = raw[kind, offset]
            if place > 0:
                block = block * keeps[place]
            if kind == 0:
                store((ham_high, ham_low), cols(place), split(block))
            else:
                held[kind - 1, place] = block
                rows = slice((kind - 1) * B, kind * B)
                left_high[rows, cols(place)], left_low[rows, cols(place)] = split(block)
    owners.wait()
    atoms = jnp.broadcast_to(atom_ref[0], (ATOMS, B))
    members[...] = -(lax.broadcasted_iota(jnp.int32, (ATOMS, B), 0) == atoms).astype(f32)


def first_half(left, place, start, near, diagonal):
    both = dot(part(left, slice(0, 3 * B), cols(place)), beside(split(near[0]), split(near[3])))
    mixed = split(start[:, cols(place)] + both[:, :B])
    prop, inner = rows_of(mixed)
    behind = dot(inner, split(near[1]))
    imag = dot(prop, split(near[2])) - behind[B:]
    return mixed, diagonal + both[:, B:], -behind[:B], imag


def second_half(mixed, near):
    prop, inner = rows_of(mixed)
    ahead = dot(prop, beside(split(near[0]), split(near[2]), split(near[3])))
    behind = dot(inner, split(near[1]))
    return ahead[:, cols(0)], ahead[:, cols(1)] - behind[:B], ahead[:, cols(2)] - behind[B:]


def send_more(more, held, place):
    more[0] = held[1, 0]
    for kind in range(3):
        more[1 + kind] = held[kind, place]


def third_kernel(left_high, left_low, ham_high, ham_low, held, three, der_hbm, start, diagonal, other, der, sem):
    copy = pltpu.make_async_copy(der_hbm, der, sem)
    copy.start()
    left = (left_high, left_low)
    start[...] = dot(part(left, slice(0, 3 * B), cols(0)), part((ham_high, ham_low), slice(0, B), cols(0, 5)))
    mixed, diagonal[...], real, other[1, 0] = first_half(left, 3, start, three, start[:, cols(0)])
    added, other[0, 1], other[1, 1] = second_half(mixed, three[4:])
    other[0, 0] = real + added
    copy.wait()


def four_kernel(
    left_high, left_low, start, diagonal, four, mixed_high, mixed_low, diagonal_out, other
):
    mixed, diagonal_out[...], other[0], other[1] = first_half((left_high, left_low), 4, start, four, diagonal[...])
    mixed_high[...], mixed_low[...] = mixed


def more_kernel(arrived, after, held, one_more, two_more, four_more):
    send_more(one_more, held, 1)
    send_more(two_more, held, 2)
    send_more(four_more, held, 4)


def fourth_kernel(left_high, left_low, start, diagonal, one, mixed_high, mixed_low, diagonal_out, other):
    mixed, diagonal_out[...], other[0], other[1] = first_half((left_high, left_low), 1, start, one, diagonal[...])
    mixed_high[...], mixed_low[...] = mixed


def fifth_kernel(
    left_high, left_low, start, diagonal, held, der_ref, other_one, other_three, other_four, two,
    new, mixed_high, mixed_low, self_high, self_low, real_two, comm, weighted, c1, c2, c3, c4
):
    order = order_of()
    left = (left_high, left_low)
    mixed, total, real_two[...], imag_two = first_half(left, 2, start, two, diagonal[...])
    mixed_high[...], mixed_low[...] = mixed
    at_self = split(total)
    self_high[...], self_low[...] = at_self
    whole = cols(0, 5)
    ahead = dot(part(at_self, slice(0, B), cols(0)), part(left, slice(2 * B, 3 * B), whole))
    behind = dot(part(at_self, slice(2 * B, 3 * B), cols(0)), part(left, slice(0, B), whole))
    imag_comm = ahead - behind
    comm[...] = imag_comm[:, cols(0)] + other_three[1, 1]
    sums = [None] * 3
    for place, column in enumerate((c1, c2, c3, c4), 1):
        imag = (other_one[1], imag_two, other_three[1, 0], other_four[1])[place - 1]
        real_new = held[1, place] + time_step * (imag_comm[:, cols(place)] + imag)
        new[place - 1] = real_new
        for direction in range(3):
            product = real_new * der_ref[direction, 0, 0, order[place]]
            sums[direction] = product if place == 1 else sums[direction] + product
            column[direction : direction + 1, :] = jnp.sum(product, axis=0, keepdims=True)
    for direction in range(3):
        weighted[direction] = sums[direction]


def later_kernel(arrived, c1, c4, c1_out, c4_out):
    c1_out[...] = c1[...]
    c4_out[...] = c4[...]


def real_kernel(
    held, new, left_high, left_low, self_high, self_low, other_one, real_two, other_three, other_four, weighted,
    imag_part, high_four, low_four, four, out_hbm, comm, imag_out, row_part, imag_new, sems
):
    order = order_of()
    copies = start_all(
        [pltpu.make_async_copy(new.at[at], out_hbm.at[0, 0, 0, order[1 + at]], sems.at[0, at]) for at in range(4)]
    )
    left = (left_high, left_low)
    whole = cols(0, 5)
    at_self = (self_high, self_low)
    ahead = dot(part(at_self, slice(0, B), cols(0)), part(left, slice(B, 2 * B), whole))
    behind = dot(part(at_self, slice(B, 2 * B), cols(0)), part(left, slice(0, B), whole))
    real_comm = ahead - behind
    added, real_four, imag_four = second_half((high_four[...], low_four[...]), four)
    imag_out[...] = imag_part[...] + imag_four
    for at, (place, other) in enumerate(((3, other_three[0, 0]), (4, other_four[0] + added))):
        imag_new[at] = held[2, place] - time_step * (real_comm[:, cols(place)] + other)
        copies += start_all(
            [pltpu.make_async_copy(imag_new.at[at], out_hbm.at[1, 0, 0, order[place]], sems.at[1, at])]
        )
    comm[0] = real_comm[:, cols(0)] + other_three[0, 1] + real_four
    comm[1] = real_comm[:, cols(1)] + other_one[0]
    comm[2] = real_comm[:, cols(2)] + real_two[...]
    for direction in range(3):
        row_part[direction : direction + 1, :] = jnp.sum(weighted[direction].T, axis=0, keepdims=True)
    for copy in copies:
        copy.wait()


def sixth_kernel(
    held, der_ref, members, high_one, low_one, high_two, low_two, imag_part, comm, row_part, one, two, c1, c2, c3, c4, old_hbm,
    out_hbm, forces_hbm, new, forces_ref, sems
):
    order = order_of()
    prop, inner = rows_of(beside((high_one[...], low_one[...]), (high_two[...], low_two[...])))
    near = [tuple(jnp.concatenate(x, axis=0) for x in zip(split(one[1 + kind]), split(two[1 + kind]))) for kind in range(3)]
    behind = dot(inner, near[0])
    real_new = held[1, 0] + time_step * (imag_part[...] + dot(prop, near[2]) - behind[B:])
    new[0] = real_new
    copies = start_all([pltpu.make_async_copy(new.at[0], out_hbm.at[0, 0, 0, 0], sems.at[0])])
    new[1] = held[2, 0] - time_step * (comm[0] + dot(prop, near[1]) - behind[:B])
    for place, message, mixed in ((1, one, (high_one, low_one)), (2, two, (high_two, low_two))):
        added = dot(rows_of((mixed[0][...], mixed[1][...]))[0], split(message[0]))
        new[1 + place] = held[2, place] - time_step * (comm[place] + added)
    copies += start_all(
        [pltpu.make_async_copy(new.at[1 + at], out_hbm.at[1, 0, 0, order[at]], sems.at[1 + at]) for at in range(3)]
    )
    parts = []
    for direction in range(3):
        product = real_new * der_ref[direction, 0, 0, 0]
        parts.append(jnp.sum(product + product.T, axis=0, keepdims=True))
    orbital = jnp.concatenate(parts, axis=0) + row_part[...] + ((c1[...] + c2[...]) + (c3[...] + c4[...]))
    forces = lax.dot_general(
        orbital, members[...], (((1,), (1,)), ((), ())), precision=lax.Precision.HIGHEST, preferred_element_type=f32
    )
    for direction in range(3):
        forces_ref[direction] = forces[direction : direction + 1]
    copies += start_all([pltpu.make_async_copy(forces_ref, forces_hbm, sems.at[4])])
    for copy in copies:
        copy.wait()


def call(kernel, shapes, in_specs, products, args, out_specs=None, scratch=(), aliases={}):
    moved = sum(4 * x.size for x in args) + sum(4 * x.size for x in shapes)
    return pl.pallas_call(
        kernel,
        out_shape=shapes,
        in_specs=in_specs,
        out_specs=out_specs or [vmem] * len(shapes),
        scratch_shapes=scratch,
        input_output_aliases=aliases,
        compiler_params=pltpu.CompilerParams(vmem_limit_bytes=32 * 2**20),
        cost_estimate=pl.CostEstimate(flops=products * 6 * B**3, bytes_accessed=moved, transcendentals=0),
    )(*args)


def local(hamiltonian, inverse_margin, density, cutoff, derivative, atom_of):
    def shape(*dims, kind=f32):
        return jax.ShapeDtypeStruct(dims, kind)

    args = (hamiltonian, inverse_margin, density, cutoff, derivative, atom_of)
    hamiltonian, inverse_margin, density, cutoff, derivative, atom_of = (
        pltpu.with_memory_space_constraint(x, pltpu.HBM) for x in args
    )
    flags = pltpu.SMEM((1, 1, 5), jnp.int32)
    message = shape(4, B, B)
    first_one, rest = call(
        first_kernel,
        [message, shape(2, B, B)],
        [hbm] * 4,
        0,
        (cutoff, hamiltonian, inverse_margin, density),
        scratch=[pltpu.VMEM((5, B, B), f32), flags, dma(()), dma((3,))],
    )
    near_one = swapped(first_one, 1)
    (first_four,) = call(functools.partial(next_kernel, 0), [message], [vmem] * 2, 0, (first_one, rest))
    near_four = swapped(first_four, 4)
    (first_two,) = call(functools.partial(next_kernel, 1), [message], [vmem] * 2, 500, (first_four, rest))
    near_two = swapped(first_two, 2)
    (send_three,) = call(
        whole_first_kernel,
        [shape(8, B, B)],
        [hbm] * 4 + [vmem],
        500,
        (cutoff, hamiltonian, inverse_margin, density, first_two),
        scratch=[flags, dma(()), dma((5,))],
    )
    near_three = swapped(send_three, 3)
    left = [shape(3 * B, 5 * B, kind=bf16)] * 2
    ham = [shape(B, 5 * B, kind=bf16)] * 2
    held, left_high, left_low, ham_high, ham_low, members = call(
        second_kernel,
        [shape(3, 5, B, B)] + left + ham + [shape(ATOMS, B)],
        [hbm] * 6,
        2000,
        (cutoff, hamiltonian, inverse_margin, density, atom_of, send_three),
        scratch=[pltpu.VMEM((4, 5, B, B), f32), flags, pltpu.VMEM((1, 1, B), jnp.int32), dma(()), dma(()), dma((4,))],
    )
    mixed = [shape(3 * B, B, kind=bf16)] * 2
    both = shape(2, 2, B, B)
    start, diagonal, other_three, derivative = call(
        third_kernel,
        [shape(3 * B, 5 * B), shape(3 * B, B), shape(2, 2, B, B), shape(*derivative.shape)],
        [vmem] * 6 + [hbm],
        8000,
        (left_high, left_low, ham_high, ham_low, held, near_three, derivative),
        scratch=[dma(())],
    )
    one_more, two_more, four_more = call(more_kernel, [message] * 3, [vmem] * 3, 300, (near_four, other_three, held))
    near_four_more = swapped(four_more, 4)
    near_one_more = swapped(one_more, 1)
    near_two_more = swapped(two_more, 2)
    high_four, low_four, diagonal, other_four = call(
        four_kernel,
        mixed + [shape(3 * B, B), shape(2, B, B)],
        [vmem] * 5,
        8,
        (left_high, left_low, start, diagonal, near_four),
    )
    high_one, low_one, diagonal, other_one = call(
        fourth_kernel,
        mixed + [shape(3 * B, B), shape(2, B, B)],
        [vmem] * 5,
        10,
        (left_high, left_low, start, diagonal, near_one),
    )
    block = shape(B, B)
    new, high_two, low_two, self_high, self_low, real_two, imag_part, weighted, *columns = call(
        fifth_kernel,
        [message] + mixed * 2 + [block, block, shape(3, B, B)] + [shape(3, B)] * 4,
        [vmem] * 10,
        22,
        (left_high, left_low, start, diagonal, held, derivative, other_one, other_three, other_four, near_two),
    )
    c1, c2, c3, c4 = columns
    c2, c3 = swapped(c2, 2), swapped(c3, 3)
    c1, c4 = call(later_kernel, [shape(3, B)] * 2, [vmem] * 3, 0, (c3, c1, c4))
    columns = (swapped(c1, 1), c2, c3, swapped(c4, 4))
    args = (held, new, left_high, left_low, self_high, self_low, other_one, real_two, other_three, other_four, weighted)
    args += (imag_part, high_four, low_four, near_four_more)
    out, comm, imag_part, row_part = call(
        real_kernel,
        [shape(*density.shape), shape(3, B, B), shape(B, B), shape(3, B)],
        [vmem] * 15,
        10,
        args,
        out_specs=[hbm] + [vmem] * 3,
        scratch=[pltpu.VMEM((2, B, B), f32), dma((2, 4))],
    )
    args = (held, derivative, members, high_one, low_one, high_two, low_two, imag_part, comm, row_part)
    args += (near_one_more, near_two_more, *columns, out)
    new_density, forces = call(
        sixth_kernel,
        [shape(*density.shape), shape(3, 1, ATOMS)],
        [vmem] * 16 + [hbm],
        10,
        args,
        out_specs=[hbm, hbm],
        scratch=[pltpu.VMEM((4, B, B), f32), pltpu.VMEM((3, 1, ATOMS), f32), dma((5,))],
        aliases={16: 0},
    )
    return new_density, forces.reshape(1, 1, 3, ATOMS)


def solution(mesh):
    placed = (
        P("gx", "gy", None, None, None),
        P("gx", "gy", None, None, None),
        P(None, "gx", "gy", None, None, None),
        P("gx", "gy", None),
        P(None, "gx", "gy", None, None, None),
        P("gx", "gy", None),
    )
    return jax.shard_map(
        local,
        mesh=mesh,
        in_specs=placed,
        out_specs=(P(None, "gx", "gy", None, None, None), P("gx", "gy", None, None)),
        check_vma=False,
    )
```

```python
import functools

import jax
import jax.numpy as jnp
from jax import lax
from jax.experimental import pallas as pl
from jax.experimental.pallas import tpu as pltpu
from jax.sharding import PartitionSpec as P

B = 128
ATOMS = 64

time_step = 0.25
vmem = pl.BlockSpec(memory_space=pltpu.VMEM)
hbm = pl.BlockSpec(memory_space=pltpu.HBM)
f32 = jnp.float32
bf16 = jnp.bfloat16
dma = pltpu.SemaphoreType.DMA


def swapped(cells, edge):
    axis = "gx" if edge < 3 else "gy"
    count = lax.axis_size(axis)
    assert count % 2 == 0
    first = 0 if edge in (1, 3) else 1
    pairs = []
    for i in range(first, count, 2):
        j = (i + 1) % count
        pairs += [(i, j), (j, i)]
    return lax.ppermute(cells, axis, pairs)


def order_of():
    odd_x = lax.rem(lax.axis_index("gx"), 2)
    odd_y = lax.rem(lax.axis_index("gy"), 2)
    return 0, 1 + odd_x, 2 - odd_x, 3 + odd_y, 4 - odd_y


def cols(place, count=1):
    return slice(place * B, (place + count) * B)


def split(values):
    high = values.astype(bf16)
    return high, (values - high.astype(f32)).astype(bf16)


def beside(*pairs):
    return tuple(jnp.concatenate(parts, axis=1) for parts in zip(*pairs))


def dot(left, right):
    def one(a, b):
        return jnp.dot(a, b, preferred_element_type=f32)

    return one(left[0], right[0]) + (one(left[0], right[1]) + one(left[1], right[0]))


def part(pair, rows, columns):
    return pair[0][rows, columns], pair[1][rows, columns]


def rows_of(pair):
    return (pair[0][:B], pair[1][:B]), (pair[0][B:], pair[1][B:])


def store(pair, columns, values):
    pair[0][:, columns], pair[1][:, columns] = values


def start_all(copies):
    for copy in copies:
        copy.start()
    return copies


def first_kernel(cutoff_hbm, ham_hbm, inv_hbm, rho_hbm, one, rest, ham, cutoff_ref, cutoff_sem, sems):
    flags = pltpu.make_async_copy(cutoff_hbm, cutoff_ref, cutoff_sem)
    flags.start()
    copies = start_all(
        [
            pltpu.make_async_copy(ham_hbm.at[0, 0], ham, sems.at[0]),
            pltpu.make_async_copy(inv_hbm.at[0, 0, 0], one.at[1], sems.at[1]),
            pltpu.make_async_copy(rho_hbm.at[1, 0, 0, 0], one.at[2], sems.at[2]),
        ]
    )
    order = order_of()
    flags.wait()
    for copy in copies:
        copy.wait()
    one[0] = ham[0]
    for target, at, place in ((one, 3, 1), (rest, 0, 4), (rest, 1, 2)):
        target[at] = ham[order[place]] * cutoff_ref[0, 0, order[place]].astype(f32)


def next_kernel(at, message, rest, out):
    out[:3] = message[:3]
    out[3] = rest[at]


def whole_first_kernel(cutoff_hbm, ham_hbm, inv_hbm, rho_hbm, message, out, cutoff_ref, cutoff_sem, sems):
    flags = pltpu.make_async_copy(cutoff_hbm, cutoff_ref, cutoff_sem)
    flags.start()
    offset = order_of()[3]
    sources = (ham_hbm.at[0, 0, offset], rho_hbm.at[0, 0, 0, 0], inv_hbm.at[0, 0, offset], rho_hbm.at[0, 0, 0, offset])
    sources += (rho_hbm.at[1, 0, 0, offset],)
    copies = start_all([pltpu.make_async_copy(source, out.at[3 + at], sems.at[at]) for at, source in enumerate(sources)])
    out[:3] = message[:3]
    flags.wait()
    keep = cutoff_ref[0, 0, offset].astype(f32)
    for copy in copies:
        copy.wait()
    for at in (3, 5, 6, 7):
        out[at] = out[at] * keep


def second_kernel(
    cutoff_hbm, ham_hbm, inv_hbm, rho_hbm, atom_hbm, after, held, left_high, left_low, ham_high, ham_low, members,
    raw, cutoff_ref, atom_ref, cutoff_sem, atom_sem, sems
):
    flags = pltpu.make_async_copy(cutoff_hbm, cutoff_ref, cutoff_sem)
    flags.start()
    sources = (ham_hbm.at[0, 0], inv_hbm.at[0, 0], rho_hbm.at[0, 0, 0], rho_hbm.at[1, 0, 0])
    copies = start_all([pltpu.make_async_copy(source, raw.at[at], sems.at[at]) for at, source in enumerate(sources)])
    owners = pltpu.make_async_copy(atom_hbm, atom_ref, atom_sem)
    owners.start()
    order = order_of()
    flags.wait()
    keeps = [cutoff_ref[0, 0, offset].astype(f32) for offset in order]
    for kind, copy in enumerate(copies):
        copy.wait()
        for place, offset in enumerate(order):
            block = raw[kind, offset]
            if place > 0:
                block = block * keeps[place]
            if kind == 0:
                store((ham_high, ham_low), cols(place), split(block))
            else:
                held[kind - 1, place] = block
                rows = slice((kind - 1) * B, kind * B)
                left_high[rows, cols(place)], left_low[rows, cols(place)] = split(block)
    owners.wait()
    atoms = jnp.broadcast_to(atom_ref[0], (ATOMS, B))
    members[...] = (-(lax.broadcasted_iota(jnp.int32, (ATOMS, B), 0) == atoms).astype(f32)).astype(bf16)


def first_half(left, place, start, near, diagonal):
    both = dot(part(left, slice(0, 3 * B), cols(place)), beside(split(near[0]), split(near[3])))
    mixed = split(start[:, cols(place)] + both[:, :B])
    prop, inner = rows_of(mixed)
    behind = dot(inner, split(near[1]))
    imag = dot(prop, split(near[2])) - behind[B:]
    return mixed, diagonal + both[:, B:], -behind[:B], imag


def second_half(mixed, near):
    prop, inner = rows_of(mixed)
    ahead = dot(prop, beside(split(near[0]), split(near[2]), split(near[3])))
    behind = dot(inner, split(near[1]))
    return ahead[:, cols(0)], ahead[:, cols(1)] - behind[:B], ahead[:, cols(2)] - behind[B:]


def send_more(more, held, place):
    more[0] = held[1, 0]
    for kind in range(3):
        more[1 + kind] = held[kind, place]


def third_kernel(left_high, left_low, ham_high, ham_low, held, three, der_hbm, start, diagonal, other, der, sem):
    copy = pltpu.make_async_copy(der_hbm, der, sem)
    copy.start()
    left = (left_high, left_low)
    start[...] = dot(part(left, slice(0, 3 * B), cols(0)), part((ham_high, ham_low), slice(0, B), cols(0, 5)))
    mixed, diagonal[...], real, other[1, 0] = first_half(left, 3, start, three, start[:, cols(0)])
    added, other[0, 1], other[1, 1] = second_half(mixed, three[4:])
    other[0, 0] = real + added
    copy.wait()


def four_kernel(
    left_high, left_low, start, diagonal, four, mixed_high, mixed_low, diagonal_out, other
):
    mixed, diagonal_out[...], other[0], other[1] = first_half((left_high, left_low), 4, start, four, diagonal[...])
    mixed_high[...], mixed_low[...] = mixed


def more_kernel(arrived, after, held, one_more, two_more, four_more):
    send_more(one_more, held, 1)
    send_more(two_more, held, 2)
    send_more(four_more, held, 4)


def fourth_kernel(left_high, left_low, start, diagonal, one, mixed_high, mixed_low, diagonal_out, other):
    mixed, diagonal_out[...], other[0], other[1] = first_half((left_high, left_low), 1, start, one, diagonal[...])
    mixed_high[...], mixed_low[...] = mixed


def fifth_kernel(
    left_high, left_low, start, diagonal, held, der_ref, other_one, other_three, other_four, two,
    new, mixed_high, mixed_low, self_high, self_low, real_two, comm, weighted, c1, c2, c3, c4
):
    order = order_of()
    left = (left_high, left_low)
    mixed, total, real_two[...], imag_two = first_half(left, 2, start, two, diagonal[...])
    mixed_high[...], mixed_low[...] = mixed
    at_self = split(total)
    self_high[...], self_low[...] = at_self
    whole = cols(0, 5)
    ahead = dot(part(at_self, slice(0, B), cols(0)), part(left, slice(2 * B, 3 * B), whole))
    behind = dot(part(at_self, slice(2 * B, 3 * B), cols(0)), part(left, slice(0, B), whole))
    imag_comm = ahead - behind
    comm[...] = imag_comm[:, cols(0)] + other_three[1, 1]
    sums = [None] * 3
    for place, column in enumerate((c1, c2, c3, c4), 1):
        imag = (other_one[1], imag_two, other_three[1, 0], other_four[1])[place - 1]
        real_new = held[1, place] + time_step * (imag_comm[:, cols(place)] + imag)
        new[place - 1] = real_new
        for direction in range(3):
            product = real_new * der_ref[direction, 0, 0, order[place]]
            sums[direction] = product if place == 1 else sums[direction] + product
            column[direction : direction + 1, :] = jnp.sum(product, axis=0, keepdims=True)
    for direction in range(3):
        weighted[direction] = sums[direction]


def later_kernel(arrived, c1, c4, c1_out, c4_out):
    c1_out[...] = c1[...]
    c4_out[...] = c4[...]


def real_kernel(
    held, new, left_high, left_low, self_high, self_low, other_one, real_two, other_three, other_four, weighted,
    imag_part, high_four, low_four, four, out_hbm, comm, imag_out, row_part, imag_new, sems
):
    order = order_of()
    copies = start_all(
        [pltpu.make_async_copy(new.at[at], out_hbm.at[0, 0, 0, order[1 + at]], sems.at[0, at]) for at in range(4)]
    )
    left = (left_high, left_low)
    whole = cols(0, 5)
    at_self = (self_high, self_low)
    ahead = dot(part(at_self, slice(0, B), cols(0)), part(left, slice(B, 2 * B), whole))
    behind = dot(part(at_self, slice(B, 2 * B), cols(0)), part(left, slice(0, B), whole))
    real_comm = ahead - behind
    added, real_four, imag_four = second_half((high_four[...], low_four[...]), four)
    imag_out[...] = imag_part[...] + imag_four
    for at, (place, other) in enumerate(((3, other_three[0, 0]), (4, other_four[0] + added))):
        imag_new[at] = held[2, place] - time_step * (real_comm[:, cols(place)] + other)
        copies += start_all(
            [pltpu.make_async_copy(imag_new.at[at], out_hbm.at[1, 0, 0, order[place]], sems.at[1, at])]
        )
    comm[0] = real_comm[:, cols(0)] + other_three[0, 1] + real_four
    comm[1] = real_comm[:, cols(1)] + other_one[0]
    comm[2] = real_comm[:, cols(2)] + real_two[...]
    for direction in range(3):
        row_part[direction : direction + 1, :] = jnp.sum(weighted[direction].T, axis=0, keepdims=True)
    for copy in copies:
        copy.wait()


def sixth_kernel(
    held, der_ref, members, high_one, low_one, high_two, low_two, imag_part, comm, row_part, one, two, c1, c2, c3, c4, old_hbm,
    out_hbm, forces_hbm, new, forces_ref, sems
):
    order = order_of()
    prop, inner = rows_of(beside((high_one[...], low_one[...]), (high_two[...], low_two[...])))
    near = [tuple(jnp.concatenate(x, axis=0) for x in zip(split(one[1 + kind]), split(two[1 + kind]))) for kind in range(3)]
    behind = dot(inner, near[0])
    real_new = held[1, 0] + time_step * (imag_part[...] + dot(prop, near[2]) - behind[B:])
    new[0] = real_new
    copies = start_all([pltpu.make_async_copy(new.at[0], out_hbm.at[0, 0, 0, 0], sems.at[0])])
    new[1] = held[2, 0] - time_step * (comm[0] + dot(prop, near[1]) - behind[:B])
    for place, message, mixed in ((1, one, (high_one, low_one)), (2, two, (high_two, low_two))):
        added = dot(rows_of((mixed[0][...], mixed[1][...]))[0], split(message[0]))
        new[1 + place] = held[2, place] - time_step * (comm[place] + added)
    copies += start_all(
        [pltpu.make_async_copy(new.at[1 + at], out_hbm.at[1, 0, 0, order[at]], sems.at[1 + at]) for at in range(3)]
    )
    parts = []
    for direction in range(3):
        product = real_new * der_ref[direction, 0, 0, 0]
        parts.append(jnp.sum(product + product.T, axis=0, keepdims=True))
    orbital = jnp.concatenate(parts, axis=0) + row_part[...] + ((c1[...] + c2[...]) + (c3[...] + c4[...]))
    high, low = [
        lax.dot_general(some, members[...], (((1,), (1,)), ((), ())), preferred_element_type=f32) for some in split(orbital)
    ]
    forces = high + low
    for direction in range(3):
        forces_ref[direction] = forces[direction : direction + 1]
    copies += start_all([pltpu.make_async_copy(forces_ref, forces_hbm, sems.at[4])])
    for copy in copies:
        copy.wait()


def call(kernel, shapes, in_specs, products, args, out_specs=None, scratch=(), aliases={}):
    moved = sum(4 * x.size for x in args) + sum(4 * x.size for x in shapes)
    return pl.pallas_call(
        kernel,
        out_shape=shapes,
        in_specs=in_specs,
        out_specs=out_specs or [vmem] * len(shapes),
        scratch_shapes=scratch,
        input_output_aliases=aliases,
        compiler_params=pltpu.CompilerParams(vmem_limit_bytes=32 * 2**20),
        cost_estimate=pl.CostEstimate(flops=products * 6 * B**3, bytes_accessed=moved, transcendentals=0),
    )(*args)


def local(hamiltonian, inverse_margin, density, cutoff, derivative, atom_of):
    def shape(*dims, kind=f32):
        return jax.ShapeDtypeStruct(dims, kind)

    args = (hamiltonian, inverse_margin, density, cutoff, derivative, atom_of)
    hamiltonian, inverse_margin, density, cutoff, derivative, atom_of = (
        pltpu.with_memory_space_constraint(x, pltpu.HBM) for x in args
    )
    flags = pltpu.SMEM((1, 1, 5), jnp.int32)
    message = shape(4, B, B)
    first_one, rest = call(
        first_kernel,
        [message, shape(2, B, B)],
        [hbm] * 4,
        0,
        (cutoff, hamiltonian, inverse_margin, density),
        scratch=[pltpu.VMEM((5, B, B), f32), flags, dma(()), dma((3,))],
    )
    near_one = swapped(first_one, 1)
    (first_four,) = call(functools.partial(next_kernel, 0), [message], [vmem] * 2, 0, (first_one, rest))
    near_four = swapped(first_four, 4)
    (first_two,) = call(functools.partial(next_kernel, 1), [message], [vmem] * 2, 500, (first_four, rest))
    near_two = swapped(first_two, 2)
    (send_three,) = call(
        whole_first_kernel,
        [shape(8, B, B)],
        [hbm] * 4 + [vmem],
        500,
        (cutoff, hamiltonian, inverse_margin, density, first_two),
        scratch=[flags, dma(()), dma((5,))],
    )
    near_three = swapped(send_three, 3)
    left = [shape(3 * B, 5 * B, kind=bf16)] * 2
    ham = [shape(B, 5 * B, kind=bf16)] * 2
    held, left_high, left_low, ham_high, ham_low, members = call(
        second_kernel,
        [shape(3, 5, B, B)] + left + ham + [shape(ATOMS, B, kind=bf16)],
        [hbm] * 6,
        2000,
        (cutoff, hamiltonian, inverse_margin, density, atom_of, send_three),
        scratch=[pltpu.VMEM((4, 5, B, B), f32), flags, pltpu.VMEM((1, 1, B), jnp.int32), dma(()), dma(()), dma((4,))],
    )
    mixed = [shape(3 * B, B, kind=bf16)] * 2
    both = shape(2, 2, B, B)
    start, diagonal, other_three, derivative = call(
        third_kernel,
        [shape(3 * B, 5 * B), shape(3 * B, B), shape(2, 2, B, B), shape(*derivative.shape)],
        [vmem] * 6 + [hbm],
        8000,
        (left_high, left_low, ham_high, ham_low, held, near_three, derivative),
        scratch=[dma(())],
    )
    one_more, two_more, four_more = call(more_kernel, [message] * 3, [vmem] * 3, 300, (near_four, other_three, held))
    near_four_more = swapped(four_more, 4)
    near_one_more = swapped(one_more, 1)
    near_two_more = swapped(two_more, 2)
    high_four, low_four, diagonal, other_four = call(
        four_kernel,
        mixed + [shape(3 * B, B), shape(2, B, B)],
        [vmem] * 5,
        8,
        (left_high, left_low, start, diagonal, near_four),
    )
    high_one, low_one, diagonal, other_one = call(
        fourth_kernel,
        mixed + [shape(3 * B, B), shape(2, B, B)],
        [vmem] * 5,
        10,
        (left_high, left_low, start, diagonal, near_one),
    )
    block = shape(B, B)
    new, high_two, low_two, self_high, self_low, real_two, imag_part, weighted, *columns = call(
        fifth_kernel,
        [message] + mixed * 2 + [block, block, shape(3, B, B)] + [shape(3, B)] * 4,
        [vmem] * 10,
        22,
        (left_high, left_low, start, diagonal, held, derivative, other_one, other_three, other_four, near_two),
    )
    c1, c2, c3, c4 = columns
    c2, c3 = swapped(c2, 2), swapped(c3, 3)
    c1, c4 = call(later_kernel, [shape(3, B)] * 2, [vmem] * 3, 0, (c3, c1, c4))
    columns = (swapped(c1, 1), c2, c3, swapped(c4, 4))
    args = (held, new, left_high, left_low, self_high, self_low, other_one, real_two, other_three, other_four, weighted)
    args += (imag_part, high_four, low_four, near_four_more)
    out, comm, imag_part, row_part = call(
        real_kernel,
        [shape(*density.shape), shape(3, B, B), shape(B, B), shape(3, B)],
        [vmem] * 15,
        10,
        args,
        out_specs=[hbm] + [vmem] * 3,
        scratch=[pltpu.VMEM((2, B, B), f32), dma((2, 4))],
    )
    args = (held, derivative, members, high_one, low_one, high_two, low_two, imag_part, comm, row_part)
    args += (near_one_more, near_two_more, *columns, out)
    new_density, forces = call(
        sixth_kernel,
        [shape(*density.shape), shape(3, 1, ATOMS)],
        [vmem] * 16 + [hbm],
        10,
        args,
        out_specs=[hbm, hbm],
        scratch=[pltpu.VMEM((4, B, B), f32), pltpu.VMEM((3, 1, ATOMS), f32), dma((5,))],
        aliases={16: 0},
    )
    return new_density, forces.reshape(1, 1, 3, ATOMS)


def solution(mesh):
    placed = (
        P("gx", "gy", None, None, None),
        P("gx", "gy", None, None, None),
        P(None, "gx", "gy", None, None, None),
        P("gx", "gy", None),
        P(None, "gx", "gy", None, None, None),
        P("gx", "gy", None),
    )
    return jax.shard_map(
        local,
        mesh=mesh,
        in_specs=placed,
        out_specs=(P(None, "gx", "gy", None, None, None), P("gx", "gy", None, None)),
        check_vma=False,
    )
```

```python
import functools

import jax
import jax.numpy as jnp
from jax import lax
from jax.experimental import pallas as pl
from jax.experimental.pallas import tpu as pltpu
from jax.sharding import PartitionSpec as P

B = 128
ATOMS = 64

time_step = 0.25
vmem = pl.BlockSpec(memory_space=pltpu.VMEM)
hbm = pl.BlockSpec(memory_space=pltpu.HBM)
f32 = jnp.float32
bf16 = jnp.bfloat16
dma = pltpu.SemaphoreType.DMA


def swapped(cells, edge):
    axis = "gx" if edge < 3 else "gy"
    count = lax.axis_size(axis)
    assert count % 2 == 0
    first = 0 if edge in (1, 3) else 1
    pairs = []
    for i in range(first, count, 2):
        j = (i + 1) % count
        pairs += [(i, j), (j, i)]
    return lax.ppermute(cells, axis, pairs)


def order_of():
    odd_x = lax.rem(lax.axis_index("gx"), 2)
    odd_y = lax.rem(lax.axis_index("gy"), 2)
    return 0, 1 + odd_x, 2 - odd_x, 3 + odd_y, 4 - odd_y


def cols(place, count=1):
    return slice(place * B, (place + count) * B)


def split(values):
    high = values.astype(bf16)
    return high, (values - high.astype(f32)).astype(bf16)


def beside(*pairs):
    return tuple(jnp.concatenate(parts, axis=1) for parts in zip(*pairs))


def dot(left, right):
    def one(a, b):
        return jnp.dot(a, b, preferred_element_type=f32)

    return one(left[0], right[0]) + (one(left[0], right[1]) + one(left[1], right[0]))


def part(pair, rows, columns):
    return pair[0][rows, columns], pair[1][rows, columns]


def rows_of(pair):
    return (pair[0][:B], pair[1][:B]), (pair[0][B:], pair[1][B:])


def store(pair, columns, values):
    pair[0][:, columns], pair[1][:, columns] = values


def start_all(copies):
    for copy in copies:
        copy.start()
    return copies


def first_kernel(cutoff_hbm, ham_hbm, inv_hbm, rho_hbm, one, rest, ham, cutoff_ref, cutoff_sem, sems):
    flags = pltpu.make_async_copy(cutoff_hbm, cutoff_ref, cutoff_sem)
    flags.start()
    copies = start_all(
        [
            pltpu.make_async_copy(ham_hbm.at[0, 0], ham, sems.at[0]),
            pltpu.make_async_copy(inv_hbm.at[0, 0, 0], one.at[1], sems.at[1]),
            pltpu.make_async_copy(rho_hbm.at[1, 0, 0, 0], one.at[2], sems.at[2]),
        ]
    )
    order = order_of()
    flags.wait()
    for copy in copies:
        copy.wait()
    one[0] = ham[0]
    for target, at, place in ((one, 3, 1), (rest, 0, 4), (rest, 1, 2)):
        target[at] = ham[order[place]] * cutoff_ref[0, 0, order[place]].astype(f32)


def next_kernel(at, message, rest, out):
    out[:3] = message[:3]
    out[3] = rest[at]


def whole_first_kernel(cutoff_hbm, ham_hbm, inv_hbm, rho_hbm, message, out, cutoff_ref, cutoff_sem, sems):
    flags = pltpu.make_async_copy(cutoff_hbm, cutoff_ref, cutoff_sem)
    flags.start()
    offset = order_of()[3]
    sources = (ham_hbm.at[0, 0, offset], rho_hbm.at[0, 0, 0, 0], inv_hbm.at[0, 0, offset], rho_hbm.at[0, 0, 0, offset])
    sources += (rho_hbm.at[1, 0, 0, offset],)
    copies = start_all([pltpu.make_async_copy(source, out.at[3 + at], sems.at[at]) for at, source in enumerate(sources)])
    out[:3] = message[:3]
    flags.wait()
    keep = cutoff_ref[0, 0, offset].astype(f32)
    for copy in copies:
        copy.wait()
    for at in (3, 5, 6, 7):
        out[at] = out[at] * keep


def second_kernel(
    cutoff_hbm, ham_hbm, inv_hbm, rho_hbm, atom_hbm, after, held, left_high, left_low, ham_high, ham_low, members,
    raw, cutoff_ref, atom_ref, cutoff_sem, atom_sem, sems
):
    flags = pltpu.make_async_copy(cutoff_hbm, cutoff_ref, cutoff_sem)
    flags.start()
    sources = (ham_hbm.at[0, 0], inv_hbm.at[0, 0], rho_hbm.at[0, 0, 0], rho_hbm.at[1, 0, 0])
    copies = start_all([pltpu.make_async_copy(source, raw.at[at], sems.at[at]) for at, source in enumerate(sources)])
    owners = pltpu.make_async_copy(atom_hbm, atom_ref, atom_sem)
    owners.start()
    order = order_of()
    flags.wait()
    keeps = [cutoff_ref[0, 0, offset].astype(f32) for offset in order]
    for kind, copy in enumerate(copies):
        copy.wait()
        for place, offset in enumerate(order):
            block = raw[kind, offset]
            if place > 0:
                block = block * keeps[place]
            if kind == 0:
                store((ham_high, ham_low), cols(place), split(block))
            else:
                held[kind - 1, place] = block
                rows = slice((kind - 1) * B, kind * B)
                left_high[rows, cols(place)], left_low[rows, cols(place)] = split(block)
    owners.wait()
    atoms = jnp.broadcast_to(atom_ref[0], (ATOMS, B))
    members[...] = (-(lax.broadcasted_iota(jnp.int32, (ATOMS, B), 0) == atoms).astype(f32)).astype(bf16)


def first_half(left, place, start, near, diagonal):
    both = dot(part(left, slice(0, 3 * B), cols(place)), beside(split(near[0]), split(near[3])))
    mixed = split(start[:, cols(place)] + both[:, :B])
    prop, inner = rows_of(mixed)
    behind = dot(inner, split(near[1]))
    imag = dot(prop, split(near[2])) - behind[B:]
    return mixed, diagonal + both[:, B:], -behind[:B], imag


def second_half(mixed, near):
    prop, inner = rows_of(mixed)
    ahead = dot(prop, beside(split(near[0]), split(near[2]), split(near[3])))
    behind = dot(inner, split(near[1]))
    return ahead[:, cols(0)], ahead[:, cols(1)] - behind[:B], ahead[:, cols(2)] - behind[B:]


def send_more(more, held, place):
    more[0] = held[1, 0]
    for kind in range(3):
        more[1 + kind] = held[kind, place]


def third_kernel(left_high, left_low, ham_high, ham_low, held, three, der_hbm, start, diagonal, other, der, sem):
    copy = pltpu.make_async_copy(der_hbm, der, sem)
    copy.start()
    left = (left_high, left_low)
    start[...] = dot(part(left, slice(0, 3 * B), cols(0)), part((ham_high, ham_low), slice(0, B), cols(0, 5)))
    mixed, diagonal[...], real, other[1, 0] = first_half(left, 3, start, three, start[:, cols(0)])
    added, other[0, 1], other[1, 1] = second_half(mixed, three[4:])
    other[0, 0] = real + added
    copy.wait()


def four_kernel(
    left_high, left_low, start, diagonal, four, mixed_high, mixed_low, diagonal_out, other
):
    mixed, diagonal_out[...], other[0], other[1] = first_half((left_high, left_low), 4, start, four, diagonal[...])
    mixed_high[...], mixed_low[...] = mixed


def more_kernel(arrived, after, held, one_more, two_more, four_more):
    send_more(one_more, held, 1)
    send_more(two_more, held, 2)
    send_more(four_more, held, 4)


def fourth_kernel(left_high, left_low, start, diagonal, one, mixed_high, mixed_low, diagonal_out, other):
    mixed, diagonal_out[...], other[0], other[1] = first_half((left_high, left_low), 1, start, one, diagonal[...])
    mixed_high[...], mixed_low[...] = mixed


def fifth_kernel(
    left_high, left_low, start, diagonal, held, der_ref, other_one, other_three, other_four, two,
    new, mixed_high, mixed_low, self_high, self_low, real_two, comm, weighted, c1, c2, c3, c4
):
    order = order_of()
    left = (left_high, left_low)
    mixed, total, real_two[...], imag_two = first_half(left, 2, start, two, diagonal[...])
    mixed_high[...], mixed_low[...] = mixed
    at_self = split(total)
    self_high[...], self_low[...] = at_self
    whole = cols(0, 5)
    ahead = dot(part(at_self, slice(0, B), cols(0)), part(left, slice(2 * B, 3 * B), whole))
    behind = dot(part(at_self, slice(2 * B, 3 * B), cols(0)), part(left, slice(0, B), whole))
    imag_comm = ahead - behind
    comm[...] = imag_comm[:, cols(0)] + other_three[1, 1]
    sums = [None] * 3
    for place, column in enumerate((c1, c2, c3, c4), 1):
        imag = (other_one[1], imag_two, other_three[1, 0], other_four[1])[place - 1]
        real_new = held[1, place] + time_step * (imag_comm[:, cols(place)] + imag)
        new[place - 1] = real_new
        for direction in range(3):
            product = real_new * der_ref[direction, 0, 0, order[place]]
            sums[direction] = product if place == 1 else sums[direction] + product
            column[direction : direction + 1, :] = jnp.sum(product, axis=0, keepdims=True)
    for direction in range(3):
        weighted[direction] = sums[direction]


def later_kernel(arrived, c1, c4, c1_out, c4_out):
    c1_out[...] = c1[...]
    c4_out[...] = c4[...]


def real_kernel(
    held, new, left_high, left_low, self_high, self_low, other_one, real_two, other_three, other_four, weighted,
    imag_part, high_four, low_four, four, out_hbm, comm, imag_out, row_part, imag_new, sems
):
    order = order_of()
    copies = start_all(
        [pltpu.make_async_copy(new.at[at], out_hbm.at[0, 0, 0, order[1 + at]], sems.at[0, at]) for at in range(4)]
    )
    left = (left_high, left_low)
    whole = cols(0, 5)
    at_self = (self_high, self_low)
    ahead = dot(part(at_self, slice(0, B), cols(0)), part(left, slice(B, 2 * B), whole))
    behind = dot(part(at_self, slice(B, 2 * B), cols(0)), part(left, slice(0, B), whole))
    real_comm = ahead - behind
    added, real_four, imag_four = second_half((high_four[...], low_four[...]), four)
    imag_out[...] = imag_part[...] + imag_four
    for at, (place, other) in enumerate(((3, other_three[0, 0]), (4, other_four[0] + added))):
        imag_new[at] = held[2, place] - time_step * (real_comm[:, cols(place)] + other)
        copies += start_all(
            [pltpu.make_async_copy(imag_new.at[at], out_hbm.at[1, 0, 0, order[place]], sems.at[1, at])]
        )
    comm[0] = real_comm[:, cols(0)] + other_three[0, 1] + real_four
    comm[1] = real_comm[:, cols(1)] + other_one[0]
    comm[2] = real_comm[:, cols(2)] + real_two[...]
    for direction in range(3):
        row_part[direction : direction + 1, :] = jnp.sum(weighted[direction].T, axis=0, keepdims=True)
    for copy in copies:
        copy.wait()


def sixth_kernel(
    held, der_ref, members, high_one, low_one, high_two, low_two, imag_part, comm, row_part, one, two, c1, c2, c3, c4, old_hbm,
    out_hbm, forces_hbm, new, forces_ref, sems
):
    order = order_of()
    prop, inner = rows_of(beside((high_one[...], low_one[...]), (high_two[...], low_two[...])))
    near = [tuple(jnp.concatenate(x, axis=0) for x in zip(split(one[1 + kind]), split(two[1 + kind]))) for kind in range(3)]
    behind = dot(inner, near[0])
    ahead = dot(prop, beside(near[2], near[1]))
    real_new = held[1, 0] + time_step * (imag_part[...] + ahead[:, :B] - behind[B:])
    new[0] = real_new
    copies = start_all([pltpu.make_async_copy(new.at[0], out_hbm.at[0, 0, 0, 0], sems.at[0])])
    new[1] = held[2, 0] - time_step * (comm[0] + ahead[:, B:] - behind[:B])
    for place, message, mixed in ((1, one, (high_one, low_one)), (2, two, (high_two, low_two))):
        added = dot(rows_of((mixed[0][...], mixed[1][...]))[0], split(message[0]))
        new[1 + place] = held[2, place] - time_step * (comm[place] + added)
    copies += start_all(
        [pltpu.make_async_copy(new.at[1 + at], out_hbm.at[1, 0, 0, order[at]], sems.at[1 + at]) for at in range(3)]
    )
    parts = []
    for direction in range(3):
        product = real_new * der_ref[direction, 0, 0, 0]
        parts.append(jnp.sum(product + product.T, axis=0, keepdims=True))
    orbital = jnp.concatenate(parts, axis=0) + row_part[...] + ((c1[...] + c2[...]) + (c3[...] + c4[...]))
    high, low = [
        lax.dot_general(some, members[...], (((1,), (1,)), ((), ())), preferred_element_type=f32) for some in split(orbital)
    ]
    forces = high + low
    for direction in range(3):
        forces_ref[direction] = forces[direction : direction + 1]
    copies += start_all([pltpu.make_async_copy(forces_ref, forces_hbm, sems.at[4])])
    for copy in copies:
        copy.wait()


def call(kernel, shapes, in_specs, products, args, out_specs=None, scratch=(), aliases={}):
    moved = sum(4 * x.size for x in args) + sum(4 * x.size for x in shapes)
    return pl.pallas_call(
        kernel,
        out_shape=shapes,
        in_specs=in_specs,
        out_specs=out_specs or [vmem] * len(shapes),
        scratch_shapes=scratch,
        input_output_aliases=aliases,
        compiler_params=pltpu.CompilerParams(vmem_limit_bytes=32 * 2**20),
        cost_estimate=pl.CostEstimate(flops=products * 6 * B**3, bytes_accessed=moved, transcendentals=0),
    )(*args)


def local(hamiltonian, inverse_margin, density, cutoff, derivative, atom_of):
    def shape(*dims, kind=f32):
        return jax.ShapeDtypeStruct(dims, kind)

    args = (hamiltonian, inverse_margin, density, cutoff, derivative, atom_of)
    hamiltonian, inverse_margin, density, cutoff, derivative, atom_of = (
        pltpu.with_memory_space_constraint(x, pltpu.HBM) for x in args
    )
    flags = pltpu.SMEM((1, 1, 5), jnp.int32)
    message = shape(4, B, B)
    first_one, rest = call(
        first_kernel,
        [message, shape(2, B, B)],
        [hbm] * 4,
        0,
        (cutoff, hamiltonian, inverse_margin, density),
        scratch=[pltpu.VMEM((5, B, B), f32), flags, dma(()), dma((3,))],
    )
    near_one = swapped(first_one, 1)
    (first_four,) = call(functools.partial(next_kernel, 0), [message], [vmem] * 2, 0, (first_one, rest))
    near_four = swapped(first_four, 4)
    (first_two,) = call(functools.partial(next_kernel, 1), [message], [vmem] * 2, 500, (first_four, rest))
    near_two = swapped(first_two, 2)
    (send_three,) = call(
        whole_first_kernel,
        [shape(8, B, B)],
        [hbm] * 4 + [vmem],
        500,
        (cutoff, hamiltonian, inverse_margin, density, first_two),
        scratch=[flags, dma(()), dma((5,))],
    )
    near_three = swapped(send_three, 3)
    left = [shape(3 * B, 5 * B, kind=bf16)] * 2
    ham = [shape(B, 5 * B, kind=bf16)] * 2
    held, left_high, left_low, ham_high, ham_low, members = call(
        second_kernel,
        [shape(3, 5, B, B)] + left + ham + [shape(ATOMS, B, kind=bf16)],
        [hbm] * 6,
        2000,
        (cutoff, hamiltonian, inverse_margin, density, atom_of, send_three),
        scratch=[pltpu.VMEM((4, 5, B, B), f32), flags, pltpu.VMEM((1, 1, B), jnp.int32), dma(()), dma(()), dma((4,))],
    )
    mixed = [shape(3 * B, B, kind=bf16)] * 2
    both = shape(2, 2, B, B)
    start, diagonal, other_three, derivative = call(
        third_kernel,
        [shape(3 * B, 5 * B), shape(3 * B, B), shape(2, 2, B, B), shape(*derivative.shape)],
        [vmem] * 6 + [hbm],
        8000,
        (left_high, left_low, ham_high, ham_low, held, near_three, derivative),
        scratch=[dma(())],
    )
    one_more, two_more, four_more = call(more_kernel, [message] * 3, [vmem] * 3, 300, (near_four, other_three, held))
    near_four_more = swapped(four_more, 4)
    near_one_more = swapped(one_more, 1)
    near_two_more = swapped(two_more, 2)
    high_four, low_four, diagonal, other_four = call(
        four_kernel,
        mixed + [shape(3 * B, B), shape(2, B, B)],
        [vmem] * 5,
        8,
        (left_high, left_low, start, diagonal, near_four),
    )
    high_one, low_one, diagonal, other_one = call(
        fourth_kernel,
        mixed + [shape(3 * B, B), shape(2, B, B)],
        [vmem] * 5,
        10,
        (left_high, left_low, start, diagonal, near_one),
    )
    block = shape(B, B)
    new, high_two, low_two, self_high, self_low, real_two, imag_part, weighted, *columns = call(
        fifth_kernel,
        [message] + mixed * 2 + [block, block, shape(3, B, B)] + [shape(3, B)] * 4,
        [vmem] * 10,
        22,
        (left_high, left_low, start, diagonal, held, derivative, other_one, other_three, other_four, near_two),
    )
    c1, c2, c3, c4 = columns
    c2, c3 = swapped(c2, 2), swapped(c3, 3)
    c1, c4 = call(later_kernel, [shape(3, B)] * 2, [vmem] * 3, 0, (c3, c1, c4))
    columns = (swapped(c1, 1), c2, c3, swapped(c4, 4))
    args = (held, new, left_high, left_low, self_high, self_low, other_one, real_two, other_three, other_four, weighted)
    args += (imag_part, high_four, low_four, near_four_more)
    out, comm, imag_part, row_part = call(
        real_kernel,
        [shape(*density.shape), shape(3, B, B), shape(B, B), shape(3, B)],
        [vmem] * 15,
        10,
        args,
        out_specs=[hbm] + [vmem] * 3,
        scratch=[pltpu.VMEM((2, B, B), f32), dma((2, 4))],
    )
    args = (held, derivative, members, high_one, low_one, high_two, low_two, imag_part, comm, row_part)
    args += (near_one_more, near_two_more, *columns, out)
    new_density, forces = call(
        sixth_kernel,
        [shape(*density.shape), shape(3, 1, ATOMS)],
        [vmem] * 16 + [hbm],
        10,
        args,
        out_specs=[hbm, hbm],
        scratch=[pltpu.VMEM((4, B, B), f32), pltpu.VMEM((3, 1, ATOMS), f32), dma((5,))],
        aliases={16: 0},
    )
    return new_density, forces.reshape(1, 1, 3, ATOMS)


def solution(mesh):
    placed = (
        P("gx", "gy", None, None, None),
        P("gx", "gy", None, None, None),
        P(None, "gx", "gy", None, None, None),
        P("gx", "gy", None),
        P(None, "gx", "gy", None, None, None),
        P("gx", "gy", None),
    )
    return jax.shard_map(
        local,
        mesh=mesh,
        in_specs=placed,
        out_specs=(P(None, "gx", "gy", None, None, None), P("gx", "gy", None, None)),
        check_vma=False,
    )
```
